32 devices in a mesh: fsdp: 16 (over z, y, x), seq: 2 (over core).
Axes of the slice: x: 2, y: 2, z: 4, core: 2. Of those that a mesh axis runs over, the one named last changes fastest.
Arguments:
- tokens: bfloat16 [2, 16, 1024, 768], P(None, 'fsdp', 'seq'), may hold values from -6 to 6
- lengths: int32 [2, 16], P(None, 'fsdp'), may hold values from 256 to 1024, as said below
- norm_gain: float32 [768], replicated, may hold values from 0.1 to 1.9
- in_weight: bfloat16 [768, 3352], P(('fsdp', 'seq')), may hold values from -0.21875 to 0.21875
- conv_weight: float32 [4, 1792], replicated, may hold values from -3 to 3
- conv_bias: float32 [1792], replicated, may hold values from -3 to 3
- dt_bias: float32 [24], replicated, may hold values from -7 to -3
- a_log: float32 [24], replicated, may hold values from 0 to 2.77
- skip_gain: float32 [24], replicated, may hold values from 0.5 to 2
- out_gain: float32 [1536], replicated, may hold values from 0.1 to 1.9
- out_weight: bfloat16 [1536, 768], P(None, ('fsdp', 'seq')), may hold values from -0.15625 to 0.15625
- out_grad: bfloat16 [2, 16, 1024, 768], P(None, 'fsdp', 'seq'), may hold values from -6 to 6
Outputs:
- mixed: bfloat16 [2, 16, 1024, 768], P(None, 'fsdp', 'seq')
- tokens_grad: float32 [2, 16, 1024, 768], P(None, 'fsdp', 'seq')
- norm_gain_grad: float32 [768], replicated
- in_weight_grad: float32 [768, 3352], P(('fsdp', 'seq'))
- conv_weight_grad: float32 [4, 1792], replicated
- conv_bias_grad: float32 [1792], replicated
- dt_bias_grad: float32 [24], replicated
- a_log_grad: float32 [24], replicated
- skip_gain_grad: float32 [24], replicated
- out_gain_grad: float32 [1536], replicated
- out_weight_grad: float32 [1536, 768], P(None, ('fsdp', 'seq'))
The draws below stay inside these ranges and needn't reach their ends.
Inputs may be any that keep to these rules, and one draw needn't show every extreme that they name: `lengths`: among the 2 slots of each slot index s, one chosen from the seed has length 1024 and another 256; any others are drawn evenly between.
All inputs are finite; a program needn't handle non-finite values.
Results may differ from the reference program's by a relative error of at most 0.012.
Values may be sent and summed in bfloat16 or wider, within the bound.
A program may use at most 256 MiB of HBM per device.

```python
import jax
import jax.numpy as jnp
from jax import lax

D = 768
HEADS = 24
HEADDIM = 64
NSTATE = 128
CONV = 4
GROUP = 256
MB = 2
INNER = 1536
CONVCH = 1792
PROJ = 3352
SLOT_LEN = 1024
MINLEN = 256
SLOTS = 16


def draw_lengths(key, part):
    key = jax.random.fold_in(key, 7)
    uneven = jax.random.randint(jax.random.fold_in(key, 1), (MB, SLOTS), MINLEN, SLOT_LEN + 1)
    column_keys = jax.random.split(jax.random.fold_in(key, 2), SLOTS)
    ranking = jax.vmap(lambda column: jax.random.permutation(column, MB))(column_keys)
    ranking = jnp.transpose(ranking)
    longest = jnp.where(ranking == 0, SLOT_LEN, uneven)
    return jnp.where(ranking == 1, MINLEN, longest).astype(jnp.int32)


def with_spikes(values, key, source, target, blocks, factor):
    owner, partner = [(jnp.arange(values.shape[dim]) // (values.shape[dim] // blocks)).reshape([-1 if axis == dim else 1 for axis in range(values.ndim)]) for dim in (source, target)]
    chosen = jax.random.permutation(key, blocks)[partner]
    strong = (owner == chosen) | (owner == (partner + blocks // 2) % blocks)
    return jnp.where(strong, factor * values, values)


def level_of(key, extent, pieces, low, top_value):
    gain = 1.0
    for dim, blocks in pieces:
        steps = jax.random.uniform(jax.random.fold_in(jax.random.fold_in(key, 6), dim), (blocks,), jnp.float32, low / len(pieces), top_value / len(pieces))
        gain = gain * jnp.repeat(jnp.exp(steps), extent[dim] // blocks).reshape((-1,) + (1,) * (len(extent) - 1 - dim))
    return gain


def normal_values(own_key, dims, width, reach, pieces=(), kind=jnp.bfloat16):
    drawn = width * jax.random.normal(own_key, dims, jnp.float32)
    if pieces:
        drawn = drawn * level_of(own_key, dims, pieces, -0.22, 0.18)
    return jnp.clip(drawn, -reach, reach).astype(kind)


def bell_draw_with(rng, dims, width, reach, cuts, heavy, kind=jnp.bfloat16):
    drawn = width * jax.random.normal(rng, dims, jnp.float32)
    if cuts:
        drawn = drawn * level_of(rng, dims, cuts, -0.22, 0.18)
    return jnp.clip(with_spikes(drawn, jax.random.fold_in(rng, 3), *heavy), -reach, reach).astype(kind)


def setup_inputs(seed: int = 0) -> dict:
    seeds = jax.random.split(jax.random.key(seed), 13)
    tokens = normal_values(seeds[0], (MB, SLOTS, SLOT_LEN, D), 1.0, 6.0, ((1, 16), (2, 2)))
    lengths = draw_lengths(jax.random.fold_in(seeds[12], 71), 0)
    norm_gain = jnp.clip(1.0 + 0.18 * jax.random.normal(seeds[2], (D,), jnp.float32), 0.1, 1.9)
    in_weight = normal_values(seeds[3], (D, PROJ), D ** -0.5, 0.21875, ((0, 32),))
    conv_weight = normal_values(seeds[4], (CONV, CONVCH), CONV ** -0.5, 3.0, (), jnp.float32)
    conv_bias = normal_values(seeds[5], (CONVCH,), 0.5, 3.0, (), jnp.float32)
    dt_bias = jnp.clip(jax.random.uniform(seeds[6], (HEADS,), jnp.float32, -7.0, -3.0), -7.0, -3.0)
    a_log = jnp.clip(jax.random.uniform(seeds[7], (HEADS,), jnp.float32, 0.0, 2.77), 0.0, 2.77)
    skip_gain = jnp.clip(jax.random.uniform(seeds[8], (HEADS,), jnp.float32, 0.5, 2.0), 0.5, 2.0)
    out_gain = jnp.clip(1.0 + 0.18 * jax.random.normal(seeds[9], (INNER,), jnp.float32), 0.1, 1.9)
    out_weight = normal_values(seeds[10], (INNER, D), INNER ** -0.5, 0.15625, ((1, 32),))
    out_grad = bell_draw_with(seeds[11], (MB, SLOTS, SLOT_LEN, D), 1.0, 6.0, ((1, 16), (2, 2)), (1, 3, 16, 2.0))
    return {"tokens": tokens, "lengths": lengths, "norm_gain": norm_gain, "in_weight": in_weight, "conv_weight": conv_weight, "conv_bias": conv_bias, "dt_bias": dt_bias, "a_log": a_log, "skip_gain": skip_gain, "out_gain": out_gain, "out_weight": out_weight, "out_grad": out_grad}


eps_norm = 1e-05

@jax.custom_vjp
def low(v):
    return lax.optimization_barrier(v.astype(jnp.bfloat16)).astype(jnp.float32)

@jax.custom_vjp
def low_back(v):
    return v

def low_keep(v):
    return (low(v), None)

def low_pass(kept, grad):
    return (grad,)

def back_keep(v):
    return (v, None)

def back_low(kept, grad):
    return (low(grad),)
low.defvjp(low_keep, low_pass)
low_back.defvjp(back_keep, back_low)

def matmul(left_op, right_op):
    return jnp.matmul(left_op, right_op, precision=lax.Precision.HIGHEST)

def within_part(scores, cumulative, step_blocks, x_blocks):
    blocks = x_blocks.shape[0]
    causal = jnp.arange(GROUP)[:, None] >= jnp.arange(GROUP)[None, :]
    cum_heads = jnp.swapaxes(cumulative, 1, 2)
    log_gap = cum_heads[:, :, :, None] - cum_heads[:, :, None, :]
    log_gap = jnp.where(causal, log_gap, 0.0)
    fade_mask = jnp.where(causal, jnp.exp(log_gap), 0.0)
    mixing = low(scores[:, None] * fade_mask * jnp.swapaxes(step_blocks, 1, 2)[:, :, None, :])
    heads_x = x_blocks.reshape(blocks, GROUP, HEADS, HEADDIM).transpose(0, 2, 1, 3)
    within = matmul(mixing, heads_x)
    return within.transpose(0, 2, 1, 3).reshape(blocks, GROUP, INNER)

def state_mixer(conv_out, step_size, log_rate):
    blocks = SLOT_LEN // GROUP
    x_blocks = conv_out[:, :INNER].reshape(blocks, GROUP, INNER)
    key_part = conv_out[:, INNER:INNER + NSTATE].reshape(blocks, GROUP, NSTATE)
    query_part = conv_out[:, INNER + NSTATE:].reshape(blocks, GROUP, NSTATE)
    step_blocks = step_size.reshape(blocks, GROUP, HEADS)
    cumulative = jnp.cumsum(log_rate.reshape(blocks, GROUP, HEADS), axis=1)
    block_total = cumulative[:, -1]
    scores = low_back(matmul(query_part, jnp.swapaxes(key_part, 1, 2)))
    within = within_part(scores, cumulative, step_blocks, x_blocks)
    weight_in = jnp.exp(block_total[:, None, :] - cumulative) * step_blocks
    scaled = low(x_blocks * jnp.repeat(weight_in, HEADDIM, axis=-1))
    states = low_back(matmul(jnp.swapaxes(key_part, 1, 2), scaled))
    running = jnp.zeros((NSTATE, INNER), jnp.float32)
    carried = []
    for ordinal in range(blocks):
        held_state = low(running)
        inner_term = low_back(matmul(query_part[ordinal], held_state))
        carried.append(inner_term * jnp.repeat(jnp.exp(cumulative[ordinal]), HEADDIM, axis=-1))
        running = running * jnp.repeat(jnp.exp(block_total[ordinal]), HEADDIM)[None, :] + states[ordinal]
    return within + jnp.stack(carried)

def mixer_forward(params, seq_x, valid_rows):
    norm_gain, in_weight, conv_weight, conv_bias, dt_bias, a_log, skip_gain, out_gain, out_weight = params
    inv_root = lax.rsqrt(lax.optimization_barrier(jnp.mean(seq_x * seq_x, axis=-1, keepdims=True)) + eps_norm)
    normed = low(seq_x * inv_root * norm_gain)
    projected = low_back(matmul(normed, in_weight))
    gate_part = projected[:, :INNER]
    conv_low = low(projected[:, INNER:INNER + CONVCH])
    dt_raw = projected[:, INNER + CONVCH:]
    padded = jnp.concatenate([jnp.zeros((CONV - 1, CONVCH), jnp.float32), conv_low], axis=0)
    conv_acc = conv_bias + conv_weight[0] * padded[0:SLOT_LEN]
    for ordinal in range(1, CONV):
        conv_acc = conv_acc + conv_weight[ordinal] * padded[ordinal:ordinal + SLOT_LEN]
    conv_out = low(jax.nn.silu(conv_acc))
    step_size = jax.nn.softplus(dt_raw + dt_bias)
    log_rate = step_size * -jnp.exp(a_log)
    mixed_ssd = state_mixer(conv_out, step_size, log_rate).reshape(SLOT_LEN, INNER)
    ssd = low_back(mixed_ssd + jnp.repeat(skip_gain, HEADDIM) * conv_out[:, :INNER])
    gated = ssd * jax.nn.silu(gate_part)
    gate_root = lax.rsqrt(lax.optimization_barrier(jnp.mean(gated * gated, axis=-1, keepdims=True)) + eps_norm)
    out_normed = low(gated * gate_root * out_gain)
    branch = low_back(matmul(out_normed, out_weight))
    return valid_rows * (seq_x + branch)

def reference(tokens, lengths, norm_gain, in_weight, conv_weight, conv_bias, dt_bias, a_log, skip_gain, out_gain, out_weight, out_grad):
    params = (norm_gain, in_weight.astype(jnp.float32), conv_weight, conv_bias, dt_bias, a_log, skip_gain, out_gain, out_weight.astype(jnp.float32))
    flat_tokens = tokens.reshape(MB * SLOTS, SLOT_LEN, D)
    flat_grads = out_grad.reshape(MB * SLOTS, SLOT_LEN, D)
    flat_lengths = lengths.reshape(MB * SLOTS)

    def per_slot(grad_total, slot_item):
        seq_tokens, seq_grad, length = slot_item
        valid_rows = (jnp.arange(SLOT_LEN, dtype=jnp.int32) < length).astype(jnp.float32)[:, None]

        def forward(param_set, seq_x):
            return mixer_forward(param_set, seq_x, valid_rows)
        output, pullback = jax.vjp(forward, params, seq_tokens.astype(jnp.float32))
        param_grads, token_grads = pullback(seq_grad.astype(jnp.float32))
        grad_total = jax.tree.map(jnp.add, grad_total, param_grads)
        return (grad_total, (output.astype(jnp.bfloat16), token_grads))
    zero_grads = jax.tree.map(jnp.zeros_like, params)
    grad_total, (mixed, tokens_grad) = lax.scan(per_slot, zero_grads, (flat_tokens, flat_grads, flat_lengths))
    norm_grad, in_grad, conv_w_grad, conv_b_grad, dtb_grad, alog_grad, skip_grad, gain_grad, out_w_grad = grad_total
    return (mixed.reshape(MB, SLOTS, SLOT_LEN, D), tokens_grad.reshape(MB, SLOTS, SLOT_LEN, D), norm_grad, in_grad, conv_w_grad, conv_b_grad, dtb_grad, alog_grad, skip_grad, gain_grad, out_w_grad)
```

```python
import functools

import jax
import jax.numpy as jnp
from jax import lax
from jax.experimental import pallas as pl
from jax.experimental.pallas import tpu as pltpu
from jax.sharding import PartitionSpec as P

D = 768
HEADS = 24
HEADDIM = 64
NSTATE = 128
CONV = 4
GROUP = 256
INNER = 1536
CONVCH = 1792
PROJ = 3352
EPS = 1e-05

BLOCKS = 3
ROWS = BLOCKS * GROUP
LANES = 128
AT_DT = CONVCH
AT_GATE = CONVCH + LANES
AT_OUT = AT_GATE + INNER
WIDE = AT_OUT + INNER
QUADS = INNER // 256

BF = jnp.bfloat16
F32 = jnp.float32


def dot(a, b):
    return lax.dot_general(a, b, (((1,), (0,)), ((), ())), preferred_element_type=F32)


def dot_nt(a, b):
    return lax.dot_general(a, b, (((1,), (1,)), ((), ())), preferred_element_type=F32)


def sigmoid(v):
    return 0.5 * jnp.tanh(0.5 * v) + 0.5


def halves(v):
    high = v.astype(BF)
    return high, (v - high.astype(F32)).astype(BF)


def side_by_side(v):
    return jnp.concatenate(halves(v), axis=1)


def exact_sum(triangle, v):
    high, rest = halves(v)
    low = (v - high.astype(F32) - rest.astype(F32)).astype(BF)
    parts = dot(triangle, jnp.concatenate([high, rest, low], axis=1))
    return parts[:, :LANES] + parts[:, LANES : 2 * LANES] + parts[:, 2 * LANES :]


def rows_of(b):
    return pl.ds(pl.multiple_of(b * GROUP, GROUP), GROUP)


def quad_of(q):
    return pl.ds(pl.multiple_of(q * 256, 256), 256)


def fold(v):
    total = v[0:8]
    for i in range(1, v.shape[0] // 8):
        total = total + v[8 * i : 8 * i + 8]
    return total


def iota(shape, dim):
    return lax.broadcasted_iota(jnp.int32, shape, dim)


def mixer(
    tok, og, w, norm_gain, convp, headp, innerp,
    mixed, tgrad, wgrad, g_norm, g_conv, g_head, g_inner,
    normed, normed_t, db_t, clow, cout, wide, ssd, dssd, outn, dproj, back, dtb, cumb,
    cut, spread, sco, run1, run2, held, dheld, dst, dqb, halo, halo_next,
    flow, edge_in, state_in, dstate_in, dedge_in, send_sem, recv_sem,
):
    seq = lax.axis_index("seq")
    other = {"seq": 1 - seq}

    barrier = pltpu.get_barrier_semaphore()
    pl.semaphore_signal(barrier, inc=1, device_id=other, device_id_type=pl.DeviceIdType.MESH)
    pl.semaphore_wait(barrier, 1)

    def remote(i, src, dst):
        return pltpu.make_async_remote_copy(
            src_ref=src, dst_ref=dst, send_sem=send_sem.at[i], recv_sem=recv_sem.at[i],
            device_id=other, device_id_type=pl.DeviceIdType.MESH,
        )

    edge_copy = remote(0, clow.at[pl.ds(2 * GROUP - 16, 16), :], edge_in)
    state_copy = remote(1, run2, state_in)
    dstate_copy = remote(2, dheld.at[0], dstate_in)
    dedge_copy = remote(3, halo_next.at[0], dedge_in)

    is_second = (seq == 1).astype(F32)
    is_first = 1.0 - is_second

    def make_spread(q, _):
        shape = (256, 256)
        head = (iota(shape, 1) + q * 256) >> 6
        spread[:, quad_of(q)] = (head == (iota(shape, 0) & 127)).astype(F32).astype(BF)
        return 0

    lax.fori_loop(0, QUADS, make_spread, 0)
    tri_shape = (GROUP, GROUP)
    lower = (iota(tri_shape, 0) >= iota(tri_shape, 1)).astype(F32).astype(BF)
    upper = (iota(tri_shape, 0) <= iota(tri_shape, 1)).astype(F32).astype(BF)
    half = GROUP // 2
    causal = iota((half, half), 0) >= iota((half, half), 1)
    causal_t = iota((half, half), 0) <= iota((half, half), 1)
    first_head = iota((GROUP, LANES), 1) < HEADDIM

    g_norm[...] = jnp.zeros_like(g_norm)
    g_conv[...] = jnp.zeros_like(g_conv)
    g_head[...] = jnp.zeros_like(g_head)
    g_inner[...] = jnp.zeros_like(g_inner)

    def norm_rows(i, _):
        rows = pl.ds(pl.multiple_of(i * 64, 64), 64)
        v = tok[rows, :].astype(F32)
        root = lax.rsqrt(jnp.mean(v * v, axis=1, keepdims=True) + EPS)
        normed[rows, :] = (v * root * norm_gain[...]).astype(BF)
        return 0

    lax.fori_loop(0, ROWS // 64, norm_rows, 0)

    def proj_conv(j, _):
        clow[:, quad_of(j)] = dot(normed[...], w[:, quad_of(j)]).astype(BF)
        return 0

    lax.fori_loop(0, CONVCH // 256, proj_conv, 0)
    edge_copy.start()
    dtb[...] = dot(normed[...], w[:, AT_DT:AT_GATE])

    def turn(b, _):
        rows = rows_of(b)
        normed_t[:, rows] = normed[rows, :].T
        db_t[:, rows] = og[rows, :].T
        return 0

    lax.fori_loop(0, BLOCKS, turn, 0)

    def proj_gate(j, _):
        at = pl.ds(pl.multiple_of(AT_GATE + j * 256, 128), 256)
        wide[:, quad_of(j)] = dot(normed[...], w[:, at])
        return 0

    lax.fori_loop(0, QUADS, proj_gate, 0)

    edge_copy.wait()
    halo[0] = edge_in[8:16, :].astype(F32) * is_second
    halo[1] = clow[GROUP - 16 : GROUP, :].astype(F32)[8:16]
    halo[2] = jnp.zeros((8, CONVCH), F32)

    def conv_acc(values, before, cols):
        rows = values.shape[0]
        ext = jnp.concatenate([before, values], axis=0)
        shifted = [ext[5 + k : 5 + k + rows] for k in range(CONV)]
        acc = convp[4:5, cols]
        for k in range(CONV):
            acc = acc + convp[k : k + 1, cols] * shifted[k]
        return acc, shifted

    def head_rows(b):
        z = dtb[rows_of(b), :] + headp[0:1, :]
        step = jnp.maximum(z, 0.0) + jnp.log1p(jnp.exp(-jnp.abs(z)))
        return z, step

    def shifted_log(cum, step):
        return cum - jnp.log(jnp.maximum(step, 1e-37))

    def to_first(v, q):
        return pltpu.roll(v, lax.rem(LANES - 4 * q, LANES), 1)

    def forward_block(b, with_states):
        rows = rows_of(b)

        def conv_cols(c, _):
            cols = pl.ds(pl.multiple_of(c * LANES, LANES), LANES)
            acc, _ = conv_acc(clow[rows, cols].astype(F32), halo[b, :, cols], cols)
            cout[rows, cols] = (acc * sigmoid(acc)).astype(BF)
            return 0

        lax.fori_loop(0, CONVCH // LANES, conv_cols, 0)

        z, step = head_rows(b)
        cum = exact_sum(lower, step * -jnp.exp(headp[1:2, :]))
        cumb[rows, :] = cum
        total = cum[GROUP - 1 : GROUP, :]
        moved_t = shifted_log(cum, step).T
        for q in range(QUADS):
            cut[q, 0:4, :] = moved_t[4 * q : 4 * q + 4, :]
        weight = side_by_side(jnp.exp(total - cum) * step)
        key = cout[rows, INNER : INNER + NSTATE]
        query = cout[rows, INNER + NSTATE :]
        key_t = key.T
        sco[...] = dot_nt(query, key)

        def quad(q, _):
            cols = quad_of(q)
            xq = cout[rows, cols]
            if with_states:
                scaled = (xq.astype(F32) * dot(weight, spread[:, cols])).astype(BF)
                part = dot(key_t, scaled)
                if with_states == 1:
                    run1[:, cols] = part
                else:
                    run2[:, cols] = part
            near = to_first(cum, q)
            skip = innerp[1:2, cols]
            for j in range(2):
                lanes = slice(j * LANES, (j + 1) * LANES)
                xp = xq[:, lanes]
                zero = jnp.zeros_like(xp)
                x_ab = (jnp.where(first_head, xp, zero), jnp.where(first_head, zero, xp))
                top, bottom = [], []
                for e in range(2):
                    h = 2 * j + e
                    col_top, col_bottom = near[:half, h : h + 1], near[half:, h : h + 1]
                    row = cut[q, h : h + 1, :]
                    row_left, row_right = row[:, :half], row[:, half:]
                    gap = jnp.where(causal, col_top - row_left, -1e30)
                    top.append((sco[:half, :half] * jnp.exp(gap)).astype(BF))
                    bottom.append((sco[half:, :half] * jnp.exp(col_bottom - row_left)).astype(BF))
                    gap = jnp.where(causal, col_bottom - row_right, -1e30)
                    bottom.append((sco[half:, half:] * jnp.exp(gap)).astype(BF))
                out_top = dot(
                    jnp.concatenate(top, axis=1), jnp.concatenate([v[:half] for v in x_ab], axis=0)
                )
                out_bottom = dot(jnp.concatenate(bottom, axis=1), jnp.concatenate(x_ab, axis=0))
                place = pl.ds(pl.multiple_of(q * 256 + j * LANES, LANES), LANES)
                xf = xp.astype(F32) * skip[:, lanes]
                top_rows = pl.ds(pl.multiple_of(b * GROUP, GROUP), half)
                bottom_rows = pl.ds(pl.multiple_of(b * GROUP + half, half), half)
                ssd[top_rows, place] = out_top + xf[:half]
                ssd[bottom_rows, place] = out_bottom + xf[half:]
            return 0

        lax.fori_loop(0, QUADS, quad, 0)

    def decay_of(b):
        last = cumb[pl.ds(b * GROUP + GROUP - 8, 8), :]
        return dot(side_by_side(jnp.exp(last)), spread[...])[7:8, :]

    forward_block(0, 1)
    forward_block(1, 2)
    decay_0, decay_1 = decay_of(0), decay_of(1)
    run2[...] = run2[...] + decay_1 * run1[...]
    state_copy.start()
    forward_block(2, 0)
    state_copy.wait()

    entry = state_in[...] * is_second
    held[0] = entry.astype(BF)
    state_in[...] = entry
    run1[...] = run1[...] + decay_0 * state_in[...]
    held[1] = run1[...].astype(BF)
    run2[...] = entry

    def carry_block(b, _):
        rows = rows_of(b)
        query = cout[rows, INNER + NSTATE :]
        fade = side_by_side(jnp.exp(cumb[rows, :]))

        def quad(q, _):
            cols = quad_of(q)
            ssd[rows, cols] += dot(query, held[b, :, cols]) * dot(fade, spread[:, cols])
            return 0

        return lax.fori_loop(0, QUADS, quad, 0)

    lax.fori_loop(0, 2, carry_block, 0)

    gain = innerp[0:1, :]

    def gate_block(b, _):
        rows = rows_of(b)

        def grad_quad(q, _):
            at = pl.ds(pl.multiple_of(AT_OUT + q * 256, 128), 256)
            back[0:GROUP, quad_of(q)] = dot(og[rows, :], w[:, at])
            return 0

        lax.fori_loop(0, QUADS, grad_quad, 0)

        def gate_rows(i, _):
            here = pl.ds(pl.multiple_of(b * GROUP + i * 16, 16), 16)
            d_out = back[pl.ds(pl.multiple_of(i * 16, 16), 16), 0:INNER]
            g, s = wide[here, 0:INNER], ssd[here, :]
            sg = sigmoid(g)
            silu = g * sg
            gated = s * silu
            root = lax.rsqrt(jnp.mean(gated * gated, axis=1, keepdims=True) + EPS)
            v = gated * root
            outn[here, :] = (v * gain).astype(BF)
            g_inner[0:8, :] += fold(d_out * v)
            a = gain * d_out
            d_gated = root * (a - v * jnp.mean(v * a, axis=1, keepdims=True))
            d_s = (d_gated * silu).astype(BF)
            dssd[here, :] = d_s
            g_inner[8:16, :] += fold(d_s.astype(F32) * cout[here, 0:INNER].astype(F32))
            dproj[here, AT_GATE:AT_OUT] = (d_gated * s * (sg * (1.0 + g * (1.0 - sg)))).astype(BF)
            return 0

        return lax.fori_loop(0, GROUP // 16, gate_rows, 0)

    lax.fori_loop(0, BLOCKS, gate_block, 0)

    def state_back(b, _):
        rows = rows_of(b)
        query_t = cout[rows, INNER + NSTATE :].T
        fade = side_by_side(jnp.exp(cumb[rows, :]))

        def quad(q, dq):
            cols = quad_of(q)
            dz = (dot(fade, spread[:, cols]) * dssd[rows, cols].astype(F32)).astype(BF)
            dheld[b, :, cols] = dot(query_t, dz)
            return dq + dot_nt(dz, held[b, :, cols])

        dqb[rows, :] = lax.fori_loop(0, QUADS, quad, jnp.zeros((GROUP, NSTATE), F32))
        return 0

    lax.fori_loop(0, 2, state_back, 0)
    dqb[2 * GROUP :, :] = jnp.zeros((GROUP, NSTATE), F32)
    dheld[0] = dheld[0] + decay_0 * dheld[1]
    dstate_copy.start()

    def out_block(b, _):
        rows = rows_of(b)
        branch = dot_nt(outn[rows, :], w[:, AT_OUT:])
        mixed[rows, :] = (tok[rows, :].astype(F32) + branch).astype(BF)
        return 0

    lax.fori_loop(0, BLOCKS, out_block, 0)

    def out_grad_quad(q, _):
        at = pl.ds(pl.multiple_of(AT_OUT + q * 256, 128), 256)
        wgrad[:, at] = dot(db_t[...], outn[:, quad_of(q)]).astype(BF)
        return 0

    lax.fori_loop(0, QUADS, out_grad_quad, 0)

    def backward_block(b, state):
        rows = rows_of(b)
        z, step = head_rows(b)
        cum = cumb[rows, :]
        total = cum[GROUP - 1 : GROUP, :]
        moved = shifted_log(cum, step)
        cum_t = cum.T
        for q in range(QUADS):
            cut[q, 0:4, :] = cum_t[4 * q : 4 * q + 4, :]
        weight = side_by_side(jnp.exp(total - cum) * step)
        key = cout[rows, INNER : INNER + NSTATE]
        query = cout[rows, INNER + NSTATE :]
        sco[...] = dot_nt(key, query)
        ds = back.at[0:GROUP, INNER : INNER + 256]
        ds[...] = jnp.zeros((GROUP, GROUP), F32)

        def quad(q, carry):
            dk, give, take = carry
            cols = quad_of(q)
            xq = cout[rows, cols]
            dq4 = dssd[rows, cols]
            skip = innerp[1:2, cols]
            if state is not None:
                spread_w = dot(weight, spread[:, cols])
                d_states = dst[state, :, cols]
                dx_state = spread_w * dot(key, d_states)
                flow[0:8, cols] = fold(xq.astype(F32) * dx_state)
                dk = dk + dot_nt((xq.astype(F32) * spread_w).astype(BF), d_states)
            near = to_first(moved, q)
            for j in range(2):
                lanes = slice(j * LANES, (j + 1) * LANES)
                xp, dp = xq[:, lanes], dq4[:, lanes]
                zero = jnp.zeros_like(xp)
                d_ab = (jnp.where(first_head, dp, zero), jnp.where(first_head, zero, dp))
                top, bottom = [], []
                for e in range(2):
                    h = 2 * j + e
                    dm_top = dot_nt(xp[:half], d_ab[e])
                    dm_bottom = dot_nt(xp[half:], d_ab[e][half:])
                    col_top, col_bottom = near[:half, h : h + 1], near[half:, h : h + 1]
                    row = cut[q, h : h + 1, :]
                    row_left, row_right = row[:, :half], row[:, half:]
                    fade = jnp.exp(jnp.where(causal_t, row_left - col_top, -1e30))
                    ds[:half, :half] += dm_top[:, :half] * fade
                    top.append((sco[:half, :half] * fade).astype(BF))
                    fade = jnp.exp(row_right - col_top)
                    ds[:half, half:] += dm_top[:, half:] * fade
                    top.append((sco[:half, half:] * fade).astype(BF))
                    fade = jnp.exp(jnp.where(causal_t, row_right - col_bottom, -1e30))
                    ds[half:, half:] += dm_bottom * fade
                    bottom.append((sco[half:, half:] * fade).astype(BF))
                dx_top = dot(jnp.concatenate(top, axis=1), jnp.concatenate(d_ab, axis=0))
                dx_bottom = dot(
                    jnp.concatenate(bottom, axis=1),
                    jnp.concatenate([v[half:] for v in d_ab], axis=0),
                )
                dxp = jnp.concatenate([dx_top, dx_bottom], axis=0)
                if state is not None:
                    dxp = dxp + dx_state[:, lanes]
                place = pl.ds(pl.multiple_of(q * 256 + j * LANES, LANES), LANES)
                xf, df = xp.astype(F32), dp.astype(F32)
                kept = skip[:, lanes]
                pick = (
                    iota((2 * LANES, LANES), 1)
                    == 4 * q + 2 * j + ((iota((2 * LANES, LANES), 0) & 127) >> 6)
                )
                pick = pick.astype(F32).astype(BF)
                give = give + dot(side_by_side(xf * dxp), pick)
                take = take + dot(side_by_side(df * (ssd[rows, place] - kept * xf)), pick)
                wide[rows, place] = dxp + kept * df
            return dk, give, take

        nothing = jnp.zeros((GROUP, LANES), F32)
        dk, give, take = lax.fori_loop(0, QUADS, quad, (nothing, nothing, nothing))
        d_scores = ds[...].astype(BF)
        wide[rows, INNER : INNER + NSTATE] = dk + dot(d_scores, query)
        wide[rows, INNER + NSTATE : CONVCH] = dqb[rows, :] + dot(d_scores.T, key)

        back_sum = exact_sum(upper, take - give)
        if state is not None:
            summed = jnp.sum(flow[...], axis=0, keepdims=True)
            if state == 1:
                kept = jnp.sum(run1[...] * dstate_in[...], axis=0, keepdims=True)
                summed = summed + decay_1 * kept
            else:
                kept = jnp.sum(run2[...] * state_in[...], axis=0, keepdims=True)
                summed = summed + decay_0 * kept
            high, low = halves(jnp.broadcast_to(summed, (8, INNER)))
            by_head = dot_nt(high, spread[0:LANES, :]) + dot_nt(low, spread[0:LANES, :])
            back_sum = back_sum + by_head[0:1, :]
        rate = -jnp.exp(headp[1:2, :])
        sg = sigmoid(z)
        ratio = jnp.where(z < -15.0, 1.0, sg / jnp.maximum(step, 1e-37))
        d_pre = give * ratio + rate * back_sum * sg
        g_head[0:8, :] += fold(d_pre)
        g_head[8:16, :] += fold(back_sum * (step * rate))
        dproj[rows, AT_DT:AT_GATE] = d_pre.astype(BF)

    backward_block(2, None)
    dstate_copy.wait()
    dstate_in[...] = dstate_in[...] * is_first
    dst[1] = dstate_in[...].astype(BF)
    state_in[...] = dheld[1] + decay_1 * dstate_in[...]
    dst[0] = state_in[...].astype(BF)
    backward_block(1, 1)
    backward_block(0, 0)

    def edge_cols(c, _):
        cols = pl.ds(pl.multiple_of(c * LANES, LANES), LANES)
        for b in range(2):
            first = clow[b * GROUP : b * GROUP + 16, cols].astype(F32)
            acc, _ = conv_acc(first, halo[b, :, cols], cols)
            sg = sigmoid(acc)
            d_acc = wide[b * GROUP : b * GROUP + 16, cols] * (sg * (1.0 + acc * (1.0 - sg)))
            halo_next[b, :, cols] = d_acc[0:8]
        return 0

    lax.fori_loop(0, CONVCH // LANES, edge_cols, 0)
    halo_next[2] = jnp.zeros((8, CONVCH), F32)
    dedge_copy.start()

    def conv_back(b, after):
        rows = rows_of(b)

        def conv_cols(c, _):
            cols = pl.ds(pl.multiple_of(c * LANES, LANES), LANES)
            acc, shifted = conv_acc(clow[rows, cols].astype(F32), halo[b, :, cols], cols)
            sg = sigmoid(acc)
            d_acc = wide[rows, cols] * (sg * (1.0 + acc * (1.0 - sg)))
            for k in range(CONV):
                g_conv[8 * k : 8 * k + 8, cols] += fold(d_acc * shifted[k])
            g_conv[32:40, cols] += fold(d_acc)
            ext = jnp.concatenate([d_acc, after[:, cols]], axis=0)
            d_in = convp[3:4, cols] * d_acc
            for k in range(CONV - 1):
                d_in = d_in + convp[k : k + 1, cols] * ext[3 - k : 3 - k + GROUP]
            dproj[rows, cols] = d_in.astype(BF)
            return 0

        lax.fori_loop(0, CONVCH // LANES, conv_cols, 0)

    conv_back(2, halo_next.at[2])
    conv_back(0, halo_next.at[1])
    dedge_copy.wait()
    dedge_in[...] = dedge_in[...] * is_first
    conv_back(1, dedge_in)

    def in_grad_quad(j, _):
        wgrad[:, quad_of(j)] = dot(normed_t[...], dproj[:, quad_of(j)]).astype(BF)
        return 0

    lax.fori_loop(0, AT_OUT // 256, in_grad_quad, 0)
    last = slice(AT_OUT - 128, AT_OUT)
    wgrad[:, last] = dot(normed_t[...], dproj[:, last]).astype(BF)

    def in_block(b, _):
        rows = rows_of(b)
        tgrad[rows, :] = dot_nt(dproj[rows, :], w[:, 0:AT_OUT])
        return 0

    lax.fori_loop(0, BLOCKS, in_block, 0)

    def norm_back(i, _):
        rows = pl.ds(pl.multiple_of(i * 32, 32), 32)
        v = tok[rows, :].astype(F32)
        root = lax.rsqrt(jnp.mean(v * v, axis=1, keepdims=True) + EPS)
        y = v * root
        dn = tgrad[rows, :]
        g_norm[...] += fold(dn * y)
        bb = norm_gain[...] * dn
        d_v = root * (bb - y * jnp.mean(y * bb, axis=1, keepdims=True))
        tgrad[rows, :] = og[rows, :].astype(F32) + d_v
        return 0

    lax.fori_loop(0, ROWS // 32, norm_back, 0)


def call_mixer(tok, og, w, norm_gain, convp, headp, innerp):
    vmem = pl.BlockSpec(memory_space=pltpu.VMEM)
    outs = (
        ((ROWS, D), BF), ((ROWS, D), F32), ((D, WIDE), BF), ((8, D), F32),
        ((40, CONVCH), F32), ((16, LANES), F32), ((16, INNER), F32),
    )
    scratch = (
        ((ROWS, D), BF), ((D, ROWS), BF), ((D, ROWS), BF), ((ROWS, CONVCH), BF),
        ((ROWS, CONVCH), BF), ((ROWS, CONVCH), F32), ((ROWS, INNER), F32), ((ROWS, INNER), BF),
        ((ROWS, INNER), BF), ((ROWS, AT_OUT), BF), ((GROUP, CONVCH), F32), ((ROWS, LANES), F32),
        ((ROWS, LANES), F32), ((QUADS, 8, GROUP), F32), ((256, INNER), BF), ((GROUP, GROUP), F32),
        ((NSTATE, INNER), F32), ((NSTATE, INNER), F32), ((2, NSTATE, INNER), BF),
        ((2, NSTATE, INNER), F32), ((2, NSTATE, INNER), BF), ((ROWS, NSTATE), F32),
        ((3, 8, CONVCH), F32), ((3, 8, CONVCH), F32), ((8, INNER), F32), ((16, CONVCH), BF), ((NSTATE, INNER), F32),
        ((NSTATE, INNER), F32), ((8, CONVCH), F32),
    )
    return pl.pallas_call(
        mixer,
        out_shape=[jax.ShapeDtypeStruct(s, t) for s, t in outs],
        in_specs=[vmem] * 7,
        out_specs=[vmem] * len(outs),
        scratch_shapes=[pltpu.VMEM(s, t) for s, t in scratch]
        + [pltpu.SemaphoreType.DMA((4,)), pltpu.SemaphoreType.DMA((4,))],
        compiler_params=pltpu.CompilerParams(
            collective_id=0, has_side_effects=True, vmem_limit_bytes=62 * 1024 * 1024
        ),
        name="mixer",
    )(tok, og, w, norm_gain, convp, headp, innerp)


def shards(
    tokens, lengths, norm_gain, in_weight, conv_weight, conv_bias, dt_bias, a_log, skip_gain,
    out_gain, out_weight, out_grad,
):
    both = ("fsdp", "seq")
    row_count = tokens.shape[2]
    positions = lax.axis_index("seq") * row_count + jnp.arange(row_count, dtype=jnp.int32)
    first_long = lengths[0, 0] > lengths[1, 0]
    short_valid = (positions < jnp.minimum(lengths[0, 0], lengths[1, 0]))[:, None]

    def packed(a):
        return jnp.concatenate(
            [jnp.where(first_long, a[0, 0], a[1, 0]),
             jnp.where(first_long, a[1, 0, :GROUP], a[0, 0, :GROUP])], axis=0)

    tok = packed(tokens)
    og = packed(out_grad)
    mask = jnp.concatenate([jnp.ones((row_count, 1), bool), short_valid[:GROUP]], axis=0)
    og = jnp.where(mask, og, jnp.zeros_like(og))
    own = in_weight.shape[0]
    sent = jnp.concatenate(
        [in_weight[:, INNER:], jnp.zeros((own, LANES - HEADS), BF), in_weight[:, :INNER],
         out_weight.T], axis=1)
    w = lax.all_gather(sent, both, axis=0, tiled=True)
    convp = jnp.concatenate([conv_weight, conv_bias[None], jnp.zeros((3, CONVCH), F32)], axis=0)
    headp = jnp.pad(jnp.stack([dt_bias, a_log]), ((0, 6), (0, LANES - HEADS)))
    innerp = jnp.pad(jnp.stack([out_gain, jnp.repeat(skip_gain, HEADDIM)]), ((0, 6), (0, 0)))
    mixed, tgrad, wgrad, g_norm, g_conv, g_head, g_inner = call_mixer(
        tok, og, w, norm_gain[None], convp, headp, innerp
    )
    summed = lax.psum_scatter(wgrad, both, scatter_dimension=0, tiled=True).astype(F32)
    in_grad = jnp.concatenate(
        [summed[:, AT_GATE:AT_OUT], summed[:, :CONVCH], summed[:, AT_DT : AT_DT + HEADS]], axis=1
    )
    out_w_grad = summed[:, AT_OUT:].T
    small = (
        g_norm.sum(0), g_conv.reshape(5, 8, CONVCH).sum(1), g_head.reshape(2, 8, LANES).sum(1),
        g_inner.reshape(2, 8, INNER).sum(1),
    )
    norm_grad, conv_g, head_g, inner_g = lax.psum(small, both)

    def unpacked(a):
        long = a[:row_count]
        short = jnp.where(short_valid, jnp.pad(a[row_count:], ((0, row_count - GROUP), (0, 0))), 0)
        short = short.astype(a.dtype)
        return jnp.stack([jnp.where(first_long, long, short), jnp.where(first_long, short, long)])[
            :, None
        ]

    return (
        unpacked(mixed), unpacked(tgrad), norm_grad, in_grad, conv_g[:4], conv_g[4],
        head_g[0, :HEADS], head_g[1, :HEADS],
        inner_g[1].reshape(HEADS, HEADDIM).sum(1), inner_g[0], out_w_grad,
    )


def solution(mesh):
    spread = P(None, "fsdp", "seq", None)
    both = ("fsdp", "seq")
    return jax.shard_map(
        shards,
        mesh=mesh,
        in_specs=(
            spread, P(None, "fsdp"), P(), P(both, None), P(), P(), P(), P(), P(), P(),
            P(None, both), spread,
        ),
        out_specs=(
            spread, spread, P(), P(both, None), P(), P(), P(), P(), P(), P(), P(None, both),
        ),
        check_vma=False,
    )
```

```python
import functools
import types

import jax
import jax.numpy as jnp
from jax import lax
from jax.experimental import pallas as pl
from jax.experimental.pallas import tpu as pltpu
from jax.sharding import PartitionSpec as P

D = 768
HEADS = 24
HEADDIM = 64
NSTATE = 128
CONV = 4
GROUP = 256
INNER = 1536
CONVCH = 1792
PROJ = 3352
EPS = 1e-05

BLOCKS = 3
ROWS = BLOCKS * GROUP
EDGE = 16
LANES = 128
QUADS = INNER // 256
AT_DT = 256
AT_X = 512
AT_GATE = AT_X + INNER
AT_OUT = AT_GATE + INNER
WIDE = AT_OUT + INNER
CX = 2 * NSTATE
CHUNK = 768
CHUNKS = QUADS + 1
SLOTS = 4
GATHERS = ((0, 512), (512, 512), (1024, 1024), (AT_GATE, INNER), (AT_OUT, INNER))
PLANE = 4

BF = jnp.bfloat16
F32 = jnp.float32
MESH = pl.DeviceIdType.MESH


def dot(a, b):
    return lax.dot_general(a, b, (((1,), (0,)), ((), ())), preferred_element_type=F32)


def dot_nt(a, b):
    return lax.dot_general(a, b, (((1,), (1,)), ((), ())), preferred_element_type=F32)


def sigmoid(v):
    return 0.5 * jnp.tanh(0.5 * v) + 0.5


def halves(v):
    high = v.astype(BF)
    return high, (v - high.astype(F32)).astype(BF)


def side_by_side(v):
    return jnp.concatenate(halves(v), axis=1)


def exact_sum(triangle, v):
    high, rest = halves(v)
    low = (v - high.astype(F32) - rest.astype(F32)).astype(BF)
    parts = dot(triangle, jnp.concatenate([high, rest, low], axis=1))
    return parts[:, :LANES] + parts[:, LANES : 2 * LANES] + parts[:, 2 * LANES :]


def span(start, size, multiple=None):
    return pl.ds(pl.multiple_of(start, multiple or size), size)


def rows_of(b):
    return span(b * GROUP, GROUP)


def heads_of(q):
    return span(q * 256, 256)


def fold(v):
    total = v[0:8]
    for i in range(1, v.shape[0] // 8):
        total = total + v[8 * i : 8 * i + 8]
    return total


def iota(shape, dim):
    return lax.broadcasted_iota(jnp.int32, shape, dim)


def loop(count, body):
    def step(i, _):
        body(i)
        return 0

    lax.fori_loop(0, count, step, 0)


def silu_slope(v, sg):
    return sg * (1.0 + v * (1.0 - sg))


def mixer(names, fused, nz, *refs):
    r = types.SimpleNamespace(**dict(zip(names, refs)))
    seq = lax.axis_index("seq")
    f = lax.axis_index("fsdp")
    z_at, p_at = f // PLANE, f % PLANE
    sibling = {"seq": 1 - seq}
    is_second = (seq == 1).astype(F32)
    is_first = 1.0 - is_second

    def plane_peer(j):
        if j == 1:
            return p_at + 1 - 2 * (p_at % 2)
        if j == 2:
            return p_at + 2 - 4 * (p_at // 2)
        return 3 - p_at

    def z_peer(j):
        return (z_at + j + nz) % nz

    def on_plane(j):
        return {"fsdp": z_at * PLANE + plane_peer(j)}

    def on_chain(j):
        return {"fsdp": z_peer(j) * PLANE + p_at}

    peers = [sibling]
    if fused:
        peers += [on_plane(j) for j in range(1, PLANE)] + [on_chain(j) for j in range(1, nz)]
    barrier = pltpu.get_barrier_semaphore()
    for peer in peers:
        pl.semaphore_signal(barrier, inc=1, device_id=peer, device_id_type=MESH)
    pl.semaphore_wait(barrier, len(peers))

    def remote(src, dst, send, recv, device):
        return pltpu.make_async_remote_copy(
            src_ref=src, dst_ref=dst, send_sem=send, recv_sem=recv, device_id=device,
            device_id_type=MESH,
        )

    def pair_copy(i, src, dst):
        return remote(src, dst, r.pair_send.at[i], r.pair_recv.at[i], sibling)

    w = r.w
    own = D // (2 * nz * PLANE) if fused else 0
    slab = 2 * own

    def part(c):
        low, size = GATHERS[c]
        return span(low + seq * (size // 2), size // 2, 128)

    def slab_of(index):
        return span(index * slab, slab, 16)

    def gather_copy(c, k, index, device):
        at = w.at[slab_of(index), part(c)]
        return remote(at, at, r.g_send.at[c, k], r.g_recv.at[c, k], device)

    def chain_copy(c, j):
        return gather_copy(c, j - 1, f, on_chain(j))

    def plane_copy(c, j, back):
        index = (z_at - back + nz) % nz * PLANE + p_at
        return gather_copy(c, nz - 1 + (j - 1) * nz + back, index, on_plane(j))

    def last_copy(c):
        at = w.at[:, part(c)]
        k = nz - 1 + (PLANE - 1) * nz
        return remote(at, at, r.g_send.at[c, k], r.g_recv.at[c, k], sibling)

    def gather_own(c):
        cols = part(c)
        mine, theirs = r.shard[:, cols], r.shard_in[:, cols]
        first = jnp.where(seq == 0, mine, theirs)
        second = jnp.where(seq == 0, theirs, mine)
        w[slab_of(f), cols] = jnp.concatenate([first, second], axis=0).astype(BF)

    def gather_1(c):
        for j in range(1, nz):
            chain_copy(c, j).start()
        for j in range(1, PLANE):
            plane_copy(c, j, 0).start()

    def gather_2(c):
        for back in range(1, nz):
            chain_copy(c, back).wait_recv()
            for j in range(1, PLANE):
                plane_copy(c, j, back).start()

    def gather_3(c):
        for j in range(1, PLANE):
            for back in range(nz):
                plane_copy(c, j, back).wait_recv()
        last_copy(c).start()

    def gather_4(c):
        last_copy(c).wait_recv()

    def gather_end(c):
        for j in range(1, nz):
            chain_copy(c, j).wait_send()
        for j in range(1, PLANE):
            for back in range(nz):
                plane_copy(c, j, back).wait_send()
        last_copy(c).wait_send()

    def size_of(g):
        return 256 if isinstance(g, int) and g == QUADS else CHUNK // 2

    def lanes_of(g, which):
        size = size_of(g)
        return span(which * size, size, 128)

    def place_of(g):
        return g % SLOTS

    def sum_copy_0(g):
        n = size_of(g)
        src = r.wg.at[place_of(g), :, :, :, lanes_of(g, 1 - seq)]
        dst = r.r0.at[g, :, :, :, 0:n]
        return remote(src, dst, r.s_send.at[g, 0], r.s_recv.at[g, 0], sibling)

    def sum_copy_1(g, j):
        n = size_of(g)
        src = r.wg.at[place_of(g), :, plane_peer(j), :, lanes_of(g, seq)]
        dst = r.r1.at[g, j - 1, :, :, 0:n]
        return remote(src, dst, r.s_send.at[g, j], r.s_recv.at[g, j], on_plane(j))

    def sum_copy_2(g, j):
        n = size_of(g)
        k = PLANE - 1 + j
        src = r.wg.at[place_of(g), z_peer(j), p_at, :, lanes_of(g, seq)]
        dst = r.r2.at[g, j - 1, :, 0:n]
        return remote(src, dst, r.s_send.at[g, k], r.s_recv.at[g, k], on_chain(j))

    def sum_copy_3(g):
        n = size_of(g)
        k = PLANE - 1 + nz
        src = r.fin.at[g, span((1 - seq) * own, own, 8), 0:n]
        dst = r.gsum.at[g, :, 0:n]
        return remote(src, dst, r.s_send.at[g, k], r.s_recv.at[g, k], sibling)

    def sum_0(g):
        if fused:
            sum_copy_0(g).start()

    def sum_1(g):
        if not fused:
            return
        copy = sum_copy_0(g)
        copy.wait_send()
        copy.wait_recv()
        n, here, lanes = size_of(g), place_of(g), lanes_of(g, seq)

        def add(i):
            zi, pi = i // PLANE, i % PLANE
            mine = r.wg[here, zi, pi, :, lanes].astype(F32)
            r.wg[here, zi, pi, :, lanes] = (mine + r.r0[g, zi, pi, :, 0:n].astype(F32)).astype(BF)

        loop(nz * PLANE, add)
        for j in (3, 1, 2):
            sum_copy_1(g, j).start()

    def sum_2(g):
        if not fused:
            return
        n, here, lanes = size_of(g), place_of(g), lanes_of(g, seq)
        for j in range(1, PLANE):
            copy = sum_copy_1(g, j)
            copy.wait_send()
            copy.wait_recv()

        def add(zi):
            total = r.wg[here, zi, p_at, :, lanes].astype(F32)
            for j in range(PLANE - 1):
                total = total + r.r1[g, j, zi, :, 0:n].astype(F32)
            r.wg[here, zi, p_at, :, lanes] = total.astype(BF)

        loop(nz, add)
        for j in range(1, nz):
            sum_copy_2(g, j).start()

    def sum_3(g):
        if not fused:
            return
        n, here, lanes = size_of(g), place_of(g), lanes_of(g, seq)
        for j in range(1, nz):
            copy = sum_copy_2(g, j)
            copy.wait_send()
            copy.wait_recv()
        total = r.wg[here, z_at, p_at, :, lanes].astype(F32)
        for j in range(nz - 1):
            total = total + r.r2[g, j, :, 0:n].astype(F32)
        r.fin[g, :, 0:n] = total
        sum_copy_3(g).start()

    def sum_4(g):
        if not fused:
            return
        copy = sum_copy_3(g)
        copy.wait_send()
        copy.wait_recv()

    def put_grad(g, low, value):
        size = value.shape[1]
        if fused:
            parts = value.astype(BF).reshape(nz, PLANE, slab, size)
            r.wg[place_of(g), :, :, :, low : low + size] = parts
        else:
            r.wgrad[:, span(g * CHUNK + low, size, 128)] = value.astype(BF)

    edge_copy = pair_copy(0, r.tok.at[2 * GROUP - EDGE : 2 * GROUP, :], r.edge_in)
    edge_copy.start()
    if fused:
        shard_copy = pair_copy(1, r.shard, r.shard_in)
        shard_copy.start()

    def make_spread(q):
        shape = (256, 256)
        head = (iota(shape, 1) + q * 256) >> 6
        r.spread[:, span(q * 256, 256)] = (head == (iota(shape, 0) & 127)).astype(F32).astype(BF)

    if fused:
        shard_copy.wait()
        for c in range(len(GATHERS)):
            gather_own(c)
            if c < 2:
                gather_1(c)

    loop(QUADS, make_spread)
    tri_shape = (GROUP, GROUP)
    lower = (iota(tri_shape, 0) >= iota(tri_shape, 1)).astype(F32).astype(BF)
    upper = (iota(tri_shape, 0) <= iota(tri_shape, 1)).astype(F32).astype(BF)
    half = GROUP // 2
    causal = iota((half, half), 0) >= iota((half, half), 1)
    causal_t = iota((half, half), 0) <= iota((half, half), 1)
    first_head = iota((GROUP, LANES), 1) < HEADDIM
    rate = -jnp.exp(r.headp[1:2, :])

    r.g_norm[...] = jnp.zeros_like(r.g_norm)
    r.g_conv[...] = jnp.zeros_like(r.g_conv)
    r.g_head[...] = jnp.zeros_like(r.g_head)
    r.g_inner[...] = jnp.zeros_like(r.g_inner)
    r.halo[2] = jnp.zeros((8, CONVCH), F32)
    r.dproj[:, AT_DT + LANES : AT_X] = jnp.zeros((ROWS, AT_X - AT_DT - LANES), BF)

    def norm_of(v):
        root = lax.rsqrt(jnp.mean(v * v, axis=1, keepdims=True) + EPS)
        return (v * root * r.norm_gain[...]).astype(BF)

    def norm_rows(i):
        rows = span(i * 64, 64)
        r.normed[rows, :] = norm_of(r.tok[rows, :].astype(F32))

    loop(ROWS // 64, norm_rows)
    edge_copy.wait()
    r.normed[ROWS:, :] = norm_of(r.edge_in[...].astype(F32) * is_second)

    def turn(b):
        rows = rows_of(b)
        r.normed_t[:, rows] = r.normed[rows, :].T
        r.db_t[:, rows] = r.og[rows, :].T

    loop(BLOCKS, turn)

    if fused:
        gather_2(0)
        gather_2(1)
        gather_1(2)
        gather_3(0)
        gather_4(0)

    def conv_acc(values, before, cols):
        rows = values.shape[0]
        ext = jnp.concatenate([before, values], axis=0)
        shifted = [ext[5 + k : 5 + k + rows] for k in range(CONV)]
        acc = r.convp[4:5, cols]
        for k in range(CONV):
            acc = acc + r.convp[k : k + 1, cols] * shifted[k]
        return acc, shifted

    def project(at, to):
        low = dot(r.normed[...], w[:, at]).astype(BF)
        r.clow[:, to] = low
        r.halo[0, :, to] = low[ROWS : ROWS + EDGE].astype(F32)[EDGE - 8 :]
        r.halo[1, :, to] = low[GROUP - 16 : GROUP].astype(F32)[8:]

    def conv_forward(b, cols):
        rows = rows_of(b)
        acc, _ = conv_acc(r.clow[rows, cols].astype(F32), r.halo[b, :, cols], cols)
        r.cout[rows, cols] = (acc * sigmoid(acc)).astype(BF)

    project(pl.ds(0, CX), pl.ds(0, CX))
    r.dtb[...] = dot(r.normed[0:ROWS, :], w[:, AT_DT : AT_DT + LANES])

    def head_rows(b):
        z = r.dtb[rows_of(b), :] + r.headp[0:1, :]
        step = jnp.maximum(z, 0.0) + jnp.log1p(jnp.exp(-jnp.abs(z)))
        return z, step

    def prepare(b):
        rows = rows_of(b)
        conv_forward(b, pl.ds(0, LANES))
        conv_forward(b, pl.ds(LANES, LANES))
        z, step = head_rows(b)
        cum = exact_sum(lower, step * rate)
        moved = cum - jnp.log(jnp.maximum(step, 1e-37))
        r.cumb[rows, :] = cum
        r.moved[rows, :] = moved
        cum_t, moved_t = cum.T, moved.T
        for q in range(QUADS):
            r.cut[b, q, 0:4, :] = moved_t[4 * q : 4 * q + 4, :]
            r.cut[b, q, 4:8, :] = cum_t[4 * q : 4 * q + 4, :]
        r.weight[rows, :] = side_by_side(jnp.exp(cum[GROUP - 1 : GROUP, :] - cum) * step)
        r.fade[rows, :] = side_by_side(jnp.exp(cum))
        key, query = r.cout[rows, 0:NSTATE], r.cout[rows, NSTATE:CX]
        r.turned[b, 0:NSTATE, :] = key.T
        r.turned[b, NSTATE:CX, :] = query.T
        r.sco[b] = dot_nt(query, key)

    loop(BLOCKS, prepare)

    def to_first(v, q):
        return pltpu.roll(v, (LANES - 4 * q) % LANES, 1)

    def forward_block(b, q):
        rows = rows_of(b)
        cols = span(CX + q * 256, 256)
        heads = span(q * 256, 256)
        for i in range(2):
            conv_forward(b, span(CX + q * 256 + i * LANES, LANES))
        xq = r.cout[rows, cols]

        @pl.when(b < 2)
        def _():
            spread_w = dot(r.weight[rows, :], r.spread[:, heads])
            scaled = (xq.astype(F32) * spread_w).astype(BF)
            r.runs[b, :, heads] = dot(r.turned[b, 0:NSTATE, :], scaled)

        near = to_first(r.cumb[rows, :], q)
        skip = r.innerp[1:2, heads]
        for j in range(2):
            lanes = slice(j * LANES, (j + 1) * LANES)
            xp = xq[:, lanes]
            zero = jnp.zeros_like(xp)
            x_ab = (jnp.where(first_head, xp, zero), jnp.where(first_head, zero, xp))
            top, bottom = [], []
            for e in range(2):
                h = 2 * j + e
                col_top, col_bottom = near[:half, h : h + 1], near[half:, h : h + 1]
                row = r.cut[b, q, h : h + 1, :]
                row_left, row_right = row[:, :half], row[:, half:]
                gap = jnp.where(causal, col_top - row_left, -1e30)
                top.append((r.sco[b, :half, :half] * jnp.exp(gap)).astype(BF))
                fade = jnp.exp(col_bottom - row_left)
                bottom.append((r.sco[b, half:, :half] * fade).astype(BF))
                gap = jnp.where(causal, col_bottom - row_right, -1e30)
                bottom.append((r.sco[b, half:, half:] * jnp.exp(gap)).astype(BF))
            out_top = dot(
                jnp.concatenate(top, axis=1), jnp.concatenate([v[:half] for v in x_ab], axis=0)
            )
            out_bottom = dot(jnp.concatenate(bottom, axis=1), jnp.concatenate(x_ab, axis=0))
            place = span(q * 256 + j * LANES, LANES)
            xf = xp.astype(F32) * skip[:, lanes]
            r.ssd[span(b * GROUP, half), place] = out_top + xf[:half]
            r.ssd[span(b * GROUP + half, half), place] = out_bottom + xf[half:]

    def forward_quad(q):
        if fused:

            @pl.when(q == 0)
            def _():
                gather_3(1)
                gather_2(2)
                gather_1(3)
                gather_4(1)

            @pl.when(q == 1)
            def _():
                gather_3(2)
                gather_1(4)

            @pl.when(q == 2)
            def _():
                gather_4(2)
                gather_2(3)

            @pl.when(q == 3)
            def _():
                gather_2(4)

            @pl.when(q == 4)
            def _():
                gather_3(3)

        project(span(AT_X + q * 256, 256), span(CX + q * 256, 256))
        loop(BLOCKS, lambda b: forward_block(b, q))

    loop(QUADS, forward_quad)

    def decay_of(b):
        last = r.cumb[b * GROUP + GROUP - 8 : (b + 1) * GROUP, :]
        return dot(side_by_side(jnp.exp(last)), r.spread[...])[7:8, :]

    decay_0, decay_1 = decay_of(0), decay_of(1)
    r.runs[1] = r.runs[1] + decay_1 * r.runs[0]
    state_copy = pair_copy(2, r.runs.at[1], r.state_in)
    state_copy.start()
    if fused:
        gather_3(4)
        gather_4(3)

    def carry_block(b):
        rows = rows_of(b)
        query = r.cout[rows, NSTATE:CX]

        def quad(q):
            cols = span(q * 256, 256)
            r.ssd[rows, cols] += dot(query, r.held[b, :, cols]) * dot(
                r.fade[rows, :], r.spread[:, cols]
            )

        loop(QUADS, quad)

    gain = r.innerp[0:1, :]

    def gate_project(b):
        rows = rows_of(b)

        def quad(q):
            cols = span(q * 256, 256)
            r.gate[:, cols] = dot(r.normed[rows, :], w[:, span(AT_GATE + q * 256, 256)])

        loop(QUADS, quad)

    def out_back(b):
        rows = rows_of(b)

        def quad(q):
            cols = span(q * 256, 256)
            r.back[:, cols] = dot(r.og[rows, :], w[:, span(AT_OUT + q * 256, 256)])

        loop(QUADS, quad)

    def gate_block(b):
        def gate_rows(i):
            here = span(b * GROUP + i * 16, 16)
            local = span(i * 16, 16)
            d_out, g, s = r.back[local, :], r.gate[local, :], r.ssd[here, :]
            sg = sigmoid(g)
            silu = g * sg
            gated = s * silu
            root = lax.rsqrt(jnp.mean(gated * gated, axis=1, keepdims=True) + EPS)
            v = gated * root
            r.dproj[here, AT_X:AT_GATE] = (v * gain).astype(BF)
            r.g_inner[0:8, :] += fold(d_out * v)
            a = gain * d_out
            d_gated = root * (a - v * jnp.mean(v * a, axis=1, keepdims=True))
            d_s = (d_gated * silu).astype(BF)
            r.dssd[here, :] = d_s
            r.g_inner[8:16, :] += fold(d_s.astype(F32) * r.cout[here, CX:].astype(F32))
            r.dproj[here, AT_GATE:AT_OUT] = (d_gated * s * silu_slope(g, sg)).astype(BF)

        loop(GROUP // 16, gate_rows)

    gate_project(2)
    if fused:
        gather_4(4)
    out_back(2)
    gate_block(2)
    state_copy.wait()
    r.state_in[...] = r.state_in[...] * is_second
    r.held[0] = r.state_in[...].astype(BF)
    r.runs[0] = r.runs[0] + decay_0 * r.state_in[...]
    r.held[1] = r.runs[0].astype(BF)
    r.runs[1] = r.state_in[...]

    def gate_long(b):
        gate_project(b)
        out_back(b)
        carry_block(b)
        gate_block(b)

    loop(2, gate_long)

    def state_back(b):
        rows = rows_of(b)

        def quad(q, dq):
            cols = span(q * 256, 256)
            spread_f = dot(r.fade[rows, :], r.spread[:, cols])
            dz = (spread_f * r.dssd[rows, cols].astype(F32)).astype(BF)
            r.dheld[b, :, cols] = dot(r.turned[b, NSTATE:CX, :], dz)
            return dq + dot_nt(dz, r.held[b, :, cols])

        r.dqb[rows, :] = lax.fori_loop(0, QUADS, quad, jnp.zeros((GROUP, NSTATE), F32))

    loop(2, state_back)
    r.dqb[2 * GROUP :, :] = jnp.zeros((GROUP, NSTATE), F32)
    r.dheld[0] = r.dheld[0] + decay_0 * r.dheld[1]
    dstate_copy = pair_copy(3, r.dheld.at[0], r.dstate_in)
    dstate_copy.start()

    def out_block(b):
        rows = rows_of(b)
        branch = dot_nt(r.dproj[rows, AT_X:AT_GATE], w[:, AT_OUT:])
        r.normed[rows, :] = (r.tok[rows, :].astype(F32) + branch).astype(BF)

    loop(BLOCKS, out_block)
    mixed_copy = pltpu.make_async_copy(r.normed.at[0:ROWS, :], r.mixed, r.local.at[0])
    mixed_copy.start()

    def ds_of(b):
        return r.back.at[:, heads_of(b)]

    def give_of(b):
        return r.back.at[:, span(CHUNK + b * LANES, LANES)]

    def take_of(b):
        return r.back.at[:, span(CHUNK + (BLOCKS + b) * LANES, LANES)]

    def prepare_back(b):
        rows = rows_of(b)
        r.sco[b] = dot_nt(r.cout[rows, 0:NSTATE], r.cout[rows, NSTATE:CX])
        ds_of(b)[...] = jnp.zeros((GROUP, GROUP), F32)
        nothing = jnp.zeros((GROUP, LANES), F32)
        r.dkb[rows, :] = nothing
        give_of(b)[...] = nothing
        take_of(b)[...] = nothing

    loop(BLOCKS, prepare_back)
    dstate_copy.wait()
    r.dstate_in[...] = r.dstate_in[...] * is_first
    r.dst[1] = r.dstate_in[...].astype(BF)
    r.state_in[...] = r.dheld[1] + decay_1 * r.dstate_in[...]
    r.dst[0] = r.state_in[...].astype(BF)

    def backward_block(b, q):
        rows = rows_of(b)
        heads = span(q * 256, 256)
        xq = r.cout[rows, span(CX + q * 256, 256)]
        dq4 = r.dssd[rows, heads]
        skip = r.innerp[1:2, heads]
        dx, ds = r.gate.at[:, heads_of(b)], ds_of(b)
        give, take = give_of(b), take_of(b)

        @pl.when(b < 2)
        def _():
            spread_w = dot(r.weight[rows, :], r.spread[:, heads])
            d_states = r.dst[b, :, heads]
            dx_state = spread_w * dot(r.cout[rows, 0:NSTATE], d_states)
            r.flow[b, 0:8, heads] = fold(xq.astype(F32) * dx_state)
            r.dkb[rows, :] += dot_nt((xq.astype(F32) * spread_w).astype(BF), d_states)
            dx[...] = dx_state

        @pl.when(b == 2)
        def _():
            dx[...] = jnp.zeros((GROUP, 256), F32)

        near = to_first(r.moved[rows, :], q)
        for j in range(2):
            lanes = slice(j * LANES, (j + 1) * LANES)
            xp, dp = xq[:, lanes], dq4[:, lanes]
            zero = jnp.zeros_like(xp)
            d_ab = (jnp.where(first_head, dp, zero), jnp.where(first_head, zero, dp))
            top, bottom = [], []
            for e in range(2):
                h = 2 * j + e
                dm_top = dot_nt(xp[:half], d_ab[e])
                dm_bottom = dot_nt(xp[half:], d_ab[e][half:])
                col_top, col_bottom = near[:half, h : h + 1], near[half:, h : h + 1]
                row = r.cut[b, q, 4 + h : 5 + h, :]
                row_left, row_right = row[:, :half], row[:, half:]
                fade = jnp.exp(jnp.where(causal_t, row_left - col_top, -1e30))
                ds[:half, :half] += dm_top[:, :half] * fade
                top.append((r.sco[b, :half, :half] * fade).astype(BF))
                fade = jnp.exp(row_right - col_top)
                ds[:half, half:] += dm_top[:, half:] * fade
                top.append((r.sco[b, :half, half:] * fade).astype(BF))
                fade = jnp.exp(jnp.where(causal_t, row_right - col_bottom, -1e30))
                ds[half:, half:] += dm_bottom * fade
                bottom.append((r.sco[b, half:, half:] * fade).astype(BF))
            dx_top = dot(jnp.concatenate(top, axis=1), jnp.concatenate(d_ab, axis=0))
            dx_bottom = dot(
                jnp.concatenate(bottom, axis=1), jnp.concatenate([v[half:] for v in d_ab], axis=0)
            )
            dxp = jnp.concatenate([dx_top, dx_bottom], axis=0) + dx[:, lanes]
            xf, df = xp.astype(F32), dp.astype(F32)
            kept = skip[:, lanes]
            head = 4 * q + 2 * j + ((iota((2 * LANES, LANES), 0) & 127) >> 6)
            pick = (iota((2 * LANES, LANES), 1) == head).astype(F32).astype(BF)
            ssd = r.ssd[rows, span(q * 256 + j * LANES, LANES)]
            give[...] += dot(side_by_side(xf * dxp), pick)
            take[...] += dot(side_by_side(df * (ssd - kept * xf)), pick)
            dx[:, lanes] = dxp + kept * df

    def edge_grad(b, source, cols):
        first = r.clow[b * GROUP : b * GROUP + 16, cols].astype(F32)
        acc, _ = conv_acc(first, r.halo[b, :, cols], cols)
        d_acc = r.gate[0:16, span(b * 256 + source, LANES)] * silu_slope(acc, sigmoid(acc))
        r.halo_next[b, :, cols] = d_acc[0:8]

    def conv_back(b, source, cols, to, after):
        rows = rows_of(b)
        acc, shifted = conv_acc(r.clow[rows, cols].astype(F32), r.halo[b, :, cols], cols)
        d_acc = r.gate[:, span(b * 256 + source, LANES)] * silu_slope(acc, sigmoid(acc))
        for k in range(CONV):
            r.g_conv[8 * k : 8 * k + 8, cols] += fold(d_acc * shifted[k])
        r.g_conv[32:40, cols] += fold(d_acc)
        ext = jnp.concatenate([d_acc, after], axis=0)
        d_in = r.convp[3:4, cols] * d_acc
        for k in range(CONV - 1):
            d_in = d_in + r.convp[k : k + 1, cols] * ext[3 - k : 3 - k + GROUP]
        r.dproj[rows, to] = d_in.astype(BF)

    def edge_copy_back(i, cols):
        src, dst = r.halo_next.at[0, :, cols], r.dedge_in.at[:, cols]
        return remote(src, dst, r.edge_send.at[i], r.edge_recv.at[i], sibling)

    def conv_back_all(i, at, to):
        cols = span(at, 256)

        def chunk(k):
            return k * LANES, span(at + k * LANES, LANES), span(to + k * LANES, LANES)

        for k in range(2):
            edge_grad(0, *chunk(k)[:2])
            edge_grad(1, *chunk(k)[:2])
        edge_copy_back(i, cols).start()
        for k in range(2):
            conv_back(2, *chunk(k), jnp.zeros((8, LANES), F32))
            conv_back(0, *chunk(k), r.halo_next[1, :, chunk(k)[1]])
        edge_copy_back(i, cols).wait()
        for k in range(2):
            conv_back(1, *chunk(k), r.dedge_in[:, chunk(k)[1]] * is_first)

    def backward_quad(q):
        heads = span(q * 256, 256)
        put_grad(q, 512, dot(r.db_t[...], r.dproj[:, span(AT_X + q * 256, 256)]))
        put_grad(q, 256, dot(r.normed_t[...], r.dproj[:, span(AT_GATE + q * 256, 256)]))

        @pl.when(q >= 1)
        def _():
            sum_1(q - 1)

        loop(BLOCKS, lambda b: backward_block(b, q))

        @pl.when(q >= 2)
        def _():
            sum_2(q - 2)

        @pl.when(q >= 3)
        def _():
            sum_3(q - 3)

        conv_back_all(q, CX + q * 256, AT_X + q * 256)
        put_grad(q, 0, dot(r.normed_t[...], r.dproj[:, span(AT_X + q * 256, 256)]))
        sum_0(q)

    loop(QUADS, backward_quad)
    last = QUADS

    def backward_rest(b):
        rows = rows_of(b)
        key, query = r.cout[rows, 0:NSTATE], r.cout[rows, NSTATE:CX]
        d_scores = ds_of(b)[...].astype(BF)
        r.gate[:, span(b * 256, NSTATE, 128)] = r.dkb[rows, :] + dot(d_scores, query)
        r.gate[:, span(b * 256 + NSTATE, NSTATE, 128)] = r.dqb[rows, :] + dot(d_scores.T, key)
        give = give_of(b)[...]
        give_of(b)[...] = exact_sum(upper, take_of(b)[...] - give)
        z, step = head_rows(b)
        ratio = jnp.where(z < -15.0, 1.0, sigmoid(z) / jnp.maximum(step, 1e-37))
        take_of(b)[...] = give * ratio

    loop(BLOCKS, backward_rest)

    def block_total(b, run, grad, decay):
        kept = jnp.sum(run[...] * grad[...], axis=0, keepdims=True)
        summed = jnp.sum(r.flow[b], axis=0, keepdims=True) + decay * kept
        high, low = halves(jnp.broadcast_to(summed, (8, INNER)))
        by_head = dot_nt(high, r.spread[0:LANES, :]) + dot_nt(low, r.spread[0:LANES, :])
        rows = rows_of(b)
        give_of(b)[...] = give_of(b)[...] + by_head[0:1, :]

    block_total(0, r.runs.at[1], r.state_in, decay_0)
    block_total(1, r.runs.at[0], r.dstate_in, decay_1)

    def step_grad(b):
        rows = rows_of(b)
        z, step = head_rows(b)
        back_sum = give_of(b)[...]
        d_pre = take_of(b)[...] + rate * back_sum * sigmoid(z)
        r.g_head[0:8, :] += fold(d_pre)
        r.g_head[8:16, :] += fold(back_sum * (step * rate))
        r.dproj[rows, AT_DT : AT_DT + LANES] = d_pre.astype(BF)

    loop(BLOCKS, step_grad)
    sum_1(last - 1)
    conv_back_all(last, 0, 0)
    put_grad(last, 0, dot(r.normed_t[...], r.dproj[:, 0:AT_X]))
    sum_0(last)
    sum_2(last - 2)
    sum_3(last - 3)

    def in_block(b):
        rows = rows_of(b)
        r.ssd[rows, 0:D] = dot_nt(r.dproj[rows, :], w[:, 0:AT_OUT])

    in_block(2)
    sum_1(last)
    sum_2(last - 1)
    sum_3(last - 2)
    loop(2, in_block)
    sum_2(last)
    sum_3(last - 1)

    def norm_back(i):
        rows = span(i * 32, 32)
        v = r.tok[rows, :].astype(F32)
        root = lax.rsqrt(jnp.mean(v * v, axis=1, keepdims=True) + EPS)
        y = v * root
        dn = r.ssd[rows, 0:D]
        r.g_norm[...] += fold(dn * y)
        bb = r.norm_gain[...] * dn
        d_v = root * (bb - y * jnp.mean(y * bb, axis=1, keepdims=True))
        r.ssd[rows, 0:D] = r.og[rows, :].astype(F32) + d_v

    loop(ROWS // 32, norm_back)
    tgrad_copy = pltpu.make_async_copy(r.ssd.at[:, 0:D], r.tgrad, r.local.at[1])
    tgrad_copy.start()

    def total(v):
        return jnp.sum(v, axis=0, keepdims=True)

    for k in range(CONV + 1):
        r.small[0, k : k + 1, :] = total(r.g_conv[8 * k : 8 * k + 8, :])
    r.small[0, 5:6, 0:INNER] = total(r.g_inner[0:8, :])
    r.small[0, 5:6, INNER : INNER + LANES] = total(r.g_head[0:8, :])
    r.small[0, 5:6, INNER + LANES :] = total(r.g_head[8:16, :])
    r.small[0, 6:7, 0:INNER] = total(r.g_inner[8:16, :])
    r.small[0, 6:7, INNER:] = jnp.zeros((1, CX), F32)
    r.small[0, 7:8, 0:D] = total(r.g_norm[...])
    r.small[0, 7:8, D:] = jnp.zeros((1, CONVCH - D), F32)
    if fused:

        def exchange(level, first, count, device):
            copies = []
            for j in range(count):
                k = first + j
                copy = remote(
                    r.small.at[level], r.small_in.at[k], r.t_send.at[k], r.t_recv.at[k],
                    device(j + 1),
                )
                copy.start()
                copies.append(copy)
            for copy in copies:
                copy.wait()
            value = r.small[level]
            for j in range(count):
                value = value + r.small_in[first + j]
            return value

        r.small[1] = exchange(0, 0, 1, lambda j: sibling)
        r.small[2] = exchange(1, 1, PLANE - 1, on_plane)
        r.small_out[...] = exchange(2, PLANE, nz - 1, on_chain)
        sum_3(last)
        for g in range(CHUNKS):
            sum_4(g)
            n = size_of(g)
            mine = r.fin[g, span(seq * own, own, 8), 0:n]
            theirs = r.gsum[g, :, 0:n]
            r.wsum[g, 0, :, 0:n] = jnp.where(seq == 0, mine, theirs)
            r.wsum[g, 1, :, 0:n] = jnp.where(seq == 0, theirs, mine)
        for c in range(len(GATHERS)):
            gather_end(c)
    else:
        r.small_out[...] = r.small[0]
    mixed_copy.wait()
    tgrad_copy.wait()


def call_mixer(fused, nz, tok, og, weights, norm_gain, convp, headp, innerp):
    vmem = pl.BlockSpec(memory_space=pltpu.VMEM)
    hbm = pl.BlockSpec(memory_space=pl.ANY)
    own = D // (2 * nz * PLANE) if fused else 0
    ins = ["tok", "og", "shard" if fused else "w", "norm_gain", "convp", "headp", "innerp"]
    outs = {"mixed": ((ROWS, D), BF), "tgrad": ((ROWS, D), F32), "small_out": ((8, CONVCH), F32)}
    scratch = {
        "normed": ((ROWS + EDGE, D), BF), "normed_t": ((D, ROWS), BF), "db_t": ((D, ROWS), BF),
        "clow": ((ROWS + EDGE, CONVCH), BF), "cout": ((ROWS, CONVCH), BF),
        "gate": ((GROUP, INNER), F32), "back": ((GROUP, INNER), F32), "ssd": ((ROWS, INNER), F32),
        "dssd": ((ROWS, INNER), BF), "dproj": ((ROWS, AT_OUT), BF),
        "dtb": ((ROWS, LANES), F32), "cumb": ((ROWS, LANES), F32), "moved": ((ROWS, LANES), F32),
        "weight": ((ROWS, 256), BF), "fade": ((ROWS, 256), BF),
        "cut": ((BLOCKS, QUADS, 8, GROUP), F32), "spread": ((256, INNER), BF),
        "turned": ((BLOCKS, CX, GROUP), BF), "sco": ((BLOCKS, GROUP, GROUP), F32), "dkb": ((ROWS, LANES), F32), "dqb": ((ROWS, LANES), F32),
        "runs": ((2, NSTATE, INNER), F32), "held": ((2, NSTATE, INNER), BF),
        "dheld": ((2, NSTATE, INNER), F32), "dst": ((2, NSTATE, INNER), BF),
        "flow": ((2, 8, INNER), F32), "halo": ((BLOCKS, 8, CONVCH), F32),
        "halo_next": ((2, 8, CONVCH), F32), "edge_in": ((EDGE, D), BF),
        "state_in": ((NSTATE, INNER), F32), "dstate_in": ((NSTATE, INNER), F32),
        "dedge_in": ((8, CONVCH), F32), "g_norm": ((8, D), F32), "g_conv": ((40, CONVCH), F32),
        "g_head": ((16, LANES), F32), "g_inner": ((16, INNER), F32), "small": ((3, 8, CONVCH), F32),
    }
    dma = pltpu.SemaphoreType.DMA
    sems = {
        "pair_send": dma((4,)), "pair_recv": dma((4,)), "edge_send": dma((CHUNKS,)),
        "edge_recv": dma((CHUNKS,)), "local": dma((2,)),
    }
    if fused:
        part = CHUNK // 2
        outs["wsum"] = ((CHUNKS, 2, own, part), F32)
        scratch |= {
            "w": ((D, WIDE), BF), "shard_in": ((own, WIDE), F32),
            "wg": ((SLOTS, nz, PLANE, 2 * own, CHUNK), BF),
            "r0": ((CHUNKS, nz, PLANE, 2 * own, part), BF),
            "r1": ((CHUNKS, PLANE - 1, nz, 2 * own, part), BF),
            "r2": ((CHUNKS, nz - 1, 2 * own, part), BF), "fin": ((CHUNKS, 2 * own, part), F32),
            "gsum": ((CHUNKS, own, part), F32), "small_in": ((PLANE + nz - 1, 8, CONVCH), F32),
        }
        arrivals = nz - 1 + (PLANE - 1) * nz + 1
        sems |= {
            "g_send": dma((len(GATHERS), arrivals)), "g_recv": dma((len(GATHERS), arrivals)),
            "s_send": dma((CHUNKS, PLANE + nz)), "s_recv": dma((CHUNKS, PLANE + nz)),
            "t_send": dma((PLANE + nz - 1,)), "t_recv": dma((PLANE + nz - 1,)),
        }
    else:
        outs["wgrad"] = ((D, QUADS * CHUNK + AT_X), BF)
    names = ins + list(outs) + list(scratch) + list(sems)
    return pl.pallas_call(
        functools.partial(mixer, names, fused, nz),
        out_shape=[jax.ShapeDtypeStruct(s, t) for s, t in outs.values()],
        in_specs=[vmem] * len(ins),
        out_specs=[hbm, hbm, vmem, vmem],
        scratch_shapes=[pltpu.VMEM(s, t) for s, t in scratch.values()] + list(sems.values()),
        compiler_params=pltpu.CompilerParams(
            collective_id=0, has_side_effects=True, vmem_limit_bytes=63 * 1024 * 1024
        ),
        name="mixer",
    )(tok, og, weights, norm_gain, convp, headp, innerp)


def shards(
    tokens, lengths, norm_gain, in_weight, conv_weight, conv_bias, dt_bias, a_log, skip_gain,
    out_gain, out_weight, out_grad,
):
    both = ("fsdp", "seq")
    row_count = tokens.shape[2]
    own = in_weight.shape[0]
    nf = lax.axis_size("fsdp")
    fused = nf % PLANE == 0 and (2 * own) % 16 == 0 and own % 8 == 0
    nz = nf // PLANE if fused else 1
    positions = lax.axis_index("seq") * row_count + jnp.arange(row_count, dtype=jnp.int32)
    first_long = lengths[0, 0] > lengths[1, 0]
    short_valid = (positions < jnp.minimum(lengths[0, 0], lengths[1, 0]))[:, None]

    def packed(a):
        return jnp.concatenate(
            [jnp.where(first_long, a[0, 0], a[1, 0]),
             jnp.where(first_long, a[1, 0, :GROUP], a[0, 0, :GROUP])], axis=0)

    tok = packed(tokens)
    og = packed(out_grad)
    mask = jnp.concatenate([jnp.ones((row_count, 1), bool), short_valid[:GROUP]], axis=0)
    og = jnp.where(mask, og, jnp.zeros_like(og))
    kind = F32 if fused else BF
    own_weights = jnp.concatenate(
        [in_weight[:, 2 * INNER :], jnp.zeros((own, 2 * LANES - HEADS), BF),
         in_weight[:, INNER : 2 * INNER], in_weight[:, :INNER], out_weight.T], axis=1
    ).astype(kind)
    weights = own_weights
    if not fused:
        weights = lax.all_gather(own_weights, both, axis=0, tiled=True)

    def key_first(a):
        return jnp.concatenate([a[..., INNER:], a[..., :INNER]], axis=-1)

    convp = key_first(
        jnp.concatenate([conv_weight, conv_bias[None], jnp.zeros((3, CONVCH), F32)], axis=0)
    )
    headp = jnp.pad(jnp.stack([dt_bias, a_log]), ((0, 6), (0, LANES - HEADS)))
    innerp = jnp.pad(jnp.stack([out_gain, jnp.repeat(skip_gain, HEADDIM)]), ((0, 6), (0, 0)))
    mixed, tgrad, small, wsum = call_mixer(
        fused, nz, tok, og, weights, norm_gain[None], convp, headp, innerp
    )
    if fused:
        chunks = wsum[:QUADS].transpose(2, 0, 1, 3).reshape(own, QUADS, 3, 256)
        rest = wsum[QUADS, :, :, :256].transpose(1, 0, 2).reshape(own, AT_X)
    else:
        summed = lax.psum_scatter(wsum, both, scatter_dimension=0, tiled=True).astype(F32)
        chunks = summed[:, : QUADS * CHUNK].reshape(own, QUADS, 3, 256)
        rest = summed[:, QUADS * CHUNK :]
        small = lax.psum(small, both)
    x_grad, gate_grad, out_w_grad = (chunks[:, :, i].reshape(own, INNER) for i in range(3))
    in_grad = jnp.concatenate([gate_grad, x_grad, rest[:, : AT_DT + HEADS]], axis=1)
    conv_g = jnp.concatenate([small[:5, CX:], small[:5, :CX]], axis=1)

    def unpacked(a):
        long = a[:row_count]
        short = jnp.where(short_valid, jnp.pad(a[row_count:], ((0, row_count - GROUP), (0, 0))), 0)
        short = short.astype(a.dtype)
        return jnp.stack([jnp.where(first_long, long, short), jnp.where(first_long, short, long)])[
            :, None
        ]

    return (
        unpacked(mixed), unpacked(tgrad), small[7, :D], in_grad, conv_g[:4], conv_g[4],
        small[5, INNER : INNER + HEADS], small[5, INNER + LANES : INNER + LANES + HEADS],
        small[6, :INNER].reshape(HEADS, HEADDIM).sum(1), small[5, :INNER], out_w_grad.T,
    )


def solution(mesh):
    spread = P(None, "fsdp", "seq", None)
    both = ("fsdp", "seq")
    return jax.shard_map(
        shards,
        mesh=mesh,
        in_specs=(
            spread, P(None, "fsdp"), P(), P(both, None), P(), P(), P(), P(), P(), P(),
            P(None, both), spread,
        ),
        out_specs=(
            spread, spread, P(), P(both, None), P(), P(), P(), P(), P(), P(), P(None, both),
        ),
        check_vma=False,
    )
```

```python
import functools
import types

import jax
import jax.numpy as jnp
from jax import lax
from jax.experimental import pallas as pl
from jax.experimental.pallas import tpu as pltpu
from jax.sharding import PartitionSpec as P

D = 768
HEADS = 24
HEADDIM = 64
NSTATE = 128
CONV = 4
GROUP = 256
INNER = 1536
CONVCH = 1792
PROJ = 3352
EPS = 1e-05

BLOCKS = 3
ROWS = BLOCKS * GROUP
EDGE = 16
LANES = 128
QUADS = INNER // 256
AT_DT = 256
AT_X = 512
AT_GATE = AT_X + INNER
AT_OUT = AT_GATE + INNER
WIDE = AT_OUT + INNER
CX = 2 * NSTATE
CHUNK = 768
WIDE_CHUNKS = 4
CHUNKS = WIDE_CHUNKS + QUADS + 1
UNITS = 7
SLOTS = 4
GATHERS = ((0, 512), (512, 512), (1024, 1024), (AT_GATE, INNER), (AT_OUT, INNER))
PLANE = 4

BF = jnp.bfloat16
F32 = jnp.float32
MESH = pl.DeviceIdType.MESH


def dot(a, b):
    return lax.dot_general(a, b, (((1,), (0,)), ((), ())), preferred_element_type=F32)


def dot_nt(a, b):
    return lax.dot_general(a, b, (((1,), (1,)), ((), ())), preferred_element_type=F32)


def sigmoid(v):
    return 0.5 * jnp.tanh(0.5 * v) + 0.5


def halves(v):
    high = v.astype(BF)
    return high, (v - high.astype(F32)).astype(BF)


def side_by_side(v):
    return jnp.concatenate(halves(v), axis=1)


def exact_sum(triangle, v):
    high, rest = halves(v)
    low = (v - high.astype(F32) - rest.astype(F32)).astype(BF)
    parts = dot(triangle, jnp.concatenate([high, rest, low], axis=1))
    return parts[:, :LANES] + parts[:, LANES : 2 * LANES] + parts[:, 2 * LANES :]


def span(start, size, multiple=None):
    return pl.ds(pl.multiple_of(start, multiple or size), size)


def rows_of(b):
    return span(b * GROUP, GROUP)


def heads_of(q):
    return span(q * 256, 256)


def fold(v):
    total = v[0:8]
    for i in range(1, v.shape[0] // 8):
        total = total + v[8 * i : 8 * i + 8]
    return total


def iota(shape, dim):
    return lax.broadcasted_iota(jnp.int32, shape, dim)


def loop(count, body):
    def step(i, _):
        body(i)
        return 0

    lax.fori_loop(0, count, step, 0)


def silu_slope(v, sg):
    return sg * (1.0 + v * (1.0 - sg))


def mixer(names, fused, nz, *refs):
    r = types.SimpleNamespace(**dict(zip(names, refs)))
    seq = lax.axis_index("seq")
    f = lax.axis_index("fsdp")
    z_at, p_at = f // PLANE, f % PLANE
    sibling = {"seq": 1 - seq}
    is_second = (seq == 1).astype(F32)
    is_first = 1.0 - is_second

    def plane_peer(j):
        if j == 1:
            return p_at + 1 - 2 * (p_at % 2)
        if j == 2:
            return p_at + 2 - 4 * (p_at // 2)
        return 3 - p_at

    def z_peer(j):
        return (z_at + j + nz) % nz

    def on_plane(j):
        return {"fsdp": z_at * PLANE + plane_peer(j)}

    def on_chain(j):
        return {"fsdp": z_peer(j) * PLANE + p_at}

    peers = [sibling]
    if fused:
        peers += [on_plane(j) for j in range(1, PLANE)] + [on_chain(j) for j in range(1, nz)]
    barrier = pltpu.get_barrier_semaphore()
    for peer in peers:
        pl.semaphore_signal(barrier, inc=1, device_id=peer, device_id_type=MESH)

    part_rows = r.tokens.shape[2]
    raw = [buf.at[0:part_rows, m * D : (m + 1) * D] for buf in (r.dssd, r.cout) for m in range(2)]
    raw_copies = []
    for i in range(4):
        src = (r.tokens, r.out_grad)[i // 2].at[i % 2, 0]
        raw_copies.append(pltpu.make_async_copy(src, raw[i], r.local.at[2 + i]))
        raw_copies[i].start()

    if fused:
        wide = 2 * INNER
        r.shard[:, 0:CX] = r.in_weight[:, wide : wide + CX].astype(F32)
        steps = r.in_weight[:, wide + CX :].astype(F32)
        fill = jnp.zeros((steps.shape[0], AT_X - CX - HEADS), F32)
        r.shard[:, CX:AT_X] = jnp.concatenate([steps, fill], axis=1)
        r.shard[:, AT_X:AT_GATE] = r.in_weight[:, INNER:wide].astype(F32)
        r.shard[:, AT_GATE:AT_OUT] = r.in_weight[:, 0:INNER].astype(F32)
        r.shard[:, AT_OUT:] = r.out_weight[...].astype(F32)

    pl.semaphore_wait(barrier, len(peers))

    def remote(src, dst, send, recv, device):
        return pltpu.make_async_remote_copy(
            src_ref=src, dst_ref=dst, send_sem=send, recv_sem=recv, device_id=device,
            device_id_type=MESH,
        )

    def pair_copy(i, src, dst):
        return remote(src, dst, r.pair_send.at[i], r.pair_recv.at[i], sibling)

    w = r.w
    own = D // (2 * nz * PLANE) if fused else 0
    slab = 2 * own

    def part(c):
        low, size = GATHERS[c]
        return span(low + seq * (size // 2), size // 2, 128)

    def slab_of(index):
        return span(index * slab, slab, 16)

    def gather_copy(c, k, index, device):
        at = w.at[slab_of(index), part(c)]
        return remote(at, at, r.g_send.at[c, k], r.g_recv.at[c, k], device)

    def chain_copy(c, j):
        return gather_copy(c, j - 1, f, on_chain(j))

    def plane_copy(c, kind, back):
        low, size = GATHERS[c]
        owner = (p_at, p_at, plane_peer(1), plane_peer(2))[kind]
        cols = part(c)
        if kind >= 2:
            cols = span(low + seq * (size // 2) + (kind - 2) * (size // 4), size // 4, 128)
        at = w.at[slab_of((z_at - back + nz) % nz * PLANE + owner), cols]
        k = nz - 1 + back * 4 + kind
        device = on_plane((1, 2, 2, 1)[kind])
        return remote(at, at, r.g_send.at[c, k], r.g_recv.at[c, k], device)

    def last_copy(c):
        at = w.at[:, part(c)]
        k = nz - 1 + 4 * nz
        return remote(at, at, r.g_send.at[c, k], r.g_recv.at[c, k], sibling)

    def gather_own(c):
        cols = part(c)
        mine, theirs = r.shard[:, cols], r.shard_in[:, cols]
        first = jnp.where(seq == 0, mine, theirs)
        second = jnp.where(seq == 0, theirs, mine)
        w[slab_of(f), cols] = jnp.concatenate([first, second], axis=0).astype(BF)

    def gather_0(c):
        for j in range(1, nz):
            chain_copy(c, j).start()

    def gather_1(c):
        for kind in range(2):
            plane_copy(c, kind, 0).start()

    def gather_2(c):
        for back in range(1, nz):
            chain_copy(c, back).wait_recv()
            for kind in range(2):
                plane_copy(c, kind, back).start()

    def gather_3(c):
        for back in range(nz):
            for kind in range(2):
                plane_copy(c, kind, back).wait_recv()
                plane_copy(c, kind + 2, back).start()

    def gather_4(c):
        for back in range(nz):
            for kind in range(2, 4):
                plane_copy(c, kind, back).wait_recv()
        last_copy(c).start()

    def gather_5(c):
        last_copy(c).wait_recv()

    def gather_end(c):
        for j in range(1, nz):
            chain_copy(c, j).wait_send()
        for kind in range(4):
            for back in range(nz):
                plane_copy(c, kind, back).wait_send()
        last_copy(c).wait_send()

    def wide_chunk(i):
        return i, i, 0, CHUNK // 2, i, 0

    def quad_chunk(q):
        return WIDE_CHUNKS + q, q // 3, (q % 3) * 256, 128, WIDE_CHUNKS + q // 3, (q % 3) * 128

    last_chunk = (WIDE_CHUNKS + QUADS, 2, 0, AT_X // 2, UNITS - 1, 0)

    def source(g, which):
        return span(g[2] + which * g[3], g[3], 128)

    def target(g):
        return span(g[5], g[3], 128)

    def sum_copy_0(g):
        src = r.wg.at[g[1], :, :, :, source(g, 1 - seq)]
        dst = r.r0.at[g[4], :, :, :, target(g)]
        return remote(src, dst, r.s_send.at[g[0], 0], r.s_recv.at[g[0], 0], sibling)

    def sum_copy_1(g, j):
        src = r.wg.at[g[1], :, plane_peer(j), :, source(g, seq)]
        dst = r.r1.at[g[4], j - 1, :, :, target(g)]
        return remote(src, dst, r.s_send.at[g[0], j], r.s_recv.at[g[0], j], on_plane(j))

    def sum_copy_2(g, j):
        k = PLANE - 1 + j
        src = r.wg.at[g[1], z_peer(j), p_at, :, source(g, seq)]
        dst = r.r2.at[g[4], j - 1, :, target(g)]
        return remote(src, dst, r.s_send.at[g[0], k], r.s_recv.at[g[0], k], on_chain(j))

    def sum_copy_3(g):
        k = PLANE - 1 + nz
        src = r.fin.at[g[4], span((1 - seq) * own, own, 8), target(g)]
        dst = r.gsum.at[g[4], :, target(g)]
        return remote(src, dst, r.s_send.at[g[0], k], r.s_recv.at[g[0], k], sibling)

    def finish(copy):
        copy.wait_send()
        copy.wait_recv()

    def sum_0(g):
        if fused:
            sum_copy_0(g).start()

    def sum_1(g):
        if not fused:
            return
        finish(sum_copy_0(g))

        def add(i):
            at = (g[1], i // PLANE, i % PLANE, slice(None), source(g, seq))
            theirs = r.r0[g[4], i // PLANE, i % PLANE, :, target(g)]
            r.wg[at] = (r.wg[at].astype(F32) + theirs.astype(F32)).astype(BF)

        loop(nz * PLANE, add)
        for j in (3, 1, 2):
            sum_copy_1(g, j).start()

    def sum_2(g):
        if not fused:
            return
        for j in range(1, PLANE):
            finish(sum_copy_1(g, j))

        def add(zi):
            at = (g[1], zi, p_at, slice(None), source(g, seq))
            value = r.wg[at].astype(F32)
            for j in range(PLANE - 1):
                value = value + r.r1[g[4], j, zi, :, target(g)].astype(F32)
            r.wg[at] = value.astype(BF)

        loop(nz, add)
        for j in range(1, nz):
            sum_copy_2(g, j).start()

    def sum_3(g):
        if not fused:
            return
        for j in range(1, nz):
            finish(sum_copy_2(g, j))
        value = r.wg[g[1], z_at, p_at, :, source(g, seq)].astype(F32)
        for j in range(nz - 1):
            value = value + r.r2[g[4], j, :, target(g)].astype(F32)
        r.fin[g[4], :, target(g)] = value
        sum_copy_3(g).start()

    def sum_4(g):
        finish(sum_copy_3(g))

    def put_grad(g, low, value):
        size = value.shape[1]
        if fused:
            parts = value.astype(BF).reshape(nz, PLANE, slab, size)
            r.wg[g[1], :, :, :, span(g[2] + low, size, 128)] = parts
        else:
            first = g[4] * CHUNK + (g[2] if g[3] == 128 else 0)
            r.wgrad[:, span(first + low, size, 128)] = value.astype(BF)

    def shard_copy(c):
        low, size = GATHERS[c]
        cols = span(low + (1 - seq) * (size // 2), size // 2, 128)
        return pair_copy(4 + c, r.shard.at[:, cols], r.shard_in.at[:, cols])

    if fused:
        for c in range(len(GATHERS)):
            shard_copy(c).start()

    def make_spread(q):
        shape = (256, 256)
        head = (iota(shape, 1) + q * 256) >> 6
        r.spread[:, span(q * 256, 256)] = (head == (iota(shape, 0) & 127)).astype(F32).astype(BF)

    if fused:
        for c in range(len(GATHERS)):
            shard_copy(c).wait()
            gather_own(c)
            if c < 2:
                gather_0(c)
                gather_1(c)
        gather_0(2)

    r.convp[0:CONV, 0:CX] = r.conv_weight[:, INNER:]
    r.convp[0:CONV, CX:] = r.conv_weight[:, 0:INNER]
    bias = r.conv_bias[...].reshape(1, CONVCH)
    r.convp[4:5, 0:CX] = bias[:, INNER:]
    r.convp[4:5, CX:] = bias[:, 0:INNER]
    r.headp[...] = jnp.zeros_like(r.headp)
    for i, v in enumerate((r.dt_bias, r.a_log, r.skip_gain)):
        r.headp[i : i + 1, 0:HEADS] = v[...].reshape(1, HEADS)
    norm_gain = r.norm_gain[...].reshape(1, D)

    first_long = r.lengths[0, 0] > r.lengths[1, 0]
    shortest = jnp.minimum(r.lengths[0, 0], r.lengths[1, 0])
    for i in range(4):
        raw_copies[i].wait()

    def pick_rows(i):
        here = span(i * 64, 64)
        for to, k in ((r.tok, 0), (r.og, 2)):
            to[here, :] = jnp.where(first_long, raw[k][here, :], raw[k + 1][here, :])

    def pick_short(i):
        here, there = span(i * 64, 64), span(2 * GROUP + i * 64, 64)
        r.tok[there, :] = jnp.where(first_long, raw[1][here, :], raw[0][here, :])
        valid = (seq * part_rows + i * 64 + iota((64, D), 0) < shortest).astype(F32)
        picked = jnp.where(first_long, raw[3][here, :], raw[2][here, :])
        r.og[there, :] = (picked.astype(F32) * valid).astype(BF)

    loop(2 * GROUP // 64, pick_rows)
    edge_copy = pair_copy(0, r.tok.at[2 * GROUP - EDGE : 2 * GROUP, :], r.edge_in)
    edge_copy.start()
    loop(GROUP // 64, pick_short)

    loop(QUADS, make_spread)
    r.innerp[0:1, :] = r.out_gain[...].reshape(1, INNER)
    r.innerp[1:2, :] = dot(side_by_side(r.headp[...]), r.spread[...])[2:3, :]
    tri_shape = (GROUP, GROUP)
    lower = (iota(tri_shape, 0) >= iota(tri_shape, 1)).astype(F32).astype(BF)
    upper = (iota(tri_shape, 0) <= iota(tri_shape, 1)).astype(F32).astype(BF)
    half = GROUP // 2
    causal = iota((half, half), 0) >= iota((half, half), 1)
    causal_t = iota((half, half), 0) <= iota((half, half), 1)
    first_head = iota((GROUP, LANES), 1) < HEADDIM
    rate = -jnp.exp(r.headp[1:2, :])

    r.g_norm[...] = jnp.zeros_like(r.g_norm)
    r.g_conv[...] = jnp.zeros_like(r.g_conv)
    r.g_head[...] = jnp.zeros_like(r.g_head)
    r.g_inner[...] = jnp.zeros_like(r.g_inner)
    r.halo[2] = jnp.zeros((8, CONVCH), F32)
    r.dproj[:, AT_DT + LANES : AT_X] = jnp.zeros((ROWS, AT_X - AT_DT - LANES), BF)

    def norm_of(v):
        root = lax.rsqrt(jnp.mean(v * v, axis=1, keepdims=True) + EPS)
        return (v * root * norm_gain).astype(BF)

    def norm_rows(i):
        rows = span(i * 64, 64)
        r.normed[rows, :] = norm_of(r.tok[rows, :].astype(F32))

    loop(ROWS // 64, norm_rows)
    edge_copy.wait()
    r.normed[ROWS:, :] = norm_of(r.edge_in[...].astype(F32) * is_second)

    if fused:
        gather_2(0)
        gather_1(2)
        gather_0(3)

    def turn(b):
        rows = rows_of(b)
        r.normed_t[:, rows] = r.normed[rows, :].T
        r.db_t[:, rows] = r.og[rows, :].T

    loop(BLOCKS, turn)

    if fused:
        gather_2(1)
        gather_3(0)
        gather_4(0)
        gather_3(1)
        gather_5(0)

    def conv_acc(values, before, cols):
        rows = values.shape[0]
        ext = jnp.concatenate([before, values], axis=0)
        shifted = [ext[5 + k : 5 + k + rows] for k in range(CONV)]
        acc = r.convp[4:5, cols]
        for k in range(CONV):
            acc = acc + r.convp[k : k + 1, cols] * shifted[k]
        return acc, shifted

    def project(at, to):
        low = dot(r.normed[...], w[:, at]).astype(BF)
        r.clow[:, to] = low
        r.halo[0, :, to] = low[ROWS : ROWS + EDGE].astype(F32)[EDGE - 8 :]
        r.halo[1, :, to] = low[GROUP - 16 : GROUP].astype(F32)[8:]

    def conv_forward(b, cols):
        rows = rows_of(b)
        acc, _ = conv_acc(r.clow[rows, cols].astype(F32), r.halo[b, :, cols], cols)
        r.cout[rows, cols] = (acc * sigmoid(acc)).astype(BF)

    project(pl.ds(0, CX), pl.ds(0, CX))
    r.dtb[...] = dot(r.normed[0:ROWS, :], w[:, AT_DT : AT_DT + LANES])

    def head_rows(b):
        z = r.dtb[rows_of(b), :] + r.headp[0:1, :]
        step = jnp.maximum(z, 0.0) + jnp.log1p(jnp.exp(-jnp.abs(z)))
        return z, step

    def prepare(b):
        rows = rows_of(b)
        conv_forward(b, pl.ds(0, LANES))
        conv_forward(b, pl.ds(LANES, LANES))
        z, step = head_rows(b)
        cum = exact_sum(lower, step * rate)
        moved = cum - jnp.log(jnp.maximum(step, 1e-37))
        r.cumb[rows, :] = cum
        r.moved[rows, :] = moved
        cum_t, moved_t = cum.T, moved.T
        for q in range(QUADS):
            r.cut[b, q, 0:4, :] = moved_t[4 * q : 4 * q + 4, :]
            r.cut[b, q, 4:8, :] = cum_t[4 * q : 4 * q + 4, :]
        r.weight[rows, :] = side_by_side(jnp.exp(cum[GROUP - 1 : GROUP, :] - cum) * step)
        r.fade[rows, :] = side_by_side(jnp.exp(cum))
        key, query = r.cout[rows, 0:NSTATE], r.cout[rows, NSTATE:CX]
        r.turned[b, 0:NSTATE, :] = key.T
        r.turned[b, NSTATE:CX, :] = query.T
        r.sco[b] = dot_nt(query, key)

    loop(BLOCKS, prepare)

    def to_first(v, q):
        return pltpu.roll(v, (LANES - 4 * q) % LANES, 1)

    def forward_block(b, q):
        rows = rows_of(b)
        cols = span(CX + q * 256, 256)
        heads = span(q * 256, 256)
        for i in range(2):
            conv_forward(b, span(CX + q * 256 + i * LANES, LANES))
        xq = r.cout[rows, cols]

        @pl.when(b < 2)
        def _():
            spread_w = dot(r.weight[rows, :], r.spread[:, heads])
            scaled = (xq.astype(F32) * spread_w).astype(BF)
            r.runs[b, :, heads] = dot(r.turned[b, 0:NSTATE, :], scaled)

        near = to_first(r.cumb[rows, :], q)
        skip = r.innerp[1:2, heads]
        for j in range(2):
            lanes = slice(j * LANES, (j + 1) * LANES)
            xp = xq[:, lanes]
            zero = jnp.zeros_like(xp)
            x_ab = (jnp.where(first_head, xp, zero), jnp.where(first_head, zero, xp))
            top, bottom = [], []
            for e in range(2):
                h = 2 * j + e
                col_top, col_bottom = near[:half, h : h + 1], near[half:, h : h + 1]
                row = r.cut[b, q, h : h + 1, :]
                row_left, row_right = row[:, :half], row[:, half:]
                gap = jnp.where(causal, col_top - row_left, -1e30)
                top.append((r.sco[b, :half, :half] * jnp.exp(gap)).astype(BF))
                fade = jnp.exp(col_bottom - row_left)
                bottom.append((r.sco[b, half:, :half] * fade).astype(BF))
                gap = jnp.where(causal, col_bottom - row_right, -1e30)
                bottom.append((r.sco[b, half:, half:] * jnp.exp(gap)).astype(BF))
            out_top = dot(
                jnp.concatenate(top, axis=1), jnp.concatenate([v[:half] for v in x_ab], axis=0)
            )
            out_bottom = dot(jnp.concatenate(bottom, axis=1), jnp.concatenate(x_ab, axis=0))
            place = span(q * 256 + j * LANES, LANES)
            xf = xp.astype(F32) * skip[:, lanes]
            r.ssd[span(b * GROUP, half), place] = out_top + xf[:half]
            r.ssd[span(b * GROUP + half, half), place] = out_bottom + xf[half:]

    def forward_quad(q):
        if fused:

            @pl.when(q == 0)
            def _():
                gather_2(2)
                gather_0(4)
                gather_4(1)
                gather_1(3)
                gather_5(1)

            @pl.when(q == 1)
            def _():
                gather_3(2)
                gather_2(3)

            @pl.when(q == 2)
            def _():
                gather_4(2)
                gather_1(4)
                gather_3(3)
                gather_5(2)

            @pl.when(q == 3)
            def _():
                gather_2(4)

            @pl.when(q == 4)
            def _():
                gather_4(3)

            @pl.when(q == 5)
            def _():
                gather_3(4)

        project(span(AT_X + q * 256, 256), span(CX + q * 256, 256))
        loop(BLOCKS, lambda b: forward_block(b, q))

    loop(QUADS, forward_quad)

    def decay_of(b):
        last = r.cumb[b * GROUP + GROUP - 8 : (b + 1) * GROUP, :]
        return dot(side_by_side(jnp.exp(last)), r.spread[...])[7:8, :]

    decay_0, decay_1 = decay_of(0), decay_of(1)
    r.runs[1] = r.runs[1] + decay_1 * r.runs[0]
    state_copy = pair_copy(2, r.runs.at[1], r.state_in)
    state_copy.start()
    if fused:
        gather_4(4)
        gather_5(3)

    def carry_block(b):
        rows = rows_of(b)
        query = r.cout[rows, NSTATE:CX]

        def quad(q):
            cols = span(q * 256, 256)
            r.ssd[rows, cols] += dot(query, r.held[b, :, cols]) * dot(
                r.fade[rows, :], r.spread[:, cols]
            )

        loop(QUADS, quad)

    gain = r.innerp[0:1, :]

    def gate_project(b):
        rows = rows_of(b)

        def quad(q):
            cols = span(q * 256, 256)
            r.gate[:, cols] = dot(r.normed[rows, :], w[:, span(AT_GATE + q * 256, 256)])

        loop(QUADS, quad)

    def out_back(b):
        rows = rows_of(b)

        def quad(q):
            cols = span(q * 256, 256)
            r.back[:, cols] = dot(r.og[rows, :], w[:, span(AT_OUT + q * 256, 256)])

        loop(QUADS, quad)

    def gate_block(b):
        def gate_rows(i):
            here = span(b * GROUP + i * 16, 16)
            local = span(i * 16, 16)
            d_out, g, s = r.back[local, :], r.gate[local, :], r.ssd[here, :]
            sg = sigmoid(g)
            silu = g * sg
            gated = s * silu
            root = lax.rsqrt(jnp.mean(gated * gated, axis=1, keepdims=True) + EPS)
            v = gated * root
            r.dproj[here, AT_X:AT_GATE] = (v * gain).astype(BF)
            r.g_inner[0:8, :] += fold(d_out * v)
            a = gain * d_out
            d_gated = root * (a - v * jnp.mean(v * a, axis=1, keepdims=True))
            d_s = (d_gated * silu).astype(BF)
            r.dssd[here, :] = d_s
            r.g_inner[8:16, :] += fold(d_s.astype(F32) * r.cout[here, CX:].astype(F32))
            r.dproj[here, AT_GATE:AT_OUT] = (d_gated * s * silu_slope(g, sg)).astype(BF)

        loop(GROUP // 16, gate_rows)

    gate_project(2)
    if fused:
        gather_5(4)
    out_back(2)
    gate_block(2)
    state_copy.wait()
    r.state_in[...] = r.state_in[...] * is_second
    r.held[0] = r.state_in[...].astype(BF)
    r.runs[0] = r.runs[0] + decay_0 * r.state_in[...]
    r.held[1] = r.runs[0].astype(BF)
    r.runs[1] = r.state_in[...]

    def gate_long(b):
        gate_project(b)
        out_back(b)
        carry_block(b)
        gate_block(b)

    loop(2, gate_long)

    def wide_grad(i):
        g = wide_chunk(i)
        left = r.db_t if i < 2 else r.normed_t
        first = (AT_X if i < 2 else AT_GATE) + (i % 2) * CHUNK

        def tile(k):
            put_grad(g, k * 256, dot(left[...], r.dproj[:, span(first + k * 256, 256)]))

        loop(CHUNK // 256, tile)
        sum_0(g)

    for i in range(WIDE_CHUNKS):
        wide_grad(i)
    sum_1(wide_chunk(0))

    def state_back(b):
        rows = rows_of(b)

        def quad(q, dq):
            cols = span(q * 256, 256)
            spread_f = dot(r.fade[rows, :], r.spread[:, cols])
            dz = (spread_f * r.dssd[rows, cols].astype(F32)).astype(BF)
            r.dheld[b, :, cols] = dot(r.turned[b, NSTATE:CX, :], dz)
            return dq + dot_nt(dz, r.held[b, :, cols])

        r.dqb[rows, :] = lax.fori_loop(0, QUADS, quad, jnp.zeros((GROUP, NSTATE), F32))

    loop(2, state_back)
    r.dqb[2 * GROUP :, :] = jnp.zeros((GROUP, NSTATE), F32)
    r.dheld[0] = r.dheld[0] + decay_0 * r.dheld[1]
    dstate_copy = pair_copy(3, r.dheld.at[0], r.dstate_in)
    dstate_copy.start()
    sum_1(wide_chunk(1))

    def out_block(b):
        rows = rows_of(b)
        branch = dot_nt(r.dproj[rows, AT_X:AT_GATE], w[:, AT_OUT:])
        r.normed[rows, :] = (r.tok[rows, :].astype(F32) + branch).astype(BF)

    loop(BLOCKS, out_block)
    mixed_copy = pltpu.make_async_copy(r.normed.at[0:ROWS, :], r.mixed, r.local.at[0])
    mixed_copy.start()
    sum_1(wide_chunk(2))

    def ds_of(b):
        return r.back.at[:, heads_of(b)]

    def give_of(b):
        return r.back.at[:, span(CHUNK + b * LANES, LANES)]

    def take_of(b):
        return r.back.at[:, span(CHUNK + (BLOCKS + b) * LANES, LANES)]

    def prepare_back(b):
        rows = rows_of(b)
        r.sco[b] = dot_nt(r.cout[rows, 0:NSTATE], r.cout[rows, NSTATE:CX])
        ds_of(b)[...] = jnp.zeros((GROUP, GROUP), F32)
        nothing = jnp.zeros((GROUP, LANES), F32)
        r.dkb[rows, :] = nothing
        give_of(b)[...] = nothing
        take_of(b)[...] = nothing

    loop(BLOCKS, prepare_back)
    dstate_copy.wait()
    r.dstate_in[...] = r.dstate_in[...] * is_first
    r.dst[1] = r.dstate_in[...].astype(BF)
    r.state_in[...] = r.dheld[1] + decay_1 * r.dstate_in[...]
    r.dst[0] = r.state_in[...].astype(BF)

    def backward_block(b, q):
        rows = rows_of(b)
        heads = span(q * 256, 256)
        xq = r.cout[rows, span(CX + q * 256, 256)]
        dq4 = r.dssd[rows, heads]
        skip = r.innerp[1:2, heads]
        dx, ds = r.gate.at[:, heads_of(b)], ds_of(b)
        give, take = give_of(b), take_of(b)

        @pl.when(b < 2)
        def _():
            spread_w = dot(r.weight[rows, :], r.spread[:, heads])
            d_states = r.dst[b, :, heads]
            dx_state = spread_w * dot(r.cout[rows, 0:NSTATE], d_states)
            r.flow[b, 0:8, heads] = fold(xq.astype(F32) * dx_state)
            r.dkb[rows, :] += dot_nt((xq.astype(F32) * spread_w).astype(BF), d_states)
            dx[...] = dx_state

        @pl.when(b == 2)
        def _():
            dx[...] = jnp.zeros((GROUP, 256), F32)

        near = to_first(r.moved[rows, :], q)
        for j in range(2):
            lanes = slice(j * LANES, (j + 1) * LANES)
            xp, dp = xq[:, lanes], dq4[:, lanes]
            zero = jnp.zeros_like(xp)
            d_ab = (jnp.where(first_head, dp, zero), jnp.where(first_head, zero, dp))
            top, bottom = [], []
            for e in range(2):
                h = 2 * j + e
                dm_top = dot_nt(xp[:half], d_ab[e])
                dm_bottom = dot_nt(xp[half:], d_ab[e][half:])
                col_top, col_bottom = near[:half, h : h + 1], near[half:, h : h + 1]
                row = r.cut[b, q, 4 + h : 5 + h, :]
                row_left, row_right = row[:, :half], row[:, half:]
                fade = jnp.exp(jnp.where(causal_t, row_left - col_top, -1e30))
                ds[:half, :half] += dm_top[:, :half] * fade
                top.append((r.sco[b, :half, :half] * fade).astype(BF))
                fade = jnp.exp(row_right - col_top)
                ds[:half, half:] += dm_top[:, half:] * fade
                top.append((r.sco[b, :half, half:] * fade).astype(BF))
                fade = jnp.exp(jnp.where(causal_t, row_right - col_bottom, -1e30))
                ds[half:, half:] += dm_bottom * fade
                bottom.append((r.sco[b, half:, half:] * fade).astype(BF))
            dx_top = dot(jnp.concatenate(top, axis=1), jnp.concatenate(d_ab, axis=0))
            dx_bottom = dot(
                jnp.concatenate(bottom, axis=1), jnp.concatenate([v[half:] for v in d_ab], axis=0)
            )
            dxp = jnp.concatenate([dx_top, dx_bottom], axis=0) + dx[:, lanes]
            xf, df = xp.astype(F32), dp.astype(F32)
            kept = skip[:, lanes]
            head = 4 * q + 2 * j + ((iota((2 * LANES, LANES), 0) & 127) >> 6)
            pick = (iota((2 * LANES, LANES), 1) == head).astype(F32).astype(BF)
            ssd = r.ssd[rows, span(q * 256 + j * LANES, LANES)]
            give[...] += dot(side_by_side(xf * dxp), pick)
            take[...] += dot(side_by_side(df * (ssd - kept * xf)), pick)
            dx[:, lanes] = dxp + kept * df

    def edge_grad(b, source, cols):
        first = r.clow[b * GROUP : b * GROUP + 16, cols].astype(F32)
        acc, _ = conv_acc(first, r.halo[b, :, cols], cols)
        d_acc = r.gate[0:16, span(b * 256 + source, LANES)] * silu_slope(acc, sigmoid(acc))
        r.halo_next[b, :, cols] = d_acc[0:8]

    def conv_back(b, source, cols, to, after):
        rows = rows_of(b)
        acc, shifted = conv_acc(r.clow[rows, cols].astype(F32), r.halo[b, :, cols], cols)
        d_acc = r.gate[:, span(b * 256 + source, LANES)] * silu_slope(acc, sigmoid(acc))
        for k in range(CONV):
            r.g_conv[8 * k : 8 * k + 8, cols] += fold(d_acc * shifted[k])
        r.g_conv[32:40, cols] += fold(d_acc)
        ext = jnp.concatenate([d_acc, after], axis=0)
        d_in = r.convp[3:4, cols] * d_acc
        for k in range(CONV - 1):
            d_in = d_in + r.convp[k : k + 1, cols] * ext[3 - k : 3 - k + GROUP]
        r.dproj[rows, to] = d_in.astype(BF)

    def edge_copy_back(i, cols):
        src, dst = r.halo_next.at[0, :, cols], r.dedge_in.at[:, cols]
        return remote(src, dst, r.edge_send.at[i], r.edge_recv.at[i], sibling)

    def conv_back_all(i, at, to):
        cols = span(at, 256)

        def chunk(k):
            return k * LANES, span(at + k * LANES, LANES), span(to + k * LANES, LANES)

        for k in range(2):
            edge_grad(0, *chunk(k)[:2])
            edge_grad(1, *chunk(k)[:2])
        edge_copy_back(i, cols).start()
        for k in range(2):
            conv_back(2, *chunk(k), jnp.zeros((8, LANES), F32))
            conv_back(0, *chunk(k), r.halo_next[1, :, chunk(k)[1]])
        edge_copy_back(i, cols).wait()
        for k in range(2):
            conv_back(1, *chunk(k), r.dedge_in[:, chunk(k)[1]] * is_first)

    def backward_quad(q):
        for i in range(WIDE_CHUNKS):

            @pl.when(q == i)
            def _():
                sum_2(wide_chunk(i))

        @pl.when(q == 0)
        def _():
            sum_1(wide_chunk(3))

        loop(BLOCKS, lambda b: backward_block(b, q))

        for i in range(WIDE_CHUNKS):

            @pl.when(q == i)
            def _():
                sum_3(wide_chunk(i))

        @pl.when(q >= 1)
        def _():
            sum_1(quad_chunk(q - 1))

        @pl.when(q >= 2)
        def _():
            sum_2(quad_chunk(q - 2))

        @pl.when(q >= 3)
        def _():
            sum_3(quad_chunk(q - 3))

        conv_back_all(q, CX + q * 256, AT_X + q * 256)
        g = quad_chunk(q)
        put_grad(g, 0, dot(r.normed_t[...], r.dproj[:, span(AT_X + q * 256, 256)]))
        sum_0(g)

    loop(QUADS, backward_quad)

    def backward_rest(b):
        rows = rows_of(b)
        key, query = r.cout[rows, 0:NSTATE], r.cout[rows, NSTATE:CX]
        d_scores = ds_of(b)[...].astype(BF)
        r.gate[:, span(b * 256, NSTATE, 128)] = r.dkb[rows, :] + dot(d_scores, query)
        r.gate[:, span(b * 256 + NSTATE, NSTATE, 128)] = r.dqb[rows, :] + dot(d_scores.T, key)
        give = give_of(b)[...]
        give_of(b)[...] = exact_sum(upper, take_of(b)[...] - give)
        z, step = head_rows(b)
        ratio = jnp.where(z < -15.0, 1.0, sigmoid(z) / jnp.maximum(step, 1e-37))
        take_of(b)[...] = give * ratio

    loop(BLOCKS, backward_rest)

    def block_total(b, run, grad, decay):
        kept = jnp.sum(run[...] * grad[...], axis=0, keepdims=True)
        summed = jnp.sum(r.flow[b], axis=0, keepdims=True) + decay * kept
        high, low = halves(jnp.broadcast_to(summed, (8, INNER)))
        by_head = dot_nt(high, r.spread[0:LANES, :]) + dot_nt(low, r.spread[0:LANES, :])
        rows = rows_of(b)
        give_of(b)[...] = give_of(b)[...] + by_head[0:1, :]

    block_total(0, r.runs.at[1], r.state_in, decay_0)
    block_total(1, r.runs.at[0], r.dstate_in, decay_1)

    def step_grad(b):
        rows = rows_of(b)
        z, step = head_rows(b)
        back_sum = give_of(b)[...]
        d_pre = take_of(b)[...] + rate * back_sum * sigmoid(z)
        r.g_head[0:8, :] += fold(d_pre)
        r.g_head[8:16, :] += fold(back_sum * (step * rate))
        r.dproj[rows, AT_DT : AT_DT + LANES] = d_pre.astype(BF)

    loop(BLOCKS, step_grad)
    sum_1(quad_chunk(5))
    conv_back_all(QUADS, 0, 0)
    put_grad(last_chunk, 0, dot(r.normed_t[...], r.dproj[:, 0:AT_X]))
    sum_0(last_chunk)
    sum_2(quad_chunk(4))
    sum_3(quad_chunk(3))

    def in_block(b):
        rows = rows_of(b)
        r.ssd[rows, 0:D] = dot_nt(r.dproj[rows, :], w[:, 0:AT_OUT])

    in_block(2)
    sum_1(last_chunk)
    sum_2(quad_chunk(5))
    sum_3(quad_chunk(4))
    loop(2, in_block)
    sum_2(last_chunk)
    sum_3(quad_chunk(5))

    def norm_back(i):
        rows = span(i * 32, 32)
        v = r.tok[rows, :].astype(F32)
        root = lax.rsqrt(jnp.mean(v * v, axis=1, keepdims=True) + EPS)
        y = v * root
        dn = r.ssd[rows, 0:D]
        r.g_norm[...] += fold(dn * y)
        bb = norm_gain * dn
        d_v = root * (bb - y * jnp.mean(y * bb, axis=1, keepdims=True))
        r.ssd[rows, 0:D] = r.og[rows, :].astype(F32) + d_v

    loop(ROWS // 32, norm_back)
    tgrad_copy = pltpu.make_async_copy(r.ssd.at[:, 0:D], r.tgrad, r.local.at[1])
    tgrad_copy.start()

    def total(v):
        return jnp.sum(v, axis=0, keepdims=True)

    for k in range(CONV + 1):
        r.small[0, k : k + 1, :] = total(r.g_conv[8 * k : 8 * k + 8, :])
    r.small[0, 5:6, 0:INNER] = total(r.g_inner[0:8, :])
    r.small[0, 5:6, INNER : INNER + LANES] = total(r.g_head[0:8, :])
    r.small[0, 5:6, INNER + LANES :] = total(r.g_head[8:16, :])
    high, low = halves(r.g_inner[8:16, :])
    skips = dot_nt(high, r.spread[0:LANES, :]) + dot_nt(low, r.spread[0:LANES, :])
    r.small[0, 6:7, 0:LANES] = total(skips)
    r.small[0, 6:7, LANES:] = jnp.zeros((1, CONVCH - LANES), F32)
    r.small[0, 7:8, 0:D] = total(r.g_norm[...])
    r.small[0, 7:8, D:] = jnp.zeros((1, CONVCH - D), F32)
    if fused:

        def exchange(level, first, count, device):
            copies = []
            for j in range(count):
                k = first + j
                copy = remote(
                    r.small.at[level], r.small_in.at[k], r.t_send.at[k], r.t_recv.at[k],
                    device(j + 1),
                )
                copy.start()
                copies.append(copy)
            for copy in copies:
                copy.wait()
            value = r.small[level]
            for j in range(count):
                value = value + r.small_in[first + j]
            return value

        r.small[1] = exchange(0, 0, 1, lambda j: sibling)
        r.small[2] = exchange(1, 1, PLANE - 1, on_plane)
        r.small_out[...] = exchange(2, PLANE, nz - 1, on_chain)
        sum_3(last_chunk)
        def hand_out(g, dst, first, count):
            sum_4(g)
            mine = r.fin[g[4], span(seq * own, own, 8), target(g)]
            theirs = r.gsum[g[4], :, target(g)]
            for half_at in range(2):
                value = jnp.where(seq == half_at, mine, theirs)
                size = min(g[3], count - half_at * g[3])
                at = first + half_at * g[3]
                dst[:, at : at + size] = value[:, 0:size]

        for i in range(WIDE_CHUNKS):
            dst = r.grad_out if i < 2 else r.grad_in
            hand_out(wide_chunk(i), dst, (i % 2) * CHUNK, CHUNK)
        for q in range(QUADS):
            hand_out(quad_chunk(q), r.grad_in, INNER + q * 256, 256)
        hand_out(last_chunk, r.grad_in, 2 * INNER, CX + HEADS)
        for c in range(len(GATHERS)):
            gather_end(c)
    else:
        r.small_out[...] = r.small[0]
    mixed_copy.wait()
    tgrad_copy.wait()


def call_mixer(fused, nz, arrays):
    vmem = pl.BlockSpec(memory_space=pltpu.VMEM)
    hbm = pl.BlockSpec(memory_space=pl.ANY)
    places = {"lengths": pl.BlockSpec(memory_space=pltpu.SMEM), "tokens": hbm, "out_grad": hbm}
    own = D // (2 * nz * PLANE) if fused else 0
    ins = list(arrays)
    outs = {"mixed": ((ROWS, D), BF), "tgrad": ((ROWS, D), F32), "small_out": ((8, CONVCH), F32)}
    scratch = {
        "tok": ((ROWS, D), BF), "og": ((ROWS, D), BF), "convp": ((8, CONVCH), F32),
        "headp": ((8, LANES), F32), "innerp": ((8, INNER), F32),
        "normed": ((ROWS + EDGE, D), BF), "normed_t": ((D, ROWS), BF), "db_t": ((D, ROWS), BF),
        "clow": ((ROWS + EDGE, CONVCH), BF), "cout": ((ROWS, CONVCH), BF),
        "gate": ((GROUP, INNER), F32), "back": ((GROUP, INNER), F32), "ssd": ((ROWS, INNER), F32),
        "dssd": ((ROWS, INNER), BF), "dproj": ((ROWS, AT_OUT), BF),
        "dtb": ((ROWS, LANES), F32), "cumb": ((ROWS, LANES), F32), "moved": ((ROWS, LANES), F32),
        "weight": ((ROWS, 256), BF), "fade": ((ROWS, 256), BF),
        "cut": ((BLOCKS, QUADS, 8, GROUP), F32), "spread": ((256, INNER), BF),
        "turned": ((BLOCKS, CX, GROUP), BF), "sco": ((BLOCKS, GROUP, GROUP), F32), "dkb": ((ROWS, LANES), F32), "dqb": ((ROWS, LANES), F32),
        "runs": ((2, NSTATE, INNER), F32), "held": ((2, NSTATE, INNER), BF),
        "dheld": ((2, NSTATE, INNER), F32), "dst": ((2, NSTATE, INNER), BF),
        "flow": ((2, 8, INNER), F32), "halo": ((BLOCKS, 8, CONVCH), F32),
        "halo_next": ((2, 8, CONVCH), F32), "edge_in": ((EDGE, D), BF),
        "state_in": ((NSTATE, INNER), F32), "dstate_in": ((NSTATE, INNER), F32),
        "dedge_in": ((8, CONVCH), F32), "g_norm": ((8, D), F32), "g_conv": ((40, CONVCH), F32),
        "g_head": ((16, LANES), F32), "g_inner": ((16, INNER), F32), "small": ((3, 8, CONVCH), F32),
    }
    dma = pltpu.SemaphoreType.DMA
    sems = {
        "pair_send": dma((9,)), "pair_recv": dma((9,)), "edge_send": dma((QUADS + 1,)),
        "edge_recv": dma((QUADS + 1,)), "local": dma((6,)),
    }
    if fused:
        part = CHUNK // 2
        outs |= {"grad_in": ((own, PROJ), F32), "grad_out": ((own, INNER), F32)}
        scratch |= {
            "w": ((D, WIDE), BF), "shard": ((own, WIDE), F32), "shard_in": ((own, WIDE), F32),
            "wg": ((SLOTS, nz, PLANE, 2 * own, CHUNK), BF),
            "r0": ((UNITS, nz, PLANE, 2 * own, part), BF),
            "r1": ((UNITS, PLANE - 1, nz, 2 * own, part), BF),
            "r2": ((UNITS, nz - 1, 2 * own, part), BF), "fin": ((UNITS, 2 * own, part), F32),
            "gsum": ((UNITS, own, part), F32), "small_in": ((PLANE + nz - 1, 8, CONVCH), F32),
        }
        arrivals = nz - 1 + 4 * nz + 1
        sems |= {
            "g_send": dma((len(GATHERS), arrivals)), "g_recv": dma((len(GATHERS), arrivals)),
            "s_send": dma((CHUNKS, PLANE + nz)), "s_recv": dma((CHUNKS, PLANE + nz)),
            "t_send": dma((PLANE + nz - 1,)), "t_recv": dma((PLANE + nz - 1,)),
        }
    else:
        outs["wgrad"] = ((D, WIDE), BF)
    names = ins + list(outs) + list(scratch) + list(sems)
    return pl.pallas_call(
        functools.partial(mixer, names, fused, nz),
        out_shape=[jax.ShapeDtypeStruct(s, t) for s, t in outs.values()],
        in_specs=[places.get(name, vmem) for name in ins],
        out_specs=[hbm, hbm] + [vmem] * (len(outs) - 2),
        scratch_shapes=[pltpu.VMEM(s, t) for s, t in scratch.values()] + list(sems.values()),
        compiler_params=pltpu.CompilerParams(
            collective_id=0, has_side_effects=True, vmem_limit_bytes=63 * 1024 * 1024
        ),
        name="mixer",
    )(*arrays.values())


def place_results(
    lengths, mixed, tgrad, small, grad_in, grad_out, mixed_at, tgrad_at, norm, in_at, conv, bias,
    step, rates, skip, gain, out_at, blank, blank_low, sems,
):
    seq = lax.axis_index("seq")
    long = jnp.where(lengths[0, 0] > lengths[1, 0], 0, 1)
    rows = mixed_at.shape[2]
    blank[...] = jnp.zeros_like(blank)
    blank_low[...] = jnp.zeros_like(blank_low)
    copies = []
    for i, (src, dst, zero) in enumerate(((tgrad, tgrad_at, blank), (mixed, mixed_at, blank_low))):
        first, after = dst.at[1 - long, 0, 0:GROUP, :], dst.at[1 - long, 0, GROUP:rows, :]
        whole = pltpu.make_async_copy(src.at[0:rows, :], dst.at[long, 0], sems.at[3 * i])
        used = pltpu.make_async_copy(src.at[rows : rows + GROUP, :], first, sems.at[3 * i + 1])
        unused = pltpu.make_async_copy(zero.at[0:GROUP, :], first, sems.at[3 * i + 1])
        end = pltpu.make_async_copy(zero.at[0 : rows - GROUP, :], after, sems.at[3 * i + 2])
        whole.start()
        pl.when(seq == 0)(used.start)
        pl.when(seq > 0)(unused.start)
        end.start()
        copies += [whole, used, end]
    in_at[...] = grad_in[...]
    out_at[...] = grad_out[...]
    conv[:, 0:INNER] = small[0:CONV, CX:]
    conv[:, INNER:] = small[0:CONV, 0:CX]
    bias[...] = jnp.concatenate([small[4:5, CX:], small[4:5, 0:CX]], axis=1).reshape(CONVCH)
    gain[...] = small[5:6, 0:INNER].reshape(INNER)
    step[...] = small[5:6, INNER : INNER + HEADS].reshape(HEADS)
    rates[...] = small[5:6, INNER + LANES : INNER + LANES + HEADS].reshape(HEADS)
    skip[...] = small[6:7, 0:HEADS].reshape(HEADS)
    norm[...] = small[7:8, 0:D].reshape(D)
    for c in copies:
        c.wait()


def call_place(shape, lengths, *arrays):
    vmem = pl.BlockSpec(memory_space=pltpu.VMEM)
    hbm = pl.BlockSpec(memory_space=pl.ANY)
    own = arrays[3].shape[0]
    outs = (
        (shape, BF), (shape, F32), ((D,), F32), ((own, PROJ), F32), ((CONV, CONVCH), F32),
        ((CONVCH,), F32), ((HEADS,), F32), ((HEADS,), F32), ((HEADS,), F32), ((INNER,), F32),
        ((own, INNER), F32),
    )
    rest = max(shape[2] - GROUP, GROUP)
    results = pl.pallas_call(
        place_results,
        out_shape=[jax.ShapeDtypeStruct(s, t) for s, t in outs],
        in_specs=[pl.BlockSpec(memory_space=pltpu.SMEM)] + [vmem] * len(arrays),
        out_specs=[hbm, hbm] + [vmem] * (len(outs) - 2),
        scratch_shapes=[
            pltpu.VMEM((rest, D), F32), pltpu.VMEM((rest, D), BF), pltpu.SemaphoreType.DMA((6,)),
        ],
        name="place_results",
    )(lengths, *arrays)
    return (*results[:-1], results[-1].T)


def shards(
    tokens, lengths, norm_gain, in_weight, conv_weight, conv_bias, dt_bias, a_log, skip_gain,
    out_gain, out_weight, out_grad,
):
    both = ("fsdp", "seq")
    own = in_weight.shape[0]
    nf = lax.axis_size("fsdp")
    fused = nf % PLANE == 0 and (2 * own) % 16 == 0 and own % 8 == 0
    nz = nf // PLANE if fused else 1
    arrays = {
        "lengths": lengths, "tokens": tokens, "out_grad": out_grad, "norm_gain": norm_gain,
        "conv_weight": conv_weight, "conv_bias": conv_bias, "dt_bias": dt_bias, "a_log": a_log,
        "skip_gain": skip_gain, "out_gain": out_gain,
    }
    if fused:
        arrays |= {"in_weight": in_weight, "out_weight": out_weight.T}
        mixed, tgrad, small, grad_in, grad_out = call_mixer(fused, nz, arrays)
    else:
        fill = jnp.zeros((own, AT_X - CX - HEADS), BF)
        sent = jnp.concatenate(
            [in_weight[:, 2 * INNER :], fill, in_weight[:, INNER : 2 * INNER],
             in_weight[:, :INNER], out_weight.T], axis=1)
        arrays["w"] = lax.all_gather(sent, both, axis=0, tiled=True)
        mixed, tgrad, small, wgrad = call_mixer(fused, nz, arrays)
        summed = lax.psum_scatter(wgrad, both, scatter_dimension=0, tiled=True).astype(F32)
        grad_out = summed[:, :INNER]
        grad_in = jnp.concatenate(
            [summed[:, INNER : 3 * INNER], summed[:, 3 * INNER : 3 * INNER + CX + HEADS]], axis=1
        )
        small = lax.psum(small, both)
    return call_place(tokens.shape, lengths, mixed, tgrad, small, grad_in, grad_out)


def solution(mesh):
    spread = P(None, "fsdp", "seq", None)
    both = ("fsdp", "seq")
    return jax.shard_map(
        shards,
        mesh=mesh,
        in_specs=(
            spread, P(None, "fsdp"), P(), P(both, None), P(), P(), P(), P(), P(), P(),
            P(None, both), spread,
        ),
        out_specs=(
            spread, spread, P(), P(both, None), P(), P(), P(), P(), P(), P(), P(None, both),
        ),
        check_vma=False,
    )
```

```python
import functools
import types

import jax
import jax.numpy as jnp
from jax import lax
from jax.experimental import pallas as pl
from jax.experimental.pallas import tpu as pltpu
from jax.sharding import PartitionSpec as P

D = 768
HEADS = 24
HEADDIM = 64
NSTATE = 128
CONV = 4
GROUP = 256
INNER = 1536
CONVCH = 1792
PROJ = 3352
EPS = 1e-05

BLOCKS = 3
ROWS = BLOCKS * GROUP
EDGE = 16
LANES = 128
QUADS = INNER // 256
AT_DT = 256
AT_X = 512
AT_GATE = AT_X + INNER
AT_OUT = AT_GATE + INNER
WIDE = AT_OUT + INNER
CX = 2 * NSTATE
CHUNK = 768
WIDE_CHUNKS = 4
CHUNKS = WIDE_CHUNKS + QUADS + 1
UNITS = 7
SLOTS = 4
GATHERS = ((0, 512), (512, 512), (1024, 1024), (AT_GATE, INNER), (AT_OUT, INNER))
PLANE = 4

BF = jnp.bfloat16
F32 = jnp.float32
MESH = pl.DeviceIdType.MESH


def dot(a, b):
    return lax.dot_general(a, b, (((1,), (0,)), ((), ())), preferred_element_type=F32)


def dot_nt(a, b):
    return lax.dot_general(a, b, (((1,), (1,)), ((), ())), preferred_element_type=F32)


def sigmoid(v):
    return 0.5 * jnp.tanh(0.5 * v) + 0.5


def halves(v):
    high = v.astype(BF)
    return high, (v - high.astype(F32)).astype(BF)


def side_by_side(v):
    return jnp.concatenate(halves(v), axis=1)


def exact_sum(triangle, v):
    high, rest = halves(v)
    low = (v - high.astype(F32) - rest.astype(F32)).astype(BF)
    parts = dot(triangle, jnp.concatenate([high, rest, low], axis=1))
    return parts[:, :LANES] + parts[:, LANES : 2 * LANES] + parts[:, 2 * LANES :]


def span(start, size, multiple=None):
    return pl.ds(pl.multiple_of(start, multiple or size), size)


def rows_of(b):
    return span(b * GROUP, GROUP)


def heads_of(q):
    return span(q * 256, 256)


def fold(v):
    total = v[0:8]
    for i in range(1, v.shape[0] // 8):
        total = total + v[8 * i : 8 * i + 8]
    return total


def iota(shape, dim):
    return lax.broadcasted_iota(jnp.int32, shape, dim)


def loop(count, body):
    def step(i, _):
        body(i)
        return 0

    lax.fori_loop(0, count, step, 0)


def silu_slope(v, sg):
    return sg * (1.0 + v * (1.0 - sg))


def mixer(names, fused, nz, *refs):
    r = types.SimpleNamespace(**dict(zip(names, refs)))
    seq = lax.axis_index("seq")
    f = lax.axis_index("fsdp")
    z_at, p_at = f // PLANE, f % PLANE
    sibling = {"seq": 1 - seq}
    is_second = (seq == 1).astype(F32)
    is_first = 1.0 - is_second

    def plane_peer(j):
        if j == 1:
            return p_at + 1 - 2 * (p_at % 2)
        if j == 2:
            return p_at + 2 - 4 * (p_at // 2)
        return 3 - p_at

    def z_peer(j):
        return (z_at + j + nz) % nz

    def on_plane(j):
        return {"fsdp": z_at * PLANE + plane_peer(j)}

    def on_chain(j):
        return {"fsdp": z_peer(j) * PLANE + p_at}

    own = D // (2 * nz * PLANE) if fused else 0
    peers = [sibling]
    if fused:
        peers += [on_plane(j) for j in range(1, PLANE)] + [on_chain(j) for j in range(1, nz)]
    barrier = pltpu.get_barrier_semaphore()
    for peer in peers:
        pl.semaphore_signal(barrier, inc=1, device_id=peer, device_id_type=MESH)

    def own_columns(ref, c):
        return ref.at[c * own : (c + 1) * own, 0 : GATHERS[c][1]]

    part_rows = r.tokens.shape[2]
    raw = [buf.at[0:part_rows, m * D : (m + 1) * D] for buf in (r.dssd, r.cout) for m in range(2)]
    raw_copies = []
    for i in range(4):
        src = (r.tokens, r.out_grad)[i // 2].at[i % 2, 0]
        raw_copies.append(pltpu.make_async_copy(src, raw[i], r.local.at[2 + i]))
        raw_copies[i].start()

    if fused:
        wide = 2 * INNER
        steps = r.in_weight[:, wide + CX :].astype(F32)
        fill = jnp.zeros((steps.shape[0], AT_X - CX - HEADS), F32)
        key_query = r.in_weight[:, wide : wide + CX].astype(F32)
        own_columns(r.gate, 0)[...] = jnp.concatenate([key_query, steps, fill], axis=1)
        own_columns(r.gate, 1)[...] = r.in_weight[:, INNER : INNER + 512].astype(F32)
        own_columns(r.gate, 2)[...] = r.in_weight[:, INNER + 512 : wide].astype(F32)
        own_columns(r.gate, 3)[...] = r.in_weight[:, 0:INNER].astype(F32)
        own_columns(r.gate, 4)[...] = r.out_weight[...].astype(F32)

    pl.semaphore_wait(barrier, len(peers))

    def remote(src, dst, send, recv, device):
        return pltpu.make_async_remote_copy(
            src_ref=src, dst_ref=dst, send_sem=send, recv_sem=recv, device_id=device,
            device_id_type=MESH,
        )

    def pair_copy(i, src, dst):
        return remote(src, dst, r.pair_send.at[i], r.pair_recv.at[i], sibling)

    w = r.w
    slab = 2 * own

    def part(c):
        low, size = GATHERS[c]
        return span(low + seq * (size // 2), size // 2, 128)

    def slab_of(index):
        return span(index * slab, slab, 16)

    def gather_copy(c, k, index, device):
        at = w.at[slab_of(index), part(c)]
        return remote(at, at, r.g_send.at[c, 0], r.g_recv.at[c, k], device)

    def chain_copy(c, j):
        return gather_copy(c, 0, f, on_chain(j))

    def plane_copy(c, kind, back):
        low, size = GATHERS[c]
        owner = (p_at, p_at, plane_peer(1), plane_peer(2))[kind]
        cols = part(c)
        if kind >= 2:
            cols = span(low + seq * (size // 2) + (kind - 2) * (size // 4), size // 4, 128)
        at = w.at[slab_of((z_at - back + nz) % nz * PLANE + owner), cols]
        device = on_plane((1, 2, 2, 1)[kind])
        return remote(at, at, r.g_send.at[c, 0], r.g_recv.at[c, 1 + kind // 2], device)

    def last_copy(c):
        at = w.at[:, part(c)]
        return remote(at, at, r.g_send.at[c, 1], r.g_recv.at[c, 3], sibling)

    def wait_bytes(rows, cols, sem):
        at = w.at[0 : rows * slab // 2, cols]
        pltpu.make_async_copy(at, at, sem).wait()

    def gather_own(c):
        cols = part(c)
        half_cols = span(seq * (GATHERS[c][1] // 2), GATHERS[c][1] // 2, 128)
        mine, theirs = (own_columns(ref, c)[:, half_cols] for ref in (r.gate, r.back))
        first = jnp.where(seq == 0, mine, theirs)
        second = jnp.where(seq == 0, theirs, mine)
        w[slab_of(f), cols] = jnp.concatenate([first, second], axis=0).astype(BF)

    def gather_0(c):
        for j in range(1, nz):
            chain_copy(c, j).start()

    def gather_1(c):
        for kind in range(2):
            plane_copy(c, kind, 0).start()

    def gather_2(c):
        wait_bytes(2 * (nz - 1), part(c), r.g_recv.at[c, 0])
        for back in range(1, nz):
            for kind in range(2):
                plane_copy(c, kind, back).start()

    def gather_3(c):
        wait_bytes(4 * nz, part(c), r.g_recv.at[c, 1])
        for back in range(nz):
            for kind in range(2):
                plane_copy(c, kind + 2, back).start()

    def gather_4(c):
        wait_bytes(2 * nz, part(c), r.g_recv.at[c, 2])
        last_copy(c).start()

    def gather_5(c):
        last_copy(c).wait_recv()

    def gather_end(c):
        wait_bytes(2 * (nz - 1) + 6 * nz, part(c), r.g_send.at[c, 0])
        last_copy(c).wait_send()

    def wide_chunk(i):
        return i, i, 0, CHUNK // 2, i, 0

    def quad_chunk(q):
        return WIDE_CHUNKS + q, q // 3, (q % 3) * 256, 128, WIDE_CHUNKS + q // 3, (q % 3) * 128

    last_chunk = (WIDE_CHUNKS + QUADS, 2, 0, AT_X // 2, UNITS - 1, 0)

    def source(g, which):
        return span(g[2] + which * g[3], g[3], 128)

    def target(g):
        return span(g[5], g[3], 128)

    def sum_copy_0(g):
        src = r.wg.at[g[1], :, :, :, source(g, 1 - seq)]
        dst = r.r0.at[g[4], :, :, :, target(g)]
        return remote(src, dst, r.s_send.at[g[0]], r.s_recv.at[g[0], 0], sibling)

    def sum_copy_1(g, j):
        src = r.wg.at[g[1], :, plane_peer(j), :, source(g, seq)]
        dst = r.r1.at[g[4], j - 1, :, :, target(g)]
        return remote(src, dst, r.s_send.at[g[0]], r.s_recv.at[g[0], 1], on_plane(j))

    def sum_copy_2(g, j):
        src = r.wg.at[g[1], z_peer(j), p_at, :, source(g, seq)]
        dst = r.r2.at[g[4], j - 1, :, target(g)]
        return remote(src, dst, r.s_send.at[g[0]], r.s_recv.at[g[0], 2], on_chain(j))

    def sum_copy_3(g):
        src = r.fin.at[g[4], span((1 - seq) * own, own, 8), target(g)]
        dst = r.gsum.at[g[4], :, target(g)]
        return remote(src, dst, r.s_send.at[g[0]], r.s_recv.at[g[0], 3], sibling)

    def finish_all(g, level, at):
        pltpu.make_async_copy(at, at, r.s_send.at[g[0]]).wait()
        pltpu.make_async_copy(at, at, r.s_recv.at[g[0], level]).wait()

    def finish(copy):
        copy.wait_send()
        copy.wait_recv()

    def sum_0(g):
        if fused:
            sum_copy_0(g).start()

    def sum_1(g):
        if not fused:
            return
        finish(sum_copy_0(g))

        def add(i):
            at = (g[1], i // PLANE, i % PLANE, slice(None), source(g, seq))
            theirs = r.r0[g[4], i // PLANE, i % PLANE, :, target(g)]
            r.wg[at] = (r.wg[at].astype(F32) + theirs.astype(F32)).astype(BF)

        loop(nz * PLANE, add)
        for j in (3, 1, 2):
            sum_copy_1(g, j).start()

    def sum_2(g):
        if not fused:
            return
        finish_all(g, 1, r.r1.at[g[4], :, :, :, target(g)])

        def add(zi):
            at = (g[1], zi, p_at, slice(None), source(g, seq))
            value = r.wg[at].astype(F32)
            for j in range(PLANE - 1):
                value = value + r.r1[g[4], j, zi, :, target(g)].astype(F32)
            r.wg[at] = value.astype(BF)

        loop(nz, add)
        for j in range(1, nz):
            sum_copy_2(g, j).start()

    def sum_3(g):
        if not fused:
            return
        finish_all(g, 2, r.r2.at[g[4], :, :, target(g)])
        value = r.wg[g[1], z_at, p_at, :, source(g, seq)].astype(F32)
        for j in range(nz - 1):
            value = value + r.r2[g[4], j, :, target(g)].astype(F32)
        r.fin[g[4], :, target(g)] = value
        sum_copy_3(g).start()

    def sum_4(g):
        finish(sum_copy_3(g))

    def put_grad(g, low, value):
        size = value.shape[1]
        if fused:
            parts = value.astype(BF).reshape(nz, PLANE, slab, size)
            r.wg[g[1], :, :, :, span(g[2] + low, size, 128)] = parts
        else:
            first = g[4] * CHUNK + (g[2] if g[3] == 128 else 0)
            r.wgrad[:, span(first + low, size, 128)] = value.astype(BF)

    def shard_copy(c):
        size = GATHERS[c][1] // 2
        rows, cols = slice(c * own, (c + 1) * own), span((1 - seq) * size, size, 128)
        return pair_copy(1, r.gate.at[rows, cols], r.back.at[rows, cols])

    if fused:
        for c in range(len(GATHERS)):
            shard_copy(c).start()

    def make_spread(q):
        shape = (256, 256)
        head = (iota(shape, 1) + q * 256) >> 6
        r.spread[:, span(q * 256, 256)] = (head == (iota(shape, 0) & 127)).astype(F32).astype(BF)

    if fused:
        at = r.back.at[0 : own * (WIDE // 2) // INNER, :]
        for sem in (r.pair_send.at[1], r.pair_recv.at[1]):
            pltpu.make_async_copy(at, at, sem).wait()
        for c in range(len(GATHERS)):
            gather_own(c)
            if c < 2:
                gather_0(c)
                gather_1(c)
        gather_0(2)

    r.convp[0:CONV, 0:CX] = r.conv_weight[:, INNER:]
    r.convp[0:CONV, CX:] = r.conv_weight[:, 0:INNER]
    bias = r.conv_bias[...].reshape(1, CONVCH)
    r.convp[4:5, 0:CX] = bias[:, INNER:]
    r.convp[4:5, CX:] = bias[:, 0:INNER]
    r.headp[...] = jnp.zeros_like(r.headp)
    for i, v in enumerate((r.dt_bias, r.a_log, r.skip_gain)):
        r.headp[i : i + 1, 0:HEADS] = v[...].reshape(1, HEADS)
    norm_gain = r.norm_gain[...].reshape(1, D)

    first_long = r.lengths[0, 0] > r.lengths[1, 0]
    shortest = jnp.minimum(r.lengths[0, 0], r.lengths[1, 0])
    for i in range(4):
        raw_copies[i].wait()

    def pick_rows(i):
        here = span(i * 64, 64)
        for to, k in ((r.tok, 0), (r.og, 2)):
            to[here, :] = jnp.where(first_long, raw[k][here, :], raw[k + 1][here, :])

    def pick_short(i):
        here, there = span(i * 64, 64), span(2 * GROUP + i * 64, 64)
        r.tok[there, :] = jnp.where(first_long, raw[1][here, :], raw[0][here, :])
        valid = (seq * part_rows + i * 64 + iota((64, D), 0) < shortest).astype(F32)
        picked = jnp.where(first_long, raw[3][here, :], raw[2][here, :])
        r.og[there, :] = (picked.astype(F32) * valid).astype(BF)

    loop(2 * GROUP // 64, pick_rows)
    edge_copy = pair_copy(0, r.tok.at[2 * GROUP - EDGE : 2 * GROUP, :], r.edge_in)
    edge_copy.start()
    loop(GROUP // 64, pick_short)

    loop(QUADS, make_spread)
    r.innerp[0:1, :] = r.out_gain[...].reshape(1, INNER)
    r.innerp[1:2, :] = dot(side_by_side(r.headp[...]), r.spread[...])[2:3, :]
    tri_shape = (GROUP, GROUP)
    lower = (iota(tri_shape, 0) >= iota(tri_shape, 1)).astype(F32).astype(BF)
    upper = (iota(tri_shape, 0) <= iota(tri_shape, 1)).astype(F32).astype(BF)
    half = GROUP // 2
    causal = iota((half, half), 0) >= iota((half, half), 1)
    causal_t = iota((half, half), 0) <= iota((half, half), 1)
    first_head = iota((GROUP, LANES), 1) < HEADDIM
    rate = -jnp.exp(r.headp[1:2, :])

    r.g_norm[...] = jnp.zeros_like(r.g_norm)
    r.g_conv[...] = jnp.zeros_like(r.g_conv)
    r.g_head[...] = jnp.zeros_like(r.g_head)
    r.g_inner[...] = jnp.zeros_like(r.g_inner)
    r.halo[2] = jnp.zeros((8, CONVCH), F32)
    r.dproj[:, AT_DT + LANES : AT_X] = jnp.zeros((ROWS, AT_X - AT_DT - LANES), BF)

    def norm_of(v):
        root = lax.rsqrt(jnp.mean(v * v, axis=1, keepdims=True) + EPS)
        return (v * root * norm_gain).astype(BF)

    def norm_rows(i):
        rows = span(i * 64, 64)
        r.normed[rows, :] = norm_of(r.tok[rows, :].astype(F32))

    loop(ROWS // 64, norm_rows)
    edge_copy.wait()
    r.normed[ROWS:, :] = norm_of(r.edge_in[...].astype(F32) * is_second)

    if fused:
        gather_2(0)
        gather_1(2)
        gather_0(3)

    def turn(b):
        rows = rows_of(b)
        r.normed_t[:, rows] = r.normed[rows, :].T
        r.db_t[:, rows] = r.og[rows, :].T

    loop(BLOCKS, turn)

    if fused:
        gather_2(1)
        gather_3(0)
        gather_1(3)
        gather_4(0)
        gather_3(1)
        gather_5(0)

    def conv_acc(values, before, cols):
        rows = values.shape[0]
        ext = jnp.concatenate([before, values], axis=0)
        shifted = [ext[5 + k : 5 + k + rows] for k in range(CONV)]
        acc = r.convp[4:5, cols]
        for k in range(CONV):
            acc = acc + r.convp[k : k + 1, cols] * shifted[k]
        return acc, shifted

    def project(at, to):
        low = dot(r.normed[...], w[:, at]).astype(BF)
        r.clow[:, to] = low
        r.halo[0, :, to] = low[ROWS : ROWS + EDGE].astype(F32)[EDGE - 8 :]
        r.halo[1, :, to] = low[GROUP - 16 : GROUP].astype(F32)[8:]

    def conv_forward(b, cols):
        rows = rows_of(b)
        acc, _ = conv_acc(r.clow[rows, cols].astype(F32), r.halo[b, :, cols], cols)
        r.cout[rows, cols] = (acc * sigmoid(acc)).astype(BF)

    project(pl.ds(0, CX), pl.ds(0, CX))
    r.dtb[...] = dot(r.normed[0:ROWS, :], w[:, AT_DT : AT_DT + LANES])

    def head_rows(b):
        z = r.dtb[rows_of(b), :] + r.headp[0:1, :]
        step = jnp.maximum(z, 0.0) + jnp.log1p(jnp.exp(-jnp.abs(z)))
        return z, step

    def prepare(b):
        rows = rows_of(b)
        conv_forward(b, pl.ds(0, LANES))
        conv_forward(b, pl.ds(LANES, LANES))
        z, step = head_rows(b)
        cum = exact_sum(lower, step * rate)
        moved = cum - jnp.log(jnp.maximum(step, 1e-37))
        r.cumb[rows, :] = cum
        r.moved[rows, :] = moved
        cum_t, moved_t = cum.T, moved.T
        for q in range(QUADS):
            r.cut[b, q, 0:4, :] = moved_t[4 * q : 4 * q + 4, :]
            r.cut[b, q, 4:8, :] = cum_t[4 * q : 4 * q + 4, :]
        r.weight[rows, :] = side_by_side(jnp.exp(cum[GROUP - 1 : GROUP, :] - cum) * step)
        r.fade[rows, :] = side_by_side(jnp.exp(cum))
        key, query = r.cout[rows, 0:NSTATE], r.cout[rows, NSTATE:CX]
        r.turned[b, 0:NSTATE, :] = key.T
        r.turned[b, NSTATE:CX, :] = query.T
        r.sco[b] = dot_nt(query, key)

    loop(BLOCKS, prepare)
    if fused:
        gather_2(2)
        gather_0(4)
        gather_4(1)
        gather_1(4)
        gather_5(1)

    gather_steps = (
        (1, gather_3, 2), (1, gather_2, 3), (2, gather_4, 2), (2, gather_5, 2), (3, gather_2, 4),
        (4, gather_3, 3),
    )

    def gather_on(q):
        if fused:
            for point in range(QUADS):

                @pl.when(q == point)
                def _():
                    for at, step, c in gather_steps:
                        if at == point:
                            step(c)

    def to_first(v, q):
        return pltpu.roll(v, (LANES - 4 * q) % LANES, 1)

    def forward_block(b, q):
        rows = rows_of(b)
        cols = span(CX + q * 256, 256)
        heads = span(q * 256, 256)
        for i in range(2):
            conv_forward(b, span(CX + q * 256 + i * LANES, LANES))
        xq = r.cout[rows, cols]

        if b < 2:
            spread_w = dot(r.weight[rows, :], r.spread[:, heads])
            scaled = (xq.astype(F32) * spread_w).astype(BF)
            r.runs[b, :, heads] = dot(r.turned[b, 0:NSTATE, :], scaled)

        near = to_first(r.cumb[rows, :], q)
        skip = r.innerp[1:2, heads]
        for j in range(2):
            lanes = slice(j * LANES, (j + 1) * LANES)
            xp = xq[:, lanes]
            zero = jnp.zeros_like(xp)
            x_ab = (jnp.where(first_head, xp, zero), jnp.where(first_head, zero, xp))
            top, bottom = [], []
            for e in range(2):
                h = 2 * j + e
                col_top, col_bottom = near[:half, h : h + 1], near[half:, h : h + 1]
                row = r.cut[b, q, h : h + 1, :]
                row_left, row_right = row[:, :half], row[:, half:]
                gap = jnp.where(causal, col_top - row_left, -1e30)
                top.append((r.sco[b, :half, :half] * jnp.exp(gap)).astype(BF))
                fade = jnp.exp(col_bottom - row_left)
                bottom.append((r.sco[b, half:, :half] * fade).astype(BF))
                gap = jnp.where(causal, col_bottom - row_right, -1e30)
                bottom.append((r.sco[b, half:, half:] * jnp.exp(gap)).astype(BF))
            out_top = dot(
                jnp.concatenate(top, axis=1), jnp.concatenate([v[:half] for v in x_ab], axis=0)
            )
            out_bottom = dot(jnp.concatenate(bottom, axis=1), jnp.concatenate(x_ab, axis=0))
            place = span(q * 256 + j * LANES, LANES)
            xf = xp.astype(F32) * skip[:, lanes]
            r.ssd[span(b * GROUP, half), place] = out_top + xf[:half]
            r.ssd[span(b * GROUP + half, half), place] = out_bottom + xf[half:]

    def forward_quad(q):
        gather_on(q)
        project(span(AT_X + q * 256, 256), span(CX + q * 256, 256))
        for b in range(BLOCKS):
            forward_block(b, q)

    loop(QUADS, forward_quad)

    def decay_of(b):
        last = r.cumb[b * GROUP + GROUP - 8 : (b + 1) * GROUP, :]
        return dot(side_by_side(jnp.exp(last)), r.spread[...])[7:8, :]

    decay_0, decay_1 = decay_of(0), decay_of(1)
    r.runs[1] = r.runs[1] + decay_1 * r.runs[0]
    state_copy = pair_copy(2, r.runs.at[1], r.state_in)
    state_copy.start()
    if fused:
        gather_4(3)

    def carry_block(b):
        rows = rows_of(b)
        query = r.cout[rows, NSTATE:CX]

        def quad(q):
            cols = span(q * 256, 256)
            r.ssd[rows, cols] += dot(query, r.held[b, :, cols]) * dot(
                r.fade[rows, :], r.spread[:, cols]
            )

        loop(QUADS, quad)

    gain = r.innerp[0:1, :]

    def gate_project(b):
        rows = rows_of(b)

        def quad(q):
            at = span(AT_GATE + q * 256, 256)
            high, low = halves(dot(r.normed[rows, :], w[:, at]))
            r.dssd[rows, span(q * 256, 256)] = high
            r.dproj[rows, at] = low

        loop(QUADS, quad)

    def out_back(b):
        rows = rows_of(b)

        def quad(q):
            cols = span(q * 256, 256)
            r.back[:, cols] = dot(r.og[rows, :], w[:, span(AT_OUT + q * 256, 256)])

        loop(QUADS, quad)

    def gated_rows(here):
        g = r.dssd[here, :].astype(F32) + r.dproj[here, AT_GATE:AT_OUT].astype(F32)
        s = r.ssd[here, :]
        sg = sigmoid(g)
        silu = g * sg
        gated = s * silu
        root = lax.rsqrt(jnp.mean(gated * gated, axis=1, keepdims=True) + EPS)
        return g, s, sg, silu, gated, root

    def gate_forward(i):
        for k in range(2):
            here = span(i * 32 + k * 16, 16)
            _, _, _, _, gated, root = gated_rows(here)
            r.dproj[here, AT_X:AT_GATE] = (gated * root * gain).astype(BF)

    def gate_block(b):
        def gate_rows(i):
            here = span(b * GROUP + i * 16, 16)
            d_out = r.back[span(i * 16, 16), :]
            g, s, sg, silu, gated, root = gated_rows(here)
            a = gain * d_out
            lean = root * jnp.mean(gated * a, axis=1, keepdims=True)
            v = gated * root
            r.g_inner[0:8, :] += fold(d_out * v)
            d_gated = root * (a - v * lean)
            d_s = (d_gated * silu).astype(BF)
            r.dssd[here, :] = d_s
            r.g_inner[8:16, :] += fold(d_s.astype(F32) * r.cout[here, CX:].astype(F32))
            r.dproj[here, AT_GATE:AT_OUT] = (d_gated * s * silu_slope(g, sg)).astype(BF)

        loop(GROUP // 16, gate_rows)

    state_copy.wait()
    r.state_in[...] = r.state_in[...] * is_second
    r.held[0] = r.state_in[...].astype(BF)
    r.runs[0] = r.runs[0] + decay_0 * r.state_in[...]
    r.held[1] = r.runs[0].astype(BF)
    r.runs[1] = r.state_in[...]

    @pl.when(seq > 0)
    def _():
        carry_block(0)

    carry_block(1)

    def wide_grad(i):
        g = wide_chunk(i)
        left = r.db_t if i < 2 else r.normed_t
        first = (AT_X if i < 2 else AT_GATE) + (i % 2) * CHUNK

        def tile(k):
            put_grad(g, k * 256, dot(left[...], r.dproj[:, span(first + k * 256, 256)]))

        loop(CHUNK // 256, tile)
        sum_0(g)

    if fused:
        gather_5(3)
    loop(BLOCKS, gate_project)
    if fused:
        gather_3(4)
    loop(ROWS // 32, gate_forward)
    if fused:
        gather_4(4)
    wide_grad(0)
    wide_grad(1)
    if fused:
        gather_5(4)
    for b in range(BLOCKS):
        out_back(b)
        gate_block(b)
        if b < 2:
            sum_1(wide_chunk(b))
    wide_grad(2)
    wide_grad(3)
    sum_2(wide_chunk(0))

    def state_back(b):
        rows = rows_of(b)

        def quad(q, dq):
            cols = span(q * 256, 256)
            spread_f = dot(r.fade[rows, :], r.spread[:, cols])
            dz = (spread_f * r.dssd[rows, cols].astype(F32)).astype(BF)
            r.dheld[b, :, cols] = dot(r.turned[b, NSTATE:CX, :], dz)
            return dq + dot_nt(dz, r.held[b, :, cols])

        r.dqb[rows, :] = lax.fori_loop(0, QUADS, quad, jnp.zeros((GROUP, NSTATE), F32))

    def no_state():
        r.dheld[0] = jnp.zeros((NSTATE, INNER), F32)

    r.dqb[0:GROUP, :] = jnp.zeros((GROUP, NSTATE), F32)
    pl.when(seq > 0)(lambda: state_back(0))
    pl.when(seq == 0)(no_state)
    state_back(1)
    r.dqb[2 * GROUP :, :] = jnp.zeros((GROUP, NSTATE), F32)
    r.dheld[0] = r.dheld[0] + decay_0 * r.dheld[1]
    dstate_copy = pair_copy(3, r.dheld.at[0], r.dstate_in)
    dstate_copy.start()
    sum_1(wide_chunk(2))

    def out_block(b):
        rows = rows_of(b)
        branch = dot_nt(r.dproj[rows, AT_X:AT_GATE], w[:, AT_OUT:])
        r.normed[rows, :] = (r.tok[rows, :].astype(F32) + branch).astype(BF)

    loop(BLOCKS, out_block)
    mixed_copy = pltpu.make_async_copy(r.normed.at[0:ROWS, :], r.mixed, r.local.at[0])
    mixed_copy.start()
    sum_1(wide_chunk(3))
    sum_2(wide_chunk(1))
    sum_3(wide_chunk(0))

    def ds_of(b):
        return r.back.at[:, heads_of(b)]

    def give_of(b):
        return r.back.at[:, span(CHUNK + b * LANES, LANES)]

    def kept_of(b):
        return r.back.at[:, span(CHUNK + (BLOCKS + b) * LANES, LANES)]

    def pick_heads(q):
        row, lane = iota((8 * LANES, LANES), 0), iota((8 * LANES, LANES), 1)
        pair, kind, second = row >> 9, (row >> 8) & 1, (row & 127) >> 6
        head = 4 * q + 2 * pair + second + 64 * kind
        r.pick[...] = (lane == head).astype(F32).astype(BF)

    def prepare_back(b):
        rows = rows_of(b)
        r.sco[b] = dot_nt(r.cout[rows, 0:NSTATE], r.cout[rows, NSTATE:CX])
        ds_of(b)[...] = jnp.zeros((GROUP, GROUP), F32)
        nothing = jnp.zeros((GROUP, LANES), F32)
        r.dkb[rows, :] = nothing
        give_of(b)[...] = nothing

    loop(BLOCKS, prepare_back)
    dstate_copy.wait()
    r.dstate_in[...] = r.dstate_in[...] * is_first
    r.dst[1] = r.dstate_in[...].astype(BF)
    r.state_in[...] = r.dheld[1] + decay_1 * r.dstate_in[...]
    r.dst[0] = r.state_in[...].astype(BF)

    def backward_block(b, q):
        rows = rows_of(b)
        heads = span(q * 256, 256)
        xq = r.cout[rows, span(CX + q * 256, 256)]
        dq4 = r.dssd[rows, heads]
        skip = r.innerp[1:2, heads]
        dx, ds = r.gate.at[:, heads_of(b)], ds_of(b)

        if b < 2:
            spread_w = dot(r.weight[rows, :], r.spread[:, heads])
            d_states = r.dst[b, :, heads]
            dx_state = spread_w * dot(r.cout[rows, 0:NSTATE], d_states)
            r.flow[b, 0:8, heads] = fold(xq.astype(F32) * dx_state)
            r.dkb[rows, :] += dot_nt((xq.astype(F32) * spread_w).astype(BF), d_states)

        near = to_first(r.moved[rows, :], q)
        products = []
        for j in range(2):
            lanes = slice(j * LANES, (j + 1) * LANES)
            xp, dp = xq[:, lanes], dq4[:, lanes]
            zero = jnp.zeros_like(xp)
            d_ab = (jnp.where(first_head, dp, zero), jnp.where(first_head, zero, dp))
            top, bottom = [], []
            for e in range(2):
                h = 2 * j + e
                dm_top = dot_nt(xp[:half], d_ab[e])
                dm_bottom = dot_nt(xp[half:], d_ab[e][half:])
                col_top, col_bottom = near[:half, h : h + 1], near[half:, h : h + 1]
                row = r.cut[b, q, 4 + h : 5 + h, :]
                row_left, row_right = row[:, :half], row[:, half:]
                fade = jnp.exp(jnp.where(causal_t, row_left - col_top, -1e30))
                ds[:half, :half] += dm_top[:, :half] * fade
                top.append((r.sco[b, :half, :half] * fade).astype(BF))
                fade = jnp.exp(row_right - col_top)
                ds[:half, half:] += dm_top[:, half:] * fade
                top.append((r.sco[b, :half, half:] * fade).astype(BF))
                fade = jnp.exp(jnp.where(causal_t, row_right - col_bottom, -1e30))
                ds[half:, half:] += dm_bottom * fade
                bottom.append((r.sco[b, half:, half:] * fade).astype(BF))
            dx_top = dot(jnp.concatenate(top, axis=1), jnp.concatenate(d_ab, axis=0))
            dx_bottom = dot(
                jnp.concatenate(bottom, axis=1), jnp.concatenate([v[half:] for v in d_ab], axis=0)
            )
            dxp = jnp.concatenate([dx_top, dx_bottom], axis=0)
            if b < 2:
                dxp = dxp + dx_state[:, lanes]
            xf, df = xp.astype(F32), dp.astype(F32)
            kept = skip[:, lanes]
            ssd = r.ssd[rows, span(q * 256 + j * LANES, LANES)]
            products += [*halves(xf * dxp), *halves(df * (ssd - kept * xf))]
            dx[:, lanes] = dxp + kept * df
        give_of(b)[...] += dot(jnp.concatenate(products, axis=1), r.pick[...])

    def edge_grad(b, source, cols):
        first = r.clow[b * GROUP : b * GROUP + 16, cols].astype(F32)
        acc, _ = conv_acc(first, r.halo[b, :, cols], cols)
        d_acc = r.gate[0:16, span(b * 256 + source, LANES)] * silu_slope(acc, sigmoid(acc))
        r.halo_next[b, :, cols] = d_acc[0:8]

    def conv_back(b, source, cols, to, after):
        rows = rows_of(b)
        acc, shifted = conv_acc(r.clow[rows, cols].astype(F32), r.halo[b, :, cols], cols)
        d_acc = r.gate[:, span(b * 256 + source, LANES)] * silu_slope(acc, sigmoid(acc))
        for k in range(CONV):
            r.g_conv[8 * k : 8 * k + 8, cols] += fold(d_acc * shifted[k])
        r.g_conv[32:40, cols] += fold(d_acc)
        ext = jnp.concatenate([d_acc, after], axis=0)
        d_in = r.convp[3:4, cols] * d_acc
        for k in range(CONV - 1):
            d_in = d_in + r.convp[k : k + 1, cols] * ext[3 - k : 3 - k + GROUP]
        r.dproj[rows, to] = d_in.astype(BF)

    def edge_copy_back(i, cols):
        src, dst = r.halo_next.at[0, :, cols], r.dedge_in.at[:, cols]
        return remote(src, dst, r.edge_send.at[i], r.edge_recv.at[i], sibling)

    def first_edge(i, at):
        for k in range(2):
            edge_grad(0, k * LANES, span(at + k * LANES, LANES))
        edge_copy_back(i, span(at, 256)).start()

    def conv_back_all(i, at, to):
        cols = span(at, 256)

        def chunk(k):
            return k * LANES, span(at + k * LANES, LANES), span(to + k * LANES, LANES)

        for k in range(2):
            edge_grad(1, *chunk(k)[:2])
        for k in range(2):
            conv_back(2, *chunk(k), jnp.zeros((8, LANES), F32))
            conv_back(0, *chunk(k), r.halo_next[1, :, chunk(k)[1]])
        edge_copy_back(i, cols).wait()
        for k in range(2):
            conv_back(1, *chunk(k), r.dedge_in[:, chunk(k)[1]] * is_first)

    def backward_quad(q):
        @pl.when(q == 1)
        def _():
            sum_2(wide_chunk(2))

        @pl.when(q == 2)
        def _():
            sum_3(wide_chunk(2))
            sum_2(wide_chunk(3))

        @pl.when(q == 3)
        def _():
            sum_3(wide_chunk(3))

        pick_heads(q)
        for b in range(BLOCKS):
            backward_block(b, q)
            if b == 0:
                first_edge(q, CX + q * 256)

        @pl.when(q == 0)
        def _():
            sum_3(wide_chunk(1))

        @pl.when(q >= 1)
        def _():
            sum_1(quad_chunk(q - 1))

        @pl.when(q >= 2)
        def _():
            sum_2(quad_chunk(q - 2))

        @pl.when(q >= 3)
        def _():
            sum_3(quad_chunk(q - 3))

        conv_back_all(q, CX + q * 256, AT_X + q * 256)
        g = quad_chunk(q)
        put_grad(g, 0, dot(r.normed_t[...], r.dproj[:, span(AT_X + q * 256, 256)]))
        sum_0(g)

    loop(QUADS, backward_quad)

    def ratio_of(b):
        z, step = head_rows(b)
        return jnp.where(z < -15.0, 1.0, sigmoid(z) / jnp.maximum(step, 1e-37))

    def backward_rest(b):
        rows = rows_of(b)
        key, query = r.cout[rows, 0:NSTATE], r.cout[rows, NSTATE:CX]
        d_scores = ds_of(b)[...].astype(BF)
        r.gate[:, span(b * 256, NSTATE, 128)] = r.dkb[rows, :] + dot(d_scores, query)
        r.gate[:, span(b * 256 + NSTATE, NSTATE, 128)] = r.dqb[rows, :] + dot(d_scores.T, key)
        both_sums = give_of(b)[...]
        in_low = iota((GROUP, LANES), 1) < HEADS
        give = jnp.where(in_low, both_sums, 0.0)
        take = jnp.where(in_low, pltpu.roll(both_sums, 64, 1), 0.0)
        kept_of(b)[...] = give * ratio_of(b)
        give_of(b)[...] = exact_sum(upper, take - give)

    loop(BLOCKS, backward_rest)

    def block_total(b, run, grad, decay):
        kept = jnp.sum(run[...] * grad[...], axis=0, keepdims=True)
        summed = jnp.sum(r.flow[b], axis=0, keepdims=True) + decay * kept
        high, low = halves(jnp.broadcast_to(summed, (8, INNER)))
        by_head = dot_nt(high, r.spread[0:LANES, :]) + dot_nt(low, r.spread[0:LANES, :])
        rows = rows_of(b)
        give_of(b)[...] = give_of(b)[...] + by_head[0:1, :]

    block_total(0, r.runs.at[1], r.state_in, decay_0)
    block_total(1, r.runs.at[0], r.dstate_in, decay_1)

    def step_grad(b):
        rows = rows_of(b)
        z, step = head_rows(b)
        back_sum = give_of(b)[...]
        d_pre = kept_of(b)[...] + rate * back_sum * sigmoid(z)
        r.g_head[0:8, :] += fold(d_pre)
        r.g_head[8:16, :] += fold(back_sum * (step * rate))
        r.dproj[rows, AT_DT : AT_DT + LANES] = d_pre.astype(BF)

    loop(BLOCKS, step_grad)
    sum_1(quad_chunk(5))
    first_edge(QUADS, 0)
    conv_back_all(QUADS, 0, 0)
    put_grad(last_chunk, 0, dot(r.normed_t[...], r.dproj[:, 0:AT_X]))
    sum_0(last_chunk)
    sum_2(quad_chunk(4))
    sum_3(quad_chunk(3))

    def in_block(b):
        rows = rows_of(b)
        r.ssd[rows, 0:D] = dot_nt(r.dproj[rows, :], w[:, 0:AT_OUT])

    in_block(2)
    sum_1(last_chunk)
    sum_2(quad_chunk(5))
    sum_3(quad_chunk(4))
    loop(2, in_block)
    sum_3(quad_chunk(5))

    def norm_back(i):
        rows = span(i * 32, 32)
        v = r.tok[rows, :].astype(F32)
        root = lax.rsqrt(jnp.mean(v * v, axis=1, keepdims=True) + EPS)
        y = v * root
        dn = r.ssd[rows, 0:D]
        r.g_norm[...] += fold(dn * y)
        bb = norm_gain * dn
        d_v = root * (bb - y * jnp.mean(y * bb, axis=1, keepdims=True))
        r.ssd[rows, 0:D] = r.og[rows, :].astype(F32) + d_v

    loop(ROWS // 32, norm_back)
    tgrad_copy = pltpu.make_async_copy(r.ssd.at[:, 0:D], r.tgrad, r.local.at[1])
    tgrad_copy.start()

    def total(v):
        return jnp.sum(v, axis=0, keepdims=True)

    for k in range(CONV + 1):
        r.small[0, k : k + 1, :] = total(r.g_conv[8 * k : 8 * k + 8, :])
    r.small[0, 5:6, 0:INNER] = total(r.g_inner[0:8, :])
    r.small[0, 5:6, INNER : INNER + LANES] = total(r.g_head[0:8, :])
    r.small[0, 5:6, INNER + LANES :] = total(r.g_head[8:16, :])
    high, low = halves(r.g_inner[8:16, :])
    skips = dot_nt(high, r.spread[0:LANES, :]) + dot_nt(low, r.spread[0:LANES, :])
    r.small[0, 6:7, 0:LANES] = total(skips)
    r.small[0, 6:7, LANES:] = jnp.zeros((1, CONVCH - LANES), F32)
    r.small[0, 7:8, 0:D] = total(r.g_norm[...])
    r.small[0, 7:8, D:] = jnp.zeros((1, CONVCH - D), F32)
    if fused:

        def send_small(level, first, count, device):
            for j in range(count):
                sems = r.t_send.at[level], r.t_recv.at[level]
                dst = r.small_in.at[first + j]
                remote(r.small.at[level], dst, *sems, device(j + 1)).start()

        def add_small(level, first, count):
            at = r.small_in.at[first : first + count]
            for sem in (r.t_send.at[level], r.t_recv.at[level]):
                pltpu.make_async_copy(at, at, sem).wait()
            value = r.small[level]
            for j in range(count):
                value = value + r.small_in[first + j]
            return value

        send_small(0, 0, 1, lambda j: sibling)
        sum_2(last_chunk)
        r.small[1] = add_small(0, 0, 1)
        send_small(1, 1, PLANE - 1, on_plane)
        sum_3(last_chunk)
        r.small[2] = add_small(1, 1, PLANE - 1)
        send_small(2, PLANE, nz - 1, on_chain)

        def hand_out(g, dst, first, count):
            sum_4(g)
            mine = r.fin[g[4], span(seq * own, own, 8), target(g)]
            theirs = r.gsum[g[4], :, target(g)]
            for half_at in range(2):
                value = jnp.where(seq == half_at, mine, theirs)
                size = min(g[3], count - half_at * g[3])
                at = first + half_at * g[3]
                dst[:, at : at + size] = value[:, 0:size]

        for i in range(WIDE_CHUNKS):
            dst = r.grad_out if i < 2 else r.grad_in
            hand_out(wide_chunk(i), dst, (i % 2) * CHUNK, CHUNK)
        for q in range(QUADS):
            hand_out(quad_chunk(q), r.grad_in, INNER + q * 256, 256)
        hand_out(last_chunk, r.grad_in, 2 * INNER, CX + HEADS)
        r.small_out[...] = add_small(2, PLANE, nz - 1)
        for c in range(len(GATHERS)):
            gather_end(c)
    else:
        r.small_out[...] = r.small[0]
    mixed_copy.wait()
    tgrad_copy.wait()


def call_mixer(fused, nz, arrays):
    vmem = pl.BlockSpec(memory_space=pltpu.VMEM)
    hbm = pl.BlockSpec(memory_space=pl.ANY)
    places = {"lengths": pl.BlockSpec(memory_space=pltpu.SMEM), "tokens": hbm, "out_grad": hbm}
    own = D // (2 * nz * PLANE) if fused else 0
    ins = list(arrays)
    outs = {"mixed": ((ROWS, D), BF), "tgrad": ((ROWS, D), F32), "small_out": ((8, CONVCH), F32)}
    scratch = {
        "tok": ((ROWS, D), BF), "og": ((ROWS, D), BF), "convp": ((8, CONVCH), F32),
        "headp": ((8, LANES), F32), "innerp": ((8, INNER), F32),
        "normed": ((ROWS + EDGE, D), BF), "normed_t": ((D, ROWS), BF), "db_t": ((D, ROWS), BF),
        "clow": ((ROWS + EDGE, CONVCH), BF), "cout": ((ROWS, CONVCH), BF),
        "gate": ((GROUP, INNER), F32), "back": ((GROUP, INNER), F32), "ssd": ((ROWS, INNER), F32),
        "dssd": ((ROWS, INNER), BF), "dproj": ((ROWS, AT_OUT), BF),
        "dtb": ((ROWS, LANES), F32), "cumb": ((ROWS, LANES), F32), "moved": ((ROWS, LANES), F32),
        "weight": ((ROWS, 256), BF), "fade": ((ROWS, 256), BF),
        "pick": ((8 * LANES, LANES), BF),
        "cut": ((BLOCKS, QUADS, 8, GROUP), F32), "spread": ((256, INNER), BF),
        "turned": ((BLOCKS, CX, GROUP), BF), "sco": ((BLOCKS, GROUP, GROUP), F32), "dkb": ((ROWS, LANES), F32), "dqb": ((ROWS, LANES), F32),
        "runs": ((2, NSTATE, INNER), F32), "held": ((2, NSTATE, INNER), BF),
        "dheld": ((2, NSTATE, INNER), F32), "dst": ((2, NSTATE, INNER), BF),
        "flow": ((2, 8, INNER), F32), "halo": ((BLOCKS, 8, CONVCH), F32),
        "halo_next": ((2, 8, CONVCH), F32), "edge_in": ((EDGE, D), BF),
        "state_in": ((NSTATE, INNER), F32), "dstate_in": ((NSTATE, INNER), F32),
        "dedge_in": ((8, CONVCH), F32), "g_norm": ((8, D), F32), "g_conv": ((40, CONVCH), F32),
        "g_head": ((16, LANES), F32), "g_inner": ((16, INNER), F32), "small": ((3, 8, CONVCH), F32),
    }
    dma = pltpu.SemaphoreType.DMA
    sems = {
        "pair_send": dma((4,)), "pair_recv": dma((4,)), "edge_send": dma((QUADS + 1,)),
        "edge_recv": dma((QUADS + 1,)), "local": dma((6,)),
    }
    if fused:
        part = CHUNK // 2
        outs |= {"grad_in": ((own, PROJ), F32), "grad_out": ((own, INNER), F32)}
        scratch |= {
            "w": ((D, WIDE), BF),
            "wg": ((SLOTS, nz, PLANE, 2 * own, CHUNK), BF),
            "r0": ((UNITS, nz, PLANE, 2 * own, part), BF),
            "r1": ((UNITS, PLANE - 1, nz, 2 * own, part), BF),
            "r2": ((UNITS, nz - 1, 2 * own, part), BF), "fin": ((UNITS, 2 * own, part), F32),
            "gsum": ((UNITS, own, part), F32), "small_in": ((PLANE + nz - 1, 8, CONVCH), F32),
        }
        sems |= {
            "g_send": dma((len(GATHERS), 2)), "g_recv": dma((len(GATHERS), 4)),
            "s_send": dma((CHUNKS,)), "s_recv": dma((CHUNKS, 4)),
            "t_send": dma((3,)), "t_recv": dma((3,)),
        }
    else:
        outs["wgrad"] = ((D, WIDE), BF)
    names = ins + list(outs) + list(scratch) + list(sems)
    return pl.pallas_call(
        functools.partial(mixer, names, fused, nz),
        out_shape=[jax.ShapeDtypeStruct(s, t) for s, t in outs.values()],
        in_specs=[places.get(name, vmem) for name in ins],
        out_specs=[hbm, hbm] + [vmem] * (len(outs) - 2),
        scratch_shapes=[pltpu.VMEM(s, t) for s, t in scratch.values()] + list(sems.values()),
        compiler_params=pltpu.CompilerParams(
            collective_id=0, has_side_effects=True, vmem_limit_bytes=63 * 1024 * 1024
        ),
        name="mixer",
    )(*arrays.values())


def place_results(
    lengths, mixed, tgrad, small, grad_in, grad_out, mixed_at, tgrad_at, norm, in_at, conv, bias,
    step, rates, skip, gain, out_at, blank, blank_low, sems,
):
    seq = lax.axis_index("seq")
    long = jnp.where(lengths[0, 0] > lengths[1, 0], 0, 1)
    rows = mixed_at.shape[2]
    blank[...] = jnp.zeros_like(blank)
    blank_low[...] = jnp.zeros_like(blank_low)
    copies = []
    for i, (src, dst, zero) in enumerate(((tgrad, tgrad_at, blank), (mixed, mixed_at, blank_low))):
        first, after = dst.at[1 - long, 0, 0:GROUP, :], dst.at[1 - long, 0, GROUP:rows, :]
        whole = pltpu.make_async_copy(src.at[0:rows, :], dst.at[long, 0], sems.at[3 * i])
        used = pltpu.make_async_copy(src.at[rows : rows + GROUP, :], first, sems.at[3 * i + 1])
        unused = pltpu.make_async_copy(zero.at[0:GROUP, :], first, sems.at[3 * i + 1])
        end = pltpu.make_async_copy(zero.at[0 : rows - GROUP, :], after, sems.at[3 * i + 2])
        whole.start()
        pl.when(seq == 0)(used.start)
        pl.when(seq > 0)(unused.start)
        end.start()
        copies += [whole, used, end]
    in_at[...] = grad_in[...]
    out_at[...] = grad_out[...]
    conv[:, 0:INNER] = small[0:CONV, CX:]
    conv[:, INNER:] = small[0:CONV, 0:CX]
    bias[...] = jnp.concatenate([small[4:5, CX:], small[4:5, 0:CX]], axis=1).reshape(CONVCH)
    gain[...] = small[5:6, 0:INNER].reshape(INNER)
    step[...] = small[5:6, INNER : INNER + HEADS].reshape(HEADS)
    rates[...] = small[5:6, INNER + LANES : INNER + LANES + HEADS].reshape(HEADS)
    skip[...] = small[6:7, 0:HEADS].reshape(HEADS)
    norm[...] = small[7:8, 0:D].reshape(D)
    for c in copies:
        c.wait()


def call_place(shape, lengths, *arrays):
    vmem = pl.BlockSpec(memory_space=pltpu.VMEM)
    hbm = pl.BlockSpec(memory_space=pl.ANY)
    own = arrays[3].shape[0]
    outs = (
        (shape, BF), (shape, F32), ((D,), F32), ((own, PROJ), F32), ((CONV, CONVCH), F32),
        ((CONVCH,), F32), ((HEADS,), F32), ((HEADS,), F32), ((HEADS,), F32), ((INNER,), F32),
        ((own, INNER), F32),
    )
    rest = max(shape[2] - GROUP, GROUP)
    results = pl.pallas_call(
        place_results,
        out_shape=[jax.ShapeDtypeStruct(s, t) for s, t in outs],
        in_specs=[pl.BlockSpec(memory_space=pltpu.SMEM)] + [vmem] * len(arrays),
        out_specs=[hbm, hbm] + [vmem] * (len(outs) - 2),
        scratch_shapes=[
            pltpu.VMEM((rest, D), F32), pltpu.VMEM((rest, D), BF), pltpu.SemaphoreType.DMA((6,)),
        ],
        name="place_results",
    )(lengths, *arrays)
    return (*results[:-1], results[-1].T)


def shards(
    tokens, lengths, norm_gain, in_weight, conv_weight, conv_bias, dt_bias, a_log, skip_gain,
    out_gain, out_weight, out_grad,
):
    both = ("fsdp", "seq")
    own = in_weight.shape[0]
    nf = lax.axis_size("fsdp")
    fused = nf % PLANE == 0 and (2 * own) % 16 == 0 and own % 8 == 0
    nz = nf // PLANE if fused else 1
    arrays = {
        "lengths": lengths, "tokens": tokens, "out_grad": out_grad, "norm_gain": norm_gain,
        "conv_weight": conv_weight, "conv_bias": conv_bias, "dt_bias": dt_bias, "a_log": a_log,
        "skip_gain": skip_gain, "out_gain": out_gain,
    }
    if fused:
        arrays |= {"in_weight": in_weight, "out_weight": out_weight.T}
        mixed, tgrad, small, grad_in, grad_out = call_mixer(fused, nz, arrays)
    else:
        fill = jnp.zeros((own, AT_X - CX - HEADS), BF)
        sent = jnp.concatenate(
            [in_weight[:, 2 * INNER :], fill, in_weight[:, INNER : 2 * INNER],
             in_weight[:, :INNER], out_weight.T], axis=1)
        arrays["w"] = lax.all_gather(sent, both, axis=0, tiled=True)
        mixed, tgrad, small, wgrad = call_mixer(fused, nz, arrays)
        summed = lax.psum_scatter(wgrad, both, scatter_dimension=0, tiled=True).astype(F32)
        grad_out = summed[:, :INNER]
        grad_in = jnp.concatenate(
            [summed[:, INNER : 3 * INNER], summed[:, 3 * INNER : 3 * INNER + CX + HEADS]], axis=1
        )
        small = lax.psum(small, both)
    return call_place(tokens.shape, lengths, mixed, tgrad, small, grad_in, grad_out)


def solution(mesh):
    spread = P(None, "fsdp", "seq", None)
    both = ("fsdp", "seq")
    return jax.shard_map(
        shards,
        mesh=mesh,
        in_specs=(
            spread, P(None, "fsdp"), P(), P(both, None), P(), P(), P(), P(), P(), P(),
            P(None, both), spread,
        ),
        out_specs=(
            spread, spread, P(), P(both, None), P(), P(), P(), P(), P(), P(), P(None, both),
        ),
        check_vma=False,
    )
```

```python
import functools
import types

import jax
import jax.numpy as jnp
from jax import lax
from jax.experimental import pallas as pl
from jax.experimental.pallas import tpu as pltpu
from jax.sharding import PartitionSpec as P

D = 768
HEADS = 24
HEADDIM = 64
NSTATE = 128
CONV = 4
GROUP = 256
INNER = 1536
CONVCH = 1792
PROJ = 3352
EPS = 1e-05

BLOCKS = 3
ROWS = BLOCKS * GROUP
EDGE = 16
LANES = 128
QUADS = INNER // 256
AT_DT = 256
AT_X = 512
AT_GATE = AT_X + INNER
AT_OUT = AT_GATE + INNER
WIDE = AT_OUT + INNER
CX = 2 * NSTATE
CHUNK = 768
WIDE_CHUNKS = 4
CHUNKS = WIDE_CHUNKS + QUADS + 1
UNITS = 7
SLOTS = 4
GATHERS = ((0, 512), (512, 512), (1024, 1024), (AT_GATE, INNER), (AT_OUT, INNER))
PLANE = 4

BF = jnp.bfloat16
F32 = jnp.float32
MESH = pl.DeviceIdType.MESH


def dot(a, b):
    return lax.dot_general(a, b, (((1,), (0,)), ((), ())), preferred_element_type=F32)


def dot_nt(a, b):
    return lax.dot_general(a, b, (((1,), (1,)), ((), ())), preferred_element_type=F32)


def sigmoid(v):
    return 0.5 * jnp.tanh(0.5 * v) + 0.5


def halves(v):
    high = v.astype(BF)
    return high, (v - high.astype(F32)).astype(BF)


def side_by_side(v):
    return jnp.concatenate(halves(v), axis=1)


def exact_sum(triangle, v):
    high, rest = halves(v)
    low = (v - high.astype(F32) - rest.astype(F32)).astype(BF)
    parts = dot(triangle, jnp.concatenate([high, rest, low], axis=1))
    return parts[:, :LANES] + parts[:, LANES : 2 * LANES] + parts[:, 2 * LANES :]


def span(start, size, multiple=None):
    return pl.ds(pl.multiple_of(start, multiple or size), size)


def rows_of(b):
    return span(b * GROUP, GROUP)


def heads_of(q):
    return span(q * 256, 256)


def fold(v):
    total = v[0:8]
    for i in range(1, v.shape[0] // 8):
        total = total + v[8 * i : 8 * i + 8]
    return total


def iota(shape, dim):
    return lax.broadcasted_iota(jnp.int32, shape, dim)


def loop(count, body, together=1):
    def step(i, _):
        for k in range(together):
            body(i * together + k)
        return 0

    lax.fori_loop(0, count // together, step, 0)


def silu_slope(v, sg):
    return sg * (1.0 + v * (1.0 - sg))


def mixer(names, fused, nz, *refs):
    r = types.SimpleNamespace(**dict(zip(names, refs)))
    seq = lax.axis_index("seq")
    f = lax.axis_index("fsdp")
    z_at, p_at = f // PLANE, f % PLANE
    sibling = {"seq": 1 - seq}
    is_second = (seq == 1).astype(F32)
    is_first = 1.0 - is_second

    def plane_peer(j):
        if j == 1:
            return p_at + 1 - 2 * (p_at % 2)
        if j == 2:
            return p_at + 2 - 4 * (p_at // 2)
        return 3 - p_at

    def z_peer(j):
        return (z_at + j + nz) % nz

    def on_plane(j):
        return {"fsdp": z_at * PLANE + plane_peer(j)}

    def on_chain(j):
        return {"fsdp": z_peer(j) * PLANE + p_at}

    own = D // (2 * nz * PLANE) if fused else 0
    peers = [sibling]
    if fused:
        peers += [on_plane(j) for j in range(1, PLANE)] + [on_chain(j) for j in range(1, nz)]
    barrier = pltpu.get_barrier_semaphore()
    for peer in peers:
        pl.semaphore_signal(barrier, inc=1, device_id=peer, device_id_type=MESH)

    def own_columns(ref, c):
        return ref.at[c * own : (c + 1) * own, 0 : GATHERS[c][1]]

    part_rows = r.tokens.shape[2]
    raw = [buf.at[0:part_rows, m * D : (m + 1) * D] for buf in (r.dssd, r.cout) for m in range(2)]
    raw_copies = []
    for i in range(4):
        src = (r.tokens, r.out_grad)[i // 2].at[i % 2, 0]
        raw_copies.append(pltpu.make_async_copy(src, raw[i], r.local.at[2 + i]))
        raw_copies[i].start()

    if fused:
        wide = 2 * INNER
        steps = r.in_weight[:, wide + CX :].astype(F32)
        fill = jnp.zeros((steps.shape[0], AT_X - CX - HEADS), F32)
        key_query = r.in_weight[:, wide : wide + CX].astype(F32)
        own_columns(r.gate, 0)[...] = jnp.concatenate([key_query, steps, fill], axis=1)
        own_columns(r.gate, 1)[...] = r.in_weight[:, INNER : INNER + 512].astype(F32)
        own_columns(r.gate, 2)[...] = r.in_weight[:, INNER + 512 : wide].astype(F32)
        own_columns(r.gate, 3)[...] = r.in_weight[:, 0:INNER].astype(F32)
        own_columns(r.gate, 4)[...] = r.out_weight[...].astype(F32)

    pl.semaphore_wait(barrier, len(peers))

    def remote(src, dst, send, recv, device):
        return pltpu.make_async_remote_copy(
            src_ref=src, dst_ref=dst, send_sem=send, recv_sem=recv, device_id=device,
            device_id_type=MESH,
        )

    def pair_copy(i, src, dst):
        return remote(src, dst, r.pair_send.at[i], r.pair_recv.at[i], sibling)

    w = r.w
    slab = 2 * own

    def part(c):
        low, size = GATHERS[c]
        return span(low + seq * (size // 2), size // 2, 128)

    def slab_of(index):
        return span(index * slab, slab, 16)

    def gather_copy(c, k, index, device):
        at = w.at[slab_of(index), part(c)]
        return remote(at, at, r.g_send.at[c, 0], r.g_recv.at[c, k], device)

    def chain_copy(c, j):
        return gather_copy(c, 0, f, on_chain(j))

    def plane_copy(c, kind, back):
        low, size = GATHERS[c]
        owner = (p_at, p_at, plane_peer(1), plane_peer(2))[kind]
        cols = part(c)
        if kind >= 2:
            cols = span(low + seq * (size // 2) + (kind - 2) * (size // 4), size // 4, 128)
        at = w.at[slab_of((z_at - back + nz) % nz * PLANE + owner), cols]
        device = on_plane((1, 2, 2, 1)[kind])
        return remote(at, at, r.g_send.at[c, 0], r.g_recv.at[c, 1 + kind // 2], device)

    def last_copy(c):
        at = w.at[:, part(c)]
        return remote(at, at, r.g_send.at[c, 1], r.g_recv.at[c, 3], sibling)

    def wait_bytes(rows, cols, sem):
        at = w.at[0 : rows * slab // 2, cols]
        pltpu.make_async_copy(at, at, sem).wait()

    def gather_own(c):
        cols = part(c)
        half_cols = span(seq * (GATHERS[c][1] // 2), GATHERS[c][1] // 2, 128)
        mine, theirs = (own_columns(ref, c)[:, half_cols] for ref in (r.gate, r.back))
        first = jnp.where(seq == 0, mine, theirs)
        second = jnp.where(seq == 0, theirs, mine)
        w[slab_of(f), cols] = jnp.concatenate([first, second], axis=0).astype(BF)

    def gather_0(c):
        for j in range(1, nz):
            chain_copy(c, j).start()

    def gather_1(c):
        for kind in range(2):
            plane_copy(c, kind, 0).start()

    def gather_2(c):
        wait_bytes(2 * (nz - 1), part(c), r.g_recv.at[c, 0])
        for back in range(1, nz):
            for kind in range(2):
                plane_copy(c, kind, back).start()

    def gather_3(c):
        wait_bytes(4 * nz, part(c), r.g_recv.at[c, 1])
        for back in range(nz):
            for kind in range(2):
                plane_copy(c, kind + 2, back).start()

    def gather_4(c):
        wait_bytes(2 * nz, part(c), r.g_recv.at[c, 2])
        last_copy(c).start()

    def gather_5(c):
        last_copy(c).wait_recv()

    def gather_end(c):
        wait_bytes(2 * (nz - 1) + 6 * nz, part(c), r.g_send.at[c, 0])
        last_copy(c).wait_send()

    def wide_chunk(i):
        return i, i, 0, CHUNK // 2, i, 0

    def quad_chunk(q):
        return WIDE_CHUNKS + q, q // 3, (q % 3) * 256, 128, WIDE_CHUNKS + q // 3, (q % 3) * 128

    last_chunk = (WIDE_CHUNKS + QUADS, 2, 0, AT_X // 2, UNITS - 1, 0)

    def source(g, which):
        return span(g[2] + which * g[3], g[3], 128)

    def target(g):
        return span(g[5], g[3], 128)

    def sum_copy_0(g):
        src = r.wg.at[g[1], :, :, :, source(g, 1 - seq)]
        dst = r.r0.at[g[4], :, :, :, target(g)]
        return remote(src, dst, r.s_send.at[g[0]], r.s_recv.at[g[0], 0], sibling)

    def sum_copy_1(g, j):
        src = r.wg.at[g[1], :, plane_peer(j), :, source(g, seq)]
        dst = r.r1.at[g[4], j - 1, :, :, target(g)]
        return remote(src, dst, r.s_send.at[g[0]], r.s_recv.at[g[0], 1], on_plane(j))

    def sum_copy_2(g, j):
        src = r.wg.at[g[1], z_peer(j), p_at, :, source(g, seq)]
        dst = r.r2.at[g[4], j - 1, :, target(g)]
        return remote(src, dst, r.s_send.at[g[0]], r.s_recv.at[g[0], 2], on_chain(j))

    def sum_copy_3(g):
        src = r.fin.at[g[4], span((1 - seq) * own, own, 8), target(g)]
        dst = r.gsum.at[g[4], :, target(g)]
        return remote(src, dst, r.s_send.at[g[0]], r.s_recv.at[g[0], 3], sibling)

    def finish_all(g, level, at):
        pltpu.make_async_copy(at, at, r.s_send.at[g[0]]).wait()
        pltpu.make_async_copy(at, at, r.s_recv.at[g[0], level]).wait()

    def finish(copy):
        copy.wait_send()
        copy.wait_recv()

    def sum_0(g):
        if fused:
            sum_copy_0(g).start()

    def sum_1(g):
        if not fused:
            return
        finish(sum_copy_0(g))

        def add(i):
            at = (g[1], i // PLANE, i % PLANE, slice(None), source(g, seq))
            theirs = r.r0[g[4], i // PLANE, i % PLANE, :, target(g)]
            r.wg[at] = (r.wg[at].astype(F32) + theirs.astype(F32)).astype(BF)

        loop(nz * PLANE, add, PLANE)
        for j in (3, 1, 2):
            sum_copy_1(g, j).start()

    def sum_2(g):
        if not fused:
            return
        finish_all(g, 1, r.r1.at[g[4], :, :, :, target(g)])

        def add(zi):
            at = (g[1], zi, p_at, slice(None), source(g, seq))
            value = r.wg[at].astype(F32)
            for j in range(PLANE - 1):
                value = value + r.r1[g[4], j, zi, :, target(g)].astype(F32)
            r.wg[at] = value.astype(BF)

        loop(nz, add, 2 if nz % 2 == 0 else 1)
        for j in range(1, nz):
            sum_copy_2(g, j).start()

    def sum_3(g):
        if not fused:
            return
        finish_all(g, 2, r.r2.at[g[4], :, :, target(g)])
        value = r.wg[g[1], z_at, p_at, :, source(g, seq)].astype(F32)
        for j in range(nz - 1):
            value = value + r.r2[g[4], j, :, target(g)].astype(F32)
        r.fin[g[4], :, target(g)] = value
        sum_copy_3(g).start()

    def sum_4(g):
        finish(sum_copy_3(g))

    def put_grad(g, low, value):
        size = value.shape[1]
        if fused:
            parts = value.astype(BF).reshape(nz, PLANE, slab, size)
            r.wg[g[1], :, :, :, span(g[2] + low, size, 128)] = parts
        else:
            first = g[4] * CHUNK + (g[2] if g[3] == 128 else 0)
            r.wgrad[:, span(first + low, size, 128)] = value.astype(BF)

    def shard_copy(c):
        size = GATHERS[c][1] // 2
        rows, cols = slice(c * own, (c + 1) * own), span((1 - seq) * size, size, 128)
        return pair_copy(1, r.gate.at[rows, cols], r.back.at[rows, cols])

    if fused:
        for c in range(len(GATHERS)):
            shard_copy(c).start()

    def make_spread(q):
        shape = (256, 256)
        head = (iota(shape, 1) + q * 256) >> 6
        r.spread[:, span(q * 256, 256)] = (head == (iota(shape, 0) & 127)).astype(F32).astype(BF)

    if fused:
        at = r.back.at[0 : own * (WIDE // 2) // INNER, :]
        for sem in (r.pair_send.at[1], r.pair_recv.at[1]):
            pltpu.make_async_copy(at, at, sem).wait()
        for c in range(len(GATHERS)):
            gather_own(c)
            if c < 2:
                gather_0(c)
                gather_1(c)
        gather_0(2)

    r.convp[0:CONV, 0:CX] = r.conv_weight[:, INNER:]
    r.convp[0:CONV, CX:] = r.conv_weight[:, 0:INNER]
    bias = r.conv_bias[...].reshape(1, CONVCH)
    r.convp[4:5, 0:CX] = bias[:, INNER:]
    r.convp[4:5, CX:] = bias[:, 0:INNER]
    r.headp[...] = jnp.zeros_like(r.headp)
    for i, v in enumerate((r.dt_bias, r.a_log, r.skip_gain)):
        r.headp[i : i + 1, 0:HEADS] = v[...].reshape(1, HEADS)
    norm_gain = r.norm_gain[...].reshape(1, D)

    first_long = r.lengths[0, 0] > r.lengths[1, 0]
    shortest = jnp.minimum(r.lengths[0, 0], r.lengths[1, 0])
    for i in range(4):
        raw_copies[i].wait()

    def pick_rows(i):
        here = span(i * 64, 64)
        for to, k in ((r.tok, 0), (r.og, 2)):
            to[here, :] = jnp.where(first_long, raw[k][here, :], raw[k + 1][here, :])

    def pick_short(i):
        here, there = span(i * 64, 64), span(2 * GROUP + i * 64, 64)
        r.tok[there, :] = jnp.where(first_long, raw[1][here, :], raw[0][here, :])
        valid = (seq * part_rows + i * 64 + iota((64, D), 0) < shortest).astype(F32)
        picked = jnp.where(first_long, raw[3][here, :], raw[2][here, :])
        r.og[there, :] = (picked.astype(F32) * valid).astype(BF)

    loop(2 * GROUP // 64, pick_rows)
    edge_copy = pair_copy(0, r.tok.at[2 * GROUP - EDGE : 2 * GROUP, :], r.edge_in)
    edge_copy.start()
    loop(GROUP // 64, pick_short)

    loop(QUADS, make_spread)
    r.innerp[0:1, :] = r.out_gain[...].reshape(1, INNER)
    r.innerp[1:2, :] = dot(side_by_side(r.headp[...]), r.spread[...])[2:3, :]
    tri_shape = (GROUP, GROUP)
    lower = (iota(tri_shape, 0) >= iota(tri_shape, 1)).astype(F32).astype(BF)
    upper = (iota(tri_shape, 0) <= iota(tri_shape, 1)).astype(F32).astype(BF)
    half = GROUP // 2
    causal = iota((half, half), 0) >= iota((half, half), 1)
    causal_t = iota((half, half), 0) <= iota((half, half), 1)
    first_head = iota((GROUP, LANES), 1) < HEADDIM
    rate = -jnp.exp(r.headp[1:2, :])

    r.g_norm[...] = jnp.zeros_like(r.g_norm)
    r.g_conv[...] = jnp.zeros_like(r.g_conv)
    r.g_head[...] = jnp.zeros_like(r.g_head)
    r.g_inner[...] = jnp.zeros_like(r.g_inner)
    r.halo[2] = jnp.zeros((8, CONVCH), F32)
    r.dproj[:, AT_DT + LANES : AT_X] = jnp.zeros((ROWS, AT_X - AT_DT - LANES), BF)

    def norm_of(v):
        root = lax.rsqrt(jnp.mean(v * v, axis=1, keepdims=True) + EPS)
        return (v * root * norm_gain).astype(BF)

    def norm_rows(i):
        rows = span(i * 64, 64)
        r.normed[rows, :] = norm_of(r.tok[rows, :].astype(F32))

    loop(ROWS // 64, norm_rows, 2)
    edge_copy.wait()
    r.normed[ROWS:, :] = norm_of(r.edge_in[...].astype(F32) * is_second)

    if fused:
        gather_2(0)
        gather_1(2)
        gather_0(3)

    def turn(b):
        rows = rows_of(b)
        r.normed_t[:, rows] = r.normed[rows, :].T
        r.db_t[:, rows] = r.og[rows, :].T

    loop(BLOCKS, turn, BLOCKS)

    if fused:
        gather_2(1)
        gather_3(0)
        gather_1(3)
        gather_4(0)
        gather_3(1)
        gather_5(0)

    def conv_acc(values, before, cols):
        rows = values.shape[0]
        ext = jnp.concatenate([before, values], axis=0)
        shifted = [ext[5 + k : 5 + k + rows] for k in range(CONV)]
        acc = r.convp[4:5, cols]
        for k in range(CONV):
            acc = acc + r.convp[k : k + 1, cols] * shifted[k]
        return acc, shifted

    def project(at, to):
        low = dot(r.normed[...], w[:, at]).astype(BF)
        r.clow[:, to] = low
        r.halo[0, :, to] = low[ROWS : ROWS + EDGE].astype(F32)[EDGE - 8 :]
        r.halo[1, :, to] = low[GROUP - 16 : GROUP].astype(F32)[8:]

    def conv_forward(b, cols):
        rows = rows_of(b)
        acc, _ = conv_acc(r.clow[rows, cols].astype(F32), r.halo[b, :, cols], cols)
        r.cout[rows, cols] = (acc * sigmoid(acc)).astype(BF)

    project(pl.ds(0, CX), pl.ds(0, CX))
    r.dtb[...] = dot(r.normed[0:ROWS, :], w[:, AT_DT : AT_DT + LANES])

    def head_rows(b):
        z = r.dtb[rows_of(b), :] + r.headp[0:1, :]
        step = jnp.maximum(z, 0.0) + jnp.log1p(jnp.exp(-jnp.abs(z)))
        return z, step

    def prepare(b):
        rows = rows_of(b)
        conv_forward(b, pl.ds(0, LANES))
        conv_forward(b, pl.ds(LANES, LANES))
        z, step = head_rows(b)
        cum = exact_sum(lower, step * rate)
        moved = cum - jnp.log(jnp.maximum(step, 1e-37))
        r.cumb[rows, :] = cum
        r.moved[rows, :] = moved
        cum_t, moved_t = cum.T, moved.T
        for q in range(QUADS):
            r.cut[b, q, 0:4, :] = moved_t[4 * q : 4 * q + 4, :]
            r.cut[b, q, 4:8, :] = cum_t[4 * q : 4 * q + 4, :]
        r.weight[rows, :] = side_by_side(jnp.exp(cum[GROUP - 1 : GROUP, :] - cum) * step)
        r.fade[rows, :] = side_by_side(jnp.exp(cum))
        key, query = r.cout[rows, 0:NSTATE], r.cout[rows, NSTATE:CX]
        r.turned[b, 0:NSTATE, :] = key.T
        r.turned[b, NSTATE:CX, :] = query.T
        r.sco[b] = dot_nt(query, key)

    loop(BLOCKS, prepare, BLOCKS)
    if fused:
        gather_2(2)
        gather_0(4)
        gather_4(1)
        gather_1(4)
        gather_5(1)

    gather_steps = (
        (1, gather_3, 2), (1, gather_2, 3), (2, gather_4, 2), (2, gather_5, 2), (3, gather_2, 4),
        (4, gather_3, 3),
    )

    def gather_on(q):
        if fused:
            for point in range(QUADS):

                @pl.when(q == point)
                def _():
                    for at, step, c in gather_steps:
                        if at == point:
                            step(c)

    def to_first(v, q):
        return pltpu.roll(v, (LANES - 4 * q) % LANES, 1)

    def forward_block(b, q):
        rows = rows_of(b)
        cols = span(CX + q * 256, 256)
        heads = span(q * 256, 256)
        for i in range(2):
            conv_forward(b, span(CX + q * 256 + i * LANES, LANES))
        xq = r.cout[rows, cols]

        if b < 2:
            spread_w = dot(r.weight[rows, :], r.spread[:, heads])
            scaled = (xq.astype(F32) * spread_w).astype(BF)
            r.runs[b, :, heads] = dot(r.turned[b, 0:NSTATE, :], scaled)

        near = to_first(r.cumb[rows, :], q)
        skip = r.innerp[1:2, heads]
        for j in range(2):
            lanes = slice(j * LANES, (j + 1) * LANES)
            xp = xq[:, lanes]
            zero = jnp.zeros_like(xp)
            x_ab = (jnp.where(first_head, xp, zero), jnp.where(first_head, zero, xp))
            top, bottom = [], []
            for e in range(2):
                h = 2 * j + e
                col_top, col_bottom = near[:half, h : h + 1], near[half:, h : h + 1]
                row = r.cut[b, q, h : h + 1, :]
                row_left, row_right = row[:, :half], row[:, half:]
                gap = jnp.where(causal, col_top - row_left, -1e30)
                top.append((r.sco[b, :half, :half] * jnp.exp(gap)).astype(BF))
                fade = jnp.exp(col_bottom - row_left)
                bottom.append((r.sco[b, half:, :half] * fade).astype(BF))
                gap = jnp.where(causal, col_bottom - row_right, -1e30)
                bottom.append((r.sco[b, half:, half:] * jnp.exp(gap)).astype(BF))
            out_top = dot(
                jnp.concatenate(top, axis=1), jnp.concatenate([v[:half] for v in x_ab], axis=0)
            )
            out_bottom = dot(jnp.concatenate(bottom, axis=1), jnp.concatenate(x_ab, axis=0))
            place = span(q * 256 + j * LANES, LANES)
            xf = xp.astype(F32) * skip[:, lanes]
            r.ssd[span(b * GROUP, half), place] = out_top + xf[:half]
            r.ssd[span(b * GROUP + half, half), place] = out_bottom + xf[half:]

    def forward_quad(q):
        gather_on(q)
        project(span(AT_X + q * 256, 256), span(CX + q * 256, 256))
        for b in range(BLOCKS):
            forward_block(b, q)

    loop(QUADS, forward_quad)

    def decay_of(b):
        last = r.cumb[b * GROUP + GROUP - 8 : (b + 1) * GROUP, :]
        return dot(side_by_side(jnp.exp(last)), r.spread[...])[7:8, :]

    decay_0, decay_1 = decay_of(0), decay_of(1)
    r.runs[1] = r.runs[1] + decay_1 * r.runs[0]
    state_copy = pair_copy(2, r.runs.at[1], r.state_in)
    state_copy.start()
    if fused:
        gather_4(3)

    def carry_block(b):
        rows = rows_of(b)
        query = r.cout[rows, NSTATE:CX]

        def quad(q):
            cols = span(q * 256, 256)
            r.ssd[rows, cols] += dot(query, r.held[b, :, cols]) * dot(
                r.fade[rows, :], r.spread[:, cols]
            )

        loop(QUADS, quad, 3)

    gain = r.innerp[0:1, :]

    def gate_project(q):
        at = span(AT_GATE + q * 256, 256)
        high, low = halves(dot(r.normed[0:ROWS, :], w[:, at]))
        r.dssd[:, span(q * 256, 256)] = high
        r.dproj[:, at] = low

    def out_back(b):
        rows = rows_of(b)

        def quad(q):
            cols = span(q * 256, 256)
            r.back[:, cols] = dot(r.og[rows, :], w[:, span(AT_OUT + q * 256, 256)])

        loop(QUADS, quad, 3)

    def gated_tile(here, k):
        cols = slice(k * 256, (k + 1) * 256)
        low = r.dproj[here, AT_GATE + k * 256 : AT_GATE + (k + 1) * 256]
        g = r.dssd[here, cols].astype(F32) + low.astype(F32)
        s = r.ssd[here, cols]
        sg = sigmoid(g)
        return cols, g, s, sg

    def row_mean(v):
        return jnp.sum(v, axis=1, keepdims=True) * (1.0 / INNER)

    def gate_forward(i):
        here = span(i * 32, 32)
        square = 0.0
        for k in range(QUADS):
            cols, g, s, sg = gated_tile(here, k)
            gated = s * (g * sg)
            square = square + gated * gated
            r.gate[0:32, cols] = gated
        root = lax.rsqrt(row_mean(square) + EPS)
        for k in range(QUADS):
            cols = slice(k * 256, (k + 1) * 256)
            to = slice(AT_X + k * 256, AT_X + (k + 1) * 256)
            r.dproj[here, to] = (r.gate[0:32, cols] * root * gain[:, cols]).astype(BF)

    def gate_block(b):
        def gate_rows(i):
            here = span(b * GROUP + i * 32, 32)
            local = span(i * 32, 32)
            square, mixed = 0.0, 0.0
            for k in range(QUADS):
                cols, g, s, sg = gated_tile(here, k)
                silu = g * sg
                gated = s * silu
                square = square + gated * gated
                mixed = mixed + gated * (gain[:, cols] * r.back[local, cols])
                r.gate[0:32, cols] = gated
                r.gate[32:64, cols] = silu
                r.gate[64:96, cols] = s * silu_slope(g, sg)
            root = lax.rsqrt(row_mean(square) + EPS)
            lean = root * row_mean(mixed)
            for k in range(QUADS):
                cols = slice(k * 256, (k + 1) * 256)
                d_out = r.back[local, cols]
                v = r.gate[0:32, cols] * root
                r.g_inner[0:8, cols] += fold(d_out * v)
                d_gated = root * (gain[:, cols] * d_out - v * lean)
                d_s = (d_gated * r.gate[32:64, cols]).astype(BF)
                r.dssd[here, cols] = d_s
                x = r.cout[here, CX + k * 256 : CX + (k + 1) * 256]
                r.g_inner[8:16, cols] += fold(d_s.astype(F32) * x.astype(F32))
                to = slice(AT_GATE + k * 256, AT_GATE + (k + 1) * 256)
                r.dproj[here, to] = (d_gated * r.gate[64:96, cols]).astype(BF)

        loop(GROUP // 32, gate_rows)

    state_copy.wait()
    r.state_in[...] = r.state_in[...] * is_second
    r.held[0] = r.state_in[...].astype(BF)
    r.runs[0] = r.runs[0] + decay_0 * r.state_in[...]
    r.held[1] = r.runs[0].astype(BF)
    r.runs[1] = r.state_in[...]

    @pl.when(seq > 0)
    def _():
        carry_block(0)

    carry_block(1)

    def add_norm(value, cols):
        product = value * w[:, cols].astype(F32)
        for k in range(value.shape[1] // LANES):
            r.g_norm[...] += product[:, k * LANES : (k + 1) * LANES]

    def wide_grad(i):
        g = wide_chunk(i)
        left = r.db_t if i < 2 else r.normed_t
        first = (AT_X if i < 2 else AT_GATE) + (i % 2) * CHUNK

        def tile(k):
            value = dot(left[...], r.dproj[:, span(first + k * 256, 256)])
            put_grad(g, k * 256, value)
            if i >= 2:
                add_norm(value, span(first + k * 256, 256))

        loop(CHUNK // 256, tile, 3)
        sum_0(g)

    if fused:
        gather_5(3)
    loop(QUADS, gate_project, 2)
    if fused:
        gather_3(4)
    loop(ROWS // 32, gate_forward)
    if fused:
        gather_4(4)
    wide_grad(0)
    wide_grad(1)
    if fused:
        gather_5(4)
    for b in range(BLOCKS):
        out_back(b)
        gate_block(b)
        if b < 2:
            sum_1(wide_chunk(b))
    wide_grad(2)
    wide_grad(3)
    sum_2(wide_chunk(0))

    def state_back(b):
        rows = rows_of(b)

        r.dqb[rows, :] = jnp.zeros((GROUP, NSTATE), F32)

        def quads(i):
            dq = 0.0
            for q in (3 * i, 3 * i + 1, 3 * i + 2):
                cols = heads_of(q)
                spread_f = dot(r.fade[rows, :], r.spread[:, cols])
                dz = (spread_f * r.dssd[rows, cols].astype(F32)).astype(BF)
                r.dheld[b, :, cols] = dot(r.turned[b, NSTATE:CX, :], dz)
                dq = dq + dot_nt(dz, r.held[b, :, cols])
            r.dqb[rows, :] += dq

        loop(QUADS // 3, quads)

    def no_state():
        r.dheld[0] = jnp.zeros((NSTATE, INNER), F32)

    r.dqb[0:GROUP, :] = jnp.zeros((GROUP, NSTATE), F32)
    pl.when(seq > 0)(lambda: state_back(0))
    pl.when(seq == 0)(no_state)
    state_back(1)
    r.dqb[2 * GROUP :, :] = jnp.zeros((GROUP, NSTATE), F32)
    r.dheld[0] = r.dheld[0] + decay_0 * r.dheld[1]
    dstate_copy = pair_copy(3, r.dheld.at[0], r.dstate_in)
    dstate_copy.start()
    sum_1(wide_chunk(2))

    def out_block(b):
        rows = rows_of(b)
        branch = dot_nt(r.dproj[rows, AT_X:AT_GATE], w[:, AT_OUT:])
        r.normed[rows, :] = (r.tok[rows, :].astype(F32) + branch).astype(BF)

    loop(BLOCKS, out_block)
    mixed_copy = pltpu.make_async_copy(r.normed.at[0:ROWS, :], r.mixed, r.local.at[0])
    mixed_copy.start()
    sum_1(wide_chunk(3))
    sum_2(wide_chunk(1))
    sum_3(wide_chunk(0))

    def ds_of(b):
        return r.back.at[:, heads_of(b)]

    def give_of(b):
        return r.back.at[:, span(CHUNK + b * LANES, LANES)]

    def kept_of(b):
        return r.back.at[:, span(CHUNK + (BLOCKS + b) * LANES, LANES)]

    def pick_heads(q):
        row, lane = iota((8 * LANES, LANES), 0), iota((8 * LANES, LANES), 1)
        pair, kind, second = row >> 9, (row >> 8) & 1, (row & 127) >> 6
        head = 4 * q + 2 * pair + second + 64 * kind
        r.pick[...] = (lane == head).astype(F32).astype(BF)

    def prepare_back(b):
        rows = rows_of(b)
        r.sco[b] = dot_nt(r.cout[rows, 0:NSTATE], r.cout[rows, NSTATE:CX])
        ds_of(b)[...] = jnp.zeros((GROUP, GROUP), F32)
        nothing = jnp.zeros((GROUP, LANES), F32)
        r.dkb[rows, :] = nothing
        give_of(b)[...] = nothing

    loop(BLOCKS, prepare_back)
    dstate_copy.wait()
    r.dstate_in[...] = r.dstate_in[...] * is_first
    r.held[1] = r.dstate_in[...].astype(BF)
    r.state_in[...] = r.dheld[1] + decay_1 * r.dstate_in[...]
    r.held[0] = r.state_in[...].astype(BF)

    def backward_block(b, q):
        rows = rows_of(b)
        heads = span(q * 256, 256)
        xq = r.cout[rows, span(CX + q * 256, 256)]
        dq4 = r.dssd[rows, heads]
        skip = r.innerp[1:2, heads]
        dx, ds = r.gate.at[:, heads_of(b)], ds_of(b)

        if b < 2:
            spread_w = dot(r.weight[rows, :], r.spread[:, heads])
            d_states = r.held[b, :, heads]
            dx_state = spread_w * dot(r.cout[rows, 0:NSTATE], d_states)
            r.flow[b, 0:8, heads] = fold(xq.astype(F32) * dx_state)
            r.dkb[rows, :] += dot_nt((xq.astype(F32) * spread_w).astype(BF), d_states)

        near = to_first(r.moved[rows, :], q)
        products = []
        for j in range(2):
            lanes = slice(j * LANES, (j + 1) * LANES)
            xp, dp = xq[:, lanes], dq4[:, lanes]
            zero = jnp.zeros_like(xp)
            d_ab = (jnp.where(first_head, dp, zero), jnp.where(first_head, zero, dp))
            top, bottom = [], []
            for e in range(2):
                h = 2 * j + e
                dm_top = dot_nt(xp[:half], d_ab[e])
                dm_bottom = dot_nt(xp[half:], d_ab[e][half:])
                col_top, col_bottom = near[:half, h : h + 1], near[half:, h : h + 1]
                row = r.cut[b, q, 4 + h : 5 + h, :]
                row_left, row_right = row[:, :half], row[:, half:]
                fade = jnp.exp(jnp.where(causal_t, row_left - col_top, -1e30))
                ds[:half, :half] += dm_top[:, :half] * fade
                top.append((r.sco[b, :half, :half] * fade).astype(BF))
                fade = jnp.exp(row_right - col_top)
                ds[:half, half:] += dm_top[:, half:] * fade
                top.append((r.sco[b, :half, half:] * fade).astype(BF))
                fade = jnp.exp(jnp.where(causal_t, row_right - col_bottom, -1e30))
                ds[half:, half:] += dm_bottom * fade
                bottom.append((r.sco[b, half:, half:] * fade).astype(BF))
            dx_top = dot(jnp.concatenate(top, axis=1), jnp.concatenate(d_ab, axis=0))
            dx_bottom = dot(
                jnp.concatenate(bottom, axis=1), jnp.concatenate([v[half:] for v in d_ab], axis=0)
            )
            dxp = jnp.concatenate([dx_top, dx_bottom], axis=0)
            if b < 2:
                dxp = dxp + dx_state[:, lanes]
            xf, df = xp.astype(F32), dp.astype(F32)
            kept = skip[:, lanes]
            ssd = r.ssd[rows, span(q * 256 + j * LANES, LANES)]
            products += [*halves(xf * dxp), *halves(df * (ssd - kept * xf))]
            dx[:, lanes] = dxp + kept * df
        give_of(b)[...] += dot(jnp.concatenate(products, axis=1), r.pick[...])

    def edge_grad(b, source, cols):
        first = r.clow[b * GROUP : b * GROUP + 16, cols].astype(F32)
        acc, _ = conv_acc(first, r.halo[b, :, cols], cols)
        d_acc = r.gate[0:16, span(b * 256 + source, LANES)] * silu_slope(acc, sigmoid(acc))
        r.halo_next[b, :, cols] = d_acc[0:8]

    def conv_back(b, source, cols, to, after):
        rows = rows_of(b)
        acc, shifted = conv_acc(r.clow[rows, cols].astype(F32), r.halo[b, :, cols], cols)
        d_acc = r.gate[:, span(b * 256 + source, LANES)] * silu_slope(acc, sigmoid(acc))
        for k in range(CONV):
            r.g_conv[8 * k : 8 * k + 8, cols] += fold(d_acc * shifted[k])
        r.g_conv[32:40, cols] += fold(d_acc)
        ext = jnp.concatenate([d_acc, after], axis=0)
        d_in = r.convp[3:4, cols] * d_acc
        for k in range(CONV - 1):
            d_in = d_in + r.convp[k : k + 1, cols] * ext[3 - k : 3 - k + GROUP]
        r.dproj[rows, to] = d_in.astype(BF)

    def edge_copy_back(i, cols):
        src, dst = r.halo_next.at[0, :, cols], r.dedge_in.at[:, cols]
        return remote(src, dst, r.edge_send.at[i], r.edge_recv.at[i], sibling)

    def first_edge(i, at):
        for k in range(2):
            edge_grad(0, k * LANES, span(at + k * LANES, LANES))
        edge_copy_back(i, span(at, 256)).start()

    def conv_back_all(i, at, to):
        cols = span(at, 256)

        def chunk(k):
            return k * LANES, span(at + k * LANES, LANES), span(to + k * LANES, LANES)

        for k in range(2):
            edge_grad(1, *chunk(k)[:2])
        for k in range(2):
            conv_back(2, *chunk(k), jnp.zeros((8, LANES), F32))
            conv_back(0, *chunk(k), r.halo_next[1, :, chunk(k)[1]])
        edge_copy_back(i, cols).wait()
        for k in range(2):
            conv_back(1, *chunk(k), r.dedge_in[:, chunk(k)[1]] * is_first)

    def backward_quad(q):
        @pl.when(q == 1)
        def _():
            sum_2(wide_chunk(2))

        @pl.when(q == 2)
        def _():
            sum_3(wide_chunk(2))
            sum_2(wide_chunk(3))

        @pl.when(q == 3)
        def _():
            sum_3(wide_chunk(3))

        pick_heads(q)
        for b in range(BLOCKS):
            backward_block(b, q)
            if b == 0:
                first_edge(q, CX + q * 256)

        @pl.when(q == 0)
        def _():
            sum_3(wide_chunk(1))

        @pl.when(q >= 1)
        def _():
            sum_1(quad_chunk(q - 1))

        @pl.when(q >= 2)
        def _():
            sum_2(quad_chunk(q - 2))

        @pl.when(q >= 3)
        def _():
            sum_3(quad_chunk(q - 3))

        conv_back_all(q, CX + q * 256, AT_X + q * 256)
        g = quad_chunk(q)
        value = dot(r.normed_t[...], r.dproj[:, span(AT_X + q * 256, 256)])
        put_grad(g, 0, value)
        sum_0(g)
        add_norm(value, span(AT_X + q * 256, 256))

    loop(QUADS, backward_quad)

    def ratio_of(b):
        z, step = head_rows(b)
        return jnp.where(z < -15.0, 1.0, sigmoid(z) / jnp.maximum(step, 1e-37))

    def backward_rest(b):
        rows = rows_of(b)
        key, query = r.cout[rows, 0:NSTATE], r.cout[rows, NSTATE:CX]
        d_scores = ds_of(b)[...].astype(BF)
        r.gate[:, span(b * 256, NSTATE, 128)] = r.dkb[rows, :] + dot(d_scores, query)
        r.gate[:, span(b * 256 + NSTATE, NSTATE, 128)] = r.dqb[rows, :] + dot(d_scores.T, key)
        both_sums = give_of(b)[...]
        in_low = iota((GROUP, LANES), 1) < HEADS
        give = jnp.where(in_low, both_sums, 0.0)
        take = jnp.where(in_low, pltpu.roll(both_sums, 64, 1), 0.0)
        kept_of(b)[...] = give * ratio_of(b)
        give_of(b)[...] = exact_sum(upper, take - give)

    loop(BLOCKS, backward_rest, BLOCKS)

    def block_total(b, run, grad, decay):
        kept = jnp.sum(run[...] * grad[...], axis=0, keepdims=True)
        summed = jnp.sum(r.flow[b], axis=0, keepdims=True) + decay * kept
        high, low = halves(jnp.broadcast_to(summed, (8, INNER)))
        by_head = dot_nt(high, r.spread[0:LANES, :]) + dot_nt(low, r.spread[0:LANES, :])
        rows = rows_of(b)
        give_of(b)[...] = give_of(b)[...] + by_head[0:1, :]

    block_total(0, r.runs.at[1], r.state_in, decay_0)
    block_total(1, r.runs.at[0], r.dstate_in, decay_1)

    def step_grad(b):
        rows = rows_of(b)
        z, step = head_rows(b)
        back_sum = give_of(b)[...]
        d_pre = kept_of(b)[...] + rate * back_sum * sigmoid(z)
        r.g_head[0:8, :] += fold(d_pre)
        r.g_head[8:16, :] += fold(back_sum * (step * rate))
        r.dproj[rows, AT_DT : AT_DT + LANES] = d_pre.astype(BF)

    loop(BLOCKS, step_grad, BLOCKS)
    sum_1(quad_chunk(5))
    first_edge(QUADS, 0)
    conv_back_all(QUADS, 0, 0)
    value = dot(r.normed_t[...], r.dproj[:, 0:AT_X])
    put_grad(last_chunk, 0, value)
    sum_0(last_chunk)
    add_norm(value, slice(0, AT_X))

    def total(v):
        return jnp.sum(v, axis=0, keepdims=True)

    for k in range(CONV + 1):
        r.small[0, k : k + 1, :] = total(r.g_conv[8 * k : 8 * k + 8, :])
    r.small[0, 5:6, 0:INNER] = total(r.g_inner[0:8, :])
    r.small[0, 5:6, INNER : INNER + LANES] = total(r.g_head[0:8, :])
    r.small[0, 5:6, INNER + LANES :] = total(r.g_head[8:16, :])
    high, low = halves(r.g_inner[8:16, :])
    skips = dot_nt(high, r.spread[0:LANES, :]) + dot_nt(low, r.spread[0:LANES, :])
    r.small[0, 6:7, 0:LANES] = total(skips)
    r.small[0, 6:7, LANES:] = jnp.zeros((1, CONVCH - LANES), F32)
    r.small[0, 7:8, 0:D] = total(r.g_norm[...].T) / norm_gain
    r.small[0, 7:8, D:] = jnp.zeros((1, CONVCH - D), F32)
    if fused:

        def send_small(level, first, count, device):
            for j in range(count):
                sems = r.t_send.at[level], r.t_recv.at[level]
                dst = r.small_in.at[first + j]
                remote(r.small.at[level], dst, *sems, device(j + 1)).start()

        def add_small(level, first, count):
            at = r.small_in.at[first : first + count]
            for sem in (r.t_send.at[level], r.t_recv.at[level]):
                pltpu.make_async_copy(at, at, sem).wait()
            value = r.small[level]
            for j in range(count):
                value = value + r.small_in[first + j]
            return value

        send_small(0, 0, 1, lambda j: sibling)

    def in_block(b):
        rows = rows_of(b)
        r.ssd[rows, 0:D] = dot_nt(r.dproj[rows, :], w[:, 0:AT_OUT])

    sum_1(last_chunk)
    sum_2(quad_chunk(4))
    sum_3(quad_chunk(3))
    in_block(2)
    if fused:
        r.small[1] = add_small(0, 0, 1)
        send_small(1, 1, PLANE - 1, on_plane)
    sum_2(quad_chunk(5))
    sum_3(quad_chunk(4))
    in_block(0)
    sum_2(last_chunk)
    if fused:
        r.small[2] = add_small(1, 1, PLANE - 1)
        send_small(2, PLANE, nz - 1, on_chain)
    in_block(1)
    sum_3(quad_chunk(5))

    def norm_back(i):
        rows = span(i * 32, 32)
        v = r.tok[rows, :].astype(F32)
        root = lax.rsqrt(jnp.mean(v * v, axis=1, keepdims=True) + EPS)
        y = v * root
        dn = r.ssd[rows, 0:D]
        bb = norm_gain * dn
        d_v = root * (bb - y * jnp.mean(y * bb, axis=1, keepdims=True))
        r.ssd[rows, 0:D] = r.og[rows, :].astype(F32) + d_v

    loop(ROWS // 32, norm_back, 3)
    tgrad_copy = pltpu.make_async_copy(r.ssd.at[:, 0:D], r.tgrad, r.local.at[1])
    tgrad_copy.start()

    if fused:
        sum_3(last_chunk)

        def hand_out(g, dst, first, count):
            sum_4(g)
            mine = r.fin[g[4], span(seq * own, own, 8), target(g)]
            theirs = r.gsum[g[4], :, target(g)]
            for half_at in range(2):
                value = jnp.where(seq == half_at, mine, theirs)
                size = min(g[3], count - half_at * g[3])
                at = first + half_at * g[3]
                dst[:, at : at + size] = value[:, 0:size]

        for i in range(WIDE_CHUNKS):
            dst = r.grad_out if i < 2 else r.grad_in
            hand_out(wide_chunk(i), dst, (i % 2) * CHUNK, CHUNK)
        for q in range(QUADS):
            hand_out(quad_chunk(q), r.grad_in, INNER + q * 256, 256)
        hand_out(last_chunk, r.grad_in, 2 * INNER, CX + HEADS)
        r.small_out[...] = add_small(2, PLANE, nz - 1)
        for c in range(len(GATHERS)):
            gather_end(c)
    else:
        r.small_out[...] = r.small[0]
    mixed_copy.wait()
    tgrad_copy.wait()


def call_mixer(fused, nz, arrays):
    vmem = pl.BlockSpec(memory_space=pltpu.VMEM)
    hbm = pl.BlockSpec(memory_space=pl.ANY)
    places = {"lengths": pl.BlockSpec(memory_space=pltpu.SMEM), "tokens": hbm, "out_grad": hbm}
    own = D // (2 * nz * PLANE) if fused else 0
    ins = list(arrays)
    outs = {"mixed": ((ROWS, D), BF), "tgrad": ((ROWS, D), F32), "small_out": ((8, CONVCH), F32)}
    scratch = {
        "tok": ((ROWS, D), BF), "og": ((ROWS, D), BF), "convp": ((8, CONVCH), F32),
        "headp": ((8, LANES), F32), "innerp": ((8, INNER), F32),
        "normed": ((ROWS + EDGE, D), BF), "normed_t": ((D, ROWS), BF), "db_t": ((D, ROWS), BF),
        "clow": ((ROWS + EDGE, CONVCH), BF), "cout": ((ROWS, CONVCH), BF),
        "gate": ((GROUP, INNER), F32), "back": ((GROUP, INNER), F32), "ssd": ((ROWS, INNER), F32),
        "dssd": ((ROWS, INNER), BF), "dproj": ((ROWS, AT_OUT), BF),
        "dtb": ((ROWS, LANES), F32), "cumb": ((ROWS, LANES), F32), "moved": ((ROWS, LANES), F32),
        "weight": ((ROWS, 256), BF), "fade": ((ROWS, 256), BF),
        "pick": ((8 * LANES, LANES), BF),
        "cut": ((BLOCKS, QUADS, 8, GROUP), F32), "spread": ((256, INNER), BF),
        "turned": ((BLOCKS, CX, GROUP), BF), "sco": ((BLOCKS, GROUP, GROUP), F32), "dkb": ((ROWS, LANES), F32), "dqb": ((ROWS, LANES), F32),
        "runs": ((2, NSTATE, INNER), F32), "held": ((2, NSTATE, INNER), BF),
        "dheld": ((2, NSTATE, INNER), F32),
        "flow": ((2, 8, INNER), F32), "halo": ((BLOCKS, 8, CONVCH), F32),
        "halo_next": ((2, 8, CONVCH), F32), "edge_in": ((EDGE, D), BF),
        "state_in": ((NSTATE, INNER), F32), "dstate_in": ((NSTATE, INNER), F32),
        "dedge_in": ((8, CONVCH), F32), "g_norm": ((D, LANES), F32), "g_conv": ((40, CONVCH), F32),
        "g_head": ((16, LANES), F32), "g_inner": ((16, INNER), F32), "small": ((3, 8, CONVCH), F32),
    }
    dma = pltpu.SemaphoreType.DMA
    sems = {
        "pair_send": dma((4,)), "pair_recv": dma((4,)), "edge_send": dma((QUADS + 1,)),
        "edge_recv": dma((QUADS + 1,)), "local": dma((6,)),
    }
    if fused:
        part = CHUNK // 2
        outs |= {"grad_in": ((own, PROJ), F32), "grad_out": ((own, INNER), F32)}
        scratch |= {
            "w": ((D, WIDE), BF),
            "wg": ((SLOTS, nz, PLANE, 2 * own, CHUNK), BF),
            "r0": ((UNITS, nz, PLANE, 2 * own, part), BF),
            "r1": ((UNITS, PLANE - 1, nz, 2 * own, part), BF),
            "r2": ((UNITS, nz - 1, 2 * own, part), BF), "fin": ((UNITS, 2 * own, part), F32),
            "gsum": ((UNITS, own, part), F32), "small_in": ((PLANE + nz - 1, 8, CONVCH), F32),
        }
        sems |= {
            "g_send": dma((len(GATHERS), 2)), "g_recv": dma((len(GATHERS), 4)),
            "s_send": dma((CHUNKS,)), "s_recv": dma((CHUNKS, 4)),
            "t_send": dma((3,)), "t_recv": dma((3,)),
        }
    else:
        outs["wgrad"] = ((D, WIDE), BF)
    names = ins + list(outs) + list(scratch) + list(sems)
    return pl.pallas_call(
        functools.partial(mixer, names, fused, nz),
        out_shape=[jax.ShapeDtypeStruct(s, t) for s, t in outs.values()],
        in_specs=[places.get(name, vmem) for name in ins],
        out_specs=[hbm, hbm] + [vmem] * (len(outs) - 2),
        scratch_shapes=[pltpu.VMEM(s, t) for s, t in scratch.values()] + list(sems.values()),
        compiler_params=pltpu.CompilerParams(
            collective_id=0, has_side_effects=True, vmem_limit_bytes=63 * 1024 * 1024
        ),
        name="mixer",
    )(*arrays.values())


def place_results(
    lengths, mixed, tgrad, small, grad_in, grad_out, mixed_at, tgrad_at, norm, in_at, conv, bias,
    step, rates, skip, gain, out_at, blank, blank_low, sems,
):
    seq = lax.axis_index("seq")
    long = jnp.where(lengths[0, 0] > lengths[1, 0], 0, 1)
    rows = mixed_at.shape[2]
    blank[...] = jnp.zeros_like(blank)
    blank_low[...] = jnp.zeros_like(blank_low)
    copies = []
    for i, (src, dst, zero) in enumerate(((tgrad, tgrad_at, blank), (mixed, mixed_at, blank_low))):
        first, after = dst.at[1 - long, 0, 0:GROUP, :], dst.at[1 - long, 0, GROUP:rows, :]
        whole = pltpu.make_async_copy(src.at[0:rows, :], dst.at[long, 0], sems.at[3 * i])
        used = pltpu.make_async_copy(src.at[rows : rows + GROUP, :], first, sems.at[3 * i + 1])
        unused = pltpu.make_async_copy(zero.at[0:GROUP, :], first, sems.at[3 * i + 1])
        end = pltpu.make_async_copy(zero.at[0 : rows - GROUP, :], after, sems.at[3 * i + 2])
        whole.start()
        pl.when(seq == 0)(used.start)
        pl.when(seq > 0)(unused.start)
        end.start()
        copies += [whole, used, end]
    in_at[...] = grad_in[...]
    out_at[...] = grad_out[...]
    conv[:, 0:INNER] = small[0:CONV, CX:]
    conv[:, INNER:] = small[0:CONV, 0:CX]
    bias[...] = jnp.concatenate([small[4:5, CX:], small[4:5, 0:CX]], axis=1).reshape(CONVCH)
    gain[...] = small[5:6, 0:INNER].reshape(INNER)
    step[...] = small[5:6, INNER : INNER + HEADS].reshape(HEADS)
    rates[...] = small[5:6, INNER + LANES : INNER + LANES + HEADS].reshape(HEADS)
    skip[...] = small[6:7, 0:HEADS].reshape(HEADS)
    norm[...] = small[7:8, 0:D].reshape(D)
    for c in copies:
        c.wait()


def call_place(shape, lengths, *arrays):
    vmem = pl.BlockSpec(memory_space=pltpu.VMEM)
    hbm = pl.BlockSpec(memory_space=pl.ANY)
    own = arrays[3].shape[0]
    outs = (
        (shape, BF), (shape, F32), ((D,), F32), ((own, PROJ), F32), ((CONV, CONVCH), F32),
        ((CONVCH,), F32), ((HEADS,), F32), ((HEADS,), F32), ((HEADS,), F32), ((INNER,), F32),
        ((own, INNER), F32),
    )
    rest = max(shape[2] - GROUP, GROUP)
    results = pl.pallas_call(
        place_results,
        out_shape=[jax.ShapeDtypeStruct(s, t) for s, t in outs],
        in_specs=[pl.BlockSpec(memory_space=pltpu.SMEM)] + [vmem] * len(arrays),
        out_specs=[hbm, hbm] + [vmem] * (len(outs) - 2),
        scratch_shapes=[
            pltpu.VMEM((rest, D), F32), pltpu.VMEM((rest, D), BF), pltpu.SemaphoreType.DMA((6,)),
        ],
        name="place_results",
    )(lengths, *arrays)
    return (*results[:-1], results[-1].T)


def shards(
    tokens, lengths, norm_gain, in_weight, conv_weight, conv_bias, dt_bias, a_log, skip_gain,
    out_gain, out_weight, out_grad,
):
    both = ("fsdp", "seq")
    own = in_weight.shape[0]
    nf = lax.axis_size("fsdp")
    fused = nf % PLANE == 0 and (2 * own) % 16 == 0 and own % 8 == 0
    nz = nf // PLANE if fused else 1
    arrays = {
        "lengths": lengths, "tokens": tokens, "out_grad": out_grad, "norm_gain": norm_gain,
        "conv_weight": conv_weight, "conv_bias": conv_bias, "dt_bias": dt_bias, "a_log": a_log,
        "skip_gain": skip_gain, "out_gain": out_gain,
    }
    if fused:
        arrays |= {"in_weight": in_weight, "out_weight": out_weight.T}
        mixed, tgrad, small, grad_in, grad_out = call_mixer(fused, nz, arrays)
    else:
        fill = jnp.zeros((own, AT_X - CX - HEADS), BF)
        sent = jnp.concatenate(
            [in_weight[:, 2 * INNER :], fill, in_weight[:, INNER : 2 * INNER],
             in_weight[:, :INNER], out_weight.T], axis=1)
        arrays["w"] = lax.all_gather(sent, both, axis=0, tiled=True)
        mixed, tgrad, small, wgrad = call_mixer(fused, nz, arrays)
        summed = lax.psum_scatter(wgrad, both, scatter_dimension=0, tiled=True).astype(F32)
        grad_out = summed[:, :INNER]
        grad_in = jnp.concatenate(
            [summed[:, INNER : 3 * INNER], summed[:, 3 * INNER : 3 * INNER + CX + HEADS]], axis=1
        )
        small = lax.psum(small, both)
    return call_place(tokens.shape, lengths, mixed, tgrad, small, grad_in, grad_out)


def solution(mesh):
    spread = P(None, "fsdp", "seq", None)
    both = ("fsdp", "seq")
    return jax.shard_map(
        shards,
        mesh=mesh,
        in_specs=(
            spread, P(None, "fsdp"), P(), P(both, None), P(), P(), P(), P(), P(), P(),
            P(None, both), spread,
        ),
        out_specs=(
            spread, spread, P(), P(both, None), P(), P(), P(), P(), P(), P(), P(None, both),
        ),
        check_vma=False,
    )
```

```python
import functools
import types

import jax
import jax.numpy as jnp
from jax import lax
from jax.experimental import pallas as pl
from jax.experimental.pallas import tpu as pltpu
from jax.sharding import PartitionSpec as P

D = 768
HEADS = 24
HEADDIM = 64
NSTATE = 128
CONV = 4
GROUP = 256
INNER = 1536
CONVCH = 1792
PROJ = 3352
EPS = 1e-05

BLOCKS = 3
ROWS = BLOCKS * GROUP
EDGE = 16
LANES = 128
QUADS = INNER // 256
AT_DT = 256
AT_X = 512
AT_GATE = AT_X + INNER
AT_OUT = AT_GATE + INNER
WIDE = AT_OUT + INNER
CX = 2 * NSTATE
CHUNK = 768
WIDE_CHUNKS = 4
CHUNKS = WIDE_CHUNKS + QUADS + 2
UNITS = 7
SLOTS = 4
GATHERS = (
    (0, 512), (512, 512), (1024, 512), (1536, 512), (AT_GATE, INNER), (AT_OUT, 1024),
    (AT_OUT + 1024, 512),
)
PLANE = 4

BF = jnp.bfloat16
F32 = jnp.float32
MESH = pl.DeviceIdType.MESH


def dot(a, b):
    return lax.dot_general(a, b, (((1,), (0,)), ((), ())), preferred_element_type=F32)


def dot_nt(a, b):
    return lax.dot_general(a, b, (((1,), (1,)), ((), ())), preferred_element_type=F32)


def sigmoid(v):
    return 0.5 * jnp.tanh(0.5 * v) + 0.5


def halves(v):
    high = v.astype(BF)
    return high, (v - high.astype(F32)).astype(BF)


def side_by_side(v):
    return jnp.concatenate(halves(v), axis=1)


def exact_sum(triangle, v):
    high, rest = halves(v)
    low = (v - high.astype(F32) - rest.astype(F32)).astype(BF)
    parts = dot(triangle, jnp.concatenate([high, rest, low], axis=1))
    return parts[:, :LANES] + parts[:, LANES : 2 * LANES] + parts[:, 2 * LANES :]


def span(start, size, multiple=None):
    return pl.ds(pl.multiple_of(start, multiple or size), size)


def rows_of(b):
    return span(b * GROUP, GROUP)


def heads_of(q):
    return span(q * 256, 256)


def fold(v):
    total = v[0:8]
    for i in range(1, v.shape[0] // 8):
        total = total + v[8 * i : 8 * i + 8]
    return total


def iota(shape, dim):
    return lax.broadcasted_iota(jnp.int32, shape, dim)


def loop(count, body, together=1):
    def step(i, _):
        for k in range(together):
            body(i * together + k)
        return 0

    lax.fori_loop(0, count // together, step, 0)


def silu_slope(v, sg):
    return sg * (1.0 + v * (1.0 - sg))


def mixer(names, fused, nz, *refs):
    r = types.SimpleNamespace(**dict(zip(names, refs)))
    seq = lax.axis_index("seq")
    f = lax.axis_index("fsdp")
    z_at, p_at = f // PLANE, f % PLANE
    sibling = {"seq": 1 - seq}
    is_second = (seq == 1).astype(F32)
    is_first = 1.0 - is_second

    def plane_peer(j):
        if j == 1:
            return p_at + 1 - 2 * (p_at % 2)
        if j == 2:
            return p_at + 2 - 4 * (p_at // 2)
        return 3 - p_at

    def z_peer(j):
        return (z_at + j + nz) % nz

    def on_plane(j):
        return {"fsdp": z_at * PLANE + plane_peer(j)}

    def on_chain(j):
        return {"fsdp": z_peer(j) * PLANE + p_at}

    own = D // (2 * nz * PLANE) if fused else 0
    peers = [sibling]
    if fused:
        peers += [on_plane(j) for j in range(1, PLANE)] + [on_chain(j) for j in range(1, nz)]
    barrier = pltpu.get_barrier_semaphore()
    for peer in peers:
        pl.semaphore_signal(barrier, inc=1, device_id=peer, device_id_type=MESH)

    def own_columns(ref, c):
        return ref.at[c * own : (c + 1) * own, 0 : GATHERS[c][1]]

    part_rows = r.tokens.shape[2]
    raw = [buf.at[0:part_rows, m * D : (m + 1) * D] for buf in (r.dssd, r.cout) for m in range(2)]
    raw_copies = []
    for i in range(4):
        src = (r.tokens, r.out_grad)[i // 2].at[i % 2, 0]
        raw_copies.append(pltpu.make_async_copy(src, raw[i], r.local.at[2 + i]))
        raw_copies[i].start()

    if fused:
        wide = 2 * INNER
        steps = r.in_weight[:, wide + CX :].astype(F32)
        fill = jnp.zeros((steps.shape[0], AT_X - CX - HEADS), F32)
        key_query = r.in_weight[:, wide : wide + CX].astype(F32)
        own_columns(r.gate, 0)[...] = jnp.concatenate([key_query, steps, fill], axis=1)
        own_columns(r.gate, 1)[...] = r.in_weight[:, INNER : INNER + 512].astype(F32)
        own_columns(r.gate, 2)[...] = r.in_weight[:, INNER + 512 : INNER + 1024].astype(F32)
        own_columns(r.gate, 3)[...] = r.in_weight[:, INNER + 1024 : wide].astype(F32)
        own_columns(r.gate, 4)[...] = r.in_weight[:, 0:INNER].astype(F32)
        own_columns(r.gate, 5)[...] = r.out_weight[:, 0:1024].astype(F32)
        own_columns(r.gate, 6)[...] = r.out_weight[:, 1024:].astype(F32)

    pl.semaphore_wait(barrier, len(peers))

    def remote(src, dst, send, recv, device):
        return pltpu.make_async_remote_copy(
            src_ref=src, dst_ref=dst, send_sem=send, recv_sem=recv, device_id=device,
            device_id_type=MESH,
        )

    def pair_copy(i, src, dst):
        return remote(src, dst, r.pair_send.at[i], r.pair_recv.at[i], sibling)

    w = r.w
    slab = 2 * own

    def part(c):
        low, size = GATHERS[c]
        return span(low + seq * (size // 2), size // 2, 128)

    def slab_of(index):
        return span(index * slab, slab, 16)

    def gather_copy(c, k, index, device):
        at = w.at[slab_of(index), part(c)]
        return remote(at, at, r.g_send.at[c, 0], r.g_recv.at[c, k], device)

    def chain_copy(c, j):
        return gather_copy(c, 0, f, on_chain(j))

    def plane_copy(c, kind, back):
        low, size = GATHERS[c]
        owner = (p_at, p_at, plane_peer(1), plane_peer(2))[kind]
        cols = part(c)
        if kind >= 2:
            cols = span(low + seq * (size // 2) + (kind - 2) * (size // 4), size // 4, 128)
        at = w.at[slab_of((z_at - back + nz) % nz * PLANE + owner), cols]
        device = on_plane((1, 2, 2, 1)[kind])
        return remote(at, at, r.g_send.at[c, 0], r.g_recv.at[c, 1 + kind // 2], device)

    def last_copy(c):
        at = w.at[:, part(c)]
        return remote(at, at, r.g_send.at[c, 1], r.g_recv.at[c, 3], sibling)

    def wait_bytes(rows, cols, sem):
        at = w.at[0 : rows * slab // 2, cols]
        pltpu.make_async_copy(at, at, sem).wait()

    def gather_own(c):
        cols = part(c)
        half_cols = span(seq * (GATHERS[c][1] // 2), GATHERS[c][1] // 2, 128)
        mine, theirs = (own_columns(ref, c)[:, half_cols] for ref in (r.gate, r.back))
        first = jnp.where(seq == 0, mine, theirs)
        second = jnp.where(seq == 0, theirs, mine)
        w[slab_of(f), cols] = jnp.concatenate([first, second], axis=0).astype(BF)

    def gather_0(c):
        for j in range(1, nz):
            chain_copy(c, j).start()

    def gather_1(c):
        for kind in range(2):
            plane_copy(c, kind, 0).start()

    def gather_2(c):
        wait_bytes(2 * (nz - 1), part(c), r.g_recv.at[c, 0])
        for back in range(1, nz):
            for kind in range(2):
                plane_copy(c, kind, back).start()

    def gather_3(c):
        wait_bytes(4 * nz, part(c), r.g_recv.at[c, 1])
        for back in range(nz):
            for kind in range(2):
                plane_copy(c, kind + 2, back).start()

    def gather_4(c):
        wait_bytes(2 * nz, part(c), r.g_recv.at[c, 2])
        last_copy(c).start()

    def turned_copy(c, j):
        at = w.at[span(z_at * PLANE * slab, PLANE * slab, 16), part(c)]
        return remote(at, at, r.g_send.at[c, 0], r.g_recv.at[c, 0], on_chain(j))

    def turned_2(c):
        wait_bytes(4, part(c), r.g_recv.at[c, 1])
        for kind in range(2):
            plane_copy(c, kind + 2, 0).start()

    def turned_3(c):
        wait_bytes(2, part(c), r.g_recv.at[c, 2])
        for j in range(1, nz):
            turned_copy(c, j).start()

    def turned_4(c):
        wait_bytes(2 * PLANE * (nz - 1), part(c), r.g_recv.at[c, 0])
        last_copy(c).start()

    def gather_5(c):
        last_copy(c).wait_recv()

    def gather_end(c):
        wait_bytes(2 * (nz - 1) + 6 * nz, part(c), r.g_send.at[c, 0])
        last_copy(c).wait_send()

    def wide_chunk(i):
        return i, i, 0, CHUNK // 2, i, 0

    def quad_chunk(q):
        return WIDE_CHUNKS + q, q // 3, (q % 3) * 256, 128, WIDE_CHUNKS + q // 3, (q % 3) * 128

    step_chunk = (WIDE_CHUNKS + QUADS, 2, AT_DT, LANES, UNITS - 1, 0)
    last_chunk = (WIDE_CHUNKS + QUADS + 1, 2, 0, LANES, UNITS - 1, LANES)

    def source(g, which):
        return span(g[2] + which * g[3], g[3], 128)

    def target(g):
        return span(g[5], g[3], 128)

    def sum_copy_0(g):
        src = r.wg.at[g[1], :, :, :, source(g, 1 - seq)]
        dst = r.r0.at[g[4], :, :, :, target(g)]
        return remote(src, dst, r.s_send.at[g[0]], r.s_recv.at[g[0], 0], sibling)

    def sum_copy_1(g, j):
        src = r.wg.at[g[1], :, plane_peer(j), :, source(g, seq)]
        dst = r.r1.at[g[4], j - 1, :, :, target(g)]
        return remote(src, dst, r.s_send.at[g[0]], r.s_recv.at[g[0], 1], on_plane(j))

    def sum_copy_2(g, j):
        src = r.wg.at[g[1], z_peer(j), p_at, :, source(g, seq)]
        dst = r.r2.at[g[4], j - 1, :, target(g)]
        return remote(src, dst, r.s_send.at[g[0]], r.s_recv.at[g[0], 2], on_chain(j))

    def sum_copy_3(g):
        src = r.fin.at[g[4], span((1 - seq) * own, own, 8), target(g)]
        dst = r.gsum.at[g[4], :, target(g)]
        return remote(src, dst, r.s_send.at[g[0]], r.s_recv.at[g[0], 3], sibling)

    def finish_all(g, level, at):
        pltpu.make_async_copy(at, at, r.s_send.at[g[0]]).wait()
        pltpu.make_async_copy(at, at, r.s_recv.at[g[0], level]).wait()

    def finish(copy):
        copy.wait_send()
        copy.wait_recv()

    def sum_0(g):
        if fused:
            sum_copy_0(g).start()

    def sum_1(g):
        if not fused:
            return
        finish(sum_copy_0(g))

        def add(i):
            at = (g[1], i // PLANE, i % PLANE, slice(None), source(g, seq))
            theirs = r.r0[g[4], i // PLANE, i % PLANE, :, target(g)]
            r.wg[at] = (r.wg[at].astype(F32) + theirs.astype(F32)).astype(BF)

        loop(nz * PLANE, add, PLANE)
        for j in (3, 1, 2):
            sum_copy_1(g, j).start()

    def sum_2(g):
        if not fused:
            return
        finish_all(g, 1, r.r1.at[g[4], :, :, :, target(g)])

        def add(zi):
            at = (g[1], zi, p_at, slice(None), source(g, seq))
            value = r.wg[at].astype(F32)
            for j in range(PLANE - 1):
                value = value + r.r1[g[4], j, zi, :, target(g)].astype(F32)
            r.wg[at] = value.astype(BF)

        loop(nz, add, 2 if nz % 2 == 0 else 1)
        for j in range(1, nz):
            sum_copy_2(g, j).start()

    def sum_3(g):
        if not fused:
            return
        finish_all(g, 2, r.r2.at[g[4], :, :, target(g)])
        value = r.wg[g[1], z_at, p_at, :, source(g, seq)].astype(F32)
        for j in range(nz - 1):
            value = value + r.r2[g[4], j, :, target(g)].astype(F32)
        r.fin[g[4], :, target(g)] = value
        sum_copy_3(g).start()

    def sum_4(g):
        finish(sum_copy_3(g))

    def put_grad(g, low, value):
        size = value.shape[1]
        if fused:
            parts = value.astype(BF).reshape(nz, PLANE, slab, size)
            r.wg[g[1], :, :, :, span(g[2] + low, size, 128)] = parts
        else:
            first = g[4] * CHUNK + (g[2] if g[3] == 128 else 0)
            r.wgrad[:, span(first + low, size, 128)] = value.astype(BF)

    def shard_copy(c):
        size = GATHERS[c][1] // 2
        rows, cols = slice(c * own, (c + 1) * own), span((1 - seq) * size, size, 128)
        return pair_copy(1, r.gate.at[rows, cols], r.back.at[rows, cols])

    if fused:
        for c in range(len(GATHERS)):
            shard_copy(c).start()

    def make_spread(q):
        shape = (256, 256)
        head = (iota(shape, 1) + q * 256) >> 6
        r.spread[:, span(q * 256, 256)] = (head == (iota(shape, 0) & 127)).astype(F32).astype(BF)

    if fused:
        at = r.back.at[0 : own * (WIDE // 2) // INNER, :]
        for sem in (r.pair_send.at[1], r.pair_recv.at[1]):
            pltpu.make_async_copy(at, at, sem).wait()
        for c in range(len(GATHERS)):
            gather_own(c)
            if c < 2:
                gather_0(c)
                gather_1(c)
        gather_0(2)
        gather_1(6)

    r.convp[0:CONV, 0:CX] = r.conv_weight[:, INNER:]
    r.convp[0:CONV, CX:] = r.conv_weight[:, 0:INNER]
    bias = r.conv_bias[...].reshape(1, CONVCH)
    r.convp[4:5, 0:CX] = bias[:, INNER:]
    r.convp[4:5, CX:] = bias[:, 0:INNER]
    r.headp[...] = jnp.zeros_like(r.headp)
    for i, v in enumerate((r.dt_bias, r.a_log, r.skip_gain)):
        r.headp[i : i + 1, 0:HEADS] = v[...].reshape(1, HEADS)
    norm_gain = r.norm_gain[...].reshape(1, D)

    first_long = r.lengths[0, 0] > r.lengths[0, 1]
    shortest = jnp.minimum(r.lengths[0, 0], r.lengths[0, 1])
    for i in range(4):
        raw_copies[i].wait()

    def pick_rows(i):
        here = span(i * 64, 64)
        for to, k in ((r.tok, 0), (r.og, 2)):
            to[here, :] = jnp.where(first_long, raw[k][here, :], raw[k + 1][here, :])

    def pick_short(i):
        here, there = span(i * 64, 64), span(2 * GROUP + i * 64, 64)
        r.tok[there, :] = jnp.where(first_long, raw[1][here, :], raw[0][here, :])
        valid = (seq * part_rows + i * 64 + iota((64, D), 0) < shortest).astype(F32)
        picked = jnp.where(first_long, raw[3][here, :], raw[2][here, :])
        r.og[there, :] = (picked.astype(F32) * valid).astype(BF)

    loop(2 * GROUP // 64, pick_rows)
    edge_copy = pair_copy(0, r.tok.at[2 * GROUP - EDGE : 2 * GROUP, :], r.edge_in)
    edge_copy.start()
    if fused:
        gather_2(0)
        gather_1(2)
        gather_0(3)
    loop(GROUP // 64, pick_short)

    loop(QUADS, make_spread)
    r.innerp[0:1, :] = r.out_gain[...].reshape(1, INNER)
    r.innerp[1:2, :] = dot(side_by_side(r.headp[...]), r.spread[...])[2:3, :]
    tri_shape = (GROUP, GROUP)
    lower = (iota(tri_shape, 0) >= iota(tri_shape, 1)).astype(F32).astype(BF)
    upper = (iota(tri_shape, 0) <= iota(tri_shape, 1)).astype(F32).astype(BF)
    half = GROUP // 2
    causal = iota((half, half), 0) >= iota((half, half), 1)
    causal_t = iota((half, half), 0) <= iota((half, half), 1)
    first_head = iota((GROUP, LANES), 1) < HEADDIM
    rate = -jnp.exp(r.headp[1:2, :])

    r.g_norm[...] = jnp.zeros_like(r.g_norm)
    r.g_conv[...] = jnp.zeros_like(r.g_conv)
    r.g_head[...] = jnp.zeros_like(r.g_head)
    r.g_inner[...] = jnp.zeros_like(r.g_inner)
    r.halo[2] = jnp.zeros((8, CONVCH), F32)
    r.dproj[:, AT_DT + LANES : AT_X] = jnp.zeros((ROWS, AT_X - AT_DT - LANES), BF)

    def norm_of(v):
        root = lax.rsqrt(jnp.mean(v * v, axis=1, keepdims=True) + EPS)
        return (v * root * norm_gain).astype(BF)

    def norm_rows(i):
        rows = span(i * 64, 64)
        r.normed[rows, :] = norm_of(r.tok[rows, :].astype(F32))

    loop(ROWS // 64, norm_rows, 2)
    if fused:
        gather_3(0)
        gather_2(1)
    edge_copy.wait()
    r.normed[ROWS:, :] = norm_of(r.edge_in[...].astype(F32) * is_second)

    def turn(b):
        rows = rows_of(b)
        r.normed_t[:, rows] = r.normed[rows, :].T
        r.db_t[:, rows] = r.og[rows, :].T

    loop(BLOCKS, turn, BLOCKS)

    if fused:
        gather_4(0)
        gather_3(1)
        turned_2(6)
        gather_1(3)
        gather_0(4)
        gather_5(0)

    def conv_acc(values, before, cols):
        rows = values.shape[0]
        ext = jnp.concatenate([before, values], axis=0)
        shifted = [ext[5 + k : 5 + k + rows] for k in range(CONV)]
        acc = r.convp[4:5, cols]
        for k in range(CONV):
            acc = acc + r.convp[k : k + 1, cols] * shifted[k]
        return acc, shifted

    def project(at, to):
        low = dot(r.normed[...], w[:, at]).astype(BF)
        r.clow[:, to] = low
        r.halo[0, :, to] = low[ROWS : ROWS + EDGE].astype(F32)[EDGE - 8 :]
        r.halo[1, :, to] = low[GROUP - 16 : GROUP].astype(F32)[8:]

    def conv_forward(b, cols):
        rows = rows_of(b)
        acc, _ = conv_acc(r.clow[rows, cols].astype(F32), r.halo[b, :, cols], cols)
        r.cout[rows, cols] = (acc * sigmoid(acc)).astype(BF)

    project(pl.ds(0, CX), pl.ds(0, CX))
    r.dtb[...] = dot(r.normed[0:ROWS, :], w[:, AT_DT : AT_DT + LANES])

    def head_rows(b):
        z = r.dtb[rows_of(b), :] + r.headp[0:1, :]
        step = jnp.maximum(z, 0.0) + jnp.log1p(jnp.exp(-jnp.abs(z)))
        return z, step

    def prepare(b):
        rows = rows_of(b)
        conv_forward(b, pl.ds(0, LANES))
        conv_forward(b, pl.ds(LANES, LANES))
        z, step = head_rows(b)
        cum = exact_sum(lower, step * rate)
        moved = cum - jnp.log(jnp.maximum(step, 1e-37))
        r.cumb[rows, :] = cum
        r.moved[rows, :] = moved
        cum_t, moved_t = cum.T, moved.T
        for q in range(QUADS):
            r.cut[b, q, 0:4, :] = moved_t[4 * q : 4 * q + 4, :]
            r.cut[b, q, 4:8, :] = cum_t[4 * q : 4 * q + 4, :]
        r.weight[rows, :] = side_by_side(jnp.exp(cum[GROUP - 1 : GROUP, :] - cum) * step)
        r.fade[rows, :] = side_by_side(jnp.exp(cum))
        key, query = r.cout[rows, 0:NSTATE], r.cout[rows, NSTATE:CX]
        r.turned[b, 0:NSTATE, :] = key.T
        r.turned[b, NSTATE:CX, :] = query.T
        r.sco[b] = dot_nt(query, key)

    loop(BLOCKS, prepare, BLOCKS)
    if fused:
        gather_2(2)
        gather_4(1)
        gather_2(3)
        gather_1(4)
        gather_0(5)
        gather_5(1)

    gather_steps = {
        (0, -1): ((gather_3, 2),), (1, -1): ((gather_4, 2), (gather_3, 3), (gather_1, 5)),
        (2, -1): ((gather_5, 2), (gather_4, 3), (gather_2, 4)),
        (3, -1): ((gather_2, 5), (turned_3, 6)), (4, -1): ((gather_5, 3), (gather_3, 4)),
        (5, -1): ((gather_3, 5),),
    }

    def gather_on(q, b):
        for at, steps in gather_steps.items():
            if fused and at[1] == b:

                @pl.when(q == at[0])
                def _():
                    for step, c in steps:
                        step(c)

    def to_first(v, q):
        return pltpu.roll(v, (LANES - 4 * q) % LANES, 1)

    def forward_block(b, q):
        rows = rows_of(b)
        cols = span(CX + q * 256, 256)
        heads = span(q * 256, 256)
        for i in range(2):
            conv_forward(b, span(CX + q * 256 + i * LANES, LANES))
        xq = r.cout[rows, cols]

        if b < 2:
            spread_w = dot(r.weight[rows, :], r.spread[:, heads])
            scaled = (xq.astype(F32) * spread_w).astype(BF)
            r.runs[b, :, heads] = dot(r.turned[b, 0:NSTATE, :], scaled)

        near = to_first(r.cumb[rows, :], q)
        skip = r.innerp[1:2, heads]
        for j in range(2):
            lanes = slice(j * LANES, (j + 1) * LANES)
            xp = xq[:, lanes]
            zero = jnp.zeros_like(xp)
            x_ab = (jnp.where(first_head, xp, zero), jnp.where(first_head, zero, xp))
            top, bottom = [], []
            for e in range(2):
                h = 2 * j + e
                col_top, col_bottom = near[:half, h : h + 1], near[half:, h : h + 1]
                row = r.cut[b, q, h : h + 1, :]
                row_left, row_right = row[:, :half], row[:, half:]
                gap = jnp.where(causal, col_top - row_left, -1e30)
                top.append((r.sco[b, :half, :half] * jnp.exp(gap)).astype(BF))
                fade = jnp.exp(col_bottom - row_left)
                bottom.append((r.sco[b, half:, :half] * fade).astype(BF))
                gap = jnp.where(causal, col_bottom - row_right, -1e30)
                bottom.append((r.sco[b, half:, half:] * jnp.exp(gap)).astype(BF))
            out_top = dot(
                jnp.concatenate(top, axis=1), jnp.concatenate([v[:half] for v in x_ab], axis=0)
            )
            out_bottom = dot(jnp.concatenate(bottom, axis=1), jnp.concatenate(x_ab, axis=0))
            place = span(q * 256 + j * LANES, LANES)
            xf = xp.astype(F32) * skip[:, lanes]
            r.ssd[span(b * GROUP, half), place] = out_top + xf[:half]
            r.ssd[span(b * GROUP + half, half), place] = out_bottom + xf[half:]

    def forward_quad(q):
        gather_on(q, -1)
        project(span(AT_X + q * 256, 256), span(CX + q * 256, 256))
        for b in range(BLOCKS):
            gather_on(q, b)
            forward_block(b, q)

    loop(QUADS, forward_quad)

    def decay_of(b):
        last = r.cumb[b * GROUP + GROUP - 8 : (b + 1) * GROUP, :]
        return dot(side_by_side(jnp.exp(last)), r.spread[...])[7:8, :]

    decay_0, decay_1 = decay_of(0), decay_of(1)
    r.runs[1] = r.runs[1] + decay_1 * r.runs[0]
    state_copy = pair_copy(2, r.runs.at[1], r.state_in)
    state_copy.start()
    if fused:
        gather_4(4)
        turned_4(6)

    def carry_block(b):
        rows = rows_of(b)
        query = r.cout[rows, NSTATE:CX]

        def quad(q):
            cols = span(q * 256, 256)
            r.ssd[rows, cols] += dot(query, r.held[b, :, cols]) * dot(
                r.fade[rows, :], r.spread[:, cols]
            )

        loop(QUADS, quad, 3)

    gain = r.innerp[0:1, :]

    def gate_project(q):
        at = span(AT_GATE + q * 256, 256)
        high, low = halves(dot(r.normed[0:ROWS, :], w[:, at]))
        r.dssd[:, span(q * 256, 256)] = high
        r.dproj[:, at] = low

    def out_back(b):
        rows = rows_of(b)

        def quad(q):
            cols = span(q * 256, 256)
            r.back[:, cols] = dot(r.og[rows, :], w[:, span(AT_OUT + q * 256, 256)])

        loop(QUADS, quad, 3)

    def gated_tile(here, k):
        cols = slice(k * 256, (k + 1) * 256)
        low = r.dproj[here, AT_GATE + k * 256 : AT_GATE + (k + 1) * 256]
        g = r.dssd[here, cols].astype(F32) + low.astype(F32)
        s = r.ssd[here, cols]
        sg = sigmoid(g)
        return cols, g, s, sg

    def row_mean(v):
        return jnp.sum(v, axis=1, keepdims=True) * (1.0 / INNER)

    def gate_forward(i):
        here = span(i * 32, 32)
        square = 0.0
        for k in range(QUADS):
            cols, g, s, sg = gated_tile(here, k)
            gated = s * (g * sg)
            square = square + gated * gated
            r.gate[0:32, cols] = gated
        root = lax.rsqrt(row_mean(square) + EPS)
        for k in range(QUADS):
            cols = slice(k * 256, (k + 1) * 256)
            to = slice(AT_X + k * 256, AT_X + (k + 1) * 256)
            r.dproj[here, to] = (r.gate[0:32, cols] * root * gain[:, cols]).astype(BF)

    def gate_block(b):
        def gate_rows(i):
            here = span(b * GROUP + i * 32, 32)
            local = span(i * 32, 32)
            square, mixed = 0.0, 0.0
            for k in range(QUADS):
                cols, g, s, sg = gated_tile(here, k)
                silu = g * sg
                gated = s * silu
                square = square + gated * gated
                mixed = mixed + gated * (gain[:, cols] * r.back[local, cols])
                r.gate[0:32, cols] = gated
                r.gate[32:64, cols] = silu
                r.gate[64:96, cols] = s * silu_slope(g, sg)
            root = lax.rsqrt(row_mean(square) + EPS)
            lean = root * row_mean(mixed)
            for k in range(QUADS):
                cols = slice(k * 256, (k + 1) * 256)
                d_out = r.back[local, cols]
                v = r.gate[0:32, cols] * root
                r.g_inner[0:8, cols] += fold(d_out * v)
                d_gated = root * (gain[:, cols] * d_out - v * lean)
                d_s = (d_gated * r.gate[32:64, cols]).astype(BF)
                r.dssd[here, cols] = d_s
                x = r.cout[here, CX + k * 256 : CX + (k + 1) * 256]
                r.g_inner[8:16, cols] += fold(d_s.astype(F32) * x.astype(F32))
                to = slice(AT_GATE + k * 256, AT_GATE + (k + 1) * 256)
                r.dproj[here, to] = (d_gated * r.gate[64:96, cols]).astype(BF)

        loop(GROUP // 32, gate_rows)

    state_copy.wait()
    r.state_in[...] = r.state_in[...] * is_second
    r.held[0] = r.state_in[...].astype(BF)
    r.runs[0] = r.runs[0] + decay_0 * r.state_in[...]
    r.held[1] = r.runs[0].astype(BF)
    r.runs[1] = r.state_in[...]

    @pl.when(seq > 0)
    def _():
        carry_block(0)

    carry_block(1)

    def add_norm(value, cols):
        product = value * w[:, cols].astype(F32)
        for k in range(value.shape[1] // LANES):
            r.g_norm[...] += product[:, k * LANES : (k + 1) * LANES]

    def wide_grad(i):
        g = wide_chunk(i)
        left = r.db_t if i < 2 else r.normed_t
        first = (AT_X if i < 2 else AT_GATE) + (i % 2) * CHUNK

        def tile(k):
            value = dot(left[...], r.dproj[:, span(first + k * 256, 256)])
            put_grad(g, k * 256, value)
            if i >= 2:
                add_norm(value, span(first + k * 256, 256))

        loop(CHUNK // 256, tile, 3)
        sum_0(g)

    if fused:
        gather_4(5)
        gather_5(4)
    loop(QUADS, gate_project, 2)
    loop(ROWS // 32, gate_forward)
    wide_grad(0)
    wide_grad(1)
    if fused:
        gather_5(5)
        gather_5(6)
    for b in range(2):
        out_back(b)
        gate_block(b)
        sum_1(wide_chunk(b))

    @pl.when(seq == 0)
    def _():
        out_back(2)
        gate_block(2)

    @pl.when(seq > 0)
    def _():
        r.dssd[2 * GROUP :, :] = jnp.zeros((GROUP, INNER), BF)
        r.dproj[2 * GROUP :, AT_GATE:AT_OUT] = jnp.zeros((GROUP, INNER), BF)

    wide_grad(2)
    wide_grad(3)
    sum_2(wide_chunk(0))

    def state_back(b):
        rows = rows_of(b)

        r.dqb[rows, :] = jnp.zeros((GROUP, NSTATE), F32)

        def quads(i):
            dq = 0.0
            for q in (3 * i, 3 * i + 1, 3 * i + 2):
                cols = heads_of(q)
                spread_f = dot(r.fade[rows, :], r.spread[:, cols])
                dz = (spread_f * r.dssd[rows, cols].astype(F32)).astype(BF)
                r.dheld[b, :, cols] = dot(r.turned[b, NSTATE:CX, :], dz)
                dq = dq + dot_nt(dz, r.held[b, :, cols])
            r.dqb[rows, :] += dq

        loop(QUADS // 3, quads)

    def no_state():
        r.dheld[0] = jnp.zeros((NSTATE, INNER), F32)

    r.dqb[0:GROUP, :] = jnp.zeros((GROUP, NSTATE), F32)
    pl.when(seq > 0)(lambda: state_back(0))
    pl.when(seq == 0)(no_state)
    state_back(1)
    r.dqb[2 * GROUP :, :] = jnp.zeros((GROUP, NSTATE), F32)
    r.dheld[0] = r.dheld[0] + decay_0 * r.dheld[1]
    dstate_copy = pair_copy(3, r.dheld.at[0], r.dstate_in)
    dstate_copy.start()
    sum_1(wide_chunk(2))

    def out_block(b):
        rows = rows_of(b)
        branch = dot_nt(r.dproj[rows, AT_X:AT_GATE], w[:, AT_OUT:])
        r.normed[rows, :] = (r.tok[rows, :].astype(F32) + branch).astype(BF)

    loop(BLOCKS, out_block)
    mixed_copy = pltpu.make_async_copy(r.normed.at[0:ROWS, :], r.mixed, r.local.at[0])
    mixed_copy.start()
    sum_1(wide_chunk(3))
    sum_2(wide_chunk(1))
    sum_3(wide_chunk(0))

    def ds_of(b):
        return r.back.at[:, heads_of(b)]

    def give_of(b):
        return r.back.at[:, span(CHUNK + b * LANES, LANES)]

    def kept_of(b):
        return r.back.at[:, span(CHUNK + (BLOCKS + b) * LANES, LANES)]

    def pick_heads(q):
        row, lane = iota((8 * LANES, LANES), 0), iota((8 * LANES, LANES), 1)
        pair, kind, second = row >> 9, (row >> 8) & 1, (row & 127) >> 6
        head = 4 * q + 2 * pair + second + 64 * kind
        r.pick[...] = (lane == head).astype(F32).astype(BF)

    def prepare_back(b):
        rows = rows_of(b)
        r.sco[b] = dot_nt(r.cout[rows, 0:NSTATE], r.cout[rows, NSTATE:CX])
        ds_of(b)[...] = jnp.zeros((GROUP, GROUP), F32)
        nothing = jnp.zeros((GROUP, LANES), F32)
        r.dkb[rows, :] = nothing
        give_of(b)[...] = nothing

    loop(BLOCKS, prepare_back)
    dstate_copy.wait()
    r.dstate_in[...] = r.dstate_in[...] * is_first
    r.held[1] = r.dstate_in[...].astype(BF)
    r.state_in[...] = r.dheld[1] + decay_1 * r.dstate_in[...]
    r.held[0] = r.state_in[...].astype(BF)

    def backward_block(b, q):
        rows = rows_of(b)
        heads = span(q * 256, 256)
        xq = r.cout[rows, span(CX + q * 256, 256)]
        dq4 = r.dssd[rows, heads]
        skip = r.innerp[1:2, heads]
        dx, ds = r.gate.at[:, heads_of(b)], ds_of(b)

        if b < 2:
            spread_w = dot(r.weight[rows, :], r.spread[:, heads])
            d_states = r.held[b, :, heads]
            dx_state = spread_w * dot(r.cout[rows, 0:NSTATE], d_states)
            r.flow[b, 0:8, heads] = fold(xq.astype(F32) * dx_state)
            r.dkb[rows, :] += dot_nt((xq.astype(F32) * spread_w).astype(BF), d_states)

        near = to_first(r.moved[rows, :], q)
        products = []
        for j in range(2):
            lanes = slice(j * LANES, (j + 1) * LANES)
            xp, dp = xq[:, lanes], dq4[:, lanes]
            zero = jnp.zeros_like(xp)
            d_ab = (jnp.where(first_head, dp, zero), jnp.where(first_head, zero, dp))
            top, bottom = [], []
            for e in range(2):
                h = 2 * j + e
                dm_top = dot_nt(xp[:half], d_ab[e])
                dm_bottom = dot_nt(xp[half:], d_ab[e][half:])
                col_top, col_bottom = near[:half, h : h + 1], near[half:, h : h + 1]
                row = r.cut[b, q, 4 + h : 5 + h, :]
                row_left, row_right = row[:, :half], row[:, half:]
                fade = jnp.exp(jnp.where(causal_t, row_left - col_top, -1e30))
                ds[:half, :half] += dm_top[:, :half] * fade
                top.append((r.sco[b, :half, :half] * fade).astype(BF))
                fade = jnp.exp(row_right - col_top)
                ds[:half, half:] += dm_top[:, half:] * fade
                top.append((r.sco[b, :half, half:] * fade).astype(BF))
                fade = jnp.exp(jnp.where(causal_t, row_right - col_bottom, -1e30))
                ds[half:, half:] += dm_bottom * fade
                bottom.append((r.sco[b, half:, half:] * fade).astype(BF))
            dx_top = dot(jnp.concatenate(top, axis=1), jnp.concatenate(d_ab, axis=0))
            dx_bottom = dot(
                jnp.concatenate(bottom, axis=1), jnp.concatenate([v[half:] for v in d_ab], axis=0)
            )
            dxp = jnp.concatenate([dx_top, dx_bottom], axis=0)
            if b < 2:
                dxp = dxp + dx_state[:, lanes]
            xf, df = xp.astype(F32), dp.astype(F32)
            kept = skip[:, lanes]
            ssd = r.ssd[rows, span(q * 256 + j * LANES, LANES)]
            products += [*halves(xf * dxp), *halves(df * (ssd - kept * xf))]
            dx[:, lanes] = dxp + kept * df
        give_of(b)[...] += dot(jnp.concatenate(products, axis=1), r.pick[...])

    def edge_grad(b, source, cols):
        first = r.clow[b * GROUP : b * GROUP + 16, cols].astype(F32)
        acc, _ = conv_acc(first, r.halo[b, :, cols], cols)
        d_acc = r.gate[0:16, span(b * 256 + source, LANES)] * silu_slope(acc, sigmoid(acc))
        r.halo_next[b, :, cols] = d_acc[0:8]

    def conv_back(b, source, cols, to, after):
        rows = rows_of(b)
        acc, shifted = conv_acc(r.clow[rows, cols].astype(F32), r.halo[b, :, cols], cols)
        d_acc = r.gate[:, span(b * 256 + source, LANES)] * silu_slope(acc, sigmoid(acc))
        for k in range(CONV):
            r.g_conv[8 * k : 8 * k + 8, cols] += fold(d_acc * shifted[k])
        r.g_conv[32:40, cols] += fold(d_acc)
        ext = jnp.concatenate([d_acc, after], axis=0)
        d_in = r.convp[3:4, cols] * d_acc
        for k in range(CONV - 1):
            d_in = d_in + r.convp[k : k + 1, cols] * ext[3 - k : 3 - k + GROUP]
        r.dproj[rows, to] = d_in.astype(BF)

    def edge_copy_back(i, cols):
        src, dst = r.halo_next.at[0, :, cols], r.dedge_in.at[:, cols]
        return remote(src, dst, r.edge_send.at[i], r.edge_recv.at[i], sibling)

    def first_edge(i, at):
        for k in range(2):
            edge_grad(0, k * LANES, span(at + k * LANES, LANES))
        edge_copy_back(i, span(at, 256)).start()

    def conv_back_all(i, at, to):
        cols = span(at, 256)

        def chunk(k):
            return k * LANES, span(at + k * LANES, LANES), span(to + k * LANES, LANES)

        for k in range(2):
            edge_grad(1, *chunk(k)[:2])
        for k in range(2):
            conv_back(2, *chunk(k), jnp.zeros((8, LANES), F32))
            conv_back(0, *chunk(k), r.halo_next[1, :, chunk(k)[1]])
        edge_copy_back(i, cols).wait()
        for k in range(2):
            conv_back(1, *chunk(k), r.dedge_in[:, chunk(k)[1]] * is_first)

    def backward_quad(q):
        @pl.when(q == 1)
        def _():
            sum_2(wide_chunk(2))

        @pl.when(q == 2)
        def _():
            sum_3(wide_chunk(2))
            sum_2(wide_chunk(3))

        @pl.when(q == 3)
        def _():
            sum_3(wide_chunk(3))

        pick_heads(q)
        for b in range(BLOCKS):
            backward_block(b, q)
            if b == 0:
                first_edge(q, CX + q * 256)

        @pl.when(q == 0)
        def _():
            sum_3(wide_chunk(1))

        @pl.when(q >= 1)
        def _():
            sum_1(quad_chunk(q - 1))

        @pl.when(q >= 2)
        def _():
            sum_2(quad_chunk(q - 2))

        @pl.when(q >= 3)
        def _():
            sum_3(quad_chunk(q - 3))

        conv_back_all(q, CX + q * 256, AT_X + q * 256)
        g = quad_chunk(q)
        value = dot(r.normed_t[...], r.dproj[:, span(AT_X + q * 256, 256)])
        put_grad(g, 0, value)
        sum_0(g)
        add_norm(value, span(AT_X + q * 256, 256))

    loop(QUADS, backward_quad)

    def ratio_of(b):
        z, step = head_rows(b)
        return jnp.where(z < -15.0, 1.0, sigmoid(z) / jnp.maximum(step, 1e-37))

    def backward_rest(b):
        rows = rows_of(b)
        key, query = r.cout[rows, 0:NSTATE], r.cout[rows, NSTATE:CX]
        d_scores = ds_of(b)[...].astype(BF)
        r.gate[:, span(b * 256, NSTATE, 128)] = r.dkb[rows, :] + dot(d_scores, query)
        r.gate[:, span(b * 256 + NSTATE, NSTATE, 128)] = r.dqb[rows, :] + dot(d_scores.T, key)
        both_sums = give_of(b)[...]
        in_low = iota((GROUP, LANES), 1) < HEADS
        give = jnp.where(in_low, both_sums, 0.0)
        take = jnp.where(in_low, pltpu.roll(both_sums, 64, 1), 0.0)
        kept_of(b)[...] = give * ratio_of(b)
        give_of(b)[...] = exact_sum(upper, take - give)

    loop(BLOCKS, backward_rest, BLOCKS)

    def block_total(b, run, grad, decay):
        kept = jnp.sum(run[...] * grad[...], axis=0, keepdims=True)
        summed = jnp.sum(r.flow[b], axis=0, keepdims=True) + decay * kept
        high, low = halves(jnp.broadcast_to(summed, (8, INNER)))
        by_head = dot_nt(high, r.spread[0:LANES, :]) + dot_nt(low, r.spread[0:LANES, :])
        rows = rows_of(b)
        give_of(b)[...] = give_of(b)[...] + by_head[0:1, :]

    block_total(0, r.runs.at[1], r.state_in, decay_0)
    block_total(1, r.runs.at[0], r.dstate_in, decay_1)

    def step_grad(b):
        rows = rows_of(b)
        z, step = head_rows(b)
        back_sum = give_of(b)[...]
        d_pre = kept_of(b)[...] + rate * back_sum * sigmoid(z)
        r.g_head[0:8, :] += fold(d_pre)
        r.g_head[8:16, :] += fold(back_sum * (step * rate))
        r.dproj[rows, AT_DT : AT_DT + LANES] = d_pre.astype(BF)

    loop(BLOCKS, step_grad, BLOCKS)
    sum_1(quad_chunk(5))
    first_edge(QUADS, 0)
    value = dot(r.normed_t[...], r.dproj[:, AT_DT:AT_X])
    put_grad(step_chunk, 0, value)
    sum_0(step_chunk)
    add_norm(value, slice(AT_DT, AT_X))
    conv_back_all(QUADS, 0, 0)
    value = dot(r.normed_t[...], r.dproj[:, 0:CX])
    put_grad(last_chunk, 0, value)
    sum_0(last_chunk)
    sum_1(step_chunk)
    add_norm(value, slice(0, CX))

    def total(v):
        return jnp.sum(v, axis=0, keepdims=True)

    for k in range(CONV + 1):
        r.small[0, k : k + 1, :] = total(r.g_conv[8 * k : 8 * k + 8, :])
    r.small[0, 5:6, 0:INNER] = total(r.g_inner[0:8, :])
    r.small[0, 5:6, INNER : INNER + LANES] = total(r.g_head[0:8, :])
    r.small[0, 5:6, INNER + LANES :] = total(r.g_head[8:16, :])
    high, low = halves(r.g_inner[8:16, :])
    skips = dot_nt(high, r.spread[0:LANES, :]) + dot_nt(low, r.spread[0:LANES, :])
    r.small[0, 6:7, 0:LANES] = total(skips)
    r.small[0, 6:7, LANES:] = jnp.zeros((1, CONVCH - LANES), F32)
    r.small[0, 7:8, 0:D] = total(r.g_norm[...].T) / norm_gain
    r.small[0, 7:8, D:] = jnp.zeros((1, CONVCH - D), F32)
    if fused:

        def send_small(level, first, count, device):
            for j in range(count):
                sems = r.t_send.at[level], r.t_recv.at[level]
                dst = r.small_in.at[first + j]
                remote(r.small.at[level], dst, *sems, device(j + 1)).start()

        def add_small(level, first, count):
            at = r.small_in.at[first : first + count]
            for sem in (r.t_send.at[level], r.t_recv.at[level]):
                pltpu.make_async_copy(at, at, sem).wait()
            value = r.small[level]
            for j in range(count):
                value = value + r.small_in[first + j]
            return value

        send_small(0, 0, 1, lambda j: sibling)

    def in_block(b):
        rows = rows_of(b)
        r.ssd[rows, 0:D] = dot_nt(r.dproj[rows, :], w[:, 0:AT_OUT])

    sum_1(last_chunk)
    sum_2(quad_chunk(4))
    sum_3(quad_chunk(3))
    in_block(2)
    if fused:
        r.small[1] = add_small(0, 0, 1)
        send_small(1, 1, PLANE - 1, on_plane)
    sum_2(quad_chunk(5))
    sum_2(step_chunk)
    sum_3(quad_chunk(4))
    in_block(0)
    sum_2(last_chunk)
    if fused:
        r.small[2] = add_small(1, 1, PLANE - 1)
        send_small(2, PLANE, nz - 1, on_chain)
    in_block(1)
    sum_3(quad_chunk(5))
    sum_3(step_chunk)

    def norm_back(i):
        rows = span(i * 32, 32)
        v = r.tok[rows, :].astype(F32)
        root = lax.rsqrt(jnp.mean(v * v, axis=1, keepdims=True) + EPS)
        y = v * root
        dn = r.ssd[rows, 0:D]
        bb = norm_gain * dn
        d_v = root * (bb - y * jnp.mean(y * bb, axis=1, keepdims=True))
        r.ssd[rows, 0:D] = r.og[rows, :].astype(F32) + d_v

    loop(ROWS // 32, norm_back, 3)
    tgrad_copy = pltpu.make_async_copy(r.ssd.at[:, 0:D], r.tgrad, r.local.at[1])
    tgrad_copy.start()

    if fused:
        sum_3(last_chunk)

        def hand_out(g, dst, first, count):
            sum_4(g)
            mine = r.fin[g[4], span(seq * own, own, 8), target(g)]
            theirs = r.gsum[g[4], :, target(g)]
            for half_at in range(2):
                value = jnp.where(seq == half_at, mine, theirs)
                size = min(g[3], count - half_at * g[3])
                at = first + half_at * g[3]
                if size > 0:
                    dst[:, at : at + size] = value[:, 0:size]

        for i in range(WIDE_CHUNKS):
            dst = r.grad_out if i < 2 else r.grad_in
            hand_out(wide_chunk(i), dst, (i % 2) * CHUNK, CHUNK)
        for q in range(QUADS):
            hand_out(quad_chunk(q), r.grad_in, INNER + q * 256, 256)
        hand_out(step_chunk, r.grad_in, 2 * INNER + CX, HEADS)
        hand_out(last_chunk, r.grad_in, 2 * INNER, CX)
        r.small_out[...] = add_small(2, PLANE, nz - 1)
        for c in range(len(GATHERS)):
            gather_end(c)
    else:
        r.small_out[...] = r.small[0]
    mixed_copy.wait()
    tgrad_copy.wait()


def call_mixer(fused, nz, arrays):
    vmem = pl.BlockSpec(memory_space=pltpu.VMEM)
    hbm = pl.BlockSpec(memory_space=pl.ANY)
    places = {"lengths": pl.BlockSpec(memory_space=pltpu.SMEM), "tokens": hbm, "out_grad": hbm}
    own = D // (2 * nz * PLANE) if fused else 0
    ins = list(arrays)
    outs = {"mixed": ((ROWS, D), BF), "tgrad": ((ROWS, D), F32), "small_out": ((8, CONVCH), F32)}
    scratch = {
        "tok": ((ROWS, D), BF), "og": ((ROWS, D), BF), "convp": ((8, CONVCH), F32),
        "headp": ((8, LANES), F32), "innerp": ((8, INNER), F32),
        "normed": ((ROWS + EDGE, D), BF), "normed_t": ((D, ROWS), BF), "db_t": ((D, ROWS), BF),
        "clow": ((ROWS + EDGE, CONVCH), BF), "cout": ((ROWS, CONVCH), BF),
        "gate": ((GROUP, INNER), F32), "back": ((GROUP, INNER), F32), "ssd": ((ROWS, INNER), F32),
        "dssd": ((ROWS, INNER), BF), "dproj": ((ROWS, AT_OUT), BF),
        "dtb": ((ROWS, LANES), F32), "cumb": ((ROWS, LANES), F32), "moved": ((ROWS, LANES), F32),
        "weight": ((ROWS, 256), BF), "fade": ((ROWS, 256), BF),
        "pick": ((8 * LANES, LANES), BF),
        "cut": ((BLOCKS, QUADS, 8, GROUP), F32), "spread": ((256, INNER), BF),
        "turned": ((BLOCKS, CX, GROUP), BF), "sco": ((BLOCKS, GROUP, GROUP), F32), "dkb": ((ROWS, LANES), F32), "dqb": ((ROWS, LANES), F32),
        "runs": ((2, NSTATE, INNER), F32), "held": ((2, NSTATE, INNER), BF),
        "dheld": ((2, NSTATE, INNER), F32),
        "flow": ((2, 8, INNER), F32), "halo": ((BLOCKS, 8, CONVCH), F32),
        "halo_next": ((2, 8, CONVCH), F32), "edge_in": ((EDGE, D), BF),
        "state_in": ((NSTATE, INNER), F32), "dstate_in": ((NSTATE, INNER), F32),
        "dedge_in": ((8, CONVCH), F32), "g_norm": ((D, LANES), F32), "g_conv": ((40, CONVCH), F32),
        "g_head": ((16, LANES), F32), "g_inner": ((16, INNER), F32), "small": ((3, 8, CONVCH), F32),
    }
    dma = pltpu.SemaphoreType.DMA
    sems = {
        "pair_send": dma((4,)), "pair_recv": dma((4,)), "edge_send": dma((QUADS + 1,)),
        "edge_recv": dma((QUADS + 1,)), "local": dma((6,)),
    }
    if fused:
        part = CHUNK // 2
        outs |= {"grad_in": ((own, PROJ), F32), "grad_out": ((own, INNER), F32)}
        scratch |= {
            "w": ((D, WIDE), BF),
            "wg": ((SLOTS, nz, PLANE, 2 * own, CHUNK), BF),
            "r0": ((UNITS, nz, PLANE, 2 * own, part), BF),
            "r1": ((UNITS, PLANE - 1, nz, 2 * own, part), BF),
            "r2": ((UNITS, nz - 1, 2 * own, part), BF), "fin": ((UNITS, 2 * own, part), F32),
            "gsum": ((UNITS, own, part), F32), "small_in": ((PLANE + nz - 1, 8, CONVCH), F32),
        }
        sems |= {
            "g_send": dma((len(GATHERS), 2)), "g_recv": dma((len(GATHERS), 4)),
            "s_send": dma((CHUNKS,)), "s_recv": dma((CHUNKS, 4)),
            "t_send": dma((3,)), "t_recv": dma((3,)),
        }
    else:
        outs["wgrad"] = ((D, WIDE), BF)
    names = ins + list(outs) + list(scratch) + list(sems)
    return pl.pallas_call(
        functools.partial(mixer, names, fused, nz),
        out_shape=[jax.ShapeDtypeStruct(s, t) for s, t in outs.values()],
        in_specs=[places.get(name, vmem) for name in ins],
        out_specs=[hbm, hbm] + [vmem] * (len(outs) - 2),
        scratch_shapes=[pltpu.VMEM(s, t) for s, t in scratch.values()] + list(sems.values()),
        compiler_params=pltpu.CompilerParams(
            collective_id=0, has_side_effects=True, vmem_limit_bytes=63 * 1024 * 1024
        ),
        name="mixer",
    )(*arrays.values())


def place_results(
    lengths, mixed, tgrad, small, grad_in, grad_out, mixed_at, tgrad_at, norm, in_at, conv, bias,
    step, rates, skip, gain, out_at, blank, blank_low, sems,
):
    seq = lax.axis_index("seq")
    long = jnp.where(lengths[0, 0] > lengths[0, 1], 0, 1)
    rows = mixed_at.shape[2]
    copies = []
    for i, (src, dst, zero) in enumerate(((tgrad, tgrad_at, blank), (mixed, mixed_at, blank_low))):
        first, after = dst.at[1 - long, 0, 0:GROUP, :], dst.at[1 - long, 0, GROUP:rows, :]
        whole = pltpu.make_async_copy(src.at[0:rows, :], dst.at[long, 0], sems.at[3 * i])
        used = pltpu.make_async_copy(src.at[rows : rows + GROUP, :], first, sems.at[3 * i + 1])
        unused = pltpu.make_async_copy(zero.at[0:GROUP, :], first, sems.at[3 * i + 1])
        end = pltpu.make_async_copy(zero.at[0 : rows - GROUP, :], after, sems.at[3 * i + 2])
        whole.start()
        pl.when(seq == 0)(used.start)
        zero[...] = jnp.zeros_like(zero)
        pl.when(seq > 0)(unused.start)
        end.start()
        copies += [whole, used, end]
    in_at[...] = grad_in[...]
    out_at[...] = grad_out[...]
    conv[:, 0:INNER] = small[0:CONV, CX:]
    conv[:, INNER:] = small[0:CONV, 0:CX]
    bias[...] = jnp.concatenate([small[4:5, CX:], small[4:5, 0:CX]], axis=1).reshape(CONVCH)
    gain[...] = small[5:6, 0:INNER].reshape(INNER)
    step[...] = small[5:6, INNER : INNER + HEADS].reshape(HEADS)
    rates[...] = small[5:6, INNER + LANES : INNER + LANES + HEADS].reshape(HEADS)
    skip[...] = small[6:7, 0:HEADS].reshape(HEADS)
    norm[...] = small[7:8, 0:D].reshape(D)
    for c in copies:
        c.wait()


def call_place(shape, lengths, *arrays):
    vmem = pl.BlockSpec(memory_space=pltpu.VMEM)
    hbm = pl.BlockSpec(memory_space=pl.ANY)
    own = arrays[3].shape[0]
    outs = (
        (shape, BF), (shape, F32), ((D,), F32), ((own, PROJ), F32), ((CONV, CONVCH), F32),
        ((CONVCH,), F32), ((HEADS,), F32), ((HEADS,), F32), ((HEADS,), F32), ((INNER,), F32),
        ((own, INNER), F32),
    )
    rest = max(shape[2] - GROUP, GROUP)
    results = pl.pallas_call(
        place_results,
        out_shape=[jax.ShapeDtypeStruct(s, t) for s, t in outs],
        in_specs=[pl.BlockSpec(memory_space=pltpu.SMEM)] + [vmem] * len(arrays),
        out_specs=[hbm, hbm] + [vmem] * (len(outs) - 2),
        scratch_shapes=[
            pltpu.VMEM((rest, D), F32), pltpu.VMEM((rest, D), BF), pltpu.SemaphoreType.DMA((6,)),
        ],
        name="place_results",
    )(lengths, *arrays)
    return (*results[:-1], results[-1].T)


def shards(
    tokens, lengths, norm_gain, in_weight, conv_weight, conv_bias, dt_bias, a_log, skip_gain,
    out_gain, out_weight, out_grad,
):
    both = ("fsdp", "seq")
    own = in_weight.shape[0]
    nf = lax.axis_size("fsdp")
    fused = nf % PLANE == 0 and (2 * own) % 16 == 0 and own % 8 == 0
    nz = nf // PLANE if fused else 1
    arrays = {
        "lengths": lengths.T, "tokens": tokens, "out_grad": out_grad, "norm_gain": norm_gain,
        "conv_weight": conv_weight, "conv_bias": conv_bias, "dt_bias": dt_bias, "a_log": a_log,
        "skip_gain": skip_gain, "out_gain": out_gain,
    }
    if fused:
        arrays |= {"in_weight": in_weight, "out_weight": out_weight.T}
        mixed, tgrad, small, grad_in, grad_out = call_mixer(fused, nz, arrays)
    else:
        fill = jnp.zeros((own, AT_X - CX - HEADS), BF)
        sent = jnp.concatenate(
            [in_weight[:, 2 * INNER :], fill, in_weight[:, INNER : 2 * INNER],
             in_weight[:, :INNER], out_weight.T], axis=1)
        arrays["w"] = lax.all_gather(sent, both, axis=0, tiled=True)
        mixed, tgrad, small, wgrad = call_mixer(fused, nz, arrays)
        summed = lax.psum_scatter(wgrad, both, scatter_dimension=0, tiled=True).astype(F32)
        grad_out = summed[:, :INNER]
        grad_in = jnp.concatenate(
            [summed[:, INNER : 3 * INNER], summed[:, 3 * INNER : 3 * INNER + CX + HEADS]], axis=1
        )
        small = lax.psum(small, both)
    return call_place(tokens.shape, lengths.T, mixed, tgrad, small, grad_in, grad_out)


def solution(mesh):
    spread = P(None, "fsdp", "seq", None)
    both = ("fsdp", "seq")
    return jax.shard_map(
        shards,
        mesh=mesh,
        in_specs=(
            spread, P(None, "fsdp"), P(), P(both, None), P(), P(), P(), P(), P(), P(),
            P(None, both), spread,
        ),
        out_specs=(
            spread, spread, P(), P(both, None), P(), P(), P(), P(), P(), P(), P(None, both),
        ),
        check_vma=False,
    )
```

```python
import functools
import types

import jax
import jax.numpy as jnp
from jax import lax
from jax.experimental import pallas as pl
from jax.experimental.pallas import tpu as pltpu
from jax.sharding import PartitionSpec as P

D = 768
HEADS = 24
HEADDIM = 64
NSTATE = 128
CONV = 4
GROUP = 256
INNER = 1536
CONVCH = 1792
PROJ = 3352
EPS = 1e-05

BLOCKS = 3
ROWS = BLOCKS * GROUP
EDGE = 16
LANES = 128
QUADS = INNER // 256
AT_DT = 256
AT_X = 512
AT_GATE = AT_X + INNER
AT_OUT = AT_GATE + INNER
WIDE = AT_OUT + INNER
CX = 2 * NSTATE
CHUNK = 768
WIDE_CHUNKS = 4
CHUNKS = WIDE_CHUNKS + QUADS + 2
UNITS = 7
SLOTS = 4
GATHERS = (
    (0, 512), (512, 512), (1024, 512), (1536, 512), (AT_GATE, INNER), (AT_OUT, 1024),
    (AT_OUT + 1024, 512),
)
PLANE = 4

BF = jnp.bfloat16
F32 = jnp.float32
MESH = pl.DeviceIdType.MESH


def dot(a, b):
    return lax.dot_general(a, b, (((1,), (0,)), ((), ())), preferred_element_type=F32)


def dot_nt(a, b):
    return lax.dot_general(a, b, (((1,), (1,)), ((), ())), preferred_element_type=F32)


def sigmoid(v):
    return 0.5 * jnp.tanh(0.5 * v) + 0.5


def halves(v):
    high = v.astype(BF)
    return high, (v - high.astype(F32)).astype(BF)


def side_by_side(v):
    return jnp.concatenate(halves(v), axis=1)


def exact_sum(triangle, v):
    high, rest = halves(v)
    low = (v - high.astype(F32) - rest.astype(F32)).astype(BF)
    parts = dot(triangle, jnp.concatenate([high, rest, low], axis=1))
    return parts[:, :LANES] + parts[:, LANES : 2 * LANES] + parts[:, 2 * LANES :]


def span(start, size, multiple=None):
    return pl.ds(pl.multiple_of(start, multiple or size), size)


def rows_of(b):
    return span(b * GROUP, GROUP)


def heads_of(q):
    return span(q * 256, 256)


def fold(v):
    total = v[0:8]
    for i in range(1, v.shape[0] // 8):
        total = total + v[8 * i : 8 * i + 8]
    return total


def iota(shape, dim):
    return lax.broadcasted_iota(jnp.int32, shape, dim)


def loop(count, body, together=1):
    def step(i, _):
        for k in range(together):
            body(i * together + k)
        return 0

    lax.fori_loop(0, count // together, step, 0)


def silu_slope(v, sg):
    return sg * (1.0 + v * (1.0 - sg))


def mixer(names, fused, nz, *refs):
    r = types.SimpleNamespace(**dict(zip(names, refs)))
    seq = lax.axis_index("seq")
    f = lax.axis_index("fsdp")
    z_at, p_at = f // PLANE, f % PLANE
    sibling = {"seq": 1 - seq}
    is_second = (seq == 1).astype(F32)
    is_first = 1.0 - is_second

    def plane_peer(j):
        if j == 1:
            return p_at + 1 - 2 * (p_at % 2)
        if j == 2:
            return p_at + 2 - 4 * (p_at // 2)
        return 3 - p_at

    def z_peer(j):
        return (z_at + j + nz) % nz

    def on_plane(j):
        return {"fsdp": z_at * PLANE + plane_peer(j)}

    def on_chain(j):
        return {"fsdp": z_peer(j) * PLANE + p_at}

    own = D // (2 * nz * PLANE) if fused else 0
    peers = [sibling]
    if fused:
        peers += [on_plane(j) for j in range(1, PLANE)] + [on_chain(j) for j in range(1, nz)]
    barrier = pltpu.get_barrier_semaphore()
    for peer in peers:
        pl.semaphore_signal(barrier, inc=1, device_id=peer, device_id_type=MESH)

    def own_columns(ref, c):
        return ref.at[c * own : (c + 1) * own, 0 : GATHERS[c][1]]

    part_rows = r.tokens.shape[2]
    raw = [buf.at[0:part_rows, m * D : (m + 1) * D] for buf in (r.dssd, r.cout) for m in range(2)]
    raw_copies = []
    for i in range(4):
        src = (r.tokens, r.out_grad)[i // 2].at[i % 2, 0]
        raw_copies.append(pltpu.make_async_copy(src, raw[i], r.local.at[2 + i]))
        raw_copies[i].start()

    if fused:
        wide = 2 * INNER
        steps = r.in_weight[:, wide + CX :].astype(F32)
        fill = jnp.zeros((steps.shape[0], AT_X - CX - HEADS), F32)
        key_query = r.in_weight[:, wide : wide + CX].astype(F32)
        own_columns(r.gate, 0)[...] = jnp.concatenate([key_query, steps, fill], axis=1)

    pl.semaphore_wait(barrier, len(peers))

    def remote(src, dst, send, recv, device):
        return pltpu.make_async_remote_copy(
            src_ref=src, dst_ref=dst, send_sem=send, recv_sem=recv, device_id=device,
            device_id_type=MESH,
        )

    def pair_copy(i, src, dst):
        return remote(src, dst, r.pair_send.at[i], r.pair_recv.at[i], sibling)

    w = r.w
    slab = 2 * own

    def part(c):
        low, size = GATHERS[c]
        return span(low + seq * (size // 2), size // 2, 128)

    def slab_of(index):
        return span(index * slab, slab, 16)

    def gather_copy(c, k, index, device):
        at = w.at[slab_of(index), part(c)]
        return remote(at, at, r.g_send.at[c, 0], r.g_recv.at[c, k], device)

    def chain_copy(c, j):
        return gather_copy(c, 0, f, on_chain(j))

    def plane_copy(c, kind, back):
        low, size = GATHERS[c]
        owner = (p_at, p_at, plane_peer(1), plane_peer(2), p_at)[kind]
        cols = part(c)
        if kind in (2, 3):
            cols = span(low + seq * (size // 2) + (kind - 2) * (size // 4), size // 4, 128)
        at = w.at[slab_of((z_at - back + nz) % nz * PLANE + owner), cols]
        device = on_plane((1, 2, 2, 1, 3)[kind])
        return remote(at, at, r.g_send.at[c, 0], r.g_recv.at[c, 1 + min(kind // 2, 1)], device)

    def last_copy(c):
        at = w.at[:, part(c)]
        return remote(at, at, r.g_send.at[c, 1], r.g_recv.at[c, 3], sibling)

    def wait_bytes(rows, cols, sem):
        at = w.at[0 : rows * slab // 2, cols]
        pltpu.make_async_copy(at, at, sem).wait()

    def gather_own(c):
        cols = part(c)
        half_cols = span(seq * (GATHERS[c][1] // 2), GATHERS[c][1] // 2, 128)
        mine, theirs = (own_columns(ref, c)[:, half_cols] for ref in (r.gate, r.back))
        first = jnp.where(seq == 0, mine, theirs)
        second = jnp.where(seq == 0, theirs, mine)
        w[slab_of(f), cols] = jnp.concatenate([first, second], axis=0).astype(BF)

    def gather_0(c):
        for j in range(1, nz):
            chain_copy(c, j).start()

    def gather_1(c):
        for kind in (0, 1) if c else (4, 0, 1):
            plane_copy(c, kind, 0).start()

    def gather_2(c):
        wait_bytes(2 * (nz - 1), part(c), r.g_recv.at[c, 0])
        for back in range(1, nz):
            for kind in (0, 1) if c else (4, 0, 1):
                plane_copy(c, kind, back).start()

    def gather_3(c):
        wait_bytes(4 * nz, part(c), r.g_recv.at[c, 1])
        for back in range(nz if c else 0):
            for kind in range(2):
                plane_copy(c, kind + 2, back).start()

    def gather_4(c):
        wait_bytes(2 * nz, part(c), r.g_recv.at[c, 2])
        last_copy(c).start()

    def turned_copy(c, j):
        at = w.at[span(z_at * PLANE * slab, PLANE * slab, 16), part(c)]
        return remote(at, at, r.g_send.at[c, 0], r.g_recv.at[c, 0], on_chain(j))

    def turned_2(c):
        wait_bytes(4, part(c), r.g_recv.at[c, 1])
        for kind in range(2):
            plane_copy(c, kind + 2, 0).start()

    def turned_3(c):
        wait_bytes(2, part(c), r.g_recv.at[c, 2])
        for j in range(1, nz):
            turned_copy(c, j).start()

    def turned_4(c):
        wait_bytes(2 * PLANE * (nz - 1), part(c), r.g_recv.at[c, 0])
        last_copy(c).start()

    def gather_5(c):
        last_copy(c).wait_recv()

    def gather_end(c):
        wait_bytes(2 * (nz - 1) + 6 * nz, part(c), r.g_send.at[c, 0])
        last_copy(c).wait_send()

    def wide_chunk(i):
        return i, i, 0, CHUNK // 2, i, 0

    def quad_chunk(q):
        return WIDE_CHUNKS + q, q // 3, (q % 3) * 256, 128, WIDE_CHUNKS + q // 3, (q % 3) * 128

    step_chunk = (WIDE_CHUNKS + QUADS, 2, AT_DT, LANES, UNITS - 1, 0)
    last_chunk = (WIDE_CHUNKS + QUADS + 1, 2, 0, LANES, UNITS - 1, LANES)

    def source(g, which):
        return span(g[2] + which * g[3], g[3], 128)

    def target(g):
        return span(g[5], g[3], 128)

    def sum_copy_0(g):
        src = r.wg.at[g[1], :, :, :, source(g, 1 - seq)]
        dst = r.r0.at[g[4], :, :, :, target(g)]
        return remote(src, dst, r.s_send.at[g[0]], r.s_recv.at[g[0], 0], sibling)

    def sum_copy_1(g, j):
        src = r.wg.at[g[1], :, plane_peer(j), :, source(g, seq)]
        dst = r.r1.at[g[4], j - 1, :, :, target(g)]
        return remote(src, dst, r.s_send.at[g[0]], r.s_recv.at[g[0], 1], on_plane(j))

    def sum_copy_2(g, j):
        src = r.wg.at[g[1], z_peer(j), p_at, :, source(g, seq)]
        dst = r.r2.at[g[4], j - 1, :, target(g)]
        return remote(src, dst, r.s_send.at[g[0]], r.s_recv.at[g[0], 2], on_chain(j))

    def sum_copy_3(g):
        src = r.fin.at[g[4], span((1 - seq) * own, own, 8), target(g)]
        dst = r.gsum.at[g[4], :, target(g)]
        return remote(src, dst, r.s_send.at[g[0]], r.s_recv.at[g[0], 3], sibling)

    def finish_all(g, level, at):
        pltpu.make_async_copy(at, at, r.s_send.at[g[0]]).wait()
        pltpu.make_async_copy(at, at, r.s_recv.at[g[0], level]).wait()

    def finish(copy):
        copy.wait_send()
        copy.wait_recv()

    def sum_0(g):
        if fused:
            sum_copy_0(g).start()

    def sum_1(g):
        if not fused:
            return
        finish(sum_copy_0(g))

        def add(i):
            at = (g[1], i // PLANE, i % PLANE, slice(None), source(g, seq))
            theirs = r.r0[g[4], i // PLANE, i % PLANE, :, target(g)]
            r.wg[at] = r.wg[at] + theirs

        loop(nz * PLANE, add, PLANE)
        for j in (3, 1, 2):
            sum_copy_1(g, j).start()

    def sum_2(g):
        if not fused:
            return
        finish_all(g, 1, r.r1.at[g[4], :, :, :, target(g)])

        def add(zi):
            at = (g[1], zi, p_at, slice(None), source(g, seq))
            value = r.wg[at].astype(F32)
            for j in range(PLANE - 1):
                value = value + r.r1[g[4], j, zi, :, target(g)].astype(F32)
            r.wg[at] = value.astype(BF)

        loop(nz, add, 2 if nz % 2 == 0 else 1)
        for j in range(1, nz):
            sum_copy_2(g, j).start()

    def sum_3(g):
        if not fused:
            return
        finish_all(g, 2, r.r2.at[g[4], :, :, target(g)])
        value = r.wg[g[1], z_at, p_at, :, source(g, seq)].astype(F32)
        for j in range(nz - 1):
            value = value + r.r2[g[4], j, :, target(g)].astype(F32)
        r.fin[g[4], :, target(g)] = value
        sum_copy_3(g).start()

    def sum_4(g):
        finish(sum_copy_3(g))

    def put_grad(g, low, value):
        size = value.shape[1]
        if fused:
            parts = value.astype(BF).reshape(nz, PLANE, slab, size)
            r.wg[g[1], :, :, :, span(g[2] + low, size, 128)] = parts
        else:
            first = g[4] * CHUNK + (g[2] if g[3] == 128 else 0)
            r.wgrad[:, span(first + low, size, 128)] = value.astype(BF)

    def shard_copy(c):
        size = GATHERS[c][1] // 2
        rows, cols = slice(c * own, (c + 1) * own), span((1 - seq) * size, size, 128)
        return pair_copy(1 if c else 4, r.gate.at[rows, cols], r.back.at[rows, cols])

    if fused:
        shard_copy(0).start()
        own_columns(r.gate, 1)[...] = r.in_weight[:, INNER : INNER + 512].astype(F32)
        own_columns(r.gate, 2)[...] = r.in_weight[:, INNER + 512 : INNER + 1024].astype(F32)
        own_columns(r.gate, 3)[...] = r.in_weight[:, INNER + 1024 : wide].astype(F32)
        own_columns(r.gate, 4)[...] = r.in_weight[:, 0:INNER].astype(F32)
        own_columns(r.gate, 5)[...] = r.out_weight[:, 0:1024].astype(F32)
        own_columns(r.gate, 6)[...] = r.out_weight[:, 1024:].astype(F32)
        for c in range(1, len(GATHERS)):
            shard_copy(c).start()

    def pick_heads():
        row, lane = iota((8 * LANES, LANES), 0), iota((8 * LANES, LANES), 1)
        pair, kind, second = row >> 9, (row >> 8) & 1, (row & 127) >> 6
        r.pick[...] = (lane == 2 * pair + second + 64 * kind).astype(F32).astype(BF)

    def make_spread(q):
        shape = (256, 256)
        head = (iota(shape, 1) + q * 256) >> 6
        r.spread[:, span(q * 256, 256)] = (head == (iota(shape, 0) & 127)).astype(F32).astype(BF)

    if fused:
        shard_copy(0).wait()
        gather_own(0)
        gather_0(0)
        gather_1(0)
        at = r.back.at[0 : own * (WIDE - GATHERS[0][1]) // 2 // 768, 0:768]
        for sem in (r.pair_send.at[1], r.pair_recv.at[1]):
            pltpu.make_async_copy(at, at, sem).wait()
        for c in range(1, len(GATHERS)):
            gather_own(c)
        gather_0(1)
        gather_1(1)
        gather_0(2)
        gather_1(6)

    r.convp[0:CONV, 0:CX] = r.conv_weight[:, INNER:]
    r.convp[0:CONV, CX:] = r.conv_weight[:, 0:INNER]
    bias = r.conv_bias[...].reshape(1, CONVCH)
    r.convp[4:5, 0:CX] = bias[:, INNER:]
    r.convp[4:5, CX:] = bias[:, 0:INNER]
    r.headp[...] = jnp.zeros_like(r.headp)
    for i, v in enumerate((r.dt_bias, r.a_log, r.skip_gain)):
        r.headp[i : i + 1, 0:HEADS] = v[...].reshape(1, HEADS)
    norm_gain = r.norm_gain[...].reshape(1, D)

    first_long = r.lengths[0, 0] > r.lengths[0, 1]
    shortest = jnp.minimum(r.lengths[0, 0], r.lengths[0, 1])
    for i in range(4):
        raw_copies[i].wait()

    def pick_rows(i):
        here = span(i * 64, 64)
        for to, k in ((r.tok, 0), (r.og, 2)):
            to[here, :] = jnp.where(first_long, raw[k][here, :], raw[k + 1][here, :])

    def pick_short(i):
        here, there = span(i * 64, 64), span(2 * GROUP + i * 64, 64)
        r.tok[there, :] = jnp.where(first_long, raw[1][here, :], raw[0][here, :])
        valid = (seq * part_rows + i * 64 + iota((64, D), 0) < shortest).astype(F32)
        picked = jnp.where(first_long, raw[3][here, :], raw[2][here, :])
        r.og[there, :] = (picked.astype(F32) * valid).astype(BF)

    loop(2 * GROUP // 64, pick_rows)
    edge_copy = pair_copy(0, r.tok.at[2 * GROUP - EDGE : 2 * GROUP, :], r.edge_in)
    edge_copy.start()
    if fused:
        gather_2(0)
        gather_1(2)
        gather_0(3)
    loop(GROUP // 64, pick_short)

    loop(QUADS, make_spread)
    pick_heads()
    r.innerp[0:1, :] = r.out_gain[...].reshape(1, INNER)
    r.innerp[1:2, :] = dot(side_by_side(r.headp[...]), r.spread[...])[2:3, :]
    tri_shape = (GROUP, GROUP)
    lower = (iota(tri_shape, 0) >= iota(tri_shape, 1)).astype(F32).astype(BF)
    upper = (iota(tri_shape, 0) <= iota(tri_shape, 1)).astype(F32).astype(BF)
    half = GROUP // 2
    causal = iota((half, half), 0) >= iota((half, half), 1)
    causal_t = iota((half, half), 0) <= iota((half, half), 1)
    first_head = iota((GROUP, LANES), 1) < HEADDIM
    rate = -jnp.exp(r.headp[1:2, :])

    r.g_norm[...] = jnp.zeros_like(r.g_norm)
    r.g_conv[...] = jnp.zeros_like(r.g_conv)
    r.g_head[...] = jnp.zeros_like(r.g_head)
    r.g_inner[...] = jnp.zeros_like(r.g_inner)
    r.halo[2] = jnp.zeros((8, CONVCH), F32)
    r.dproj[:, AT_DT + LANES : AT_X] = jnp.zeros((ROWS, AT_X - AT_DT - LANES), BF)

    def norm_of(v):
        root = lax.rsqrt(jnp.mean(v * v, axis=1, keepdims=True) + EPS)
        return (v * root * norm_gain).astype(BF)

    def norm_rows(i):
        rows = span(i * 64, 64)
        r.normed[rows, :] = norm_of(r.tok[rows, :].astype(F32))

    loop(ROWS // 64, norm_rows, 2)
    if fused:
        gather_3(0)
        gather_2(1)
    edge_copy.wait()
    r.normed[ROWS:, :] = norm_of(r.edge_in[...].astype(F32) * is_second)

    def turn(b):
        rows = rows_of(b)
        r.normed_t[:, rows] = r.normed[rows, :].T
        r.db_t[:, rows] = r.og[rows, :].T

    loop(BLOCKS, turn, BLOCKS)

    if fused:
        gather_4(0)
        gather_3(1)
        turned_2(6)
        gather_1(3)
        gather_0(4)
        gather_5(0)

    def conv_acc(values, before, cols):
        rows = values.shape[0]
        ext = jnp.concatenate([before, values], axis=0)
        shifted = [ext[5 + k : 5 + k + rows] for k in range(CONV)]
        acc = r.convp[4:5, cols]
        for k in range(CONV):
            acc = acc + r.convp[k : k + 1, cols] * shifted[k]
        return acc, shifted

    def project(at, to):
        low = dot(r.normed[...], w[:, at]).astype(BF)
        r.clow[:, to] = low
        r.halo[0, :, to] = low[ROWS : ROWS + EDGE].astype(F32)[EDGE - 8 :]
        r.halo[1, :, to] = low[GROUP - 16 : GROUP].astype(F32)[8:]

    def conv_forward(b, cols):
        rows = rows_of(b)
        acc, _ = conv_acc(r.clow[rows, cols].astype(F32), r.halo[b, :, cols], cols)
        r.cout[rows, cols] = (acc * sigmoid(acc)).astype(BF)

    project(pl.ds(0, CX), pl.ds(0, CX))
    r.dtb[...] = dot(r.normed[0:ROWS, :], w[:, AT_DT : AT_DT + LANES])

    def head_rows(b):
        z = r.dtb[rows_of(b), :] + r.headp[0:1, :]
        step = jnp.maximum(z, 0.0) + jnp.log1p(jnp.exp(-jnp.abs(z)))
        return z, step

    def prepare(b):
        rows = rows_of(b)
        conv_forward(b, pl.ds(0, LANES))
        conv_forward(b, pl.ds(LANES, LANES))
        z, step = head_rows(b)
        cum = exact_sum(lower, step * rate)
        moved = cum - jnp.log(jnp.maximum(step, 1e-37))
        r.cumb[rows, :] = cum
        r.moved[rows, :] = moved
        cum_t, moved_t = cum.T, moved.T
        for q in range(QUADS):
            r.cut[b, q, 0:4, :] = moved_t[4 * q : 4 * q + 4, :]
            r.cut[b, q, 4:8, :] = cum_t[4 * q : 4 * q + 4, :]
        r.weight[rows, :] = side_by_side(jnp.exp(cum[GROUP - 1 : GROUP, :] - cum) * step)
        r.fade[rows, :] = side_by_side(jnp.exp(cum))
        key, query = r.cout[rows, 0:NSTATE], r.cout[rows, NSTATE:CX]
        r.turned[b, 0:NSTATE, :] = key.T
        r.turned[b, NSTATE:CX, :] = query.T
        r.sco[b] = dot_nt(query, key)

    loop(BLOCKS, prepare, BLOCKS)
    if fused:
        gather_2(2)
        gather_4(1)
        gather_2(3)
        gather_1(4)
        gather_0(5)
        gather_5(1)

    gather_steps = {
        (0, -1): ((gather_3, 2),), (1, -1): ((gather_4, 2), (gather_3, 3), (gather_1, 5)),
        (2, -1): ((gather_5, 2), (gather_4, 3), (gather_2, 4)),
        (3, -1): ((gather_2, 5), (turned_3, 6)), (4, -1): ((gather_5, 3), (gather_3, 4)),
        (5, -1): ((gather_3, 5),),
    }

    def gather_on(q, b):
        for at, steps in gather_steps.items():
            if fused and at[1] == b:

                @pl.when(q == at[0])
                def _():
                    for step, c in steps:
                        step(c)

    def to_first(v, q):
        return pltpu.roll(v, (LANES - 4 * q) % LANES, 1)

    def forward_block(b, q):
        rows = rows_of(b)
        cols = span(CX + q * 256, 256)
        heads = span(q * 256, 256)
        for i in range(2):
            conv_forward(b, span(CX + q * 256 + i * LANES, LANES))
        xq = r.cout[rows, cols]

        if b < 2:
            spread_w = dot(r.weight[rows, :], r.spread[:, heads])
            scaled = (xq.astype(F32) * spread_w).astype(BF)
            r.runs[b, :, heads] = dot(r.turned[b, 0:NSTATE, :], scaled)

        near = to_first(r.cumb[rows, :], q)
        skip = r.innerp[1:2, heads]
        for j in range(2):
            lanes = slice(j * LANES, (j + 1) * LANES)
            xp = xq[:, lanes]
            zero = jnp.zeros_like(xp)
            x_ab = (jnp.where(first_head, xp, zero), jnp.where(first_head, zero, xp))
            top, bottom = [], []
            for e in range(2):
                h = 2 * j + e
                col_top, col_bottom = near[:half, h : h + 1], near[half:, h : h + 1]
                row = r.cut[b, q, h : h + 1, :]
                row_left, row_right = row[:, :half], row[:, half:]
                gap = jnp.where(causal, col_top - row_left, -1e30)
                top.append((r.sco[b, :half, :half] * jnp.exp(gap)).astype(BF))
                fade = jnp.exp(col_bottom - row_left)
                bottom.append((r.sco[b, half:, :half] * fade).astype(BF))
                gap = jnp.where(causal, col_bottom - row_right, -1e30)
                bottom.append((r.sco[b, half:, half:] * jnp.exp(gap)).astype(BF))
            out_top = dot(
                jnp.concatenate(top, axis=1), jnp.concatenate([v[:half] for v in x_ab], axis=0)
            )
            out_bottom = dot(jnp.concatenate(bottom, axis=1), jnp.concatenate(x_ab, axis=0))
            place = span(q * 256 + j * LANES, LANES)
            xf = xp.astype(F32) * skip[:, lanes]
            r.ssd[span(b * GROUP, half), place] = out_top + xf[:half]
            r.ssd[span(b * GROUP + half, half), place] = out_bottom + xf[half:]

    def forward_quad(q):
        gather_on(q, -1)
        project(span(AT_X + q * 256, 256), span(CX + q * 256, 256))
        for b in range(BLOCKS):
            gather_on(q, b)
            forward_block(b, q)

    loop(QUADS, forward_quad)

    def decay_of(b):
        last = r.cumb[b * GROUP + GROUP - 8 : (b + 1) * GROUP, :]
        return dot(side_by_side(jnp.exp(last)), r.spread[...])[7:8, :]

    decay_0, decay_1 = decay_of(0), decay_of(1)
    r.runs[1] = r.runs[1] + decay_1 * r.runs[0]
    state_copy = pair_copy(2, r.runs.at[1], r.state_in)
    state_copy.start()
    if fused:
        gather_4(4)
        turned_4(6)

    def carry_block(b):
        rows = rows_of(b)
        query = r.cout[rows, NSTATE:CX]

        def quad(q):
            cols = span(q * 256, 256)
            r.ssd[rows, cols] += dot(query, r.held[b, :, cols]) * dot(
                r.fade[rows, :], r.spread[:, cols]
            )

        loop(QUADS, quad, 3)

    gain = r.innerp[0:1, :]

    def gate_project(q):
        at = span(AT_GATE + q * 256, 256)
        high, low = halves(dot(r.normed[0:ROWS, :], w[:, at]))
        r.dssd[:, span(q * 256, 256)] = high
        r.dproj[:, at] = low

    def out_back(b):
        rows = rows_of(b)

        def quad(q):
            cols = span(q * 256, 256)
            r.back[:, cols] = dot(r.og[rows, :], w[:, span(AT_OUT + q * 256, 256)])

        loop(QUADS, quad, 3)

    def gated_tile(here, k):
        cols = slice(k * 256, (k + 1) * 256)
        low = r.dproj[here, AT_GATE + k * 256 : AT_GATE + (k + 1) * 256]
        g = r.dssd[here, cols].astype(F32) + low.astype(F32)
        s = r.ssd[here, cols]
        sg = sigmoid(g)
        return cols, g, s, sg

    def row_mean(v):
        return jnp.sum(v, axis=1, keepdims=True) * (1.0 / INNER)

    def gate_forward(i):
        here = span(i * 32, 32)
        square = 0.0
        for k in range(QUADS):
            cols, g, s, sg = gated_tile(here, k)
            gated = s * (g * sg)
            square = square + gated * gated
            r.gate[0:32, cols] = gated
        root = lax.rsqrt(row_mean(square) + EPS)
        for k in range(QUADS):
            cols = slice(k * 256, (k + 1) * 256)
            to = slice(AT_X + k * 256, AT_X + (k + 1) * 256)
            r.dproj[here, to] = (r.gate[0:32, cols] * root * gain[:, cols]).astype(BF)

    def gate_block(b):
        def gate_rows(i):
            here = span(b * GROUP + i * 32, 32)
            local = span(i * 32, 32)
            square, mixed = 0.0, 0.0
            for k in range(QUADS):
                cols, g, s, sg = gated_tile(here, k)
                silu = g * sg
                gated = s * silu
                square = square + gated * gated
                mixed = mixed + gated * (gain[:, cols] * r.back[local, cols])
                r.gate[0:32, cols] = gated
                r.gate[32:64, cols] = silu
                r.gate[64:96, cols] = s * silu_slope(g, sg)
            root = lax.rsqrt(row_mean(square) + EPS)
            lean = root * row_mean(mixed)
            for k in range(QUADS):
                cols = slice(k * 256, (k + 1) * 256)
                d_out = r.back[local, cols]
                v = r.gate[0:32, cols] * root
                r.g_inner[0:8, cols] += fold(d_out * v)
                d_gated = root * (gain[:, cols] * d_out - v * lean)
                d_s = (d_gated * r.gate[32:64, cols]).astype(BF)
                r.dssd[here, cols] = d_s
                x = r.cout[here, CX + k * 256 : CX + (k + 1) * 256]
                r.g_inner[8:16, cols] += fold(d_s.astype(F32) * x.astype(F32))
                to = slice(AT_GATE + k * 256, AT_GATE + (k + 1) * 256)
                r.dproj[here, to] = (d_gated * r.gate[64:96, cols]).astype(BF)

        loop(GROUP // 32, gate_rows)

    state_copy.wait()
    r.state_in[...] = r.state_in[...] * is_second
    r.held[0] = r.state_in[...].astype(BF)
    r.runs[0] = r.runs[0] + decay_0 * r.state_in[...]
    r.held[1] = r.runs[0].astype(BF)
    r.runs[1] = r.state_in[...]

    @pl.when(seq > 0)
    def _():
        carry_block(0)

    carry_block(1)

    def add_norm(value, cols):
        product = value * w[:, cols].astype(F32)
        for k in range(value.shape[1] // LANES):
            r.g_norm[...] += product[:, k * LANES : (k + 1) * LANES]

    def wide_grad(i):
        g = wide_chunk(i)
        left = r.db_t if i < 2 else r.normed_t
        first = (AT_X if i < 2 else AT_GATE) + (i % 2) * CHUNK

        def tile(k):
            value = dot(left[...], r.dproj[:, span(first + k * 256, 256)])
            put_grad(g, k * 256, value)
            if i >= 2:
                add_norm(value, span(first + k * 256, 256))

        loop(CHUNK // 256, tile, 3)
        sum_0(g)

    if fused:
        gather_4(5)
        gather_5(4)
    loop(QUADS, gate_project, 2)
    loop(ROWS // 32, gate_forward)
    wide_grad(0)
    wide_grad(1)
    if fused:
        gather_5(5)
        gather_5(6)
    for b in range(2):
        out_back(b)
        gate_block(b)
        sum_1(wide_chunk(b))

    @pl.when(seq == 0)
    def _():
        out_back(2)
        gate_block(2)

    @pl.when(seq > 0)
    def _():
        r.dssd[2 * GROUP :, :] = jnp.zeros((GROUP, INNER), BF)
        r.dproj[2 * GROUP :, AT_GATE:AT_OUT] = jnp.zeros((GROUP, INNER), BF)

    wide_grad(2)
    wide_grad(3)
    sum_2(wide_chunk(0))

    def state_back(b):
        rows = rows_of(b)

        r.dqb[rows, :] = jnp.zeros((GROUP, NSTATE), F32)

        def quads(i):
            dq = 0.0
            for q in (3 * i, 3 * i + 1, 3 * i + 2):
                cols = heads_of(q)
                spread_f = dot(r.fade[rows, :], r.spread[:, cols])
                dz = (spread_f * r.dssd[rows, cols].astype(F32)).astype(BF)
                r.dheld[b, :, cols] = dot(r.turned[b, NSTATE:CX, :], dz)
                dq = dq + dot_nt(dz, r.held[b, :, cols])
            r.dqb[rows, :] += dq

        loop(QUADS // 3, quads)

    def no_state():
        r.dheld[0] = jnp.zeros((NSTATE, INNER), F32)

    r.dqb[0:GROUP, :] = jnp.zeros((GROUP, NSTATE), F32)
    pl.when(seq > 0)(lambda: state_back(0))
    pl.when(seq == 0)(no_state)
    state_back(1)
    r.dqb[2 * GROUP :, :] = jnp.zeros((GROUP, NSTATE), F32)
    r.dheld[0] = r.dheld[0] + decay_0 * r.dheld[1]
    dstate_copy = pair_copy(3, r.dheld.at[0], r.dstate_in)
    dstate_copy.start()
    sum_1(wide_chunk(2))

    def out_block(b):
        rows = rows_of(b)
        branch = dot_nt(r.dproj[rows, AT_X:AT_GATE], w[:, AT_OUT:])
        r.normed[rows, :] = (r.tok[rows, :].astype(F32) + branch).astype(BF)

    loop(BLOCKS, out_block)
    mixed_copy = pltpu.make_async_copy(r.normed.at[0:ROWS, :], r.mixed, r.local.at[0])
    mixed_copy.start()
    sum_1(wide_chunk(3))
    sum_2(wide_chunk(1))
    sum_3(wide_chunk(0))

    def ds_of(b):
        return r.back.at[:, heads_of(b)]

    def give_of(b):
        return r.back.at[:, span(CHUNK + b * LANES, LANES)]

    def kept_of(b):
        return r.back.at[:, span(CHUNK + (BLOCKS + b) * LANES, LANES)]

    def prepare_back(b):
        rows = rows_of(b)
        r.sco[b] = dot_nt(r.cout[rows, 0:NSTATE], r.cout[rows, NSTATE:CX])
        ds_of(b)[...] = jnp.zeros((GROUP, GROUP), F32)
        nothing = jnp.zeros((GROUP, LANES), F32)
        r.dkb[rows, :] = nothing
        give_of(b)[...] = nothing

    loop(BLOCKS, prepare_back)
    dstate_copy.wait()
    r.dstate_in[...] = r.dstate_in[...] * is_first
    r.held[1] = r.dstate_in[...].astype(BF)
    r.state_in[...] = r.dheld[1] + decay_1 * r.dstate_in[...]
    r.held[0] = r.state_in[...].astype(BF)

    def backward_block(b, q):
        rows = rows_of(b)
        heads = span(q * 256, 256)
        xq = r.cout[rows, span(CX + q * 256, 256)]
        dq4 = r.dssd[rows, heads]
        skip = r.innerp[1:2, heads]
        dx, ds = r.gate.at[:, heads_of(b)], ds_of(b)

        if b < 2:
            spread_w = dot(r.weight[rows, :], r.spread[:, heads])
            d_states = r.held[b, :, heads]
            dx_state = spread_w * dot(r.cout[rows, 0:NSTATE], d_states)
            r.flow[b, 0:8, heads] = fold(xq.astype(F32) * dx_state)
            r.dkb[rows, :] += dot_nt((xq.astype(F32) * spread_w).astype(BF), d_states)

        near = to_first(r.moved[rows, :], q)
        products = []
        for j in range(2):
            lanes = slice(j * LANES, (j + 1) * LANES)
            xp, dp = xq[:, lanes], dq4[:, lanes]
            zero = jnp.zeros_like(xp)
            d_ab = (jnp.where(first_head, dp, zero), jnp.where(first_head, zero, dp))
            top, bottom = [], []
            for e in range(2):
                h = 2 * j + e
                dm_top = dot_nt(xp[:half], d_ab[e])
                dm_bottom = dot_nt(xp[half:], d_ab[e][half:])
                col_top, col_bottom = near[:half, h : h + 1], near[half:, h : h + 1]
                row = r.cut[b, q, 4 + h : 5 + h, :]
                row_left, row_right = row[:, :half], row[:, half:]
                fade = jnp.exp(jnp.where(causal_t, row_left - col_top, -1e30))
                ds[:half, :half] += dm_top[:, :half] * fade
                top.append((r.sco[b, :half, :half] * fade).astype(BF))
                fade = jnp.exp(row_right - col_top)
                ds[:half, half:] += dm_top[:, half:] * fade
                top.append((r.sco[b, :half, half:] * fade).astype(BF))
                fade = jnp.exp(jnp.where(causal_t, row_right - col_bottom, -1e30))
                ds[half:, half:] += dm_bottom * fade
                bottom.append((r.sco[b, half:, half:] * fade).astype(BF))
            dx_top = dot(jnp.concatenate(top, axis=1), jnp.concatenate(d_ab, axis=0))
            dx_bottom = dot(
                jnp.concatenate(bottom, axis=1), jnp.concatenate([v[half:] for v in d_ab], axis=0)
            )
            dxp = jnp.concatenate([dx_top, dx_bottom], axis=0)
            if b < 2:
                dxp = dxp + dx_state[:, lanes]
            xf, df = xp.astype(F32), dp.astype(F32)
            kept = skip[:, lanes]
            ssd = r.ssd[rows, span(q * 256 + j * LANES, LANES)]
            products += [*halves(xf * dxp), *halves(df * (ssd - kept * xf))]
            dx[:, lanes] = dxp + kept * df
        sums = dot(jnp.concatenate(products, axis=1), r.pick[...])
        give_of(b)[...] += pltpu.roll(sums, 4 * q, 1)

    def edge_grad(b, source, cols):
        first = r.clow[b * GROUP : b * GROUP + 16, cols].astype(F32)
        acc, _ = conv_acc(first, r.halo[b, :, cols], cols)
        d_acc = r.gate[0:16, span(b * 256 + source, LANES)] * silu_slope(acc, sigmoid(acc))
        r.halo_next[b, :, cols] = d_acc[0:8]

    def conv_back(b, source, cols, to, after):
        rows = rows_of(b)
        acc, shifted = conv_acc(r.clow[rows, cols].astype(F32), r.halo[b, :, cols], cols)
        d_acc = r.gate[:, span(b * 256 + source, LANES)] * silu_slope(acc, sigmoid(acc))
        for k in range(CONV):
            r.g_conv[8 * k : 8 * k + 8, cols] += fold(d_acc * shifted[k])
        r.g_conv[32:40, cols] += fold(d_acc)
        ext = jnp.concatenate([d_acc, after], axis=0)
        d_in = r.convp[3:4, cols] * d_acc
        for k in range(CONV - 1):
            d_in = d_in + r.convp[k : k + 1, cols] * ext[3 - k : 3 - k + GROUP]
        r.dproj[rows, to] = d_in.astype(BF)

    def edge_copy_back(i, cols):
        src, dst = r.halo_next.at[0, :, cols], r.dedge_in.at[:, cols]
        return remote(src, dst, r.edge_send.at[i], r.edge_recv.at[i], sibling)

    def first_edge(i, at):
        for k in range(2):
            edge_grad(0, k * LANES, span(at + k * LANES, LANES))
        edge_copy_back(i, span(at, 256)).start()

    def conv_back_all(i, at, to):
        cols = span(at, 256)

        def chunk(k):
            return k * LANES, span(at + k * LANES, LANES), span(to + k * LANES, LANES)

        for k in range(2):
            edge_grad(1, *chunk(k)[:2])
        for k in range(2):
            conv_back(2, *chunk(k), jnp.zeros((8, LANES), F32))
            conv_back(0, *chunk(k), r.halo_next[1, :, chunk(k)[1]])
        edge_copy_back(i, cols).wait()
        for k in range(2):
            conv_back(1, *chunk(k), r.dedge_in[:, chunk(k)[1]] * is_first)

    def backward_quad(q):
        @pl.when(q == 1)
        def _():
            sum_2(wide_chunk(2))

        @pl.when(q == 2)
        def _():
            sum_3(wide_chunk(2))

        @pl.when(q == 3)
        def _():
            sum_2(wide_chunk(3))

        @pl.when(q == 4)
        def _():
            sum_3(wide_chunk(3))

        for b in range(BLOCKS):
            backward_block(b, q)
            if b == 0:
                first_edge(q, CX + q * 256)

        @pl.when(q == 0)
        def _():
            sum_3(wide_chunk(1))

        @pl.when(q >= 1)
        def _():
            sum_1(quad_chunk(q - 1))

        @pl.when(q >= 2)
        def _():
            sum_2(quad_chunk(q - 2))

        @pl.when(q >= 3)
        def _():
            sum_3(quad_chunk(q - 3))

        conv_back_all(q, CX + q * 256, AT_X + q * 256)
        g = quad_chunk(q)
        value = dot(r.normed_t[...], r.dproj[:, span(AT_X + q * 256, 256)])
        put_grad(g, 0, value)
        sum_0(g)
        add_norm(value, span(AT_X + q * 256, 256))

    loop(QUADS, backward_quad)

    def ratio_of(b):
        z, step = head_rows(b)
        return jnp.where(z < -15.0, 1.0, sigmoid(z) / jnp.maximum(step, 1e-37))

    def backward_rest(b):
        rows = rows_of(b)
        key, query = r.cout[rows, 0:NSTATE], r.cout[rows, NSTATE:CX]
        d_scores = ds_of(b)[...].astype(BF)
        r.gate[:, span(b * 256, NSTATE, 128)] = r.dkb[rows, :] + dot(d_scores, query)
        r.gate[:, span(b * 256 + NSTATE, NSTATE, 128)] = r.dqb[rows, :] + dot(d_scores.T, key)
        both_sums = give_of(b)[...]
        in_low = iota((GROUP, LANES), 1) < HEADS
        give = jnp.where(in_low, both_sums, 0.0)
        take = jnp.where(in_low, pltpu.roll(both_sums, 64, 1), 0.0)
        kept_of(b)[...] = give * ratio_of(b)
        give_of(b)[...] = exact_sum(upper, take - give)

    loop(BLOCKS, backward_rest, BLOCKS)

    def block_total(b, run, grad, decay):
        kept = jnp.sum(run[...] * grad[...], axis=0, keepdims=True)
        summed = jnp.sum(r.flow[b], axis=0, keepdims=True) + decay * kept
        high, low = halves(jnp.broadcast_to(summed, (8, INNER)))
        by_head = dot_nt(high, r.spread[0:LANES, :]) + dot_nt(low, r.spread[0:LANES, :])
        rows = rows_of(b)
        give_of(b)[...] = give_of(b)[...] + by_head[0:1, :]

    block_total(0, r.runs.at[1], r.state_in, decay_0)
    block_total(1, r.runs.at[0], r.dstate_in, decay_1)

    def step_grad(b):
        rows = rows_of(b)
        z, step = head_rows(b)
        back_sum = give_of(b)[...]
        d_pre = kept_of(b)[...] + rate * back_sum * sigmoid(z)
        r.g_head[0:8, :] += fold(d_pre)
        r.g_head[8:16, :] += fold(back_sum * (step * rate))
        r.dproj[rows, AT_DT : AT_DT + LANES] = d_pre.astype(BF)

    loop(BLOCKS, step_grad, BLOCKS)
    sum_1(quad_chunk(5))
    first_edge(QUADS, 0)
    value = dot(r.normed_t[...], r.dproj[:, AT_DT:AT_X])
    put_grad(step_chunk, 0, value)
    sum_0(step_chunk)
    add_norm(value, slice(AT_DT, AT_X))
    conv_back_all(QUADS, 0, 0)
    value = dot(r.normed_t[...], r.dproj[:, 0:CX])
    put_grad(last_chunk, 0, value)
    sum_0(last_chunk)
    sum_1(step_chunk)
    add_norm(value, slice(0, CX))

    def total(v):
        return jnp.sum(v, axis=0, keepdims=True)

    for k in range(CONV + 1):
        r.small[0, k : k + 1, :] = total(r.g_conv[8 * k : 8 * k + 8, :])
    r.small[0, 5:6, 0:INNER] = total(r.g_inner[0:8, :])
    r.small[0, 5:6, INNER : INNER + LANES] = total(r.g_head[0:8, :])
    r.small[0, 5:6, INNER + LANES :] = total(r.g_head[8:16, :])
    high, low = halves(r.g_inner[8:16, :])
    skips = dot_nt(high, r.spread[0:LANES, :]) + dot_nt(low, r.spread[0:LANES, :])
    r.small[0, 6:7, 0:LANES] = total(skips)
    r.small[0, 6:7, LANES:] = jnp.zeros((1, CONVCH - LANES), F32)
    r.small[0, 7:8, 0:D] = total(r.g_norm[...].T) / norm_gain
    r.small[0, 7:8, D:] = jnp.zeros((1, CONVCH - D), F32)
    if fused:

        def send_small(level, first, count, device):
            for j in range(count):
                sems = r.t_send.at[level], r.t_recv.at[level]
                dst = r.small_in.at[first + j]
                remote(r.small.at[level], dst, *sems, device(j + 1)).start()

        def add_small(level, first, count):
            at = r.small_in.at[first : first + count]
            for sem in (r.t_send.at[level], r.t_recv.at[level]):
                pltpu.make_async_copy(at, at, sem).wait()
            value = r.small[level]
            for j in range(count):
                value = value + r.small_in[first + j]
            return value

        send_small(0, 0, 1, lambda j: sibling)

    def in_block(b):
        rows = rows_of(b)
        r.ssd[rows, 0:D] = dot_nt(r.dproj[rows, :], w[:, 0:AT_OUT])

    sum_1(last_chunk)
    sum_2(quad_chunk(4))
    sum_3(quad_chunk(3))
    in_block(2)
    if fused:
        r.small[1] = add_small(0, 0, 1)
        send_small(1, 1, PLANE - 1, on_plane)
    sum_2(quad_chunk(5))
    sum_2(step_chunk)
    sum_3(quad_chunk(4))
    in_block(0)
    sum_2(last_chunk)
    if fused:
        r.small[2] = add_small(1, 1, PLANE - 1)
        send_small(2, PLANE, nz - 1, on_chain)
    in_block(1)
    sum_3(quad_chunk(5))
    sum_3(step_chunk)

    def norm_back(i):
        rows = span(i * 32, 32)
        v = r.tok[rows, :].astype(F32)
        root = lax.rsqrt(jnp.mean(v * v, axis=1, keepdims=True) + EPS)
        y = v * root
        dn = r.ssd[rows, 0:D]
        bb = norm_gain * dn
        d_v = root * (bb - y * jnp.mean(y * bb, axis=1, keepdims=True))
        r.ssd[rows, 0:D] = r.og[rows, :].astype(F32) + d_v

    loop(ROWS // 32, norm_back, 3)
    tgrad_copy = pltpu.make_async_copy(r.ssd.at[:, 0:D], r.tgrad, r.local.at[1])
    tgrad_copy.start()

    if fused:
        sum_3(last_chunk)

        def hand_out(g, dst, first, count):
            sum_4(g)
            mine = r.fin[g[4], span(seq * own, own, 8), target(g)]
            theirs = r.gsum[g[4], :, target(g)]
            for half_at in range(2):
                value = jnp.where(seq == half_at, mine, theirs)
                size = min(g[3], count - half_at * g[3])
                at = first + half_at * g[3]
                if size > 0:
                    dst[:, at : at + size] = value[:, 0:size]

        for i in range(WIDE_CHUNKS):
            dst = r.grad_out if i < 2 else r.grad_in
            hand_out(wide_chunk(i), dst, (i % 2) * CHUNK, CHUNK)
        for q in range(QUADS):
            hand_out(quad_chunk(q), r.grad_in, INNER + q * 256, 256)
        hand_out(step_chunk, r.grad_in, 2 * INNER + CX, HEADS)
        hand_out(last_chunk, r.grad_in, 2 * INNER, CX)
        r.small_out[...] = add_small(2, PLANE, nz - 1)
        for c in range(len(GATHERS)):
            gather_end(c)
    else:
        r.small_out[...] = r.small[0]
    mixed_copy.wait()
    tgrad_copy.wait()


def call_mixer(fused, nz, arrays):
    vmem = pl.BlockSpec(memory_space=pltpu.VMEM)
    hbm = pl.BlockSpec(memory_space=pl.ANY)
    places = {"lengths": pl.BlockSpec(memory_space=pltpu.SMEM), "tokens": hbm, "out_grad": hbm}
    own = D // (2 * nz * PLANE) if fused else 0
    ins = list(arrays)
    outs = {"mixed": ((ROWS, D), BF), "tgrad": ((ROWS, D), F32), "small_out": ((8, CONVCH), F32)}
    scratch = {
        "tok": ((ROWS, D), BF), "og": ((ROWS, D), BF), "convp": ((8, CONVCH), F32),
        "headp": ((8, LANES), F32), "innerp": ((8, INNER), F32),
        "normed": ((ROWS + EDGE, D), BF), "normed_t": ((D, ROWS), BF), "db_t": ((D, ROWS), BF),
        "clow": ((ROWS + EDGE, CONVCH), BF), "cout": ((ROWS, CONVCH), BF),
        "gate": ((GROUP, INNER), F32), "back": ((GROUP, INNER), F32), "ssd": ((ROWS, INNER), F32),
        "dssd": ((ROWS, INNER), BF), "dproj": ((ROWS, AT_OUT), BF),
        "dtb": ((ROWS, LANES), F32), "cumb": ((ROWS, LANES), F32), "moved": ((ROWS, LANES), F32),
        "weight": ((ROWS, 256), BF), "fade": ((ROWS, 256), BF),
        "pick": ((8 * LANES, LANES), BF),
        "cut": ((BLOCKS, QUADS, 8, GROUP), F32), "spread": ((256, INNER), BF),
        "turned": ((BLOCKS, CX, GROUP), BF), "sco": ((BLOCKS, GROUP, GROUP), F32), "dkb": ((ROWS, LANES), F32), "dqb": ((ROWS, LANES), F32),
        "runs": ((2, NSTATE, INNER), F32), "held": ((2, NSTATE, INNER), BF),
        "dheld": ((2, NSTATE, INNER), F32),
        "flow": ((2, 8, INNER), F32), "halo": ((BLOCKS, 8, CONVCH), F32),
        "halo_next": ((2, 8, CONVCH), F32), "edge_in": ((EDGE, D), BF),
        "state_in": ((NSTATE, INNER), F32), "dstate_in": ((NSTATE, INNER), F32),
        "dedge_in": ((8, CONVCH), F32), "g_norm": ((D, LANES), F32), "g_conv": ((40, CONVCH), F32),
        "g_head": ((16, LANES), F32), "g_inner": ((16, INNER), F32), "small": ((3, 8, CONVCH), F32),
    }
    dma = pltpu.SemaphoreType.DMA
    sems = {
        "pair_send": dma((5,)), "pair_recv": dma((5,)), "edge_send": dma((QUADS + 1,)),
        "edge_recv": dma((QUADS + 1,)), "local": dma((6,)),
    }
    if fused:
        part = CHUNK // 2
        outs |= {"grad_in": ((own, PROJ), F32), "grad_out": ((own, INNER), F32)}
        scratch |= {
            "w": ((D, WIDE), BF),
            "wg": ((SLOTS, nz, PLANE, 2 * own, CHUNK), BF),
            "r0": ((UNITS, nz, PLANE, 2 * own, part), BF),
            "r1": ((UNITS, PLANE - 1, nz, 2 * own, part), BF),
            "r2": ((UNITS, nz - 1, 2 * own, part), BF), "fin": ((UNITS, 2 * own, part), F32),
            "gsum": ((UNITS, own, part), F32), "small_in": ((PLANE + nz - 1, 8, CONVCH), F32),
        }
        sems |= {
            "g_send": dma((len(GATHERS), 2)), "g_recv": dma((len(GATHERS), 4)),
            "s_send": dma((CHUNKS,)), "s_recv": dma((CHUNKS, 4)),
            "t_send": dma((3,)), "t_recv": dma((3,)),
        }
    else:
        outs["wgrad"] = ((D, WIDE), BF)
    names = ins + list(outs) + list(scratch) + list(sems)
    return pl.pallas_call(
        functools.partial(mixer, names, fused, nz),
        out_shape=[jax.ShapeDtypeStruct(s, t) for s, t in outs.values()],
        in_specs=[places.get(name, vmem) for name in ins],
        out_specs=[hbm, hbm] + [vmem] * (len(outs) - 2),
        scratch_shapes=[pltpu.VMEM(s, t) for s, t in scratch.values()] + list(sems.values()),
        compiler_params=pltpu.CompilerParams(
            collective_id=0, has_side_effects=True, vmem_limit_bytes=63 * 1024 * 1024
        ),
        name="mixer",
    )(*arrays.values())


def place_results(
    lengths, mixed, tgrad, small, grad_in, grad_out, mixed_at, tgrad_at, norm, in_at, conv, bias,
    step, rates, skip, gain, out_at, blank, blank_low, sems,
):
    seq = lax.axis_index("seq")
    long = jnp.where(lengths[0, 0] > lengths[0, 1], 0, 1)
    rows = mixed_at.shape[2]
    copies = []
    for i, (src, dst, zero) in enumerate(((tgrad, tgrad_at, blank), (mixed, mixed_at, blank_low))):
        first, after = dst.at[1 - long, 0, 0:GROUP, :], dst.at[1 - long, 0, GROUP:rows, :]
        whole = pltpu.make_async_copy(src.at[0:rows, :], dst.at[long, 0], sems.at[3 * i])
        used = pltpu.make_async_copy(src.at[rows : rows + GROUP, :], first, sems.at[3 * i + 1])
        unused = pltpu.make_async_copy(zero.at[0:GROUP, :], first, sems.at[3 * i + 1])
        end = pltpu.make_async_copy(zero.at[0 : rows - GROUP, :], after, sems.at[3 * i + 2])
        whole.start()
        pl.when(seq == 0)(used.start)
        zero[...] = jnp.zeros_like(zero)
        pl.when(seq > 0)(unused.start)
        end.start()
        copies += [whole, used, end]
    in_at[...] = grad_in[...]
    out_at[...] = grad_out[...]
    conv[:, 0:INNER] = small[0:CONV, CX:]
    conv[:, INNER:] = small[0:CONV, 0:CX]
    bias[...] = jnp.concatenate([small[4:5, CX:], small[4:5, 0:CX]], axis=1).reshape(CONVCH)
    gain[...] = small[5:6, 0:INNER].reshape(INNER)
    step[...] = small[5:6, INNER : INNER + HEADS].reshape(HEADS)
    rates[...] = small[5:6, INNER + LANES : INNER + LANES + HEADS].reshape(HEADS)
    skip[...] = small[6:7, 0:HEADS].reshape(HEADS)
    norm[...] = small[7:8, 0:D].reshape(D)
    for c in copies:
        c.wait()


def call_place(shape, lengths, *arrays):
    vmem = pl.BlockSpec(memory_space=pltpu.VMEM)
    hbm = pl.BlockSpec(memory_space=pl.ANY)
    own = arrays[3].shape[0]
    outs = (
        (shape, BF), (shape, F32), ((D,), F32), ((own, PROJ), F32), ((CONV, CONVCH), F32),
        ((CONVCH,), F32), ((HEADS,), F32), ((HEADS,), F32), ((HEADS,), F32), ((INNER,), F32),
        ((own, INNER), F32),
    )
    rest = max(shape[2] - GROUP, GROUP)
    results = pl.pallas_call(
        place_results,
        out_shape=[jax.ShapeDtypeStruct(s, t) for s, t in outs],
        in_specs=[pl.BlockSpec(memory_space=pltpu.SMEM)] + [vmem] * len(arrays),
        out_specs=[hbm, hbm] + [vmem] * (len(outs) - 2),
        scratch_shapes=[
            pltpu.VMEM((rest, D), F32), pltpu.VMEM((rest, D), BF), pltpu.SemaphoreType.DMA((6,)),
        ],
        name="place_results",
    )(lengths, *arrays)
    return (*results[:-1], results[-1].T)


def shards(
    tokens, lengths, norm_gain, in_weight, conv_weight, conv_bias, dt_bias, a_log, skip_gain,
    out_gain, out_weight, out_grad,
):
    both = ("fsdp", "seq")
    own = in_weight.shape[0]
    nf = lax.axis_size("fsdp")
    fused = nf % PLANE == 0 and (2 * own) % 16 == 0 and own % 8 == 0
    nz = nf // PLANE if fused else 1
    arrays = {
        "lengths": lengths.T, "tokens": tokens, "out_grad": out_grad, "norm_gain": norm_gain,
        "conv_weight": conv_weight, "conv_bias": conv_bias, "dt_bias": dt_bias, "a_log": a_log,
        "skip_gain": skip_gain, "out_gain": out_gain,
    }
    if fused:
        arrays |= {"in_weight": in_weight, "out_weight": out_weight.T}
        mixed, tgrad, small, grad_in, grad_out = call_mixer(fused, nz, arrays)
    else:
        fill = jnp.zeros((own, AT_X - CX - HEADS), BF)
        sent = jnp.concatenate(
            [in_weight[:, 2 * INNER :], fill, in_weight[:, INNER : 2 * INNER],
             in_weight[:, :INNER], out_weight.T], axis=1)
        arrays["w"] = lax.all_gather(sent, both, axis=0, tiled=True)
        mixed, tgrad, small, wgrad = call_mixer(fused, nz, arrays)
        summed = lax.psum_scatter(wgrad, both, scatter_dimension=0, tiled=True).astype(F32)
        grad_out = summed[:, :INNER]
        grad_in = jnp.concatenate(
            [summed[:, INNER : 3 * INNER], summed[:, 3 * INNER : 3 * INNER + CX + HEADS]], axis=1
        )
        small = lax.psum(small, both)
    return call_place(tokens.shape, lengths.T, mixed, tgrad, small, grad_in, grad_out)


def solution(mesh):
    spread = P(None, "fsdp", "seq", None)
    both = ("fsdp", "seq")
    return jax.shard_map(
        shards,
        mesh=mesh,
        in_specs=(
            spread, P(None, "fsdp"), P(), P(both, None), P(), P(), P(), P(), P(), P(),
            P(None, both), spread,
        ),
        out_specs=(
            spread, spread, P(), P(both, None), P(), P(), P(), P(), P(), P(), P(None, both),
        ),
        check_vma=False,
    )
```

```python
import functools
import types

import jax
import jax.numpy as jnp
from jax import lax
from jax.experimental import pallas as pl
from jax.experimental.pallas import tpu as pltpu
from jax.sharding import PartitionSpec as P

D = 768
HEADS = 24
HEADDIM = 64
NSTATE = 128
CONV = 4
GROUP = 256
INNER = 1536
CONVCH = 1792
PROJ = 3352
EPS = 1e-05

BLOCKS = 3
ROWS = BLOCKS * GROUP
EDGE = 16
LANES = 128
QUADS = INNER // 256
AT_DT = 256
AT_X = 512
AT_GATE = AT_X + INNER
AT_OUT = AT_GATE + INNER
WIDE = AT_OUT + INNER
CX = 2 * NSTATE
CHUNK = 768
WIDE_CHUNKS = 4
CHUNKS = WIDE_CHUNKS + QUADS + 2
UNITS = 7
SLOTS = 4
GATHERS = (
    (0, 512), (512, 512), (1024, 512), (1536, 512), (AT_GATE, INNER), (AT_OUT, 1024),
    (AT_OUT + 1024, 512),
)
PLANE = 4

BF = jnp.bfloat16
F32 = jnp.float32
MESH = pl.DeviceIdType.MESH


def dot(a, b):
    return lax.dot_general(a, b, (((1,), (0,)), ((), ())), preferred_element_type=F32)


def dot_nt(a, b):
    return lax.dot_general(a, b, (((1,), (1,)), ((), ())), preferred_element_type=F32)


def sigmoid(v):
    return 0.5 * jnp.tanh(0.5 * v) + 0.5


def halves(v):
    high = v.astype(BF)
    return high, (v - high.astype(F32)).astype(BF)


def side_by_side(v):
    return jnp.concatenate(halves(v), axis=1)


def exact_sum(triangle, v):
    high, rest = halves(v)
    low = (v - high.astype(F32) - rest.astype(F32)).astype(BF)
    parts = dot(triangle, jnp.concatenate([high, rest, low], axis=1))
    return parts[:, :LANES] + parts[:, LANES : 2 * LANES] + parts[:, 2 * LANES :]


def span(start, size, multiple=None):
    return pl.ds(pl.multiple_of(start, multiple or size), size)


def rows_of(b):
    return span(b * GROUP, GROUP)


def heads_of(q):
    return span(q * 256, 256)


def fold(v):
    total = v[0:8]
    for i in range(1, v.shape[0] // 8):
        total = total + v[8 * i : 8 * i + 8]
    return total


def iota(shape, dim):
    return lax.broadcasted_iota(jnp.int32, shape, dim)


def loop(count, body, together=1):
    def step(i, _):
        for k in range(together):
            body(i * together + k)
        return 0

    lax.fori_loop(0, count // together, step, 0)


def silu_slope(v, sg):
    return sg * (1.0 + v * (1.0 - sg))


def mixer(names, fused, nz, *refs):
    r = types.SimpleNamespace(**dict(zip(names, refs)))
    seq = lax.axis_index("seq")
    f = lax.axis_index("fsdp")
    z_at, p_at = f // PLANE, f % PLANE
    sibling = {"seq": 1 - seq}
    is_second = (seq == 1).astype(F32)
    is_first = 1.0 - is_second

    def plane_peer(j):
        if j == 1:
            return p_at + 1 - 2 * (p_at % 2)
        if j == 2:
            return p_at + 2 - 4 * (p_at // 2)
        return 3 - p_at

    def z_peer(j):
        return (z_at + j + nz) % nz

    def on_plane(j):
        return {"fsdp": z_at * PLANE + plane_peer(j)}

    def on_chain(j):
        return {"fsdp": z_peer(j) * PLANE + p_at}

    own = D // (2 * nz * PLANE) if fused else 0
    peers = [sibling]
    if fused:
        peers += [on_plane(j) for j in range(1, PLANE)] + [on_chain(j) for j in range(1, nz)]
    barrier = pltpu.get_barrier_semaphore()
    for peer in peers:
        pl.semaphore_signal(barrier, inc=1, device_id=peer, device_id_type=MESH)

    def own_columns(ref, c):
        return ref.at[c * own : (c + 1) * own, 0 : GATHERS[c][1]]

    part_rows = r.tokens.shape[2]
    raw = [buf.at[0:part_rows, m * D : (m + 1) * D] for buf in (r.dssd, r.cout) for m in range(2)]
    raw_copies = []
    for i in range(4):
        src = (r.tokens, r.out_grad)[i // 2].at[i % 2, 0]
        raw_copies.append(pltpu.make_async_copy(src, raw[i], r.local.at[2 + i]))
        raw_copies[i].start()

    if fused:
        wide = 2 * INNER
        steps = r.in_weight[:, wide + CX :].astype(F32)
        fill = jnp.zeros((steps.shape[0], AT_X - CX - HEADS), F32)
        key_query = r.in_weight[:, wide : wide + CX].astype(F32)
        own_columns(r.gate, 0)[...] = jnp.concatenate([key_query, steps, fill], axis=1)

    pl.semaphore_wait(barrier, len(peers))

    def remote(src, dst, send, recv, device):
        return pltpu.make_async_remote_copy(
            src_ref=src, dst_ref=dst, send_sem=send, recv_sem=recv, device_id=device,
            device_id_type=MESH,
        )

    def pair_copy(i, src, dst):
        return remote(src, dst, r.pair_send.at[i], r.pair_recv.at[i], sibling)

    w = r.w
    slab = 2 * own

    def part(c):
        low, size = GATHERS[c]
        return span(low + seq * (size // 2), size // 2, 128)

    def slab_of(index):
        return span(index * slab, slab, 16)

    def gather_copy(c, k, index, device):
        at = w.at[slab_of(index), part(c)]
        return remote(at, at, r.g_send.at[c, 0], r.g_recv.at[c, k], device)

    def chain_copy(c, j):
        return gather_copy(c, 0, f, on_chain(j))

    def plane_copy(c, kind, back):
        low, size = GATHERS[c]
        owner = (p_at, p_at, plane_peer(1), plane_peer(2), p_at)[kind]
        cols = part(c)
        if kind in (2, 3):
            cols = span(low + seq * (size // 2) + (kind - 2) * (size // 4), size // 4, 128)
        at = w.at[slab_of((z_at - back + nz) % nz * PLANE + owner), cols]
        device = on_plane((1, 2, 2, 1, 3)[kind])
        return remote(at, at, r.g_send.at[c, 0], r.g_recv.at[c, 1 + min(kind // 2, 1)], device)

    def last_copy(c):
        at = w.at[:, part(c)]
        return remote(at, at, r.g_send.at[c, 1], r.g_recv.at[c, 3], sibling)

    def wait_bytes(rows, cols, sem):
        at = w.at[0 : rows * slab // 2, cols]
        pltpu.make_async_copy(at, at, sem).wait()

    def gather_own(c):
        cols = part(c)
        half_cols = span(seq * (GATHERS[c][1] // 2), GATHERS[c][1] // 2, 128)
        mine, theirs = (own_columns(ref, c)[:, half_cols] for ref in (r.gate, r.back))
        first = jnp.where(seq == 0, mine, theirs)
        second = jnp.where(seq == 0, theirs, mine)
        w[slab_of(f), cols] = jnp.concatenate([first, second], axis=0).astype(BF)

    def gather_0(c):
        for j in range(1, nz):
            chain_copy(c, j).start()

    def gather_1(c):
        for kind in (0, 1) if c else (4, 0, 1):
            plane_copy(c, kind, 0).start()

    def gather_2(c):
        wait_bytes(2 * (nz - 1), part(c), r.g_recv.at[c, 0])
        for back in range(1, nz):
            for kind in (0, 1) if c else (4, 0, 1):
                plane_copy(c, kind, back).start()

    def gather_3(c):
        wait_bytes(4 * nz, part(c), r.g_recv.at[c, 1])
        for back in range(nz if c else 0):
            for kind in range(2):
                plane_copy(c, kind + 2, back).start()

    def gather_4(c):
        wait_bytes(2 * nz, part(c), r.g_recv.at[c, 2])
        last_copy(c).start()

    def turned_copy(c, j):
        at = w.at[span(z_at * PLANE * slab, PLANE * slab, 16), part(c)]
        return remote(at, at, r.g_send.at[c, 0], r.g_recv.at[c, 0], on_chain(j))

    def turned_2(c):
        wait_bytes(4, part(c), r.g_recv.at[c, 1])
        for kind in range(2):
            plane_copy(c, kind + 2, 0).start()

    def turned_3(c):
        wait_bytes(2, part(c), r.g_recv.at[c, 2])
        for j in range(1, nz):
            turned_copy(c, j).start()

    def turned_4(c):
        wait_bytes(2 * PLANE * (nz - 1), part(c), r.g_recv.at[c, 0])
        last_copy(c).start()

    def gather_5(c):
        last_copy(c).wait_recv()

    def gather_end(c):
        wait_bytes(2 * (nz - 1) + 6 * nz, part(c), r.g_send.at[c, 0])
        last_copy(c).wait_send()

    def wide_chunk(i):
        return i, i, 0, CHUNK // 2, i, 0

    def quad_chunk(q):
        return WIDE_CHUNKS + q, q // 3, (q % 3) * 256, 128, WIDE_CHUNKS + q // 3, (q % 3) * 128

    step_chunk = (WIDE_CHUNKS + QUADS, 2, AT_DT, LANES, UNITS - 1, 0)
    last_chunk = (WIDE_CHUNKS + QUADS + 1, 2, 0, LANES, UNITS - 1, LANES)

    def source(g, which):
        return span(g[2] + which * g[3], g[3], 128)

    def target(g):
        return span(g[5], g[3], 128)

    def sum_copy_0(g):
        src = r.wg.at[g[1], :, :, :, source(g, 1 - seq)]
        dst = r.r0.at[g[4], :, :, :, target(g)]
        return remote(src, dst, r.s_send.at[g[0]], r.s_recv.at[g[0], 0], sibling)

    def sum_copy_1(g, j):
        src = r.wg.at[g[1], :, plane_peer(j), :, source(g, seq)]
        dst = r.r1.at[g[4], j - 1, :, :, target(g)]
        return remote(src, dst, r.s_send.at[g[0]], r.s_recv.at[g[0], 1], on_plane(j))

    def sum_copy_2(g, j):
        src = r.wg.at[g[1], z_peer(j), p_at, :, source(g, seq)]
        dst = r.r2.at[g[4], j - 1, :, target(g)]
        return remote(src, dst, r.s_send.at[g[0]], r.s_recv.at[g[0], 2], on_chain(j))

    def sum_copy_3(g):
        src = r.fin.at[g[4], span((1 - seq) * own, own, 8), target(g)]
        dst = r.gsum.at[g[4], :, target(g)]
        return remote(src, dst, r.s_send.at[g[0]], r.s_recv.at[g[0], 3], sibling)

    def finish_all(g, level, at):
        pltpu.make_async_copy(at, at, r.s_send.at[g[0]]).wait()
        pltpu.make_async_copy(at, at, r.s_recv.at[g[0], level]).wait()

    def finish(copy):
        copy.wait_send()
        copy.wait_recv()

    def sum_0(g):
        if fused:
            sum_copy_0(g).start()

    def sum_1(g):
        if not fused:
            return
        finish(sum_copy_0(g))

        def add(i):
            at = (g[1], i // PLANE, i % PLANE, slice(None), source(g, seq))
            theirs = r.r0[g[4], i // PLANE, i % PLANE, :, target(g)]
            r.wg[at] = r.wg[at] + theirs

        loop(nz * PLANE, add, PLANE)
        for j in (3, 1, 2):
            sum_copy_1(g, j).start()

    def sum_2(g):
        if not fused:
            return
        finish_all(g, 1, r.r1.at[g[4], :, :, :, target(g)])

        def add(zi):
            at = (g[1], zi, p_at, slice(None), source(g, seq))
            value = r.wg[at].astype(F32)
            for j in range(PLANE - 1):
                value = value + r.r1[g[4], j, zi, :, target(g)].astype(F32)
            r.wg[at] = value.astype(BF)

        loop(nz, add, 2 if nz % 2 == 0 else 1)
        for j in range(1, nz):
            sum_copy_2(g, j).start()

    def sum_3(g):
        if not fused:
            return
        finish_all(g, 2, r.r2.at[g[4], :, :, target(g)])
        value = r.wg[g[1], z_at, p_at, :, source(g, seq)].astype(F32)
        for j in range(nz - 1):
            value = value + r.r2[g[4], j, :, target(g)].astype(F32)
        r.fin[g[4], :, target(g)] = value
        sum_copy_3(g).start()

    def sum_4(g):
        finish(sum_copy_3(g))

    def put_grad(g, low, value):
        size = value.shape[1]
        if fused:
            parts = value.astype(BF).reshape(nz, PLANE, slab, size)
            r.wg[g[1], :, :, :, span(g[2] + low, size, 128)] = parts
        else:
            first = g[4] * CHUNK + (g[2] if g[3] == 128 else 0)
            r.wgrad[:, span(first + low, size, 128)] = value.astype(BF)

    def shard_copy(c):
        size = GATHERS[c][1] // 2
        rows, cols = slice(c * own, (c + 1) * own), span((1 - seq) * size, size, 128)
        return pair_copy(1 if c else 4, r.gate.at[rows, cols], r.back.at[rows, cols])

    if fused:
        shard_copy(0).start()
        own_columns(r.gate, 1)[...] = r.in_weight[:, INNER : INNER + 512].astype(F32)
        own_columns(r.gate, 2)[...] = r.in_weight[:, INNER + 512 : INNER + 1024].astype(F32)
        own_columns(r.gate, 3)[...] = r.in_weight[:, INNER + 1024 : wide].astype(F32)
        own_columns(r.gate, 4)[...] = r.in_weight[:, 0:INNER].astype(F32)
        own_columns(r.gate, 5)[...] = r.out_weight[:, 0:1024].astype(F32)
        own_columns(r.gate, 6)[...] = r.out_weight[:, 1024:].astype(F32)
        for c in range(1, len(GATHERS)):
            shard_copy(c).start()

    def pick_heads():
        row, lane = iota((8 * LANES, LANES), 0), iota((8 * LANES, LANES), 1)
        pair, kind, second = row >> 9, (row >> 8) & 1, (row & 127) >> 6
        r.pick[...] = (lane == 2 * pair + second + 64 * kind).astype(F32).astype(BF)

    def make_spread(q):
        shape = (256, 256)
        head = (iota(shape, 1) + q * 256) >> 6
        r.spread[:, span(q * 256, 256)] = (head == (iota(shape, 0) & 127)).astype(F32).astype(BF)

    if fused:
        shard_copy(0).wait()
        gather_own(0)
        gather_0(0)
        gather_1(0)
        at = r.back.at[0 : own * (WIDE - GATHERS[0][1]) // 2 // 768, 0:768]
        for sem in (r.pair_send.at[1], r.pair_recv.at[1]):
            pltpu.make_async_copy(at, at, sem).wait()
        for c in range(1, len(GATHERS)):
            gather_own(c)
        gather_0(1)
        gather_1(1)
        gather_0(2)
        gather_1(6)

    r.convp[0:CONV, 0:CX] = r.conv_weight[:, INNER:]
    r.convp[0:CONV, CX:] = r.conv_weight[:, 0:INNER]
    bias = r.conv_bias[...].reshape(1, CONVCH)
    r.convp[4:5, 0:CX] = bias[:, INNER:]
    r.convp[4:5, CX:] = bias[:, 0:INNER]
    r.headp[...] = jnp.zeros_like(r.headp)
    for i, v in enumerate((r.dt_bias, r.a_log, r.skip_gain)):
        r.headp[i : i + 1, 0:HEADS] = v[...].reshape(1, HEADS)
    norm_gain = r.norm_gain[...].reshape(1, D)

    first_long = r.lengths[0, 0] > r.lengths[0, 1]
    shortest = jnp.minimum(r.lengths[0, 0], r.lengths[0, 1])
    for i in range(4):
        raw_copies[i].wait()

    def pick_rows(i):
        here = span(i * 64, 64)
        for to, k in ((r.tok, 0), (r.og, 2)):
            to[here, :] = jnp.where(first_long, raw[k][here, :], raw[k + 1][here, :])

    def pick_short(i):
        here, there = span(i * 64, 64), span(2 * GROUP + i * 64, 64)
        r.tok[there, :] = jnp.where(first_long, raw[1][here, :], raw[0][here, :])
        valid = (seq * part_rows + i * 64 + iota((64, D), 0) < shortest).astype(F32)
        picked = jnp.where(first_long, raw[3][here, :], raw[2][here, :])
        r.og[there, :] = (picked.astype(F32) * valid).astype(BF)

    loop(2 * GROUP // 64, pick_rows)
    edge_copy = pair_copy(0, r.tok.at[2 * GROUP - EDGE : 2 * GROUP, :], r.edge_in)
    edge_copy.start()
    if fused:
        gather_2(0)
        gather_1(2)
        gather_0(3)
    loop(GROUP // 64, pick_short)

    loop(QUADS, make_spread)
    pick_heads()
    r.innerp[0:1, :] = r.out_gain[...].reshape(1, INNER)
    r.innerp[1:2, :] = dot(side_by_side(r.headp[...]), r.spread[...])[2:3, :]
    tri_shape = (GROUP, GROUP)
    lower = (iota(tri_shape, 0) >= iota(tri_shape, 1)).astype(F32).astype(BF)
    upper = (iota(tri_shape, 0) <= iota(tri_shape, 1)).astype(F32).astype(BF)
    half = GROUP // 2
    causal = iota((half, half), 0) >= iota((half, half), 1)
    causal_t = iota((half, half), 0) <= iota((half, half), 1)
    first_head = iota((GROUP, LANES), 1) < HEADDIM
    rate = -jnp.exp(r.headp[1:2, :])

    r.g_norm[...] = jnp.zeros_like(r.g_norm)
    r.g_conv[...] = jnp.zeros_like(r.g_conv)
    r.g_head[...] = jnp.zeros_like(r.g_head)
    r.g_inner[...] = jnp.zeros_like(r.g_inner)
    r.halo[2] = jnp.zeros((8, CONVCH), F32)
    r.dproj[:, AT_DT + LANES : AT_X] = jnp.zeros((ROWS, AT_X - AT_DT - LANES), BF)

    def norm_of(v):
        root = lax.rsqrt(jnp.mean(v * v, axis=1, keepdims=True) + EPS)
        return (v * root * norm_gain).astype(BF)

    def norm_rows(i):
        rows = span(i * 64, 64)
        r.normed[rows, :] = norm_of(r.tok[rows, :].astype(F32))

    loop(ROWS // 64, norm_rows, 2)
    if fused:
        gather_3(0)
        gather_2(1)
    edge_copy.wait()
    r.normed[ROWS:, :] = norm_of(r.edge_in[...].astype(F32) * is_second)

    def turn(b):
        rows = rows_of(b)
        r.normed_t[:, rows] = r.normed[rows, :].T
        r.db_t[:, rows] = r.og[rows, :].T

    loop(BLOCKS, turn, BLOCKS)

    if fused:
        gather_4(0)
        gather_3(1)
        turned_2(6)
        gather_1(3)
        gather_0(4)
        gather_5(0)

    def conv_acc(values, before, cols):
        rows = values.shape[0]
        ext = jnp.concatenate([before, values], axis=0)
        shifted = [ext[5 + k : 5 + k + rows] for k in range(CONV)]
        acc = r.convp[4:5, cols]
        for k in range(CONV):
            acc = acc + r.convp[k : k + 1, cols] * shifted[k]
        return acc, shifted

    def project(at, to):
        low = dot(r.normed[...], w[:, at]).astype(BF)
        r.clow[:, to] = low
        r.halo[0, :, to] = low[ROWS : ROWS + EDGE].astype(F32)[EDGE - 8 :]
        r.halo[1, :, to] = low[GROUP - 16 : GROUP].astype(F32)[8:]

    def conv_forward(b, cols):
        rows = rows_of(b)
        acc, _ = conv_acc(r.clow[rows, cols].astype(F32), r.halo[b, :, cols], cols)
        r.cout[rows, cols] = (acc * sigmoid(acc)).astype(BF)

    project(pl.ds(0, CX), pl.ds(0, CX))
    r.dtb[...] = dot(r.normed[0:ROWS, :], w[:, AT_DT : AT_DT + LANES])

    def head_rows(b):
        z = r.dtb[rows_of(b), :] + r.headp[0:1, :]
        step = jnp.maximum(z, 0.0) + jnp.log1p(jnp.exp(-jnp.abs(z)))
        return z, step

    def prepare(b):
        rows = rows_of(b)
        conv_forward(b, pl.ds(0, LANES))
        conv_forward(b, pl.ds(LANES, LANES))
        z, step = head_rows(b)
        cum = exact_sum(lower, step * rate)
        moved = cum - jnp.log(jnp.maximum(step, 1e-37))
        r.cumb[rows, :] = cum
        r.moved[rows, :] = moved
        cum_t, moved_t = cum.T, moved.T
        for q in range(QUADS):
            r.cut[b, q, 0:4, :] = moved_t[4 * q : 4 * q + 4, :]
            r.cut[b, q, 4:8, :] = cum_t[4 * q : 4 * q + 4, :]
        r.weight[rows, :] = side_by_side(jnp.exp(cum[GROUP - 1 : GROUP, :] - cum) * step)
        r.fade[rows, :] = side_by_side(jnp.exp(cum))
        key, query = r.cout[rows, 0:NSTATE], r.cout[rows, NSTATE:CX]
        r.turned[b, 0:NSTATE, :] = key.T
        r.turned[b, NSTATE:CX, :] = query.T
        r.sco[b] = dot_nt(query, key)

    loop(BLOCKS, prepare, BLOCKS)
    if fused:
        gather_2(2)
        gather_4(1)
        gather_2(3)
        gather_1(4)
        gather_0(5)
        gather_5(1)

    gather_steps = {
        (0, -1): ((gather_3, 2),), (1, -1): ((gather_4, 2), (gather_3, 3), (gather_1, 5)),
        (2, -1): ((gather_5, 2), (gather_4, 3), (gather_2, 4)),
        (3, -1): ((gather_2, 5), (turned_3, 6)), (4, -1): ((gather_5, 3), (gather_3, 4)),
    }

    def gather_on(q, b):
        for at, steps in gather_steps.items():
            if fused and at[1] == b:

                @pl.when(q == at[0])
                def _():
                    for step, c in steps:
                        step(c)

    def to_first(v, q):
        return pltpu.roll(v, (LANES - 4 * q) % LANES, 1)

    def forward_block(b, q):
        rows = rows_of(b)
        cols = span(CX + q * 256, 256)
        heads = span(q * 256, 256)
        for i in range(2):
            conv_forward(b, span(CX + q * 256 + i * LANES, LANES))
        xq = r.cout[rows, cols]

        if b < 2:
            spread_w = dot(r.weight[rows, :], r.spread[:, heads])
            scaled = (xq.astype(F32) * spread_w).astype(BF)
            r.runs[b, :, heads] = dot(r.turned[b, 0:NSTATE, :], scaled)

        near = to_first(r.cumb[rows, :], q)
        skip = r.innerp[1:2, heads]
        for j in range(2):
            lanes = slice(j * LANES, (j + 1) * LANES)
            xp = xq[:, lanes]
            zero = jnp.zeros_like(xp)
            x_ab = (jnp.where(first_head, xp, zero), jnp.where(first_head, zero, xp))
            top, bottom = [], []
            for e in range(2):
                h = 2 * j + e
                col_top, col_bottom = near[:half, h : h + 1], near[half:, h : h + 1]
                row = r.cut[b, q, h : h + 1, :]
                row_left, row_right = row[:, :half], row[:, half:]
                gap = jnp.where(causal, col_top - row_left, -1e30)
                top.append((r.sco[b, :half, :half] * jnp.exp(gap)).astype(BF))
                fade = jnp.exp(col_bottom - row_left)
                bottom.append((r.sco[b, half:, :half] * fade).astype(BF))
                gap = jnp.where(causal, col_bottom - row_right, -1e30)
                bottom.append((r.sco[b, half:, half:] * jnp.exp(gap)).astype(BF))
            out_top = dot(
                jnp.concatenate(top, axis=1), jnp.concatenate([v[:half] for v in x_ab], axis=0)
            )
            out_bottom = dot(jnp.concatenate(bottom, axis=1), jnp.concatenate(x_ab, axis=0))
            place = span(q * 256 + j * LANES, LANES)
            xf = xp.astype(F32) * skip[:, lanes]
            r.ssd[span(b * GROUP, half), place] = out_top + xf[:half]
            r.ssd[span(b * GROUP + half, half), place] = out_bottom + xf[half:]

    def forward_quad(q):
        gather_on(q, -1)
        project(span(AT_X + q * 256, 256), span(CX + q * 256, 256))
        for b in range(BLOCKS):
            gather_on(q, b)
            forward_block(b, q)

    loop(QUADS, forward_quad)

    def decay_of(b):
        last = r.cumb[b * GROUP + GROUP - 8 : (b + 1) * GROUP, :]
        return dot(side_by_side(jnp.exp(last)), r.spread[...])[7:8, :]

    decay_0, decay_1 = decay_of(0), decay_of(1)
    r.runs[1] = r.runs[1] + decay_1 * r.runs[0]
    state_copy = pair_copy(2, r.runs.at[1], r.state_in)
    state_copy.start()
    if fused:
        gather_3(5)
        gather_4(4)
        turned_4(6)

    def carry_block(b):
        rows = rows_of(b)
        query = r.cout[rows, NSTATE:CX]

        def quad(q):
            cols = span(q * 256, 256)
            r.ssd[rows, cols] += dot(query, r.held[b, :, cols]) * dot(
                r.fade[rows, :], r.spread[:, cols]
            )

        loop(QUADS, quad, 3)

    gain = r.innerp[0:1, :]

    def gate_project(q):
        at = span(AT_GATE + q * 256, 256)
        high, low = halves(dot(r.normed[0:ROWS, :], w[:, at]))
        r.dssd[:, span(q * 256, 256)] = high
        r.dproj[:, at] = low

    def out_back(b):
        rows = rows_of(b)

        def quad(q):
            cols = span(q * 256, 256)
            r.back[:, cols] = dot(r.og[rows, :], w[:, span(AT_OUT + q * 256, 256)])

        loop(QUADS, quad, 3)

    def gated_tile(here, k):
        cols = slice(k * 256, (k + 1) * 256)
        low = r.dproj[here, AT_GATE + k * 256 : AT_GATE + (k + 1) * 256]
        g = r.dssd[here, cols].astype(F32) + low.astype(F32)
        s = r.ssd[here, cols]
        sg = sigmoid(g)
        return cols, g, s, sg

    def row_mean(v):
        return jnp.sum(v, axis=1, keepdims=True) * (1.0 / INNER)

    def gate_forward(i):
        here = span(i * 32, 32)
        square = 0.0
        for k in range(QUADS):
            cols, g, s, sg = gated_tile(here, k)
            gated = s * (g * sg)
            square = square + gated * gated
            r.gate[0:32, cols] = gated
        root = lax.rsqrt(row_mean(square) + EPS)
        for k in range(QUADS):
            cols = slice(k * 256, (k + 1) * 256)
            to = slice(AT_X + k * 256, AT_X + (k + 1) * 256)
            r.dproj[here, to] = (r.gate[0:32, cols] * root * gain[:, cols]).astype(BF)

    def gate_block(b):
        def gate_rows(i):
            here = span(b * GROUP + i * 32, 32)
            local = span(i * 32, 32)
            square, mixed = 0.0, 0.0
            for k in range(QUADS):
                cols, g, s, sg = gated_tile(here, k)
                silu = g * sg
                gated = s * silu
                square = square + gated * gated
                mixed = mixed + gated * (gain[:, cols] * r.back[local, cols])
                r.gate[0:32, cols] = gated
                r.gate[32:64, cols] = silu
                r.gate[64:96, cols] = s * silu_slope(g, sg)
            root = lax.rsqrt(row_mean(square) + EPS)
            lean = root * row_mean(mixed)
            for k in range(QUADS):
                cols = slice(k * 256, (k + 1) * 256)
                d_out = r.back[local, cols]
                v = r.gate[0:32, cols] * root
                r.g_inner[0:8, cols] += fold(d_out * v)
                d_gated = root * (gain[:, cols] * d_out - v * lean)
                d_s = (d_gated * r.gate[32:64, cols]).astype(BF)
                r.dssd[here, cols] = d_s
                x = r.cout[here, CX + k * 256 : CX + (k + 1) * 256]
                r.g_inner[8:16, cols] += fold(d_s.astype(F32) * x.astype(F32))
                to = slice(AT_GATE + k * 256, AT_GATE + (k + 1) * 256)
                r.dproj[here, to] = (d_gated * r.gate[64:96, cols]).astype(BF)

        loop(GROUP // 32, gate_rows)

    state_copy.wait()
    r.state_in[...] = r.state_in[...] * is_second
    r.held[0] = r.state_in[...].astype(BF)
    r.runs[0] = r.runs[0] + decay_0 * r.state_in[...]
    r.held[1] = r.runs[0].astype(BF)
    r.runs[1] = r.state_in[...]

    @pl.when(seq > 0)
    def _():
        carry_block(0)

    carry_block(1)

    def add_norm(value, cols):
        product = value * w[:, cols].astype(F32)
        for k in range(value.shape[1] // LANES):
            r.g_norm[...] += product[:, k * LANES : (k + 1) * LANES]

    def wide_grad(i):
        g = wide_chunk(i)
        left = r.db_t if i < 2 else r.normed_t
        first = (AT_X if i < 2 else AT_GATE) + (i % 2) * CHUNK

        def tile(k):
            value = dot(left[...], r.dproj[:, span(first + k * 256, 256)])
            put_grad(g, k * 256, value)
            if i >= 2:
                add_norm(value, span(first + k * 256, 256))

        loop(CHUNK // 256, tile, 3)
        sum_0(g)

    if fused:
        gather_4(5)
        gather_5(4)
    loop(QUADS, gate_project, 2)
    loop(ROWS // 32, gate_forward)
    wide_grad(0)
    wide_grad(1)
    if fused:
        gather_5(5)
        gather_5(6)
    for b in range(2):
        out_back(b)
        gate_block(b)
        sum_1(wide_chunk(b))

    @pl.when(seq == 0)
    def _():
        out_back(2)
        gate_block(2)

    @pl.when(seq > 0)
    def _():
        r.dssd[2 * GROUP :, :] = jnp.zeros((GROUP, INNER), BF)
        r.dproj[2 * GROUP :, AT_GATE:AT_OUT] = jnp.zeros((GROUP, INNER), BF)

    wide_grad(2)
    wide_grad(3)
    sum_2(wide_chunk(0))

    def state_back(b):
        rows = rows_of(b)

        r.dqb[rows, :] = jnp.zeros((GROUP, NSTATE), F32)

        def quads(i):
            dq = 0.0
            for q in (3 * i, 3 * i + 1, 3 * i + 2):
                cols = heads_of(q)
                spread_f = dot(r.fade[rows, :], r.spread[:, cols])
                dz = (spread_f * r.dssd[rows, cols].astype(F32)).astype(BF)
                r.dheld[b, :, cols] = dot(r.turned[b, NSTATE:CX, :], dz)
                dq = dq + dot_nt(dz, r.held[b, :, cols])
            r.dqb[rows, :] += dq

        loop(QUADS // 3, quads)

    def no_state():
        r.dheld[0] = jnp.zeros((NSTATE, INNER), F32)

    r.dqb[0:GROUP, :] = jnp.zeros((GROUP, NSTATE), F32)
    pl.when(seq > 0)(lambda: state_back(0))
    pl.when(seq == 0)(no_state)
    state_back(1)
    r.dqb[2 * GROUP :, :] = jnp.zeros((GROUP, NSTATE), F32)
    r.dheld[0] = r.dheld[0] + decay_0 * r.dheld[1]
    dstate_copy = pair_copy(3, r.dheld.at[0], r.dstate_in)
    dstate_copy.start()
    sum_1(wide_chunk(2))

    def out_block(b):
        rows = rows_of(b)
        branch = dot_nt(r.dproj[rows, AT_X:AT_GATE], w[:, AT_OUT:])
        r.normed[rows, :] = (r.tok[rows, :].astype(F32) + branch).astype(BF)

    loop(BLOCKS, out_block)
    mixed_copy = pltpu.make_async_copy(r.normed.at[0:ROWS, :], r.mixed, r.local.at[0])
    mixed_copy.start()
    sum_1(wide_chunk(3))
    sum_2(wide_chunk(1))
    sum_3(wide_chunk(0))

    def ds_of(b):
        return r.back.at[:, heads_of(b)]

    def give_of(b):
        return r.back.at[:, span(CHUNK + b * LANES, LANES)]

    def kept_of(b):
        return r.back.at[:, span(CHUNK + (BLOCKS + b) * LANES, LANES)]

    def prepare_back(b):
        rows = rows_of(b)
        r.sco[b] = dot_nt(r.cout[rows, 0:NSTATE], r.cout[rows, NSTATE:CX])
        ds_of(b)[...] = jnp.zeros((GROUP, GROUP), F32)
        nothing = jnp.zeros((GROUP, LANES), F32)
        r.dkb[rows, :] = nothing
        give_of(b)[...] = nothing

    loop(BLOCKS, prepare_back)
    dstate_copy.wait()
    r.dstate_in[...] = r.dstate_in[...] * is_first
    r.held[1] = r.dstate_in[...].astype(BF)
    r.state_in[...] = r.dheld[1] + decay_1 * r.dstate_in[...]
    r.held[0] = r.state_in[...].astype(BF)

    def backward_block(b, q):
        rows = rows_of(b)
        heads = span(q * 256, 256)
        xq = r.cout[rows, span(CX + q * 256, 256)]
        dq4 = r.dssd[rows, heads]
        skip = r.innerp[1:2, heads]
        dx, ds = r.gate.at[:, heads_of(b)], ds_of(b)

        if b < 2:
            spread_w = dot(r.weight[rows, :], r.spread[:, heads])
            d_states = r.held[b, :, heads]
            dx_state = spread_w * dot(r.cout[rows, 0:NSTATE], d_states)
            r.flow[b, 0:8, heads] = fold(xq.astype(F32) * dx_state)
            r.dkb[rows, :] += dot_nt((xq.astype(F32) * spread_w).astype(BF), d_states)

        near = to_first(r.moved[rows, :], q)
        products = []
        for j in range(2):
            lanes = slice(j * LANES, (j + 1) * LANES)
            xp, dp = xq[:, lanes], dq4[:, lanes]
            zero = jnp.zeros_like(xp)
            d_ab = (jnp.where(first_head, dp, zero), jnp.where(first_head, zero, dp))
            top, bottom = [], []
            for e in range(2):
                h = 2 * j + e
                dm_top = dot_nt(xp[:half], d_ab[e])
                dm_bottom = dot_nt(xp[half:], d_ab[e][half:])
                col_top, col_bottom = near[:half, h : h + 1], near[half:, h : h + 1]
                row = r.cut[b, q, 4 + h : 5 + h, :]
                row_left, row_right = row[:, :half], row[:, half:]
                fade = jnp.exp(jnp.where(causal_t, row_left - col_top, -1e30))
                ds[:half, :half] += dm_top[:, :half] * fade
                top.append((r.sco[b, :half, :half] * fade).astype(BF))
                fade = jnp.exp(row_right - col_top)
                ds[:half, half:] += dm_top[:, half:] * fade
                top.append((r.sco[b, :half, half:] * fade).astype(BF))
                fade = jnp.exp(jnp.where(causal_t, row_right - col_bottom, -1e30))
                ds[half:, half:] += dm_bottom * fade
                bottom.append((r.sco[b, half:, half:] * fade).astype(BF))
            dx_top = dot(jnp.concatenate(top, axis=1), jnp.concatenate(d_ab, axis=0))
            dx_bottom = dot(
                jnp.concatenate(bottom, axis=1), jnp.concatenate([v[half:] for v in d_ab], axis=0)
            )
            dxp = jnp.concatenate([dx_top, dx_bottom], axis=0)
            if b < 2:
                dxp = dxp + dx_state[:, lanes]
            xf, df = xp.astype(F32), dp.astype(F32)
            kept = skip[:, lanes]
            ssd = r.ssd[rows, span(q * 256 + j * LANES, LANES)]
            products += [*halves(xf * dxp), *halves(df * (ssd - kept * xf))]
            dx[:, lanes] = dxp + kept * df
        sums = dot(jnp.concatenate(products, axis=1), r.pick[...])
        give_of(b)[...] += pltpu.roll(sums, 4 * q, 1)

    def edge_grad(b, source, cols):
        first = r.clow[b * GROUP : b * GROUP + 16, cols].astype(F32)
        acc, _ = conv_acc(first, r.halo[b, :, cols], cols)
        d_acc = r.gate[0:16, span(b * 256 + source, LANES)] * silu_slope(acc, sigmoid(acc))
        r.halo_next[b, :, cols] = d_acc[0:8]

    def conv_back(b, source, cols, to, after):
        rows = rows_of(b)
        acc, shifted = conv_acc(r.clow[rows, cols].astype(F32), r.halo[b, :, cols], cols)
        d_acc = r.gate[:, span(b * 256 + source, LANES)] * silu_slope(acc, sigmoid(acc))
        for k in range(CONV):
            r.g_conv[8 * k : 8 * k + 8, cols] += fold(d_acc * shifted[k])
        r.g_conv[32:40, cols] += fold(d_acc)
        ext = jnp.concatenate([d_acc, after], axis=0)
        d_in = r.convp[3:4, cols] * d_acc
        for k in range(CONV - 1):
            d_in = d_in + r.convp[k : k + 1, cols] * ext[3 - k : 3 - k + GROUP]
        r.dproj[rows, to] = d_in.astype(BF)

    def edge_copy_back(i, cols):
        src, dst = r.halo_next.at[0, :, cols], r.dedge_in.at[:, cols]
        return remote(src, dst, r.edge_send.at[i], r.edge_recv.at[i], sibling)

    def first_edge(i, at):
        for k in range(2):
            edge_grad(0, k * LANES, span(at + k * LANES, LANES))
        edge_copy_back(i, span(at, 256)).start()

    def conv_back_all(i, at, to):
        cols = span(at, 256)

        def chunk(k):
            return k * LANES, span(at + k * LANES, LANES), span(to + k * LANES, LANES)

        for k in range(2):
            edge_grad(1, *chunk(k)[:2])
        for k in range(2):
            conv_back(2, *chunk(k), jnp.zeros((8, LANES), F32))
            conv_back(0, *chunk(k), r.halo_next[1, :, chunk(k)[1]])
        edge_copy_back(i, cols).wait()
        for k in range(2):
            conv_back(1, *chunk(k), r.dedge_in[:, chunk(k)[1]] * is_first)

    def backward_quad(q):
        @pl.when(q == 1)
        def _():
            sum_2(wide_chunk(2))

        @pl.when(q == 2)
        def _():
            sum_3(wide_chunk(2))

        @pl.when(q == 3)
        def _():
            sum_2(wide_chunk(3))

        @pl.when(q == 4)
        def _():
            sum_3(wide_chunk(3))

        for b in range(BLOCKS):
            backward_block(b, q)
            if b == 0:
                first_edge(q, CX + q * 256)

        @pl.when(q == 0)
        def _():
            sum_3(wide_chunk(1))

        @pl.when(q >= 1)
        def _():
            sum_1(quad_chunk(q - 1))

        @pl.when(q >= 2)
        def _():
            sum_2(quad_chunk(q - 2))

        @pl.when(q >= 3)
        def _():
            sum_3(quad_chunk(q - 3))

        conv_back_all(q, CX + q * 256, AT_X + q * 256)
        g = quad_chunk(q)
        value = dot(r.normed_t[...], r.dproj[:, span(AT_X + q * 256, 256)])
        put_grad(g, 0, value)
        sum_0(g)
        add_norm(value, span(AT_X + q * 256, 256))

    loop(QUADS, backward_quad)

    def ratio_of(b):
        z, step = head_rows(b)
        return jnp.where(z < -15.0, 1.0, sigmoid(z) / jnp.maximum(step, 1e-37))

    def backward_rest(b):
        rows = rows_of(b)
        key, query = r.cout[rows, 0:NSTATE], r.cout[rows, NSTATE:CX]
        d_scores = ds_of(b)[...].astype(BF)
        r.gate[:, span(b * 256, NSTATE, 128)] = r.dkb[rows, :] + dot(d_scores, query)
        r.gate[:, span(b * 256 + NSTATE, NSTATE, 128)] = r.dqb[rows, :] + dot(d_scores.T, key)
        both_sums = give_of(b)[...]
        in_low = iota((GROUP, LANES), 1) < HEADS
        give = jnp.where(in_low, both_sums, 0.0)
        take = jnp.where(in_low, pltpu.roll(both_sums, 64, 1), 0.0)
        kept_of(b)[...] = give * ratio_of(b)
        give_of(b)[...] = exact_sum(upper, take - give)

    loop(BLOCKS, backward_rest, BLOCKS)

    def block_total(b, run, grad, decay):
        kept = jnp.sum(run[...] * grad[...], axis=0, keepdims=True)
        summed = jnp.sum(r.flow[b], axis=0, keepdims=True) + decay * kept
        high, low = halves(jnp.broadcast_to(summed, (8, INNER)))
        by_head = dot_nt(high, r.spread[0:LANES, :]) + dot_nt(low, r.spread[0:LANES, :])
        rows = rows_of(b)
        give_of(b)[...] = give_of(b)[...] + by_head[0:1, :]

    block_total(0, r.runs.at[1], r.state_in, decay_0)
    block_total(1, r.runs.at[0], r.dstate_in, decay_1)

    def step_grad(b):
        rows = rows_of(b)
        z, step = head_rows(b)
        back_sum = give_of(b)[...]
        d_pre = kept_of(b)[...] + rate * back_sum * sigmoid(z)
        r.g_head[0:8, :] += fold(d_pre)
        r.g_head[8:16, :] += fold(back_sum * (step * rate))
        r.dproj[rows, AT_DT : AT_DT + LANES] = d_pre.astype(BF)

    loop(BLOCKS, step_grad, BLOCKS)
    sum_1(quad_chunk(5))
    first_edge(QUADS, 0)
    value = dot(r.normed_t[...], r.dproj[:, AT_DT:AT_X])
    put_grad(step_chunk, 0, value)
    sum_0(step_chunk)
    add_norm(value, slice(AT_DT, AT_X))
    conv_back_all(QUADS, 0, 0)
    value = dot(r.normed_t[...], r.dproj[:, 0:CX])
    put_grad(last_chunk, 0, value)
    sum_0(last_chunk)
    sum_1(step_chunk)
    add_norm(value, slice(0, CX))

    def total(v):
        return jnp.sum(v, axis=0, keepdims=True)

    for k in range(CONV + 1):
        r.small[0, k : k + 1, :] = total(r.g_conv[8 * k : 8 * k + 8, :])
    r.small[0, 5:6, 0:INNER] = total(r.g_inner[0:8, :])
    r.small[0, 5:6, INNER : INNER + LANES] = total(r.g_head[0:8, :])
    r.small[0, 5:6, INNER + LANES :] = total(r.g_head[8:16, :])
    high, low = halves(r.g_inner[8:16, :])
    skips = dot_nt(high, r.spread[0:LANES, :]) + dot_nt(low, r.spread[0:LANES, :])
    r.small[0, 6:7, 0:LANES] = total(skips)
    r.small[0, 6:7, LANES:] = jnp.zeros((1, CONVCH - LANES), F32)
    r.small[0, 7:8, 0:D] = total(r.g_norm[...].T) / norm_gain
    r.small[0, 7:8, D:] = jnp.zeros((1, CONVCH - D), F32)
    if fused:

        def send_small(level, first, count, device):
            for j in range(count):
                sems = r.t_send.at[level], r.t_recv.at[level]
                dst = r.small_in.at[first + j]
                remote(r.small.at[level], dst, *sems, device(j + 1)).start()

        def add_small(level, first, count):
            at = r.small_in.at[first : first + count]
            for sem in (r.t_send.at[level], r.t_recv.at[level]):
                pltpu.make_async_copy(at, at, sem).wait()
            value = r.small[level]
            for j in range(count):
                value = value + r.small_in[first + j]
            return value

        send_small(0, 0, 1, lambda j: sibling)

    def in_block(b):
        rows = rows_of(b)
        r.ssd[rows, 0:D] = dot_nt(r.dproj[rows, :], w[:, 0:AT_OUT])

    sum_1(last_chunk)
    sum_2(quad_chunk(4))
    sum_3(quad_chunk(3))
    in_block(2)
    if fused:
        r.small[1] = add_small(0, 0, 1)
        send_small(1, 1, PLANE - 1, on_plane)
    sum_2(quad_chunk(5))
    sum_2(step_chunk)
    sum_3(quad_chunk(4))
    in_block(0)
    sum_2(last_chunk)
    if fused:
        r.small[2] = add_small(1, 1, PLANE - 1)
        send_small(2, PLANE, nz - 1, on_chain)
    in_block(1)
    sum_3(quad_chunk(5))
    sum_3(step_chunk)

    def norm_back(i):
        rows = span(i * 32, 32)
        v = r.tok[rows, :].astype(F32)
        root = lax.rsqrt(jnp.mean(v * v, axis=1, keepdims=True) + EPS)
        y = v * root
        dn = r.ssd[rows, 0:D]
        bb = norm_gain * dn
        d_v = root * (bb - y * jnp.mean(y * bb, axis=1, keepdims=True))
        r.ssd[rows, 0:D] = r.og[rows, :].astype(F32) + d_v

    loop(ROWS // 32, norm_back, 3)
    tgrad_copy = pltpu.make_async_copy(r.ssd.at[:, 0:D], r.tgrad, r.local.at[1])
    tgrad_copy.start()

    if fused:
        sum_3(last_chunk)

        def hand_out(g, dst, first, count):
            sum_4(g)
            mine = r.fin[g[4], span(seq * own, own, 8), target(g)]
            theirs = r.gsum[g[4], :, target(g)]
            for half_at in range(2):
                value = jnp.where(seq == half_at, mine, theirs)
                size = min(g[3], count - half_at * g[3])
                at = first + half_at * g[3]
                if size > 0:
                    dst[:, at : at + size] = value[:, 0:size]

        for i in range(WIDE_CHUNKS):
            dst = r.grad_out if i < 2 else r.grad_in
            hand_out(wide_chunk(i), dst, (i % 2) * CHUNK, CHUNK)
        for q in range(QUADS):
            hand_out(quad_chunk(q), r.grad_in, INNER + q * 256, 256)
        hand_out(step_chunk, r.grad_in, 2 * INNER + CX, HEADS)
        hand_out(last_chunk, r.grad_in, 2 * INNER, CX)
        r.small_out[...] = add_small(2, PLANE, nz - 1)
        for c in range(len(GATHERS)):
            gather_end(c)
    else:
        r.small_out[...] = r.small[0]
    mixed_copy.wait()
    tgrad_copy.wait()


def call_mixer(fused, nz, arrays):
    vmem = pl.BlockSpec(memory_space=pltpu.VMEM)
    hbm = pl.BlockSpec(memory_space=pl.ANY)
    places = {"lengths": pl.BlockSpec(memory_space=pltpu.SMEM), "tokens": hbm, "out_grad": hbm}
    own = D // (2 * nz * PLANE) if fused else 0
    ins = list(arrays)
    outs = {"mixed": ((ROWS, D), BF), "tgrad": ((ROWS, D), F32), "small_out": ((8, CONVCH), F32)}
    scratch = {
        "tok": ((ROWS, D), BF), "og": ((ROWS, D), BF), "convp": ((8, CONVCH), F32),
        "headp": ((8, LANES), F32), "innerp": ((8, INNER), F32),
        "normed": ((ROWS + EDGE, D), BF), "normed_t": ((D, ROWS), BF), "db_t": ((D, ROWS), BF),
        "clow": ((ROWS + EDGE, CONVCH), BF), "cout": ((ROWS, CONVCH), BF),
        "gate": ((GROUP, INNER), F32), "back": ((GROUP, INNER), F32), "ssd": ((ROWS, INNER), F32),
        "dssd": ((ROWS, INNER), BF), "dproj": ((ROWS, AT_OUT), BF),
        "dtb": ((ROWS, LANES), F32), "cumb": ((ROWS, LANES), F32), "moved": ((ROWS, LANES), F32),
        "weight": ((ROWS, 256), BF), "fade": ((ROWS, 256), BF),
        "pick": ((8 * LANES, LANES), BF),
        "cut": ((BLOCKS, QUADS, 8, GROUP), F32), "spread": ((256, INNER), BF),
        "turned": ((BLOCKS, CX, GROUP), BF), "sco": ((BLOCKS, GROUP, GROUP), F32), "dkb": ((ROWS, LANES), F32), "dqb": ((ROWS, LANES), F32),
        "runs": ((2, NSTATE, INNER), F32), "held": ((2, NSTATE, INNER), BF),
        "dheld": ((2, NSTATE, INNER), F32),
        "flow": ((2, 8, INNER), F32), "halo": ((BLOCKS, 8, CONVCH), F32),
        "halo_next": ((2, 8, CONVCH), F32), "edge_in": ((EDGE, D), BF),
        "state_in": ((NSTATE, INNER), F32), "dstate_in": ((NSTATE, INNER), F32),
        "dedge_in": ((8, CONVCH), F32), "g_norm": ((D, LANES), F32), "g_conv": ((40, CONVCH), F32),
        "g_head": ((16, LANES), F32), "g_inner": ((16, INNER), F32), "small": ((3, 8, CONVCH), F32),
    }
    dma = pltpu.SemaphoreType.DMA
    sems = {
        "pair_send": dma((5,)), "pair_recv": dma((5,)), "edge_send": dma((QUADS + 1,)),
        "edge_recv": dma((QUADS + 1,)), "local": dma((6,)),
    }
    if fused:
        part = CHUNK // 2
        outs |= {"grad_in": ((own, PROJ), F32), "grad_out": ((own, INNER), F32)}
        scratch |= {
            "w": ((D, WIDE), BF),
            "wg": ((SLOTS, nz, PLANE, 2 * own, CHUNK), BF),
            "r0": ((UNITS, nz, PLANE, 2 * own, part), BF),
            "r1": ((UNITS, PLANE - 1, nz, 2 * own, part), BF),
            "r2": ((UNITS, nz - 1, 2 * own, part), BF), "fin": ((UNITS, 2 * own, part), F32),
            "gsum": ((UNITS, own, part), F32), "small_in": ((PLANE + nz - 1, 8, CONVCH), F32),
        }
        sems |= {
            "g_send": dma((len(GATHERS), 2)), "g_recv": dma((len(GATHERS), 4)),
            "s_send": dma((CHUNKS,)), "s_recv": dma((CHUNKS, 4)),
            "t_send": dma((3,)), "t_recv": dma((3,)),
        }
    else:
        outs["wgrad"] = ((D, WIDE), BF)
    names = ins + list(outs) + list(scratch) + list(sems)
    return pl.pallas_call(
        functools.partial(mixer, names, fused, nz),
        out_shape=[jax.ShapeDtypeStruct(s, t) for s, t in outs.values()],
        in_specs=[places.get(name, vmem) for name in ins],
        out_specs=[hbm, hbm] + [vmem] * (len(outs) - 2),
        scratch_shapes=[pltpu.VMEM(s, t) for s, t in scratch.values()] + list(sems.values()),
        compiler_params=pltpu.CompilerParams(
            collective_id=0, has_side_effects=True, vmem_limit_bytes=63 * 1024 * 1024
        ),
        name="mixer",
    )(*arrays.values())


def place_results(
    lengths, mixed, tgrad, small, grad_in, grad_out, mixed_at, tgrad_at, norm, in_at, conv, bias,
    step, rates, skip, gain, out_at, blank, blank_low, sems,
):
    seq = lax.axis_index("seq")
    long = jnp.where(lengths[0, 0] > lengths[0, 1], 0, 1)
    rows = mixed_at.shape[2]
    copies = []
    for i, (src, dst, zero) in enumerate(((tgrad, tgrad_at, blank), (mixed, mixed_at, blank_low))):
        first, after = dst.at[1 - long, 0, 0:GROUP, :], dst.at[1 - long, 0, GROUP:rows, :]
        whole = pltpu.make_async_copy(src.at[0:rows, :], dst.at[long, 0], sems.at[3 * i])
        used = pltpu.make_async_copy(src.at[rows : rows + GROUP, :], first, sems.at[3 * i + 1])
        unused = pltpu.make_async_copy(zero.at[0:GROUP, :], first, sems.at[3 * i + 1])
        end = pltpu.make_async_copy(zero.at[0 : rows - GROUP, :], after, sems.at[3 * i + 2])
        whole.start()
        pl.when(seq == 0)(used.start)
        zero[...] = jnp.zeros_like(zero)
        pl.when(seq > 0)(unused.start)
        end.start()
        copies += [whole, used, end]
    in_at[...] = grad_in[...]
    out_at[...] = grad_out[...]
    conv[:, 0:INNER] = small[0:CONV, CX:]
    conv[:, INNER:] = small[0:CONV, 0:CX]
    bias[...] = jnp.concatenate([small[4:5, CX:], small[4:5, 0:CX]], axis=1).reshape(CONVCH)
    gain[...] = small[5:6, 0:INNER].reshape(INNER)
    step[...] = small[5:6, INNER : INNER + HEADS].reshape(HEADS)
    rates[...] = small[5:6, INNER + LANES : INNER + LANES + HEADS].reshape(HEADS)
    skip[...] = small[6:7, 0:HEADS].reshape(HEADS)
    norm[...] = small[7:8, 0:D].reshape(D)
    for c in copies:
        c.wait()


def call_place(shape, lengths, *arrays):
    vmem = pl.BlockSpec(memory_space=pltpu.VMEM)
    hbm = pl.BlockSpec(memory_space=pl.ANY)
    own = arrays[3].shape[0]
    outs = (
        (shape, BF), (shape, F32), ((D,), F32), ((own, PROJ), F32), ((CONV, CONVCH), F32),
        ((CONVCH,), F32), ((HEADS,), F32), ((HEADS,), F32), ((HEADS,), F32), ((INNER,), F32),
        ((own, INNER), F32),
    )
    rest = max(shape[2] - GROUP, GROUP)
    results = pl.pallas_call(
        place_results,
        out_shape=[jax.ShapeDtypeStruct(s, t) for s, t in outs],
        in_specs=[pl.BlockSpec(memory_space=pltpu.SMEM)] + [vmem] * len(arrays),
        out_specs=[hbm, hbm] + [vmem] * (len(outs) - 2),
        scratch_shapes=[
            pltpu.VMEM((rest, D), F32), pltpu.VMEM((rest, D), BF), pltpu.SemaphoreType.DMA((6,)),
        ],
        name="place_results",
    )(lengths, *arrays)
    return (*results[:-1], results[-1].T)


def shards(
    tokens, lengths, norm_gain, in_weight, conv_weight, conv_bias, dt_bias, a_log, skip_gain,
    out_gain, out_weight, out_grad,
):
    both = ("fsdp", "seq")
    own = in_weight.shape[0]
    nf = lax.axis_size("fsdp")
    fused = nf % PLANE == 0 and (2 * own) % 16 == 0 and own % 8 == 0
    nz = nf // PLANE if fused else 1
    arrays = {
        "lengths": lengths.T, "tokens": tokens, "out_grad": out_grad, "norm_gain": norm_gain,
        "conv_weight": conv_weight, "conv_bias": conv_bias, "dt_bias": dt_bias, "a_log": a_log,
        "skip_gain": skip_gain, "out_gain": out_gain,
    }
    if fused:
        arrays |= {"in_weight": in_weight, "out_weight": out_weight.T}
        mixed, tgrad, small, grad_in, grad_out = call_mixer(fused, nz, arrays)
    else:
        fill = jnp.zeros((own, AT_X - CX - HEADS), BF)
        sent = jnp.concatenate(
            [in_weight[:, 2 * INNER :], fill, in_weight[:, INNER : 2 * INNER],
             in_weight[:, :INNER], out_weight.T], axis=1)
        arrays["w"] = lax.all_gather(sent, both, axis=0, tiled=True)
        mixed, tgrad, small, wgrad = call_mixer(fused, nz, arrays)
        summed = lax.psum_scatter(wgrad, both, scatter_dimension=0, tiled=True).astype(F32)
        grad_out = summed[:, :INNER]
        grad_in = jnp.concatenate(
            [summed[:, INNER : 3 * INNER], summed[:, 3 * INNER : 3 * INNER + CX + HEADS]], axis=1
        )
        small = lax.psum(small, both)
    return call_place(tokens.shape, lengths.T, mixed, tgrad, small, grad_in, grad_out)


def solution(mesh):
    spread = P(None, "fsdp", "seq", None)
    both = ("fsdp", "seq")
    return jax.shard_map(
        shards,
        mesh=mesh,
        in_specs=(
            spread, P(None, "fsdp"), P(), P(both, None), P(), P(), P(), P(), P(), P(),
            P(None, both), spread,
        ),
        out_specs=(
            spread, spread, P(), P(both, None), P(), P(), P(), P(), P(), P(), P(None, both),
        ),
        check_vma=False,
    )
```
